128 devices in a mesh: seq: 8 (over x_lo, z), fsdp: 16 (over x_hi, y, core).
Axes of the slice: x: 4 (x_hi: 2, x_lo: 2; x = x_hi * 2 + x_lo), y: 4, z: 4, core: 2. Of those that a mesh axis runs over, the one named last changes fastest.
Arguments:
- latent: bfloat16 [16, 1024, 1408], P('fsdp', 'seq'), may hold values from -6 to 6
- skip_input: bfloat16 [16, 1024, 1408], P('fsdp', 'seq'), may hold values from -6 to 6
- text_tokens: bfloat16 [16, 333, 1024], P('fsdp'), may hold values from -6 to 6
- condition: bfloat16 [16, 1408], P('fsdp'), may hold values from -6 to 6
- positions: int32 [1024, 2], P('seq'), may hold values from 0 to 63
- cotangent: bfloat16 [16, 1024, 1408], P('fsdp', 'seq'), may hold values from -6 to 6
- skip_gain: bfloat16 [2816], P('fsdp'), may hold values from 0.5 to 1.5
- skip_shift: bfloat16 [2816], P('fsdp'), may hold values from -2 to 2
- skip_weight: bfloat16 [2816, 1408], P('fsdp'), may hold values from -0.109375 to 0.109375
- skip_bias: bfloat16 [1408], P('fsdp'), may hold values from -2 to 2
- mod_weight: bfloat16 [1408, 1408], P('fsdp'), may hold values from -0.15625 to 0.15625
- mod_bias: bfloat16 [1408], P('fsdp'), may hold values from -2 to 2
- norm1_gain: bfloat16 [1408], P('fsdp'), may hold values from 0.5 to 1.5
- norm1_shift: bfloat16 [1408], P('fsdp'), may hold values from -2 to 2
- qkv_weight: bfloat16 [1408, 4224], P('fsdp'), may hold values from -0.15625 to 0.15625
- qkv_bias: bfloat16 [4224], P('fsdp'), may hold values from -2 to 2
- head_gains: bfloat16 [4, 88], replicated, may hold values from 0.5 to 1.5
- head_shifts: bfloat16 [3, 88], replicated, may hold values from -2 to 2
- attn_weight: bfloat16 [1408, 1408], P('fsdp'), may hold values from -0.3125 to 0.3125
- attn_bias: bfloat16 [1408], P('fsdp'), may hold values from -2 to 2
- norm3_gain: bfloat16 [1408], P('fsdp'), may hold values from 0.5 to 1.5
- norm3_shift: bfloat16 [1408], P('fsdp'), may hold values from -2 to 2
- cross_q_weight: bfloat16 [1408, 1408], P('fsdp'), may hold values from -0.15625 to 0.15625
- cross_q_bias: bfloat16 [1408], P('fsdp'), may hold values from -2 to 2
- cross_kv_weight: bfloat16 [1024, 2816], P('fsdp'), may hold values from -0.1875 to 0.1875
- cross_kv_bias: bfloat16 [2816], P('fsdp'), may hold values from -2 to 2
- cross_weight: bfloat16 [1408, 1408], P('fsdp'), may hold values from -0.3125 to 0.3125
- cross_bias: bfloat16 [1408], P('fsdp'), may hold values from -2 to 2
- norm2_gain: bfloat16 [1408], P('fsdp'), may hold values from 0.5 to 1.5
- norm2_shift: bfloat16 [1408], P('fsdp'), may hold values from -2 to 2
- fc1_weight: bfloat16 [1408, 6144], P('fsdp'), may hold values from -0.15625 to 0.15625
- fc1_bias: bfloat16 [6144], P('fsdp'), may hold values from -2 to 2
- fc2_weight: bfloat16 [6144, 1408], P('fsdp'), may hold values from -0.078125 to 0.078125
- fc2_bias: bfloat16 [1408], P('fsdp'), may hold values from -2 to 2
Outputs:
- layer_out: bfloat16 [16, 1024, 1408], P('fsdp', 'seq')
- latent_grad: bfloat16 [16, 1024, 1408], P('fsdp', 'seq')
- skip_grad: bfloat16 [16, 1024, 1408], P('fsdp', 'seq')
- text_grad: bfloat16 [16, 333, 1024], P('fsdp')
- condition_grad: float32 [16, 1408], P('fsdp')
- skip_gain_grad: float32 [2816], P('fsdp')
- skip_shift_grad: float32 [2816], P('fsdp')
- skip_weight_grad: float32 [2816, 1408], P('fsdp')
- skip_bias_grad: float32 [1408], P('fsdp')
- mod_weight_grad: float32 [1408, 1408], P('fsdp')
- mod_bias_grad: float32 [1408], P('fsdp')
- norm1_gain_grad: float32 [1408], P('fsdp')
- norm1_shift_grad: float32 [1408], P('fsdp')
- qkv_weight_grad: float32 [1408, 4224], P('fsdp')
- qkv_bias_grad: float32 [2816], P('fsdp')
- value_bias_grad: float32 [1408], P('fsdp')
- head_gains_grad: float32 [4, 88], replicated
- head_shifts_grad: float32 [3, 88], replicated
- attn_weight_grad: float32 [1408, 1408], P('fsdp')
- attn_bias_grad: float32 [1408], P('fsdp')
- norm3_gain_grad: float32 [1408], P('fsdp')
- norm3_shift_grad: float32 [1408], P('fsdp')
- cross_q_weight_grad: float32 [1408, 1408], P('fsdp')
- cross_q_bias_grad: float32 [1408], P('fsdp')
- cross_kv_weight_grad: float32 [1024, 2816], P('fsdp')
- cross_kv_bias_grad: float32 [2816], P('fsdp')
- cross_weight_grad: float32 [1408, 1408], P('fsdp')
- cross_bias_grad: float32 [1408], P('fsdp')
- norm2_gain_grad: float32 [1408], P('fsdp')
- norm2_shift_grad: float32 [1408], P('fsdp')
- fc1_weight_grad: float32 [1408, 6144], P('fsdp')
- fc1_bias_grad: float32 [6144], P('fsdp')
- fc2_weight_grad: float32 [6144, 1408], P('fsdp')
- fc2_bias_grad: float32 [1408], P('fsdp')
The draws below stay inside these ranges and needn't reach their ends.
All inputs are finite; a program needn't handle non-finite values.
Results may differ from the reference program's by a relative error of at most 0.03.
Values may be sent and summed in bfloat16 or wider, within the bound.
No kernel may reach another device: no remote copies, remote signals or barrier semaphores. Data moves between devices by JAX's collectives and lax.ppermute only.
A program may use at most 320 MiB of HBM per device.

```python
import math
import jax
import jax.numpy as jnp
from jax import lax

D = 1408
HEADS = 16
HD = 88
FF = 6144
CT = 1024
TXT = 333
SEQ_LEN = 1024
BATCH = 16


def place_ends(entries, rng, least, top_value):
    longest = entries.shape.index(max(entries.shape))
    spots = []
    for shift in (0, 1):
        where = [jax.random.randint(jax.random.fold_in(rng, axis), (), 0, length) for axis, length in enumerate(entries.shape)]
        where[longest] = (where[longest] + shift) % entries.shape[longest]
        spots.append(tuple(where))
    return entries.at[spots[0]].set(least).at[spots[1]].set(top_value)


def steps_of(key, extent, shards, least, high):
    def one(axis_at, blocks):
        draws = jax.random.uniform(jax.random.fold_in(jax.random.fold_in(key, 6), axis_at), (blocks,), jnp.float32, least / len(shards), high / len(shards))
        return jnp.repeat(jnp.exp(draws), extent[axis_at] // blocks).reshape((-1,) + (1,) * (len(extent) - axis_at - 1))

    gain = one(*shards[0])
    for cut in shards[1:]:
        gain = gain * one(*cut)
    return gain


def normal_values(stream_key, extent, deviation, reach, cuts=(), kind=jnp.bfloat16):
    result = deviation * jax.random.normal(stream_key, extent, jnp.float32)
    if cuts:
        result = result * steps_of(stream_key, extent, cuts, -0.22, 0.18)
    return jnp.clip(result, -reach, reach).astype(kind)


def setup_inputs(seed: int = 0) -> dict:
    seeds = jax.random.split(jax.random.key(seed), 35)
    latent = normal_values(seeds[0], (BATCH, SEQ_LEN, D), 1.0, 6.0, ((0, 16), (1, 8)))
    skip_input = normal_values(seeds[1], (BATCH, SEQ_LEN, D), 1.0, 6.0, ((0, 16), (1, 8)))
    text_tokens = normal_values(seeds[2], (BATCH, TXT, CT), 1.0, 6.0, ((0, 16),))
    condition = normal_values(seeds[3], (BATCH, D), 1.0, 6.0, ((0, 16),))
    positions = place_ends(jax.random.randint(seeds[4], (SEQ_LEN, 2), 0, 64), jax.random.fold_in(seeds[4], 1), 0, 63).astype(jnp.int32)
    cotangent = normal_values(seeds[5], (BATCH, SEQ_LEN, D), 1.0, 6.0, ((0, 16), (1, 8)))
    skip_gain = jnp.clip(1.0 + 0.1 * jax.random.normal(seeds[6], (2 * D,), jnp.float32), 0.5, 1.5).astype(jnp.bfloat16)
    skip_shift = normal_values(seeds[7], (2 * D,), 0.3, 2.0, ((0, 16),))
    skip_weight = normal_values(seeds[8], (2 * D, D), (2 * D) ** -0.5, 0.109375, ((0, 16),))
    skip_bias = normal_values(seeds[9], (D,), 0.3, 2.0, ((0, 16),))
    mod_weight = normal_values(seeds[10], (D, D), D ** -0.5, 0.15625, ((0, 16),))
    mod_bias = normal_values(seeds[11], (D,), 0.3, 2.0, ((0, 16),))
    norm1_gain = jnp.clip(1.0 + 0.1 * jax.random.normal(seeds[12], (D,), jnp.float32), 0.5, 1.5).astype(jnp.bfloat16)
    norm1_shift = normal_values(seeds[13], (D,), 0.3, 2.0, ((0, 16),))
    qkv_weight = normal_values(seeds[14], (D, 3 * D), D ** -0.5, 0.15625, ((0, 16),))
    qkv_bias = normal_values(seeds[15], (3 * D,), 0.3, 2.0, ((0, 16),))
    head_gains = jnp.clip(1.0 + 0.1 * jax.random.normal(seeds[16], (4, HD), jnp.float32), 0.5, 1.5).astype(jnp.bfloat16)
    head_shifts = normal_values(seeds[17], (3, HD), 0.3, 2.0)
    attn_weight = normal_values(seeds[18], (D, D), (D // 4) ** -0.5, 0.3125, ((0, 16),))
    attn_bias = normal_values(seeds[19], (D,), 0.3, 2.0, ((0, 16),))
    norm3_gain = jnp.clip(1.0 + 0.1 * jax.random.normal(seeds[20], (D,), jnp.float32), 0.5, 1.5).astype(jnp.bfloat16)
    norm3_shift = normal_values(seeds[21], (D,), 0.3, 2.0, ((0, 16),))
    cross_q_weight = normal_values(seeds[22], (D, D), D ** -0.5, 0.15625, ((0, 16),))
    cross_q_bias = normal_values(seeds[23], (D,), 0.3, 2.0, ((0, 16),))
    cross_kv_weight = normal_values(seeds[24], (CT, 2 * D), CT ** -0.5, 0.1875, ((0, 16),))
    cross_kv_bias = normal_values(seeds[25], (2 * D,), 0.3, 2.0, ((0, 16),))
    cross_weight = normal_values(seeds[26], (D, D), (D // 4) ** -0.5, 0.3125, ((0, 16),))
    cross_bias = normal_values(seeds[27], (D,), 0.3, 2.0, ((0, 16),))
    norm2_gain = jnp.clip(1.0 + 0.1 * jax.random.normal(seeds[28], (D,), jnp.float32), 0.5, 1.5).astype(jnp.bfloat16)
    norm2_shift = normal_values(seeds[29], (D,), 0.3, 2.0, ((0, 16),))
    fc1_weight = normal_values(seeds[30], (D, FF), D ** -0.5, 0.15625, ((0, 16),))
    fc1_bias = normal_values(seeds[31], (FF,), 0.3, 2.0, ((0, 16),))
    fc2_weight = normal_values(seeds[32], (FF, D), FF ** -0.5, 0.078125, ((0, 16),))
    fc2_bias = normal_values(seeds[33], (D,), 0.3, 2.0, ((0, 16),))
    return {"latent": latent, "skip_input": skip_input, "text_tokens": text_tokens, "condition": condition, "positions": positions, "cotangent": cotangent, "skip_gain": skip_gain, "skip_shift": skip_shift, "skip_weight": skip_weight, "skip_bias": skip_bias, "mod_weight": mod_weight, "mod_bias": mod_bias, "norm1_gain": norm1_gain, "norm1_shift": norm1_shift, "qkv_weight": qkv_weight, "qkv_bias": qkv_bias, "head_gains": head_gains, "head_shifts": head_shifts, "attn_weight": attn_weight, "attn_bias": attn_bias, "norm3_gain": norm3_gain, "norm3_shift": norm3_shift, "cross_q_weight": cross_q_weight, "cross_q_bias": cross_q_bias, "cross_kv_weight": cross_kv_weight, "cross_kv_bias": cross_kv_bias, "cross_weight": cross_weight, "cross_bias": cross_bias, "norm2_gain": norm2_gain, "norm2_shift": norm2_shift, "fc1_weight": fc1_weight, "fc1_bias": fc1_bias, "fc2_weight": fc2_weight, "fc2_bias": fc2_bias}


@jax.custom_vjp
def low(v):
    return lax.optimization_barrier(v.astype(jnp.bfloat16)).astype(jnp.float32)

@jax.custom_vjp
def low_back(v):
    return v

def low_keep(v):
    return (low(v), None)

def low_pass(kept, grad):
    return (grad,)

def back_keep(v):
    return (v, None)

def back_low(kept, grad):
    return (low(grad),)
low.defvjp(low_keep, low_pass)
low_back.defvjp(back_keep, back_low)

def matmul(left_side, right_side):
    return jnp.dot(left_side, right_side, precision=lax.Precision.HIGHEST, preferred_element_type=jnp.float32)

def layer_norm(inputs, gain_vector, shift_vector):
    centred = inputs - lax.optimization_barrier(jnp.mean(inputs, -1, keepdims=True))
    variance = lax.optimization_barrier(jnp.mean(centred * centred, -1, keepdims=True))
    return centred * lax.rsqrt(variance + 1e-06) * gain_vector + shift_vector

def rotary_tables(positions, head_dim):
    quarter = head_dim // 4
    exponent = jnp.arange(quarter, dtype=jnp.float32) * (2.0 / (head_dim // 2))
    inverse = jnp.power(jnp.float32(10000.0), -exponent)
    places = positions.astype(jnp.float32)
    angle_rows = places[:, 0:1] * inverse
    angle_cols = places[:, 1:2] * inverse
    return (jnp.cos(angle_rows), jnp.sin(angle_rows), jnp.cos(angle_cols), jnp.sin(angle_cols))

def rotate(inputs, tables):
    cos_rows, sin_rows, cos_cols, sin_cols = tuple((one_table[:, None, :] for one_table in tables))
    quarter = inputs.shape[-1] // 4
    first_a = inputs[..., :quarter]
    first_b = inputs[..., quarter:2 * quarter]
    second_a = inputs[..., 2 * quarter:3 * quarter]
    second_b = inputs[..., 3 * quarter:]
    return jnp.concatenate([first_a * cos_rows - first_b * sin_rows, first_a * sin_rows + first_b * cos_rows, second_a * cos_cols - second_b * sin_cols, second_a * sin_cols + second_b * cos_cols], -1)

def attention(queries, keys_in, values_in):
    score_scale = 1.0 / math.sqrt(HD)

    def one_head(items):
        head_query, head_keys, head_values = items
        raw_scores = low_back(matmul(head_query, head_keys.T))
        probs = jax.nn.softmax(raw_scores * score_scale, axis=-1)
        return matmul(low(probs), head_values)
    mixed = lax.map(jax.checkpoint(one_head), (jnp.swapaxes(queries, 0, 1), jnp.swapaxes(keys_in, 0, 1), jnp.swapaxes(values_in, 0, 1)))
    return jnp.swapaxes(mixed, 0, 1).reshape(queries.shape[0], D)

def layer(latent_row, skip_row, text_row, condition_row, tables, params):
    skip_gain, skip_shift, skip_weight, skip_bias, mod_weight, mod_bias, norm1_gain, norm1_shift, qkv_weight, qkv_bias, head_gains, head_shifts, attn_weight, attn_bias, norm3_gain, norm3_shift, cross_q_weight, cross_q_bias, cross_kv_weight, cross_kv_bias, cross_weight, cross_bias, norm2_gain, norm2_shift, fc1_weight, fc1_bias, fc2_weight, fc2_bias = params
    joined = jnp.concatenate([latent_row, skip_row], -1)
    normed = low(layer_norm(joined, skip_gain, skip_shift))
    stream = low_back(matmul(normed, skip_weight) + skip_bias)
    lifted = low(jax.nn.silu(condition_row)[None, :])
    shift_row = matmul(lifted, mod_weight) + mod_bias
    entry = low(layer_norm(stream, norm1_gain, norm1_shift) + shift_row)
    packed = low_back(matmul(entry, qkv_weight) + qkv_bias)
    query_pre = packed[:, :D].reshape(SEQ_LEN, HEADS, HD)
    key_pre = packed[:, D:2 * D].reshape(SEQ_LEN, HEADS, HD)
    queries = low_back(low(rotate(layer_norm(query_pre, head_gains[0], head_shifts[0]), tables)))
    keys_now = low_back(low(rotate(layer_norm(key_pre, head_gains[1], head_shifts[1]), tables)))
    values_now = low(packed[:, 2 * D:].reshape(SEQ_LEN, HEADS, HD))
    mixed = low_back(low(attention(queries, keys_now, values_now)))
    stream = stream + low_back(matmul(mixed, attn_weight) + attn_bias)
    cross_in = low(layer_norm(stream, norm3_gain, norm3_shift))
    cross_pre = low_back(matmul(cross_in, cross_q_weight) + cross_q_bias).reshape(SEQ_LEN, HEADS, HD)
    cross_queries = low_back(low(rotate(layer_norm(cross_pre, head_gains[2], head_shifts[2]), tables)))
    text_packed = low_back(matmul(text_row, cross_kv_weight) + cross_kv_bias)
    text_keys = low(layer_norm(text_packed[:, :D].reshape(TXT, HEADS, HD), head_gains[3], 0.0))
    text_values = low(text_packed[:, D:].reshape(TXT, HEADS, HD))
    cross_mixed = low_back(low(attention(cross_queries, text_keys, text_values)))
    stream = stream + low_back(matmul(cross_mixed, cross_weight) + cross_bias)
    mlp_in = low(layer_norm(stream, norm2_gain, norm2_shift))
    hidden = low_back(matmul(mlp_in, fc1_weight) + fc1_bias)
    hidden = low(jax.nn.gelu(hidden, approximate=True))
    return stream + low_back(matmul(hidden, fc2_weight) + fc2_bias)

def reference(latent, skip_input, text_tokens, condition, positions, cotangent, skip_gain, skip_shift, skip_weight, skip_bias, mod_weight, mod_bias, norm1_gain, norm1_shift, qkv_weight, qkv_bias, head_gains, head_shifts, attn_weight, attn_bias, norm3_gain, norm3_shift, cross_q_weight, cross_q_bias, cross_kv_weight, cross_kv_bias, cross_weight, cross_bias, norm2_gain, norm2_shift, fc1_weight, fc1_bias, fc2_weight, fc2_bias):
    tables = rotary_tables(positions, HD)
    params = tuple((weight_arg.astype(jnp.float32) for weight_arg in (skip_gain, skip_shift, skip_weight, skip_bias, mod_weight, mod_bias, norm1_gain, norm1_shift, qkv_weight, qkv_bias, head_gains, head_shifts, attn_weight, attn_bias, norm3_gain, norm3_shift, cross_q_weight, cross_q_bias, cross_kv_weight, cross_kv_bias, cross_weight, cross_bias, norm2_gain, norm2_shift, fc1_weight, fc1_bias, fc2_weight, fc2_bias)))

    def forward(latent_all, skip_all, text_all, condition_all, params_all):
        return lax.map(lambda items: layer(items[0], items[1], items[2], items[3], tables, params_all), (latent_all, skip_all, text_all, condition_all))
    layer_out, pull_back = jax.vjp(forward, latent.astype(jnp.float32), skip_input.astype(jnp.float32), text_tokens.astype(jnp.float32), condition.astype(jnp.float32), params)
    latent_grad, skip_grad, text_grad, condition_grad, param_grads = pull_back(cotangent.astype(jnp.float32))
    packed_bias_grad = param_grads[9]
    return (layer_out.astype(jnp.bfloat16), latent_grad.astype(jnp.bfloat16), skip_grad.astype(jnp.bfloat16), text_grad.astype(jnp.bfloat16), condition_grad, param_grads[0], param_grads[1], param_grads[2], param_grads[3], param_grads[4], param_grads[5], param_grads[6], param_grads[7], param_grads[8], packed_bias_grad[:2 * D], packed_bias_grad[2 * D:], param_grads[10], param_grads[11], param_grads[12], param_grads[13], param_grads[14], param_grads[15], param_grads[16], param_grads[17], param_grads[18], param_grads[19], param_grads[20], param_grads[21], param_grads[22], param_grads[23], param_grads[24], param_grads[25], param_grads[26], param_grads[27])
```

```python
import functools
import math

import jax
import jax.numpy as jnp
from jax import lax
from jax.experimental import pallas as pl
from jax.experimental.pallas import tpu as pltpu
from jax.sharding import PartitionSpec as P


def layer_norm(inputs, gain_vector, shift_vector):
    centred = inputs - jnp.mean(inputs, -1, keepdims=True)
    variance = jnp.mean(centred * centred, -1, keepdims=True)
    return centred * lax.rsqrt(variance + 1e-06) * gain_vector + shift_vector


def rotary_tables(positions, head_dim):
    quarter = head_dim // 4
    exponent = jnp.arange(quarter, dtype=jnp.float32) * (2.0 / (head_dim // 2))
    inverse = jnp.power(jnp.float32(10000.0), -exponent)
    places = positions.astype(jnp.float32)
    angle_rows = places[:, 0:1] * inverse
    angle_cols = places[:, 1:2] * inverse
    return (jnp.cos(angle_rows), jnp.sin(angle_rows), jnp.cos(angle_cols), jnp.sin(angle_cols))


def rotate(inputs, tables):
    cos_rows, sin_rows, cos_cols, sin_cols = tuple((one_table[:, None, :] for one_table in tables))
    quarter = inputs.shape[-1] // 4
    first_a = inputs[..., :quarter]
    first_b = inputs[..., quarter : 2 * quarter]
    second_a = inputs[..., 2 * quarter : 3 * quarter]
    second_b = inputs[..., 3 * quarter :]
    return jnp.concatenate(
        [
            first_a * cos_rows - first_b * sin_rows,
            first_a * sin_rows + first_b * cos_rows,
            second_a * cos_cols - second_b * sin_cols,
            second_a * sin_cols + second_b * cos_cols,
        ],
        -1,
    )


def head_norm(inputs, gain_vector, shift_vector, head_dim):
    row_count = inputs.shape[0]
    shaped = inputs.reshape(row_count, -1, head_dim)
    return layer_norm(shaped, gain_vector, shift_vector).reshape(row_count, -1)


def head_rotary(inputs, gain_vector, shift_vector, tables, head_dim):
    row_count = inputs.shape[0]
    shaped = inputs.reshape(row_count, -1, head_dim)
    return rotate(layer_norm(shaped, gain_vector, shift_vector), tables).reshape(row_count, -1)


def matmul(left_side, right_side):
    return jnp.dot(left_side, right_side, preferred_element_type=jnp.float32)


def contract_rows(left_side, right_side):
    return lax.dot_general(
        left_side, right_side, (((0,), (0,)), ((), ())), preferred_element_type=jnp.float32
    )


def contract_cols(left_side, right_side):
    return lax.dot_general(
        left_side, right_side, (((1,), (1,)), ((), ())), preferred_element_type=jnp.float32
    )


def column_sums(grads_low):
    return jnp.sum(grads_low.astype(jnp.float32), 0)


def to_float(vectors):
    return tuple((one_vector.astype(jnp.float32) for one_vector in vectors))


def forward_kernel(query_ref, keys_ref, values_ref, mixed_ref, totals_ref, *, scale, valid):
    scores = contract_cols(query_ref[0], keys_ref[0]) * scale
    if valid < scores.shape[1]:
        column = lax.broadcasted_iota(jnp.int32, scores.shape, 1)
        scores = jnp.where(column < valid, scores, -1e30)
    row_top = jnp.max(scores, -1, keepdims=True)
    weights = jnp.exp(scores - row_top)
    totals = jnp.sum(weights, -1, keepdims=True)
    probs = (weights * (1.0 / totals)).astype(jnp.bfloat16)
    mixed_ref[0] = matmul(probs, values_ref[0]).astype(mixed_ref.dtype)
    totals_ref[0] = row_top + jnp.log(totals)


def attend(queries, keys_in, values_in, valid):
    heads, row_count, head_dim = queries.shape
    key_count = keys_in.shape[1]
    block_rows = min(512, row_count)
    rows_spec = pl.BlockSpec((1, block_rows, head_dim), lambda h, i: (h, i, 0))
    keys_spec = pl.BlockSpec((1, key_count, head_dim), lambda h, i: (h, 0, 0))
    return pl.pallas_call(
        functools.partial(forward_kernel, scale=1.0 / math.sqrt(head_dim), valid=valid),
        grid=(heads, row_count // block_rows),
        in_specs=[rows_spec, keys_spec, keys_spec],
        out_specs=[rows_spec, pl.BlockSpec((1, block_rows, 1), lambda h, i: (h, i, 0))],
        out_shape=[
            jax.ShapeDtypeStruct(queries.shape, jnp.bfloat16),
            jax.ShapeDtypeStruct((heads, row_count, 1), jnp.float32),
        ],
        compiler_params=pltpu.CompilerParams(vmem_limit_bytes=40 * 1024 * 1024),
        cost_estimate=pl.CostEstimate(
            flops=4 * heads * row_count * key_count * head_dim,
            bytes_accessed=4 * heads * (row_count + key_count) * head_dim,
            transcendentals=heads * row_count * key_count,
        ),
        name="attend",
    )(queries, keys_in, values_in)


def backward_kernel(
    query_ref,
    keys_ref,
    values_ref,
    totals_ref,
    grad_ref,
    query_grad_ref,
    keys_grad_ref,
    values_grad_ref,
    *,
    scale,
    valid,
):
    query_block = query_ref[0]
    grad_block = grad_ref[0]
    keys_now = keys_ref[0]
    probs = jnp.exp(contract_cols(query_block, keys_now) * scale - totals_ref[0])
    if valid < probs.shape[1]:
        column = lax.broadcasted_iota(jnp.int32, probs.shape, 1)
        probs = jnp.where(column < valid, probs, 0.0)
    weighted = probs * contract_cols(grad_block, values_ref[0])
    scores_grad = weighted - probs * jnp.sum(weighted, -1, keepdims=True)
    scores_low = (scores_grad * scale).astype(jnp.bfloat16)
    query_grad_ref[0] = matmul(scores_low, keys_now).astype(query_grad_ref.dtype)
    keys_part = contract_rows(scores_low, query_block)
    values_part = contract_rows(probs.astype(jnp.bfloat16), grad_block)

    @pl.when(pl.program_id(1) == 0)
    def _():
        keys_grad_ref[0] = keys_part
        values_grad_ref[0] = values_part

    @pl.when(pl.program_id(1) != 0)
    def _():
        keys_grad_ref[0] += keys_part
        values_grad_ref[0] += values_part


def attend_back(queries, keys_in, values_in, totals, grad_out, valid):
    heads, row_count, head_dim = queries.shape
    key_count = keys_in.shape[1]
    block_rows = min(512, row_count)
    rows_spec = pl.BlockSpec((1, block_rows, head_dim), lambda h, i: (h, i, 0))
    keys_spec = pl.BlockSpec((1, key_count, head_dim), lambda h, i: (h, 0, 0))
    totals_spec = pl.BlockSpec((1, block_rows, 1), lambda h, i: (h, i, 0))
    return pl.pallas_call(
        functools.partial(backward_kernel, scale=1.0 / math.sqrt(head_dim), valid=valid),
        grid=(heads, row_count // block_rows),
        in_specs=[rows_spec, keys_spec, keys_spec, totals_spec, rows_spec],
        out_specs=[rows_spec, keys_spec, keys_spec],
        out_shape=[
            jax.ShapeDtypeStruct(queries.shape, jnp.bfloat16),
            jax.ShapeDtypeStruct(keys_in.shape, jnp.float32),
            jax.ShapeDtypeStruct(keys_in.shape, jnp.float32),
        ],
        compiler_params=pltpu.CompilerParams(vmem_limit_bytes=40 * 1024 * 1024),
        cost_estimate=pl.CostEstimate(
            flops=10 * heads * row_count * key_count * head_dim,
            bytes_accessed=8 * heads * (row_count + key_count) * head_dim,
            transcendentals=heads * row_count * key_count,
        ),
        name="attend_back",
    )(queries, keys_in, values_in, totals, grad_out)


def swap(blocks, axis_name):
    return lax.all_to_all(blocks, axis_name, split_axis=0, concat_axis=0, tiled=True)


def spread(part, axis_name):
    size = lax.axis_size(axis_name)
    return swap(jnp.broadcast_to(part[None], (size,) + part.shape), axis_name)


def gather_tokens(part):
    blocks = spread(part, "seq")
    return blocks.reshape((-1,) + part.shape[1:])


def sum_tokens(partial):
    size = lax.axis_size("seq")
    blocks = partial.astype(jnp.bfloat16).reshape((size, -1) + partial.shape[1:])
    return jnp.sum(swap(blocks, "seq").astype(jnp.float32), 0)


def column_blocks(values):
    size = lax.axis_size("seq")
    rows = values.shape[0]
    return values.reshape(rows, size, -1).transpose(1, 0, 2)


def own_columns(weight, groups, size, place):
    rows = weight.shape[0]
    parts = weight.reshape(rows, groups, size, -1)
    taken = lax.dynamic_slice_in_dim(parts, place, 1, 2)
    return taken.reshape(rows, -1)


def heads_first(values, head_dim):
    rows = values.shape[0]
    return values.reshape(rows, -1, head_dim).transpose(1, 0, 2)


def heads_last(values):
    return values.transpose(1, 0, 2).reshape(values.shape[1], -1)


def local(
    latent,
    skip_input,
    text_tokens,
    condition,
    positions,
    cotangent,
    skip_gain,
    skip_shift,
    skip_weight,
    skip_bias,
    mod_weight,
    mod_bias,
    norm1_gain,
    norm1_shift,
    qkv_weight,
    qkv_bias,
    head_gains,
    head_shifts,
    attn_weight,
    attn_bias,
    norm3_gain,
    norm3_shift,
    cross_q_weight,
    cross_q_bias,
    cross_kv_weight,
    cross_kv_bias,
    cross_weight,
    cross_bias,
    norm2_gain,
    norm2_shift,
    fc1_weight,
    fc1_bias,
    fc2_weight,
    fc2_bias,
):
    ways = lax.axis_size("seq")
    owners = lax.axis_size("fsdp")
    place = lax.axis_index("seq")
    head_dim = head_gains.shape[1]
    tokens, model_width = latent.shape[1:]
    width = model_width // ways
    low = jnp.bfloat16
    gain_table = head_gains.astype(jnp.float32)
    shift_table = head_shifts.astype(jnp.float32)
    tables = rotary_tables(positions, head_dim)

    half = skip_weight.shape[0] // 2
    own_rows = model_width // owners
    packed_own = own_columns(qkv_weight, 3, ways, place)
    packed_pad = -packed_own.shape[1] % 128
    text_own = own_columns(cross_kv_weight, 2, ways, place)
    text_cols = text_own.size // own_rows
    first_own = jnp.concatenate(
        [
            skip_weight[:half],
            skip_weight[half:],
            jnp.pad(packed_own, ((0, 0), (0, packed_pad))),
            text_own.reshape(own_rows, text_cols),
        ],
        1,
    )
    first_rows = lax.all_gather(first_own, "fsdp", axis=0, tiled=True)
    second_own = jnp.concatenate([attn_weight, cross_q_weight, cross_weight], 1)
    second_rows = lax.all_gather(second_own, "fsdp", axis=0, tiled=True)
    unit_rows = fc2_weight.shape[0] // ways
    down_own = lax.dynamic_slice_in_dim(fc2_weight, place * unit_rows, unit_rows, 0)
    up_own = own_columns(fc1_weight, owners, ways, place)
    units = up_own.shape[1]
    third_own = jnp.concatenate([up_own, down_own.reshape(own_rows, units)], 1)
    third_rows = lax.all_gather(third_own, "fsdp", axis=0, tiled=True)
    sk_first = first_rows[:, :model_width]
    sk_second = first_rows[:, model_width : 2 * model_width]
    pk_weight = first_rows[:, 2 * model_width : 2 * model_width + 3 * width]
    kv_weight = first_rows[:, 2 * model_width + 3 * width + packed_pad :].reshape(-1, 2 * width)
    at_weight = second_rows[:, :model_width]
    cq_weight = second_rows[:, model_width : 2 * model_width]
    cr_weight = second_rows[:, 2 * model_width :]
    up_weight = third_rows[:, :units]
    down_weight = third_rows[:, units:].reshape(units, model_width)

    lifted_f, silu_pull = jax.vjp(jax.nn.silu, condition.astype(jnp.float32))
    lifted = lifted_f.astype(low)
    vectors = (
        skip_gain,
        skip_shift,
        skip_bias,
        mod_bias,
        norm1_gain,
        norm1_shift,
        qkv_bias,
        attn_bias,
        norm3_gain,
        norm3_shift,
        cross_q_bias,
        cross_kv_bias,
        cross_bias,
        norm2_gain,
        norm2_shift,
        fc1_bias,
        fc2_bias,
    )
    vector_own = jnp.concatenate(vectors)
    vector_all = swap(
        jnp.concatenate(
            [
                jnp.broadcast_to(vector_own[None], (owners, vector_own.shape[0])),
                lifted.reshape(owners, own_rows),
            ],
            1,
        ),
        "fsdp",
    )
    pieces = []
    start = 0
    for one_vector in vectors:
        size = one_vector.shape[0]
        pieces.append(vector_all[:, start : start + size].reshape(-1).astype(jnp.float32))
        start += size
    lifted_own = vector_all[:, start:]
    (
        sk_gain,
        sk_shift,
        sk_bias,
        md_bias,
        one_gain,
        one_shift,
        pk_bias,
        at_bias,
        three_gain,
        three_shift,
        cq_bias,
        kv_bias,
        cr_bias,
        two_gain,
        two_shift,
        up_bias,
        down_bias,
    ) = pieces
    pk_bias_own = own_columns(pk_bias[None], 3, ways, place)[0]
    kv_bias_own = own_columns(kv_bias[None], 2, ways, place)[0]
    up_bias_own = own_columns(up_bias[None], owners, ways, place)[0]
    shift_row = (
        jnp.sum(swap(matmul(lifted_own, mod_weight), "fsdp"), 0, keepdims=True) + md_bias
    )
    places_all = gather_tokens(positions.astype(jnp.float32))
    tables_all = rotary_tables(places_all, head_dim)

    joined = jnp.concatenate([latent[0], skip_input[0]], 1).astype(jnp.float32)
    normed_f, skip_pull = jax.vjp(layer_norm, joined, sk_gain, sk_shift)
    normed = normed_f.astype(low)
    normed_halves = normed.reshape(tokens, owners, 2, half).transpose(2, 0, 1, 3)
    normed_halves = normed_halves.reshape(2, tokens, model_width)
    stream_zero = (
        matmul(normed_halves[0], sk_first) + matmul(normed_halves[1], sk_second) + sk_bias
    )
    normed_all = gather_tokens(normed)
    entry_f, one_pull = jax.vjp(layer_norm, stream_zero, one_gain, one_shift)
    entry = (entry_f + shift_row).astype(low)

    entry_all = gather_tokens(entry)
    packed = matmul(entry_all, pk_weight) + pk_bias_own

    def prepare(query_pre, key_pre, gains_in, shifts_in):
        return (
            head_rotary(query_pre, gains_in[0], shifts_in[0], tables_all, head_dim),
            head_rotary(key_pre, gains_in[1], shifts_in[1], tables_all, head_dim),
        )

    (query_f, key_f), prep_pull = jax.vjp(
        prepare, packed[:, :width], packed[:, width : 2 * width], gain_table, shift_table
    )
    query_h = heads_first(query_f.astype(low), head_dim)
    key_h = heads_first(key_f.astype(low), head_dim)
    value_h = heads_first(packed[:, 2 * width :].astype(low), head_dim)
    all_tokens = query_h.shape[1]
    mixed_h, self_totals = attend(query_h, key_h, value_h, all_tokens)

    def to_heads(values):
        return swap(column_blocks(values), "seq").reshape(all_tokens, -1)

    def to_tokens(values_h):
        blocks = swap(heads_last(values_h).reshape(ways, tokens, width), "seq")
        return blocks.transpose(1, 0, 2).reshape(tokens, model_width)

    mixed = to_tokens(mixed_h)
    stream_one = stream_zero + matmul(mixed, at_weight) + at_bias
    mixed_all = gather_tokens(mixed)

    cross_in_f, three_pull = jax.vjp(layer_norm, stream_one, three_gain, three_shift)
    cross_in = cross_in_f.astype(low)
    cross_pre = matmul(cross_in, cq_weight) + cq_bias
    cross_query_f, cq_pull = jax.vjp(
        lambda values_in, gains_in, shifts_in: head_rotary(
            values_in, gains_in[2], shifts_in[2], tables, head_dim
        ),
        cross_pre,
        gain_table,
        shift_table,
    )
    cross_query_h = heads_first(to_heads(cross_query_f.astype(low)), head_dim)
    cross_in_all = gather_tokens(cross_in)
    text_now = text_tokens[0]
    text_count = text_now.shape[0]
    text_packed = matmul(text_now, kv_weight) + kv_bias_own
    text_keys_f, tk_pull = jax.vjp(
        lambda values_in, gains_in: head_norm(values_in, gains_in[3], 0.0, head_dim),
        text_packed[:, :width],
        gain_table,
    )
    text_pad = ((0, 0), (0, -text_count % 128), (0, 0))
    text_keys = jnp.pad(heads_first(text_keys_f.astype(low), head_dim), text_pad)
    text_values = jnp.pad(heads_first(text_packed[:, width:].astype(low), head_dim), text_pad)
    cross_h, cross_totals = attend(cross_query_h, text_keys, text_values, text_count)
    cross_mixed = to_tokens(cross_h)
    stream_two = stream_one + matmul(cross_mixed, cr_weight) + cr_bias
    cross_mixed_all = gather_tokens(cross_mixed)

    mlp_in_f, two_pull = jax.vjp(layer_norm, stream_two, two_gain, two_shift)
    mlp_all = gather_tokens(mlp_in_f.astype(low))
    hidden_pre = matmul(mlp_all, up_weight) + up_bias_own
    hidden_f, gelu_pull = jax.vjp(
        lambda values_in: jax.nn.gelu(values_in, approximate=True), hidden_pre
    )
    hidden = hidden_f.astype(low)
    stream_three = stream_two + sum_tokens(matmul(hidden, down_weight)) + down_bias
    layer_out = stream_three.astype(low)[None]
    grad_all = gather_tokens(cotangent[0])
    grad_three = cotangent[0].astype(jnp.float32)
    down_bias_grad = column_sums(cotangent[0])
    pre_grad = gelu_pull(contract_cols(grad_all, down_weight))[0].astype(low)
    up_bias_grad = column_sums(pre_grad)
    stream_part, two_gain_grad, two_shift_grad = two_pull(
        sum_tokens(contract_cols(pre_grad, up_weight))
    )
    stream_grad = grad_three + stream_part
    down_grad = contract_rows(hidden, grad_all)
    up_grad = contract_rows(mlp_all, pre_grad)

    def settle(parts):
        joined_parts = jnp.concatenate(
            [part.astype(low).reshape(owners, own_rows, -1) for part in parts], 2
        )
        return lax.psum_scatter(joined_parts, "fsdp", scatter_dimension=0, tiled=False)

    mlp_owned = settle((up_grad, down_grad))

    grad_low = stream_grad.astype(low)
    cr_bias_grad = column_sums(grad_low)
    cross_mixed_grad = contract_cols(grad_low, cr_weight).astype(low)

    def to_heads_many(parts):
        blocks = swap(jnp.stack([column_blocks(part) for part in parts], 1), "seq")
        return [blocks[:, i].reshape(all_tokens, width) for i in range(len(parts))]

    grad_cols, cross_grad = to_heads_many((grad_low, cross_mixed_grad))
    cross_query_grad_h, text_key_grad, text_value_grad = attend_back(
        cross_query_h,
        text_keys,
        text_values,
        cross_totals,
        heads_first(cross_grad, head_dim),
        text_count,
    )
    cross_query_grad = to_tokens(cross_query_grad_h)
    cr_weight_grad = contract_rows(cross_mixed_all, grad_cols)
    cross_pre_grad, gains_from_cross, shifts_from_cross = cq_pull(
        cross_query_grad.astype(jnp.float32)
    )
    cross_pre_low = cross_pre_grad.astype(low)
    cq_bias_grad = column_sums(cross_pre_low)
    stream_part, three_gain_grad, three_shift_grad = three_pull(
        contract_cols(cross_pre_low, cq_weight)
    )
    stream_grad = stream_grad + stream_part
    key_pre_grad, gains_from_text = tk_pull(heads_last(text_key_grad)[:text_count])
    text_grad_low = jnp.concatenate(
        [key_pre_grad.astype(low), heads_last(text_value_grad)[:text_count].astype(low)], 1
    )
    kv_weight_grad = contract_rows(text_now, text_grad_low)
    kv_bias_grad = column_sums(text_grad_low)
    text_part = contract_cols(text_grad_low, kv_weight)
    text_total = lax.psum(text_part.astype(low), "seq")

    grad_low = stream_grad.astype(low)
    at_bias_grad = column_sums(grad_low)
    mixed_grad = contract_cols(grad_low, at_weight).astype(low)
    grad_cols, cross_cols, mixed_back = to_heads_many((grad_low, cross_pre_low, mixed_grad))
    query_grad, key_grad, value_grad = attend_back(
        query_h, key_h, value_h, self_totals, heads_first(mixed_back, head_dim), all_tokens
    )
    at_weight_grad = contract_rows(mixed_all, grad_cols)
    cq_weight_grad = contract_rows(cross_in_all, cross_cols)
    cross_owned = settle((cr_weight_grad, cq_weight_grad, at_weight_grad, kv_weight_grad))
    query_pre_grad, key_pre_grad2, gains_from_self, shifts_from_self = prep_pull(
        (
            heads_last(query_grad).astype(jnp.float32),
            heads_last(key_grad).astype(low).astype(jnp.float32),
        )
    )
    packed_grad = jnp.concatenate(
        [
            query_pre_grad.astype(low),
            key_pre_grad2.astype(low),
            heads_last(value_grad).astype(low),
        ],
        1,
    )
    entry_grad = sum_tokens(contract_cols(packed_grad, pk_weight))
    pk_weight_grad = contract_rows(entry_all, packed_grad)
    pk_bias_grad = column_sums(packed_grad)
    shift_part = jnp.sum(entry_grad, 0)
    stream_part, one_gain_grad, one_shift_grad = one_pull(entry_grad)
    stream_grad = stream_grad + stream_part

    grad_low = stream_grad.astype(low)
    sk_bias_grad = column_sums(grad_low)
    grad_cols = to_heads(grad_low)
    sk_weight_grad = contract_rows(normed_all, grad_cols)
    joined_halves = jnp.stack(
        [contract_cols(grad_low, sk_first), contract_cols(grad_low, sk_second)]
    )
    joined_pre = joined_halves.reshape(2, tokens, owners, half).transpose(1, 2, 0, 3)
    joined_grad, sk_gain_grad, sk_shift_grad = skip_pull(
        joined_pre.reshape(tokens, 2 * model_width)
    )

    def placed(own, groups):
        parts = jnp.zeros((groups, ways, own.shape[0] // groups), jnp.float32)
        parts = lax.dynamic_update_slice_in_dim(parts, own.reshape(groups, 1, -1), place, 1)
        return parts.reshape(-1)

    vector_grads = (
        sk_gain_grad,
        sk_shift_grad,
        sk_bias_grad,
        one_gain_grad,
        one_shift_grad,
        placed(pk_bias_grad, 3),
        at_bias_grad,
        three_gain_grad,
        three_shift_grad,
        cq_bias_grad,
        placed(kv_bias_grad, 2),
        cr_bias_grad,
        two_gain_grad,
        two_shift_grad,
        placed(up_bias_grad, owners),
        down_bias_grad,
    )
    table_grads = jnp.concatenate(
        [
            (gains_from_cross + gains_from_text + gains_from_self).reshape(-1),
            (shifts_from_cross + shifts_from_self).reshape(-1),
        ]
    )
    split_three = [part.reshape(owners, -1) for part in vector_grads]
    pk_at = 5
    pk_thirds = placed(pk_bias_grad, 3).reshape(3, model_width)
    split_three[pk_at : pk_at + 1] = [
        pk_thirds[:2].reshape(owners, -1),
        pk_thirds[2].reshape(owners, -1),
    ]
    split_three.append(jnp.broadcast_to(table_grads[None], (owners, table_grads.shape[0])))
    summed_sizes = [part.shape[1] for part in split_three]
    tail_parts = [
        sk_weight_grad.reshape(owners, -1),
        pk_weight_grad.reshape(owners, -1),
        *split_three,
        jnp.broadcast_to(shift_part[None], (owners, model_width)),
    ]
    tail_blocks = swap(jnp.concatenate([part.astype(low) for part in tail_parts], 1), "fsdp")
    summed = jnp.sum(tail_blocks[:, :-model_width].astype(jnp.float32), 0)
    tail_own = jnp.concatenate(
        [summed.astype(low), tail_blocks[:, -model_width:].reshape(-1)]
    )
    tail_all = spread(tail_own, "seq")
    sk_size = sk_weight_grad.size // owners
    pk_size = pk_weight_grad.size // owners
    sk_owned = tail_all[:, :sk_size].reshape(ways, -1, width)
    pk_owned = tail_all[:, sk_size : sk_size + pk_size].reshape(ways, own_rows, 3, width)
    tail_small = tail_all[:, sk_size + pk_size :].astype(jnp.float32)
    small_total = jnp.sum(tail_small, 0)
    vector_totals = []
    start = 0
    for size in summed_sizes:
        vector_totals.append(small_total[start : start + size])
        start += size
    table_total = vector_totals.pop()
    gains_total = table_total[: gain_table.size].reshape(gain_table.shape)
    shifts_total = table_total[gain_table.size :].reshape(shift_table.shape)
    shift_total = small_total[start:].reshape(owners, model_width)
    md_weight_grad = lax.dot_general(
        lifted_own.astype(jnp.float32),
        shift_total,
        (((0,), (0,)), ((), ())),
        precision=lax.Precision.HIGHEST,
        preferred_element_type=jnp.float32,
    )
    md_bias_grad = lax.dynamic_slice_in_dim(
        jnp.sum(shift_total, 0), lax.axis_index("fsdp") * own_rows, own_rows, 0
    )
    lifted_part = lax.dot_general(
        shift_total,
        mod_weight.astype(jnp.float32),
        (((1,), (1,)), ((), ())),
        precision=lax.Precision.HIGHEST,
        preferred_element_type=jnp.float32,
    )
    lifted_grad = swap(lifted_part, "fsdp").reshape(1, model_width)
    condition_grad = silu_pull(lifted_grad)[0]

    owned = lax.all_gather(
        jnp.concatenate([mlp_owned, cross_owned], 1), "seq", axis=0, tiled=False
    ).astype(jnp.float32)
    up_owned = owned[:, :, :units].reshape(ways, own_rows, owners, -1)
    up_total = up_owned.transpose(1, 2, 0, 3).reshape(own_rows, -1)
    down_total = owned[:, :, units : 2 * units].reshape(-1, model_width)

    def beside(blocks):
        return blocks.astype(jnp.float32).transpose(1, 0, 2).reshape(blocks.shape[1], -1)

    start = 2 * units
    cr_total = beside(owned[:, :, start : start + width])
    cq_total = beside(owned[:, :, start + width : start + 2 * width])
    at_total = beside(owned[:, :, start + 2 * width : start + 3 * width])
    kv_owned = owned[:, :, start + 3 * width :].reshape(ways, -1, 2, width)
    kv_total = kv_owned.transpose(1, 2, 0, 3).reshape(kv_owned.shape[1], -1)
    sk_total = beside(sk_owned)
    pk_total = pk_owned.astype(jnp.float32).transpose(1, 2, 0, 3).reshape(own_rows, -1)
    (
        sk_gain_total,
        sk_shift_total,
        sk_bias_total,
        one_gain_total,
        one_shift_total,
        pk_bias_total,
        value_bias_total,
        at_bias_total,
        three_gain_total,
        three_shift_total,
        cq_bias_total,
        kv_bias_total,
        cr_bias_total,
        two_gain_total,
        two_shift_total,
        up_bias_total,
        down_bias_total,
    ) = vector_totals
    return (
        layer_out,
        joined_grad[:, :model_width].astype(low)[None],
        joined_grad[:, model_width:].astype(low)[None],
        text_total[None],
        condition_grad,
        sk_gain_total,
        sk_shift_total,
        sk_total,
        sk_bias_total,
        md_weight_grad,
        md_bias_grad,
        one_gain_total,
        one_shift_total,
        pk_total,
        pk_bias_total,
        value_bias_total,
        gains_total,
        shifts_total,
        at_total,
        at_bias_total,
        three_gain_total,
        three_shift_total,
        cq_total,
        cq_bias_total,
        kv_total,
        kv_bias_total,
        cr_total,
        cr_bias_total,
        two_gain_total,
        two_shift_total,
        up_total,
        up_bias_total,
        down_total,
        down_bias_total,
    )


def solution(mesh):
    in_specs = (
        P("fsdp", "seq", None),
        P("fsdp", "seq", None),
        P("fsdp", None, None),
        P("fsdp", None),
        P("seq", None),
        P("fsdp", "seq", None),
        P("fsdp"),
        P("fsdp"),
        P("fsdp", None),
        P("fsdp"),
        P("fsdp", None),
        P("fsdp"),
        P("fsdp"),
        P("fsdp"),
        P("fsdp", None),
        P("fsdp"),
        P(),
        P(),
        P("fsdp", None),
        P("fsdp"),
        P("fsdp"),
        P("fsdp"),
        P("fsdp", None),
        P("fsdp"),
        P("fsdp", None),
        P("fsdp"),
        P("fsdp", None),
        P("fsdp"),
        P("fsdp"),
        P("fsdp"),
        P("fsdp", None),
        P("fsdp"),
        P("fsdp", None),
        P("fsdp"),
    )
    out_specs = (
        P("fsdp", "seq", None),
        P("fsdp", "seq", None),
        P("fsdp", "seq", None),
        P("fsdp", None, None),
        P("fsdp", None),
        P("fsdp"),
        P("fsdp"),
        P("fsdp", None),
        P("fsdp"),
        P("fsdp", None),
        P("fsdp"),
        P("fsdp"),
        P("fsdp"),
        P("fsdp", None),
        P("fsdp"),
        P("fsdp"),
        P(),
        P(),
        P("fsdp", None),
        P("fsdp"),
        P("fsdp"),
        P("fsdp"),
        P("fsdp", None),
        P("fsdp"),
        P("fsdp", None),
        P("fsdp"),
        P("fsdp", None),
        P("fsdp"),
        P("fsdp"),
        P("fsdp"),
        P("fsdp", None),
        P("fsdp"),
        P("fsdp", None),
        P("fsdp"),
    )
    return jax.shard_map(local, mesh=mesh, in_specs=in_specs, out_specs=out_specs, check_vma=False)
```

```python
import functools
import math

import jax
import jax.numpy as jnp
from jax import lax
from jax.experimental import pallas as pl
from jax.experimental.pallas import tpu as pltpu
from jax.sharding import PartitionSpec as P


def layer_norm(inputs, gain_vector, shift_vector):
    centred = inputs - jnp.mean(inputs, -1, keepdims=True)
    variance = jnp.mean(centred * centred, -1, keepdims=True)
    return centred * lax.rsqrt(variance + 1e-06) * gain_vector + shift_vector


def rotary_tables(positions, head_dim):
    quarter = head_dim // 4
    exponent = jnp.arange(quarter, dtype=jnp.float32) * (2.0 / (head_dim // 2))
    inverse = jnp.power(jnp.float32(10000.0), -exponent)
    places = positions.astype(jnp.float32)
    angle_rows = places[:, 0:1] * inverse
    angle_cols = places[:, 1:2] * inverse
    return (jnp.cos(angle_rows), jnp.sin(angle_rows), jnp.cos(angle_cols), jnp.sin(angle_cols))


def rotate(inputs, tables):
    cos_rows, sin_rows, cos_cols, sin_cols = tuple((one_table[:, None, :] for one_table in tables))
    quarter = inputs.shape[-1] // 4
    first_a = inputs[..., :quarter]
    first_b = inputs[..., quarter : 2 * quarter]
    second_a = inputs[..., 2 * quarter : 3 * quarter]
    second_b = inputs[..., 3 * quarter :]
    return jnp.concatenate(
        [
            first_a * cos_rows - first_b * sin_rows,
            first_a * sin_rows + first_b * cos_rows,
            second_a * cos_cols - second_b * sin_cols,
            second_a * sin_cols + second_b * cos_cols,
        ],
        -1,
    )


def head_norm(inputs, gain_vector, shift_vector, head_dim):
    row_count = inputs.shape[0]
    shaped = inputs.reshape(row_count, -1, head_dim)
    return layer_norm(shaped, gain_vector, shift_vector).reshape(row_count, -1)


def head_rotary(inputs, gain_vector, shift_vector, tables, head_dim):
    row_count = inputs.shape[0]
    shaped = inputs.reshape(row_count, -1, head_dim)
    return rotate(layer_norm(shaped, gain_vector, shift_vector), tables).reshape(row_count, -1)


def matmul(left_side, right_side):
    return jnp.dot(left_side, right_side, preferred_element_type=jnp.float32)


def contract_rows(left_side, right_side):
    return lax.dot_general(
        left_side, right_side, (((0,), (0,)), ((), ())), preferred_element_type=jnp.float32
    )


def contract_cols(left_side, right_side):
    return lax.dot_general(
        left_side, right_side, (((1,), (1,)), ((), ())), preferred_element_type=jnp.float32
    )


def column_sums(grads_low):
    return jnp.sum(grads_low.astype(jnp.float32), 0)


def to_float(vectors):
    return tuple((one_vector.astype(jnp.float32) for one_vector in vectors))


def forward_kernel(query_ref, keys_ref, values_ref, mixed_ref, totals_ref, *, scale, valid):
    for head in range(query_ref.shape[0]):
        scores = contract_cols(query_ref[head], keys_ref[head]) * scale
        if valid < scores.shape[1]:
            column = lax.broadcasted_iota(jnp.int32, scores.shape, 1)
            scores = jnp.where(column < valid, scores, -1e30)
        row_top = jnp.max(scores, -1, keepdims=True)
        weights = jnp.exp(scores - row_top)
        totals = jnp.sum(weights, -1, keepdims=True)
        probs = (weights * (1.0 / totals)).astype(jnp.bfloat16)
        mixed_ref[head] = matmul(probs, values_ref[head]).astype(mixed_ref.dtype)
        totals_ref[head] = row_top + jnp.log(totals)


def attend(queries, keys_in, values_in, valid, step_heads=1):
    heads, row_count, head_dim = queries.shape
    key_count = keys_in.shape[1]
    block_rows = min(512, row_count)
    rows_spec = pl.BlockSpec((step_heads, block_rows, head_dim), lambda h, i: (h, i, 0))
    keys_spec = pl.BlockSpec((step_heads, key_count, head_dim), lambda h, i: (h, 0, 0))
    return pl.pallas_call(
        functools.partial(forward_kernel, scale=1.0 / math.sqrt(head_dim), valid=valid),
        grid=(heads // step_heads, row_count // block_rows),
        in_specs=[rows_spec, keys_spec, keys_spec],
        out_specs=[rows_spec, pl.BlockSpec((step_heads, block_rows, 1), lambda h, i: (h, i, 0))],
        out_shape=[
            jax.ShapeDtypeStruct(queries.shape, jnp.bfloat16),
            jax.ShapeDtypeStruct((heads, row_count, 1), jnp.float32),
        ],
        compiler_params=pltpu.CompilerParams(vmem_limit_bytes=40 * 1024 * 1024),
        cost_estimate=pl.CostEstimate(
            flops=4 * heads * row_count * key_count * head_dim,
            bytes_accessed=4 * heads * (row_count + key_count) * head_dim,
            transcendentals=heads * row_count * key_count,
        ),
        name="attend",
    )(queries, keys_in, values_in)


def backward_kernel(
    query_ref,
    keys_ref,
    values_ref,
    totals_ref,
    grad_ref,
    query_grad_ref,
    keys_grad_ref,
    values_grad_ref,
    *,
    scale,
    valid,
):
    first = pl.program_id(1) == 0
    for head in range(query_ref.shape[0]):
        query_block = query_ref[head]
        grad_block = grad_ref[head]
        keys_now = keys_ref[head]
        probs = jnp.exp(contract_cols(query_block, keys_now) * scale - totals_ref[head])
        if valid < probs.shape[1]:
            column = lax.broadcasted_iota(jnp.int32, probs.shape, 1)
            probs = jnp.where(column < valid, probs, 0.0)
        weighted = probs * contract_cols(grad_block, values_ref[head])
        scores_grad = weighted - probs * jnp.sum(weighted, -1, keepdims=True)
        scores_low = (scores_grad * scale).astype(jnp.bfloat16)
        query_grad_ref[head] = matmul(scores_low, keys_now).astype(query_grad_ref.dtype)
        keys_part = contract_rows(scores_low, query_block)
        values_part = contract_rows(probs.astype(jnp.bfloat16), grad_block)

        @pl.when(first)
        def _():
            keys_grad_ref[head] = keys_part
            values_grad_ref[head] = values_part

        @pl.when(jnp.logical_not(first))
        def _():
            keys_grad_ref[head] += keys_part
            values_grad_ref[head] += values_part


def attend_back(queries, keys_in, values_in, totals, grad_out, valid, step_heads=1):
    heads, row_count, head_dim = queries.shape
    key_count = keys_in.shape[1]
    block_rows = min(512, row_count)
    rows_spec = pl.BlockSpec((step_heads, block_rows, head_dim), lambda h, i: (h, i, 0))
    keys_spec = pl.BlockSpec((step_heads, key_count, head_dim), lambda h, i: (h, 0, 0))
    totals_spec = pl.BlockSpec((step_heads, block_rows, 1), lambda h, i: (h, i, 0))
    return pl.pallas_call(
        functools.partial(backward_kernel, scale=1.0 / math.sqrt(head_dim), valid=valid),
        grid=(heads // step_heads, row_count // block_rows),
        in_specs=[rows_spec, keys_spec, keys_spec, totals_spec, rows_spec],
        out_specs=[rows_spec, keys_spec, keys_spec],
        out_shape=[
            jax.ShapeDtypeStruct(queries.shape, jnp.bfloat16),
            jax.ShapeDtypeStruct(keys_in.shape, jnp.float32),
            jax.ShapeDtypeStruct(keys_in.shape, jnp.float32),
        ],
        compiler_params=pltpu.CompilerParams(vmem_limit_bytes=40 * 1024 * 1024),
        cost_estimate=pl.CostEstimate(
            flops=10 * heads * row_count * key_count * head_dim,
            bytes_accessed=8 * heads * (row_count + key_count) * head_dim,
            transcendentals=heads * row_count * key_count,
        ),
        name="attend_back",
    )(queries, keys_in, values_in, totals, grad_out)


def swap(blocks, axis_name):
    return lax.all_to_all(blocks, axis_name, split_axis=0, concat_axis=0, tiled=True)


def spread(part, axis_name):
    size = lax.axis_size(axis_name)
    return swap(jnp.broadcast_to(part[None], (size,) + part.shape), axis_name)


def gather_tokens(part):
    blocks = spread(part, "seq")
    return blocks.reshape((-1,) + part.shape[1:])


def sum_tokens(partial):
    size = lax.axis_size("seq")
    blocks = partial.astype(jnp.bfloat16).reshape((size, -1) + partial.shape[1:])
    return jnp.sum(swap(blocks, "seq").astype(jnp.float32), 0)


def column_blocks(values):
    size = lax.axis_size("seq")
    rows = values.shape[0]
    return values.reshape(rows, size, -1).transpose(1, 0, 2)


def own_columns(weight, groups, size, place):
    rows = weight.shape[0]
    parts = weight.reshape(rows, groups, size, -1)
    taken = lax.dynamic_slice_in_dim(parts, place, 1, 2)
    return taken.reshape(rows, -1)


def after(values, others):
    return lax.optimization_barrier((values, others))[0]


def sum_owners(blocks):
    owners = blocks.shape[0]
    core = lax.axis_index("fsdp") % 2
    pairs = blocks.reshape((owners // 2, 2) + blocks.shape[1:])
    kept = lax.dynamic_index_in_dim(pairs, core, 1, False)
    sent = lax.dynamic_index_in_dim(pairs, 1 - core, 1, False)
    arrived = lax.ppermute(sent, "fsdp", [(i, i ^ 1) for i in range(owners)])
    chip = (kept.astype(jnp.float32) + arrived.astype(jnp.float32)).astype(jnp.bfloat16)
    groups = [list(range(0, owners, 2)), list(range(1, owners, 2))]
    swapped = lax.all_to_all(
        chip, "fsdp", split_axis=0, concat_axis=0, axis_index_groups=groups, tiled=True
    )
    return jnp.sum(swapped.astype(jnp.float32), 0)


def heads_first(values, head_dim):
    rows = values.shape[0]
    return values.reshape(rows, -1, head_dim).transpose(1, 0, 2)


def heads_last(values):
    return values.transpose(1, 0, 2).reshape(values.shape[1], -1)


def local(
    latent,
    skip_input,
    text_tokens,
    condition,
    positions,
    cotangent,
    skip_gain,
    skip_shift,
    skip_weight,
    skip_bias,
    mod_weight,
    mod_bias,
    norm1_gain,
    norm1_shift,
    qkv_weight,
    qkv_bias,
    head_gains,
    head_shifts,
    attn_weight,
    attn_bias,
    norm3_gain,
    norm3_shift,
    cross_q_weight,
    cross_q_bias,
    cross_kv_weight,
    cross_kv_bias,
    cross_weight,
    cross_bias,
    norm2_gain,
    norm2_shift,
    fc1_weight,
    fc1_bias,
    fc2_weight,
    fc2_bias,
):
    ways = lax.axis_size("seq")
    owners = lax.axis_size("fsdp")
    place = lax.axis_index("seq")
    head_dim = head_gains.shape[1]
    tokens, model_width = latent.shape[1:]
    width = model_width // ways
    low = jnp.bfloat16
    gain_table = head_gains.astype(jnp.float32)
    shift_table = head_shifts.astype(jnp.float32)
    tables = rotary_tables(positions, head_dim)

    half = skip_weight.shape[0] // 2
    own_rows = model_width // owners
    packed_own = own_columns(qkv_weight, 3, ways, place)
    packed_pad = -packed_own.shape[1] % 128
    text_own = own_columns(cross_kv_weight, 2, ways, place)
    text_cols = text_own.size // own_rows
    first_own = jnp.concatenate(
        [
            skip_weight[:half],
            skip_weight[half:],
            jnp.pad(packed_own, ((0, 0), (0, packed_pad))),
            text_own.reshape(own_rows, text_cols),
        ],
        1,
    )
    first_rows = lax.all_gather(first_own, "fsdp", axis=0, tiled=True)
    second_own = jnp.concatenate([attn_weight, cross_q_weight, cross_weight], 1)
    second_own = after(second_own, first_rows)
    second_rows = lax.all_gather(second_own, "fsdp", axis=0, tiled=True)
    unit_rows = fc2_weight.shape[0] // ways
    down_own = lax.dynamic_slice_in_dim(fc2_weight, place * unit_rows, unit_rows, 0)
    up_own = own_columns(fc1_weight, owners, ways, place)
    units = up_own.shape[1]
    third_own = jnp.concatenate([up_own, down_own.reshape(own_rows, units)], 1)
    third_own = after(third_own, second_rows)
    third_rows = lax.all_gather(third_own, "fsdp", axis=0, tiled=True)
    sk_first = first_rows[:, :model_width]
    sk_second = first_rows[:, model_width : 2 * model_width]
    pk_weight = first_rows[:, 2 * model_width : 2 * model_width + 3 * width]
    kv_weight = first_rows[:, 2 * model_width + 3 * width + packed_pad :].reshape(-1, 2 * width)
    at_weight = second_rows[:, :model_width]
    cq_weight = second_rows[:, model_width : 2 * model_width]
    cr_weight = second_rows[:, 2 * model_width :]
    up_weight = third_rows[:, :units]
    down_weight = third_rows[:, units:].reshape(units, model_width)

    lifted_f, silu_pull = jax.vjp(jax.nn.silu, condition.astype(jnp.float32))
    lifted = lifted_f.astype(low)
    vectors = (
        skip_gain,
        skip_shift,
        skip_bias,
        mod_bias,
        norm1_gain,
        norm1_shift,
        qkv_bias,
        attn_bias,
        norm3_gain,
        norm3_shift,
        cross_q_bias,
        cross_kv_bias,
        cross_bias,
        norm2_gain,
        norm2_shift,
        fc1_bias,
        fc2_bias,
    )
    vector_own = jnp.concatenate(vectors)
    vector_all = swap(
        jnp.concatenate(
            [
                jnp.broadcast_to(vector_own[None], (owners, vector_own.shape[0])),
                lifted.reshape(owners, own_rows),
            ],
            1,
        ),
        "fsdp",
    )
    pieces = []
    start = 0
    for one_vector in vectors:
        size = one_vector.shape[0]
        pieces.append(vector_all[:, start : start + size].reshape(-1).astype(jnp.float32))
        start += size
    lifted_own = vector_all[:, start:]
    (
        sk_gain,
        sk_shift,
        sk_bias,
        md_bias,
        one_gain,
        one_shift,
        pk_bias,
        at_bias,
        three_gain,
        three_shift,
        cq_bias,
        kv_bias,
        cr_bias,
        two_gain,
        two_shift,
        up_bias,
        down_bias,
    ) = pieces
    pk_bias_own = own_columns(pk_bias[None], 3, ways, place)[0]
    kv_bias_own = own_columns(kv_bias[None], 2, ways, place)[0]
    up_bias_own = own_columns(up_bias[None], owners, ways, place)[0]
    shift_row = (
        jnp.sum(swap(matmul(lifted_own, mod_weight), "fsdp"), 0, keepdims=True) + md_bias
    )
    places_all = gather_tokens(positions.astype(jnp.float32))
    tables_all = rotary_tables(places_all, head_dim)

    joined = jnp.concatenate([latent[0], skip_input[0]], 1).astype(jnp.float32)
    normed_f, skip_pull = jax.vjp(layer_norm, joined, sk_gain, sk_shift)
    normed = normed_f.astype(low)
    normed_halves = normed.reshape(tokens, owners, 2, half).transpose(2, 0, 1, 3)
    normed_halves = normed_halves.reshape(2, tokens, model_width)
    stream_zero = (
        matmul(normed_halves[0], sk_first) + matmul(normed_halves[1], sk_second) + sk_bias
    )
    normed_all = gather_tokens(normed)

    text_now = text_tokens[0]
    text_count = text_now.shape[0]
    text_packed = matmul(text_now, kv_weight) + kv_bias_own
    text_keys_f, tk_pull = jax.vjp(
        lambda values_in, gains_in: head_norm(values_in, gains_in[3], 0.0, head_dim),
        text_packed[:, :width],
        gain_table,
    )
    text_own = jnp.concatenate(
        [text_keys_f.astype(low), text_packed[:, width:].astype(low)], 1
    )
    text_rows = text_count + -text_count % 16
    text_own = jnp.pad(text_own, ((0, text_rows - text_count), (0, 0)))
    text_all = spread(text_own, "seq").reshape(ways, text_rows, 2, -1, head_dim)
    text_all = text_all.transpose(2, 0, 3, 1, 4).reshape(2, -1, text_rows, head_dim)
    text_all = jnp.pad(text_all, ((0, 0), (0, 0), (0, -text_rows % 128), (0, 0)))
    entry_f, one_pull = jax.vjp(layer_norm, stream_zero, one_gain, one_shift)
    entry = (entry_f + shift_row).astype(low)

    entry_all = gather_tokens(entry)
    packed = matmul(entry_all, pk_weight) + pk_bias_own

    def prepare(query_pre, key_pre, gains_in, shifts_in):
        return (
            head_rotary(query_pre, gains_in[0], shifts_in[0], tables_all, head_dim),
            head_rotary(key_pre, gains_in[1], shifts_in[1], tables_all, head_dim),
        )

    (query_f, key_f), prep_pull = jax.vjp(
        prepare, packed[:, :width], packed[:, width : 2 * width], gain_table, shift_table
    )
    query_h = heads_first(query_f.astype(low), head_dim)
    key_h = heads_first(key_f.astype(low), head_dim)
    value_h = heads_first(packed[:, 2 * width :].astype(low), head_dim)
    all_tokens = query_h.shape[1]
    mixed_h, self_totals = attend(query_h, key_h, value_h, all_tokens)

    def to_heads(values):
        return swap(column_blocks(values), "seq").reshape(all_tokens, -1)

    def to_tokens(values_h):
        blocks = swap(heads_last(values_h).reshape(ways, tokens, width), "seq")
        return blocks.transpose(1, 0, 2).reshape(tokens, model_width)

    mixed = to_tokens(mixed_h)
    stream_one = stream_zero + matmul(mixed, at_weight) + at_bias

    cross_in_f, three_pull = jax.vjp(layer_norm, stream_one, three_gain, three_shift)
    cross_in = cross_in_f.astype(low)
    cross_pre = matmul(cross_in, cq_weight) + cq_bias
    cross_query_f, cq_pull = jax.vjp(
        lambda values_in, gains_in, shifts_in: head_rotary(
            values_in, gains_in[2], shifts_in[2], tables, head_dim
        ),
        cross_pre,
        gain_table,
        shift_table,
    )
    cross_query_h = heads_first(cross_query_f.astype(low), head_dim)
    step_heads = min(4, cross_query_h.shape[0])
    cross_h, cross_totals = attend(
        cross_query_h, text_all[0], text_all[1], text_count, step_heads
    )
    cross_mixed = heads_last(cross_h)
    stream_two = stream_one + matmul(cross_mixed, cr_weight) + cr_bias

    mlp_in_f, two_pull = jax.vjp(layer_norm, stream_two, two_gain, two_shift)
    mlp_all = gather_tokens(mlp_in_f.astype(low))
    hidden_pre = matmul(mlp_all, up_weight) + up_bias_own
    hidden_f, gelu_pull = jax.vjp(
        lambda values_in: jax.nn.gelu(values_in, approximate=True), hidden_pre
    )
    hidden = hidden_f.astype(low)
    out_partial = matmul(hidden, down_weight).astype(low)
    grad_all = gather_tokens(after(cotangent[0], entry_all))
    grad_three = cotangent[0].astype(jnp.float32)
    down_bias_grad = column_sums(cotangent[0])
    pre_grad = gelu_pull(contract_cols(grad_all, down_weight))[0].astype(low)
    up_bias_grad = column_sums(pre_grad)
    mlp_in_grad = sum_tokens(contract_cols(pre_grad, up_weight))
    down_grad = contract_rows(hidden, grad_all)
    up_grad = contract_rows(mlp_all, pre_grad)
    mlp_grads = jnp.concatenate(
        [
            up_grad.astype(low).reshape(owners, own_rows, units),
            down_grad.astype(low).reshape(owners, own_rows, units),
        ],
        2,
    )
    mlp_owned = lax.psum_scatter(mlp_grads, "fsdp", scatter_dimension=0, tiled=False)
    mlp_in_grad = after(mlp_in_grad, mlp_grads)
    stream_part, two_gain_grad, two_shift_grad = two_pull(mlp_in_grad)
    stream_grad = grad_three + stream_part

    grad_low = stream_grad.astype(low)
    cr_bias_grad = column_sums(grad_low)
    cross_mixed_grad = contract_cols(grad_low, cr_weight).astype(low)

    stream_three = stream_two + sum_tokens(after(out_partial, cross_mixed_grad)) + down_bias
    layer_out = stream_three.astype(low)[None]
    cross_query_grad, text_key_part, text_value_part = attend_back(
        cross_query_h,
        text_all[0],
        text_all[1],
        cross_totals,
        heads_first(cross_mixed_grad, head_dim),
        text_count,
        step_heads,
    )
    cross_query_grad = heads_last(cross_query_grad)
    cr_weight_grad = contract_rows(cross_mixed, grad_low).astype(low)
    cross_pre_grad, gains_from_cross, shifts_from_cross = cq_pull(
        cross_query_grad.astype(jnp.float32)
    )
    cross_pre_low = cross_pre_grad.astype(low)
    cq_bias_grad = column_sums(cross_pre_low)
    stream_part, three_gain_grad, three_shift_grad = three_pull(
        contract_cols(cross_pre_low, cq_weight)
    )
    stream_grad = stream_grad + stream_part
    cq_weight_grad = contract_rows(cross_in, cross_pre_low).astype(low)

    grad_low = stream_grad.astype(low)
    at_bias_grad = column_sums(grad_low)
    mixed_grad = contract_cols(grad_low, at_weight).astype(low)
    mixed_back = to_heads(mixed_grad)
    at_weight_grad = contract_rows(mixed, grad_low).astype(low)
    row_grads = jnp.concatenate([at_weight_grad, cq_weight_grad, cr_weight_grad], 1)
    row_owned = lax.psum_scatter(
        row_grads.reshape(owners, own_rows, -1), "fsdp", scatter_dimension=0, tiled=False
    )
    mixed_back = after(mixed_back, row_grads)
    query_grad, key_grad, value_grad = attend_back(
        query_h, key_h, value_h, self_totals, heads_first(mixed_back, head_dim), all_tokens
    )

    text_parts = jnp.stack([text_key_part, text_value_part])[:, :, :text_rows].astype(low)
    text_parts = text_parts.reshape(2, ways, -1, text_rows, head_dim)
    text_parts = text_parts.transpose(1, 3, 0, 2, 4).reshape(ways, text_rows, 2 * width)
    text_kv_grad = jnp.sum(
        swap(after(text_parts, mixed_back), "seq").astype(jnp.float32), 0
    )[:text_count]
    key_pre_grad, gains_from_text = tk_pull(text_kv_grad[:, :width])
    text_grad_low = jnp.concatenate(
        [key_pre_grad.astype(low), text_kv_grad[:, width:].astype(low)], 1
    )
    kv_weight_grad = contract_rows(text_now, text_grad_low)
    kv_bias_grad = column_sums(text_grad_low)
    text_part = contract_cols(text_grad_low, kv_weight)
    text_part = jnp.pad(text_part.astype(low), ((0, -text_count % (8 * ways)), (0, 0)))
    query_pre_grad, key_pre_grad2, gains_from_self, shifts_from_self = prep_pull(
        (
            heads_last(query_grad).astype(jnp.float32),
            heads_last(key_grad).astype(low).astype(jnp.float32),
        )
    )
    packed_grad = jnp.concatenate(
        [
            query_pre_grad.astype(low),
            key_pre_grad2.astype(low),
            heads_last(value_grad).astype(low),
        ],
        1,
    )
    entry_grad = sum_tokens(contract_cols(packed_grad, pk_weight))
    pk_weight_grad = contract_rows(entry_all, packed_grad)
    pk_bias_grad = column_sums(packed_grad)
    shift_part = jnp.sum(entry_grad, 0)
    stream_part, one_gain_grad, one_shift_grad = one_pull(entry_grad)
    stream_grad = stream_grad + stream_part

    grad_low = stream_grad.astype(low)
    sk_bias_grad = column_sums(grad_low)
    shift_rows = jnp.broadcast_to(
        shift_part.astype(low).reshape(1, ways, width), (ways, ways, width)
    )
    cols_in = jnp.concatenate([column_blocks(grad_low), shift_rows], 1)
    cols_out = swap(cols_in, "seq")
    grad_cols = cols_out[:, :tokens].reshape(all_tokens, width)
    shift_total = jnp.sum(cols_out[:, tokens:].astype(jnp.float32), 0).reshape(-1)
    sk_weight_grad = contract_rows(normed_all, grad_cols)
    joined_halves = jnp.stack(
        [contract_cols(grad_low, sk_first), contract_cols(grad_low, sk_second)]
    )
    joined_pre = joined_halves.reshape(2, tokens, owners, half).transpose(1, 2, 0, 3)
    joined_grad, sk_gain_grad, sk_shift_grad = skip_pull(
        joined_pre.reshape(tokens, 2 * model_width)
    )

    def placed(own, groups):
        parts = jnp.zeros((groups, ways, own.shape[0] // groups), jnp.float32)
        parts = lax.dynamic_update_slice_in_dim(parts, own.reshape(groups, 1, -1), place, 1)
        return parts.reshape(-1)

    vector_grads = (
        sk_gain_grad,
        sk_shift_grad,
        sk_bias_grad,
        one_gain_grad,
        one_shift_grad,
        placed(pk_bias_grad, 3),
        at_bias_grad,
        three_gain_grad,
        three_shift_grad,
        cq_bias_grad,
        placed(kv_bias_grad, 2),
        cr_bias_grad,
        two_gain_grad,
        two_shift_grad,
        placed(up_bias_grad, owners),
        down_bias_grad,
    )
    table_grads = jnp.concatenate(
        [
            (gains_from_cross + gains_from_text + gains_from_self).reshape(-1),
            (shifts_from_cross + shifts_from_self).reshape(-1),
        ]
    )
    split_three = [part.reshape(owners, -1) for part in vector_grads]
    pk_at = 5
    pk_thirds = placed(pk_bias_grad, 3).reshape(3, model_width)
    split_three[pk_at : pk_at + 1] = [
        pk_thirds[:2].reshape(owners, -1),
        pk_thirds[2].reshape(owners, -1),
    ]
    split_three.append(jnp.broadcast_to(table_grads[None], (owners, table_grads.shape[0])))
    summed_sizes = [part.shape[1] for part in split_three]
    vector_rows = jnp.concatenate(split_three, 1).astype(low)
    vector_pad = -vector_rows.shape[1] % own_rows
    vector_rows = jnp.pad(vector_rows, ((0, 0), (0, vector_pad)))
    shift_low = shift_total.astype(low)
    latent_mark = jnp.arange(owners) == lax.axis_index("fsdp")
    shift_mine = jnp.where(latent_mark[:, None], shift_low[None], jnp.zeros((), low))
    shift_mine = jnp.broadcast_to(
        shift_mine.reshape(1, own_rows, -1), (owners, own_rows, owners * owners)
    )
    sk_blocks = sk_weight_grad.astype(low).reshape(owners, 2, own_rows, width)
    tail_parts = [
        sk_blocks[:, 0],
        sk_blocks[:, 1],
        pk_weight_grad.astype(low).reshape(owners, own_rows, -1),
        kv_weight_grad.astype(low).reshape(owners, own_rows, -1),
        vector_rows.reshape(owners, own_rows, -1),
        shift_mine,
    ]
    tail_sizes = [part.shape[2] for part in tail_parts]
    tail_sum = sum_owners(jnp.concatenate(tail_parts, 2))
    shift_all = tail_sum[:, -tail_sizes[-1] :].reshape(owners, model_width)

    row_blocks = column_blocks(row_owned)
    row_lanes = row_blocks.shape[2]
    text_blocks = text_part.reshape(ways, -1, text_part.shape[1])
    row_sum = jnp.sum(swap(row_blocks, "seq").astype(jnp.float32), 0)
    text_sum = jnp.sum(swap(text_blocks, "seq").astype(jnp.float32), 0)
    text_total = gather_tokens(text_sum.astype(low))[:text_count]

    tail_all = spread(tail_sum[:, : -tail_sizes[-1]].astype(low), "seq")
    owned = lax.all_gather(
        jnp.concatenate([mlp_owned, row_sum.astype(low)], 1), "seq", axis=0, tiled=False
    )

    def beside(blocks):
        return blocks.astype(jnp.float32).transpose(1, 0, 2).reshape(blocks.shape[1], -1)

    sk_total = jnp.concatenate(
        [beside(tail_all[:, :, :width]), beside(tail_all[:, :, width : 2 * width])], 0
    )
    start = 2 * width
    pk_owned = tail_all[:, :, start : start + 3 * width].astype(jnp.float32)
    pk_owned = pk_owned.reshape(ways, own_rows, 3, width)
    pk_total = pk_owned.transpose(1, 2, 0, 3).reshape(own_rows, -1)
    start += 3 * width
    kv_owned = tail_all[:, :, start : start + text_cols].astype(jnp.float32)
    kv_owned = kv_owned.reshape(ways, -1, 2, width)
    kv_total = kv_owned.transpose(1, 2, 0, 3).reshape(kv_owned.shape[1], -1)
    start += text_cols
    small_total = jnp.sum(tail_all[:, :, start:].astype(jnp.float32), 0).reshape(-1)
    vector_totals = []
    start = 0
    for size in summed_sizes:
        vector_totals.append(small_total[start : start + size])
        start += size
    table_total = vector_totals.pop()
    gains_total = table_total[: gain_table.size].reshape(gain_table.shape)
    shifts_total = table_total[gain_table.size :].reshape(shift_table.shape)
    md_weight_grad = lax.dot_general(
        lifted_own.astype(jnp.float32),
        shift_all,
        (((0,), (0,)), ((), ())),
        precision=lax.Precision.HIGHEST,
        preferred_element_type=jnp.float32,
    )
    md_bias_grad = lax.dynamic_slice_in_dim(
        jnp.sum(shift_all, 0), lax.axis_index("fsdp") * own_rows, own_rows, 0
    )
    lifted_part = lax.dot_general(
        shift_all,
        mod_weight.astype(jnp.float32),
        (((1,), (1,)), ((), ())),
        precision=lax.Precision.HIGHEST,
        preferred_element_type=jnp.float32,
    )
    lifted_grad = swap(lifted_part, "fsdp").reshape(1, model_width)
    condition_grad = silu_pull(lifted_grad)[0]

    up_owned = owned[:, :, :units].astype(jnp.float32).reshape(ways, own_rows, owners, -1)
    up_total = up_owned.transpose(1, 2, 0, 3).reshape(own_rows, -1)
    down_total = owned[:, :, units : 2 * units].astype(jnp.float32).reshape(-1, model_width)
    row_total = beside(owned[:, :, 2 * units :])
    at_total = row_total[:, :model_width]
    cq_total = row_total[:, model_width : 2 * model_width]
    cr_total = row_total[:, 2 * model_width :]
    (
        sk_gain_total,
        sk_shift_total,
        sk_bias_total,
        one_gain_total,
        one_shift_total,
        pk_bias_total,
        value_bias_total,
        at_bias_total,
        three_gain_total,
        three_shift_total,
        cq_bias_total,
        kv_bias_total,
        cr_bias_total,
        two_gain_total,
        two_shift_total,
        up_bias_total,
        down_bias_total,
    ) = vector_totals
    return (
        layer_out,
        joined_grad[:, :model_width].astype(low)[None],
        joined_grad[:, model_width:].astype(low)[None],
        text_total[None],
        condition_grad,
        sk_gain_total,
        sk_shift_total,
        sk_total,
        sk_bias_total,
        md_weight_grad,
        md_bias_grad,
        one_gain_total,
        one_shift_total,
        pk_total,
        pk_bias_total,
        value_bias_total,
        gains_total,
        shifts_total,
        at_total,
        at_bias_total,
        three_gain_total,
        three_shift_total,
        cq_total,
        cq_bias_total,
        kv_total,
        kv_bias_total,
        cr_total,
        cr_bias_total,
        two_gain_total,
        two_shift_total,
        up_total,
        up_bias_total,
        down_total,
        down_bias_total,
    )


def solution(mesh):
    in_specs = (
        P("fsdp", "seq", None),
        P("fsdp", "seq", None),
        P("fsdp", None, None),
        P("fsdp", None),
        P("seq", None),
        P("fsdp", "seq", None),
        P("fsdp"),
        P("fsdp"),
        P("fsdp", None),
        P("fsdp"),
        P("fsdp", None),
        P("fsdp"),
        P("fsdp"),
        P("fsdp"),
        P("fsdp", None),
        P("fsdp"),
        P(),
        P(),
        P("fsdp", None),
        P("fsdp"),
        P("fsdp"),
        P("fsdp"),
        P("fsdp", None),
        P("fsdp"),
        P("fsdp", None),
        P("fsdp"),
        P("fsdp", None),
        P("fsdp"),
        P("fsdp"),
        P("fsdp"),
        P("fsdp", None),
        P("fsdp"),
        P("fsdp", None),
        P("fsdp"),
    )
    out_specs = (
        P("fsdp", "seq", None),
        P("fsdp", "seq", None),
        P("fsdp", "seq", None),
        P("fsdp", None, None),
        P("fsdp", None),
        P("fsdp"),
        P("fsdp"),
        P("fsdp", None),
        P("fsdp"),
        P("fsdp", None),
        P("fsdp"),
        P("fsdp"),
        P("fsdp"),
        P("fsdp", None),
        P("fsdp"),
        P("fsdp"),
        P(),
        P(),
        P("fsdp", None),
        P("fsdp"),
        P("fsdp"),
        P("fsdp"),
        P("fsdp", None),
        P("fsdp"),
        P("fsdp", None),
        P("fsdp"),
        P("fsdp", None),
        P("fsdp"),
        P("fsdp"),
        P("fsdp"),
        P("fsdp", None),
        P("fsdp"),
        P("fsdp", None),
        P("fsdp"),
    )
    return jax.shard_map(local, mesh=mesh, in_specs=in_specs, out_specs=out_specs, check_vma=False)
```

```python
import functools
import math

import jax
import jax.numpy as jnp
from jax import lax
from jax.experimental import pallas as pl
from jax.experimental.pallas import tpu as pltpu
from jax.sharding import PartitionSpec as P


def layer_norm(inputs, gain_vector, shift_vector):
    centred = inputs - jnp.mean(inputs, -1, keepdims=True)
    variance = jnp.mean(centred * centred, -1, keepdims=True)
    return centred * lax.rsqrt(variance + 1e-06) * gain_vector + shift_vector


def rotary_tables(positions, head_dim):
    quarter = head_dim // 4
    exponent = jnp.arange(quarter, dtype=jnp.float32) * (2.0 / (head_dim // 2))
    inverse = jnp.power(jnp.float32(10000.0), -exponent)
    places = positions.astype(jnp.float32)
    angle_rows = places[:, 0:1] * inverse
    angle_cols = places[:, 1:2] * inverse
    return (jnp.cos(angle_rows), jnp.sin(angle_rows), jnp.cos(angle_cols), jnp.sin(angle_cols))


def rotate(inputs, tables):
    cos_rows, sin_rows, cos_cols, sin_cols = tuple((one_table[:, None, :] for one_table in tables))
    quarter = inputs.shape[-1] // 4
    first_a = inputs[..., :quarter]
    first_b = inputs[..., quarter : 2 * quarter]
    second_a = inputs[..., 2 * quarter : 3 * quarter]
    second_b = inputs[..., 3 * quarter :]
    return jnp.concatenate(
        [
            first_a * cos_rows - first_b * sin_rows,
            first_a * sin_rows + first_b * cos_rows,
            second_a * cos_cols - second_b * sin_cols,
            second_a * sin_cols + second_b * cos_cols,
        ],
        -1,
    )


def head_norm(inputs, gain_vector, shift_vector, head_dim):
    row_count = inputs.shape[0]
    shaped = inputs.reshape(row_count, -1, head_dim)
    return layer_norm(shaped, gain_vector, shift_vector).reshape(row_count, -1)


def head_rotary(inputs, gain_vector, shift_vector, tables, head_dim):
    row_count = inputs.shape[0]
    shaped = inputs.reshape(row_count, -1, head_dim)
    return rotate(layer_norm(shaped, gain_vector, shift_vector), tables).reshape(row_count, -1)


def matmul(left_side, right_side):
    return jnp.dot(left_side, right_side, preferred_element_type=jnp.float32)


def contract_rows(left_side, right_side):
    return lax.dot_general(
        left_side, right_side, (((0,), (0,)), ((), ())), preferred_element_type=jnp.float32
    )


def contract_cols(left_side, right_side):
    return lax.dot_general(
        left_side, right_side, (((1,), (1,)), ((), ())), preferred_element_type=jnp.float32
    )


def column_sums(grads_low):
    return jnp.sum(grads_low.astype(jnp.float32), 0)


def to_float(vectors):
    return tuple((one_vector.astype(jnp.float32) for one_vector in vectors))


def forward_kernel(query_ref, keys_ref, values_ref, mixed_ref, totals_ref, *, scale, valid):
    for head in range(query_ref.shape[0]):
        scores = contract_cols(query_ref[head], keys_ref[head]) * scale
        if valid < scores.shape[1]:
            column = lax.broadcasted_iota(jnp.int32, scores.shape, 1)
            scores = jnp.where(column < valid, scores, -1e30)
        row_top = jnp.max(scores, -1, keepdims=True)
        weights = jnp.exp(scores - row_top)
        totals = jnp.sum(weights, -1, keepdims=True)
        probs = (weights * (1.0 / totals)).astype(jnp.bfloat16)
        mixed_ref[head] = matmul(probs, values_ref[head]).astype(mixed_ref.dtype)
        totals_ref[head] = row_top + jnp.log(totals)


def attend(queries, keys_in, values_in, valid, step_heads=1):
    heads, row_count, head_dim = queries.shape
    key_count = keys_in.shape[1]
    block_rows = min(512, row_count)
    rows_spec = pl.BlockSpec((step_heads, block_rows, head_dim), lambda h, i: (h, i, 0))
    keys_spec = pl.BlockSpec((step_heads, key_count, head_dim), lambda h, i: (h, 0, 0))
    return pl.pallas_call(
        functools.partial(forward_kernel, scale=1.0 / math.sqrt(head_dim), valid=valid),
        grid=(heads // step_heads, row_count // block_rows),
        in_specs=[rows_spec, keys_spec, keys_spec],
        out_specs=[rows_spec, pl.BlockSpec((step_heads, block_rows, 1), lambda h, i: (h, i, 0))],
        out_shape=[
            jax.ShapeDtypeStruct(queries.shape, jnp.bfloat16),
            jax.ShapeDtypeStruct((heads, row_count, 1), jnp.float32),
        ],
        compiler_params=pltpu.CompilerParams(vmem_limit_bytes=40 * 1024 * 1024),
        cost_estimate=pl.CostEstimate(
            flops=4 * heads * row_count * key_count * head_dim,
            bytes_accessed=4 * heads * (row_count + key_count) * head_dim,
            transcendentals=heads * row_count * key_count,
        ),
        name="attend",
    )(queries, keys_in, values_in)


def backward_kernel(
    query_ref,
    keys_ref,
    values_ref,
    totals_ref,
    grad_ref,
    query_grad_ref,
    keys_grad_ref,
    values_grad_ref,
    *,
    scale,
    valid,
):
    first = pl.program_id(1) == 0
    for head in range(query_ref.shape[0]):
        query_block = query_ref[head]
        grad_block = grad_ref[head]
        keys_now = keys_ref[head]
        probs = jnp.exp(contract_cols(query_block, keys_now) * scale - totals_ref[head])
        if valid < probs.shape[1]:
            column = lax.broadcasted_iota(jnp.int32, probs.shape, 1)
            probs = jnp.where(column < valid, probs, 0.0)
        weighted = probs * contract_cols(grad_block, values_ref[head])
        scores_grad = weighted - probs * jnp.sum(weighted, -1, keepdims=True)
        scores_low = (scores_grad * scale).astype(jnp.bfloat16)
        query_grad_ref[head] = matmul(scores_low, keys_now).astype(query_grad_ref.dtype)
        keys_part = contract_rows(scores_low, query_block)
        values_part = contract_rows(probs.astype(jnp.bfloat16), grad_block)

        @pl.when(first)
        def _():
            keys_grad_ref[head] = keys_part
            values_grad_ref[head] = values_part

        @pl.when(jnp.logical_not(first))
        def _():
            keys_grad_ref[head] += keys_part
            values_grad_ref[head] += values_part


def attend_back(queries, keys_in, values_in, totals, grad_out, valid, step_heads=1):
    heads, row_count, head_dim = queries.shape
    key_count = keys_in.shape[1]
    block_rows = min(512, row_count)
    rows_spec = pl.BlockSpec((step_heads, block_rows, head_dim), lambda h, i: (h, i, 0))
    keys_spec = pl.BlockSpec((step_heads, key_count, head_dim), lambda h, i: (h, 0, 0))
    totals_spec = pl.BlockSpec((step_heads, block_rows, 1), lambda h, i: (h, i, 0))
    return pl.pallas_call(
        functools.partial(backward_kernel, scale=1.0 / math.sqrt(head_dim), valid=valid),
        grid=(heads // step_heads, row_count // block_rows),
        in_specs=[rows_spec, keys_spec, keys_spec, totals_spec, rows_spec],
        out_specs=[rows_spec, keys_spec, keys_spec],
        out_shape=[
            jax.ShapeDtypeStruct(queries.shape, jnp.bfloat16),
            jax.ShapeDtypeStruct(keys_in.shape, jnp.float32),
            jax.ShapeDtypeStruct(keys_in.shape, jnp.float32),
        ],
        compiler_params=pltpu.CompilerParams(vmem_limit_bytes=40 * 1024 * 1024),
        cost_estimate=pl.CostEstimate(
            flops=10 * heads * row_count * key_count * head_dim,
            bytes_accessed=8 * heads * (row_count + key_count) * head_dim,
            transcendentals=heads * row_count * key_count,
        ),
        name="attend_back",
    )(queries, keys_in, values_in, totals, grad_out)


def row_grads_kernel(left_ref, right_ref, out_ref):
    product = contract_rows(left_ref[0], right_ref[0])
    rows = out_ref.shape[1]
    for owner in range(out_ref.shape[0]):
        out_ref[owner] = product[owner * rows : (owner + 1) * rows].astype(out_ref.dtype)


def row_grads(lefts, rights, owners):
    count, tokens, width = lefts.shape
    rows = width // owners
    pair_spec = pl.BlockSpec((1, tokens, width), lambda i: (i, 0, 0))
    return pl.pallas_call(
        row_grads_kernel,
        grid=(count,),
        in_specs=[pair_spec, pair_spec],
        out_specs=pl.BlockSpec((owners, rows, width), lambda i: (0, 0, i)),
        out_shape=jax.ShapeDtypeStruct((owners, rows, count * width), jnp.bfloat16),
        compiler_params=pltpu.CompilerParams(vmem_limit_bytes=48 * 1024 * 1024),
        cost_estimate=pl.CostEstimate(
            flops=2 * count * tokens * width * width,
            bytes_accessed=2 * count * (width * width + 2 * tokens * width),
            transcendentals=0,
        ),
        name="row_grads",
    )(lefts, rights)


def side_by_side(pieces):
    return jnp.concatenate([piece.astype(jnp.float32) for piece in pieces], 1)


def tail_kernel(all_ref, skip_ref, packed_ref, text_ref, small_ref):
    ways, rows = all_ref.shape[:2]
    model_width = skip_ref.shape[1]
    width = model_width // ways

    def joined(start, count):
        return side_by_side(
            [all_ref[way, :count, start : start + width] for way in range(ways)]
        )

    skip_ref[:rows] = joined(0, rows)
    skip_ref[rows:] = joined(width, rows)
    for third in range(3):
        packed_ref[:, third * model_width : (third + 1) * model_width] = joined(
            (2 + third) * width, rows
        )
    for side in range(2):
        text_ref[:, side * model_width : (side + 1) * model_width] = joined(
            (5 + side) * width, text_ref.shape[0]
        )
    total = all_ref[0, :, 7 * width :].astype(jnp.float32)
    for way in range(1, ways):
        total += all_ref[way, :, 7 * width :].astype(jnp.float32)
    small_ref[...] = total


def lay_tail(blocks, text_rows):
    ways, rows, lanes = blocks.shape
    width = 2 * rows
    model_width = ways * width
    return pl.pallas_call(
        tail_kernel,
        out_shape=[
            jax.ShapeDtypeStruct((2 * rows, model_width), jnp.float32),
            jax.ShapeDtypeStruct((rows, 3 * model_width), jnp.float32),
            jax.ShapeDtypeStruct((text_rows, 2 * model_width), jnp.float32),
            jax.ShapeDtypeStruct((rows, lanes - 7 * width), jnp.float32),
        ],
        compiler_params=pltpu.CompilerParams(vmem_limit_bytes=40 * 1024 * 1024),
        name="lay_tail",
    )(blocks)


def units_kernel(all_ref, up_ref, down_ref):
    ways = all_ref.shape[0]
    rows, hidden = up_ref.shape
    units = hidden // ways
    owners = 16
    own = units // owners
    for owner in range(owners):
        start = owner * ways * own
        up_ref[:, start : start + ways * own] = side_by_side(
            [all_ref[way, :rows, owner * own : (owner + 1) * own] for way in range(ways)]
        )
    model_width = down_ref.shape[1]
    split = min(units, model_width)
    for way in range(ways):
        place = slice(way * own, (way + 1) * own)
        down_ref[place, :split] = all_ref[way, :own, units : units + split].astype(jnp.float32)
        if split < model_width:
            down_ref[place, split:] = all_ref[
                way, own : 2 * own, units : units + model_width - split
            ].astype(jnp.float32)


def lay_units(blocks, rows, model_width):
    ways, lines, lanes = blocks.shape
    units = lanes // 2
    return pl.pallas_call(
        units_kernel,
        out_shape=[
            jax.ShapeDtypeStruct((rows, ways * units), jnp.float32),
            jax.ShapeDtypeStruct((ways * units // 16, model_width), jnp.float32),
        ],
        compiler_params=pltpu.CompilerParams(vmem_limit_bytes=40 * 1024 * 1024),
        name="lay_units",
    )(blocks)


def fold_down(part, units, lines):
    first = part[..., :units]
    rest = part[..., units:]
    pad = [(0, 0)] * (part.ndim - 1) + [(0, units - rest.shape[-1])]
    both = jnp.concatenate([first, jnp.pad(rest, pad)], -2)
    return fit_rows(both, lines)


def fit_rows(part, lines):
    pad = [(0, 0)] * part.ndim
    pad[-2] = (0, lines - part.shape[-2])
    return jnp.pad(part, pad)


def swap(blocks, axis_name):
    return lax.all_to_all(blocks, axis_name, split_axis=0, concat_axis=0, tiled=True)


def spread(part, axis_name):
    size = lax.axis_size(axis_name)
    return swap(jnp.broadcast_to(part[None], (size,) + part.shape), axis_name)


def grid_place(axis_name):
    index = lax.axis_index(axis_name)
    if axis_name == "fsdp":
        index = index // 2
    return index // 4, index % 4


def grid_send(axis_name, pair, step):
    cores = 2 if axis_name == "fsdp" else 1
    links = []
    for index in range(8 * cores):
        chip, core = index // cores, index % cores
        target = ((chip // 4) ^ pair) * 4 + (chip % 4 + step) % 4
        links.append((index, target * cores + core))
    return lambda value: lax.ppermute(value, axis_name, links)


def grid_parts(part, axis_name):
    half = part.shape[0] // 2
    pair, ring = grid_place(axis_name)
    mate_of = grid_send(axis_name, 1, 0)
    up = grid_send(axis_name, 0, 1)
    down = grid_send(axis_name, 0, -1)
    mate = mate_of(part)
    below = up(part)
    above = down(part)
    far = jnp.concatenate([up(below[:half]), down(above[half:])], 0)
    mate_below = up(mate)
    mate_above = down(mate)
    mate_far = mate_of(far)
    here, there = pair * 4, (1 - pair) * 4
    return [
        (part, here + ring),
        (mate, there + ring),
        (below, here + (ring + 3) % 4),
        (above, here + (ring + 1) % 4),
        (mate_below, there + (ring + 3) % 4),
        (mate_above, there + (ring + 1) % 4),
        (far, here + (ring + 2) % 4),
        (mate_far, there + (ring + 2) % 4),
    ]


def gather_tokens(part):
    buffer = jnp.zeros((8,) + part.shape, part.dtype)
    for one, spot in grid_parts(part, "seq"):
        buffer = lax.dynamic_update_index_in_dim(buffer, one, spot, 0)
    return buffer.reshape((-1,) + part.shape[1:])


def gather_owners(part):
    core = lax.axis_index("fsdp") % 2
    buffer = jnp.zeros((16,) + part.shape, part.dtype)
    for one, spot in grid_parts(part, "fsdp"):
        other = lax.ppermute(one, "fsdp", [(i, i ^ 1) for i in range(16)])
        buffer = lax.dynamic_update_index_in_dim(buffer, one, 2 * spot + core, 0)
        buffer = lax.dynamic_update_index_in_dim(buffer, other, 2 * spot + 1 - core, 0)
    return buffer.reshape((-1,) + part.shape[1:])


def sum_tokens(partial):
    low = jnp.bfloat16
    blocks = partial.astype(low).reshape((8, -1) + partial.shape[1:])
    half = blocks.shape[1] // 2
    pair, ring = grid_place("seq")
    mate_of = grid_send("seq", 1, 0)
    up = grid_send("seq", 0, 1)
    down = grid_send("seq", 0, -1)

    def meant(mate, step):
        spot = jnp.where(mate, 1 - pair, pair) * 4 + (ring + step) % 4
        return lax.dynamic_index_in_dim(blocks, spot, 0, False)

    def total(*parts):
        return sum(part.astype(jnp.float32) for part in parts)

    far_mate = mate_of(meant(True, 2))
    mate_below = up(meant(True, 1))
    mate_above = down(meant(True, 3))
    far = total(meant(False, 2), far_mate).astype(low)
    far_below = up(far[:half])
    far_above = down(far[half:])
    mate = mate_of(total(meant(True, 0), mate_below, mate_above).astype(low))
    next_up = meant(False, 1)
    next_up = jnp.concatenate([total(next_up[:half], far_below).astype(low), next_up[half:]], 0)
    next_down = meant(False, 3)
    next_down = jnp.concatenate(
        [next_down[:half], total(next_down[half:], far_above).astype(low)], 0
    )
    return total(meant(False, 0), mate, up(next_up), down(next_down))


def column_blocks(values):
    size = lax.axis_size("seq")
    rows = values.shape[0]
    return values.reshape(rows, size, -1).transpose(1, 0, 2)


def own_columns(weight, groups, size, place):
    rows = weight.shape[0]
    parts = weight.reshape(rows, groups, size, -1)
    taken = lax.dynamic_slice_in_dim(parts, place, 1, 2)
    return taken.reshape(rows, -1)


def after(values, others):
    return lax.optimization_barrier((values, others))[0]


def sum_owners(blocks):
    owners = blocks.shape[0]
    core = lax.axis_index("fsdp") % 2
    pairs = blocks.reshape((owners // 2, 2) + blocks.shape[1:])
    kept = lax.dynamic_index_in_dim(pairs, core, 1, False)
    sent = lax.dynamic_index_in_dim(pairs, 1 - core, 1, False)
    arrived = lax.ppermute(sent, "fsdp", [(i, i ^ 1) for i in range(owners)])
    chip = (kept.astype(jnp.float32) + arrived.astype(jnp.float32)).astype(jnp.bfloat16)
    groups = [list(range(0, owners, 2)), list(range(1, owners, 2))]
    swapped = lax.all_to_all(
        chip, "fsdp", split_axis=0, concat_axis=0, axis_index_groups=groups, tiled=True
    )
    return jnp.sum(swapped.astype(jnp.float32), 0)


def heads_first(values, head_dim):
    rows = values.shape[0]
    return values.reshape(rows, -1, head_dim).transpose(1, 0, 2)


def heads_last(values):
    return values.transpose(1, 0, 2).reshape(values.shape[1], -1)


def local(
    latent,
    skip_input,
    text_tokens,
    condition,
    positions,
    cotangent,
    skip_gain,
    skip_shift,
    skip_weight,
    skip_bias,
    mod_weight,
    mod_bias,
    norm1_gain,
    norm1_shift,
    qkv_weight,
    qkv_bias,
    head_gains,
    head_shifts,
    attn_weight,
    attn_bias,
    norm3_gain,
    norm3_shift,
    cross_q_weight,
    cross_q_bias,
    cross_kv_weight,
    cross_kv_bias,
    cross_weight,
    cross_bias,
    norm2_gain,
    norm2_shift,
    fc1_weight,
    fc1_bias,
    fc2_weight,
    fc2_bias,
):
    ways = lax.axis_size("seq")
    owners = lax.axis_size("fsdp")
    place = lax.axis_index("seq")
    head_dim = head_gains.shape[1]
    tokens, model_width = latent.shape[1:]
    width = model_width // ways
    low = jnp.bfloat16
    gain_table = head_gains.astype(jnp.float32)
    shift_table = head_shifts.astype(jnp.float32)
    tables = rotary_tables(positions, head_dim)

    own_rows = model_width // owners
    packed_own = own_columns(qkv_weight, 3, ways, place)
    packed_pad = -packed_own.shape[1] % 128
    text_own = own_columns(cross_kv_weight, 2, ways, place)
    first_own = jnp.concatenate(
        [
            jnp.pad(packed_own, ((0, 0), (0, packed_pad))),
            fit_rows(text_own, own_rows),
        ],
        1,
    )
    first_rows = lax.all_gather(first_own, "fsdp", axis=0, tiled=False)
    second_own = jnp.concatenate([attn_weight, cross_q_weight, cross_weight], 1)
    second_own = after(second_own, first_rows)
    second_rows = lax.all_gather(second_own, "fsdp", axis=0, tiled=True)
    unit_rows = fc2_weight.shape[0] // ways
    down_own = lax.dynamic_slice_in_dim(fc2_weight, place * unit_rows, unit_rows, 0)
    up_own = own_columns(fc1_weight, owners, ways, place)
    units = up_own.shape[1]
    lines = max(own_rows, 2 * unit_rows)
    third_own = jnp.concatenate(
        [fit_rows(up_own, lines), fold_down(down_own, units, lines)], 1
    )
    third_own = after(third_own, second_rows)
    third_rows = lax.all_gather(third_own, "fsdp", axis=0, tiled=False)
    sk_weight = gather_owners(skip_weight)
    pk_weight = first_rows[:, :, : 3 * width].reshape(model_width, 3 * width)
    kv_weight = first_rows[:, : text_own.shape[0], 3 * width + packed_pad :]
    kv_weight = kv_weight.reshape(-1, 2 * width)
    up_weight = third_rows[:, :own_rows, :units].reshape(model_width, units)
    down_weight = jnp.concatenate(
        [
            third_rows[:, :unit_rows, units : units + min(units, model_width)],
            third_rows[:, unit_rows : 2 * unit_rows, units : units + max(model_width - units, 0)],
        ],
        2,
    ).reshape(units, model_width)
    at_weight = second_rows[:, :model_width]
    cq_weight = second_rows[:, model_width : 2 * model_width]
    cr_weight = second_rows[:, 2 * model_width :]

    lifted_f, silu_pull = jax.vjp(jax.nn.silu, condition.astype(jnp.float32))
    lifted = lifted_f.astype(low)
    vectors = (
        skip_gain,
        skip_shift,
        skip_bias,
        mod_bias,
        norm1_gain,
        norm1_shift,
        qkv_bias,
        attn_bias,
        norm3_gain,
        norm3_shift,
        cross_q_bias,
        cross_kv_bias,
        cross_bias,
        norm2_gain,
        norm2_shift,
        fc1_bias,
        fc2_bias,
    )
    vector_own = jnp.concatenate(vectors)
    vector_all = swap(
        jnp.concatenate(
            [
                jnp.broadcast_to(vector_own[None], (owners, vector_own.shape[0])),
                lifted.reshape(owners, own_rows),
            ],
            1,
        ),
        "fsdp",
    )
    pieces = []
    start = 0
    for one_vector in vectors:
        size = one_vector.shape[0]
        pieces.append(vector_all[:, start : start + size].reshape(-1).astype(jnp.float32))
        start += size
    lifted_own = vector_all[:, start:]
    (
        sk_gain,
        sk_shift,
        sk_bias,
        md_bias,
        one_gain,
        one_shift,
        pk_bias,
        at_bias,
        three_gain,
        three_shift,
        cq_bias,
        kv_bias,
        cr_bias,
        two_gain,
        two_shift,
        up_bias,
        down_bias,
    ) = pieces
    pk_bias_own = own_columns(pk_bias[None], 3, ways, place)[0]
    kv_bias_own = own_columns(kv_bias[None], 2, ways, place)[0]
    up_bias_own = own_columns(up_bias[None], owners, ways, place)[0]
    shift_row = (
        jnp.sum(swap(matmul(lifted_own, mod_weight), "fsdp"), 0, keepdims=True) + md_bias
    )
    places_all = spread(positions.astype(jnp.float32), "seq").reshape(-1, 2)
    tables_all = rotary_tables(places_all, head_dim)

    joined = jnp.concatenate([latent[0], skip_input[0]], 1).astype(jnp.float32)
    normed_f, skip_pull = jax.vjp(layer_norm, joined, sk_gain, sk_shift)
    normed = normed_f.astype(low)
    normed_first = gather_tokens(normed[:, :model_width])
    sk_weight = after(sk_weight, (normed_first, shift_row, places_all))
    stream_zero = matmul(normed, sk_weight) + sk_bias

    entry_f, one_pull = jax.vjp(layer_norm, stream_zero, one_gain, one_shift)
    entry = (entry_f + shift_row).astype(low)

    entry_all = gather_tokens(entry)

    text_now = text_tokens[0]
    text_count = text_now.shape[0]
    text_packed = matmul(text_now, kv_weight) + kv_bias_own
    text_keys_f, tk_pull = jax.vjp(
        lambda values_in, gains_in: head_norm(values_in, gains_in[3], 0.0, head_dim),
        text_packed[:, :width],
        gain_table,
    )
    text_own = jnp.concatenate(
        [text_keys_f.astype(low), text_packed[:, width:].astype(low)], 1
    )
    text_rows = text_count + -text_count % 16
    text_own = jnp.pad(text_own, ((0, text_rows - text_count), (0, 0)))
    text_spread = spread(after(text_own, entry_all), "seq")
    text_all = text_spread.reshape(ways, text_rows, 2, -1, head_dim)
    text_all = text_all.transpose(2, 0, 3, 1, 4).reshape(2, -1, text_rows, head_dim)
    text_all = jnp.pad(text_all, ((0, 0), (0, 0), (0, -text_rows % 128), (0, 0)))
    packed = matmul(entry_all, pk_weight) + pk_bias_own

    def prepare(query_pre, key_pre, gains_in, shifts_in):
        return (
            head_rotary(query_pre, gains_in[0], shifts_in[0], tables_all, head_dim),
            head_rotary(key_pre, gains_in[1], shifts_in[1], tables_all, head_dim),
        )

    (query_f, key_f), prep_pull = jax.vjp(
        prepare, packed[:, :width], packed[:, width : 2 * width], gain_table, shift_table
    )
    query_h = heads_first(query_f.astype(low), head_dim)
    key_h = heads_first(key_f.astype(low), head_dim)
    value_h = heads_first(packed[:, 2 * width :].astype(low), head_dim)
    all_tokens = query_h.shape[1]
    mixed_h, self_totals = attend(query_h, key_h, value_h, all_tokens)
    mixed_h = after(mixed_h, text_spread)

    def to_heads(values):
        return swap(column_blocks(values), "seq").reshape(all_tokens, -1)

    def to_tokens(values_h):
        blocks = swap(heads_last(values_h).reshape(ways, tokens, width), "seq")
        return blocks.transpose(1, 0, 2).reshape(tokens, model_width)

    mixed = to_tokens(mixed_h)
    grad_all = gather_tokens(after(cotangent[0], mixed))
    stream_one = stream_zero + matmul(mixed, at_weight) + at_bias

    cross_in_f, three_pull = jax.vjp(layer_norm, stream_one, three_gain, three_shift)
    cross_in = cross_in_f.astype(low)
    cross_pre = matmul(cross_in, cq_weight) + cq_bias
    cross_query_f, cq_pull = jax.vjp(
        lambda values_in, gains_in, shifts_in: head_rotary(
            values_in, gains_in[2], shifts_in[2], tables, head_dim
        ),
        cross_pre,
        gain_table,
        shift_table,
    )
    cross_query_h = heads_first(cross_query_f.astype(low), head_dim)
    step_heads = min(4, cross_query_h.shape[0])
    cross_h, cross_totals = attend(
        cross_query_h, text_all[0], text_all[1], text_count, step_heads
    )
    cross_mixed = heads_last(cross_h)
    stream_two = stream_one + matmul(cross_mixed, cr_weight) + cr_bias

    mlp_in_f, two_pull = jax.vjp(layer_norm, stream_two, two_gain, two_shift)
    mlp_all = gather_tokens(after(mlp_in_f.astype(low), grad_all))
    normed_second = gather_tokens(after(normed[:, model_width:], mlp_all))
    hidden_pre = matmul(mlp_all, up_weight) + up_bias_own
    hidden_f, gelu_pull = jax.vjp(
        lambda values_in: jax.nn.gelu(values_in, approximate=True), hidden_pre
    )
    hidden = hidden_f.astype(low)
    out_partial = matmul(hidden, down_weight).astype(low)
    grad_three = cotangent[0].astype(jnp.float32)
    down_bias_grad = column_sums(cotangent[0])
    pre_grad = gelu_pull(contract_cols(grad_all, down_weight))[0].astype(low)
    up_bias_grad = column_sums(pre_grad)
    mlp_in_grad = sum_tokens(after(contract_cols(pre_grad, up_weight), normed_second))
    down_grad = contract_rows(hidden, grad_all).astype(low)
    up_grad = contract_rows(mlp_all, pre_grad).astype(low)
    mlp_grads = jnp.concatenate(
        [
            fit_rows(up_grad.reshape(owners, own_rows, units), lines),
            fold_down(down_grad.reshape(owners, unit_rows, model_width), units, lines),
        ],
        2,
    )
    mlp_owned = lax.psum_scatter(mlp_grads, "fsdp", scatter_dimension=0, tiled=False)
    mlp_in_grad = after(mlp_in_grad, mlp_grads)
    stream_part, two_gain_grad, two_shift_grad = two_pull(mlp_in_grad)
    stream_grad = grad_three + stream_part

    grad_low = stream_grad.astype(low)
    cr_bias_grad = column_sums(grad_low)
    cross_mixed_grad = contract_cols(grad_low, cr_weight).astype(low)

    stream_three = stream_two + sum_tokens(after(out_partial, mlp_in_grad)) + down_bias
    layer_out = stream_three.astype(low)[None]
    cross_query_grad, text_key_part, text_value_part = attend_back(
        cross_query_h,
        text_all[0],
        text_all[1],
        cross_totals,
        heads_first(cross_mixed_grad, head_dim),
        text_count,
        step_heads,
    )
    cross_query_grad = heads_last(cross_query_grad)
    cross_out_low = grad_low
    cross_pre_grad, gains_from_cross, shifts_from_cross = cq_pull(
        cross_query_grad.astype(jnp.float32)
    )
    cross_pre_low = cross_pre_grad.astype(low)
    cq_bias_grad = column_sums(cross_pre_low)
    stream_part, three_gain_grad, three_shift_grad = three_pull(
        contract_cols(cross_pre_low, cq_weight)
    )
    stream_grad = stream_grad + stream_part

    grad_low = stream_grad.astype(low)
    at_bias_grad = column_sums(grad_low)
    mixed_grad = contract_cols(grad_low, at_weight).astype(low)
    mixed_back = to_heads(after(mixed_grad, stream_three))
    row_owned = lax.psum_scatter(
        row_grads(
            jnp.stack([mixed, cross_in, cross_mixed]),
            jnp.stack([grad_low, cross_pre_low, cross_out_low]),
            owners,
        ),
        "fsdp",
        scatter_dimension=0,
        tiled=False,
    )
    query_grad, key_grad, value_grad = attend_back(
        query_h, key_h, value_h, self_totals, heads_first(mixed_back, head_dim), all_tokens
    )

    text_parts = jnp.stack([text_key_part, text_value_part])[:, :, :text_rows].astype(low)
    text_parts = text_parts.reshape(2, ways, -1, text_rows, head_dim)
    text_parts = text_parts.transpose(1, 3, 0, 2, 4).reshape(ways, text_rows, 2 * width)
    text_kv_grad = jnp.sum(
        swap(after(text_parts, mixed_back), "seq").astype(jnp.float32), 0
    )[:text_count]
    key_pre_grad, gains_from_text = tk_pull(text_kv_grad[:, :width])
    text_grad_low = jnp.concatenate(
        [key_pre_grad.astype(low), text_kv_grad[:, width:].astype(low)], 1
    )
    kv_weight_grad = contract_rows(text_now, text_grad_low)
    kv_bias_grad = column_sums(text_grad_low)
    text_part = contract_cols(text_grad_low, kv_weight)
    text_part = jnp.pad(text_part.astype(low), ((0, -text_count % (8 * ways)), (0, 0)))
    text_blocks = text_part.reshape(ways, -1)
    text_size = text_blocks.shape[1]
    text_blocks = jnp.pad(text_blocks, ((0, 0), (0, -text_size % (8 * width))))
    text_blocks = text_blocks.reshape(ways, -1, width)
    query_pre_grad, key_pre_grad2, gains_from_self, shifts_from_self = prep_pull(
        (
            heads_last(query_grad).astype(jnp.float32),
            heads_last(key_grad).astype(low).astype(jnp.float32),
        )
    )
    packed_grad = jnp.concatenate(
        [
            query_pre_grad.astype(low),
            key_pre_grad2.astype(low),
            heads_last(value_grad).astype(low),
        ],
        1,
    )
    entry_grad = sum_tokens(after(contract_cols(packed_grad, pk_weight), text_kv_grad))
    pk_weight_grad = contract_rows(entry_all, packed_grad)
    pk_bias_grad = column_sums(packed_grad)
    shift_part = jnp.sum(entry_grad, 0)
    stream_part, one_gain_grad, one_shift_grad = one_pull(entry_grad)
    stream_grad = stream_grad + stream_part

    grad_low = stream_grad.astype(low)
    sk_bias_grad = column_sums(grad_low)
    shift_rows = jnp.broadcast_to(
        shift_part.astype(low).reshape(1, ways, width), (ways, ways, width)
    )
    cols_in = jnp.concatenate([column_blocks(grad_low), shift_rows, text_blocks], 1)
    cols_out = swap(cols_in, "seq")
    grad_cols = cols_out[:, :tokens].reshape(all_tokens, width)
    rest_sum = jnp.sum(cols_out[:, tokens:].astype(jnp.float32), 0)
    shift_total = rest_sum[:ways].reshape(-1)
    text_sum = rest_sum[ways:].reshape(-1)[:text_size].reshape(-1, text_part.shape[1])
    sk_blocks = jnp.concatenate(
        [
            contract_rows(one_half, grad_cols).astype(low).reshape(-1, 2, own_rows, width)
            for one_half in (normed_first, normed_second)
        ],
        0,
    )
    joined_grad, sk_gain_grad, sk_shift_grad = skip_pull(contract_cols(grad_low, sk_weight))

    def placed(own, groups):
        parts = jnp.zeros((groups, ways, own.shape[0] // groups), jnp.float32)
        parts = lax.dynamic_update_slice_in_dim(parts, own.reshape(groups, 1, -1), place, 1)
        return parts.reshape(-1)

    vector_grads = (
        sk_gain_grad,
        sk_shift_grad,
        sk_bias_grad,
        one_gain_grad,
        one_shift_grad,
        placed(pk_bias_grad, 3),
        at_bias_grad,
        three_gain_grad,
        three_shift_grad,
        cq_bias_grad,
        placed(kv_bias_grad, 2),
        cr_bias_grad,
        two_gain_grad,
        two_shift_grad,
        placed(up_bias_grad, owners),
        down_bias_grad,
    )
    table_grads = jnp.concatenate(
        [
            (gains_from_cross + gains_from_text + gains_from_self).reshape(-1),
            (shifts_from_cross + shifts_from_self).reshape(-1),
        ]
    )
    split_three = [part.reshape(owners, -1) for part in vector_grads]
    pk_at = 5
    pk_thirds = placed(pk_bias_grad, 3).reshape(3, model_width)
    split_three[pk_at : pk_at + 1] = [
        pk_thirds[:2].reshape(owners, -1),
        pk_thirds[2].reshape(owners, -1),
    ]
    split_three.append(jnp.broadcast_to(table_grads[None], (owners, table_grads.shape[0])))
    summed_sizes = [part.shape[1] for part in split_three]
    vector_rows = jnp.concatenate(split_three, 1).astype(low)
    vector_pad = -vector_rows.shape[1] % own_rows
    vector_rows = jnp.pad(vector_rows, ((0, 0), (0, vector_pad)))
    shift_low = shift_total.astype(low)
    latent_mark = jnp.arange(owners) == lax.axis_index("fsdp")
    shift_mine = jnp.where(latent_mark[:, None], shift_low[None], jnp.zeros((), low))
    shift_mine = jnp.broadcast_to(
        shift_mine.reshape(1, own_rows, -1), (owners, own_rows, owners * owners)
    )
    tail_parts = [
        sk_blocks[:, 0],
        sk_blocks[:, 1],
        pk_weight_grad.astype(low).reshape(owners, own_rows, -1),
        fit_rows(kv_weight_grad.astype(low).reshape(owners, -1, 2 * width), own_rows),
        vector_rows.reshape(owners, own_rows, -1),
        shift_mine,
    ]
    tail_sizes = [part.shape[2] for part in tail_parts]
    tail_sum = sum_owners(jnp.concatenate(tail_parts, 2))
    shift_all = tail_sum[:, -tail_sizes[-1] :].reshape(owners, model_width)

    row_blocks = row_owned.reshape(ways, -1, row_owned.shape[1])
    row_sum = jnp.sum(swap(row_blocks, "seq").astype(jnp.float32), 0)
    row_total = spread(row_sum.astype(low), "seq").reshape(row_owned.shape).astype(jnp.float32)
    at_total = row_total[:, :model_width]
    cq_total = row_total[:, model_width : 2 * model_width]
    cr_total = row_total[:, 2 * model_width :]

    tail_all = spread(tail_sum[:, : -tail_sizes[-1]].astype(low), "seq")
    text_total = spread(after(text_sum.astype(low), tail_all), "seq")
    text_total = text_total.reshape(-1, text_part.shape[1])[:text_count]
    sk_total, pk_total, kv_total, small_total = lay_tail(tail_all, cross_kv_weight.shape[0])
    small_total = small_total.reshape(-1)
    vector_totals = []
    start = 0
    for size in summed_sizes:
        vector_totals.append(small_total[start : start + size])
        start += size
    table_total = vector_totals.pop()
    gains_total = table_total[: gain_table.size].reshape(gain_table.shape)
    shifts_total = table_total[gain_table.size :].reshape(shift_table.shape)
    md_weight_grad = lax.dot_general(
        lifted_own.astype(jnp.float32),
        shift_all,
        (((0,), (0,)), ((), ())),
        precision=lax.Precision.HIGHEST,
        preferred_element_type=jnp.float32,
    )
    md_bias_grad = lax.dynamic_slice_in_dim(
        jnp.sum(shift_all, 0), lax.axis_index("fsdp") * own_rows, own_rows, 0
    )
    lifted_part = lax.dot_general(
        shift_all,
        mod_weight.astype(jnp.float32),
        (((1,), (1,)), ((), ())),
        precision=lax.Precision.HIGHEST,
        preferred_element_type=jnp.float32,
    )
    lifted_grad = swap(lifted_part, "fsdp").reshape(1, model_width)
    condition_grad = silu_pull(lifted_grad)[0]

    mlp_all_grads = lax.all_gather(mlp_owned, "seq", axis=0, tiled=False)
    up_total, down_total = lay_units(mlp_all_grads, own_rows, model_width)
    (
        sk_gain_total,
        sk_shift_total,
        sk_bias_total,
        one_gain_total,
        one_shift_total,
        pk_bias_total,
        value_bias_total,
        at_bias_total,
        three_gain_total,
        three_shift_total,
        cq_bias_total,
        kv_bias_total,
        cr_bias_total,
        two_gain_total,
        two_shift_total,
        up_bias_total,
        down_bias_total,
    ) = vector_totals
    return (
        layer_out,
        joined_grad[:, :model_width].astype(low)[None],
        joined_grad[:, model_width:].astype(low)[None],
        text_total[None],
        condition_grad,
        sk_gain_total,
        sk_shift_total,
        sk_total,
        sk_bias_total,
        md_weight_grad,
        md_bias_grad,
        one_gain_total,
        one_shift_total,
        pk_total,
        pk_bias_total,
        value_bias_total,
        gains_total,
        shifts_total,
        at_total,
        at_bias_total,
        three_gain_total,
        three_shift_total,
        cq_total,
        cq_bias_total,
        kv_total,
        kv_bias_total,
        cr_total,
        cr_bias_total,
        two_gain_total,
        two_shift_total,
        up_total,
        up_bias_total,
        down_total,
        down_bias_total,
    )


def solution(mesh):
    in_specs = (
        P("fsdp", "seq", None),
        P("fsdp", "seq", None),
        P("fsdp", None, None),
        P("fsdp", None),
        P("seq", None),
        P("fsdp", "seq", None),
        P("fsdp"),
        P("fsdp"),
        P("fsdp", None),
        P("fsdp"),
        P("fsdp", None),
        P("fsdp"),
        P("fsdp"),
        P("fsdp"),
        P("fsdp", None),
        P("fsdp"),
        P(),
        P(),
        P("fsdp", None),
        P("fsdp"),
        P("fsdp"),
        P("fsdp"),
        P("fsdp", None),
        P("fsdp"),
        P("fsdp", None),
        P("fsdp"),
        P("fsdp", None),
        P("fsdp"),
        P("fsdp"),
        P("fsdp"),
        P("fsdp", None),
        P("fsdp"),
        P("fsdp", None),
        P("fsdp"),
    )
    out_specs = (
        P("fsdp", "seq", None),
        P("fsdp", "seq", None),
        P("fsdp", "seq", None),
        P("fsdp", None, None),
        P("fsdp", None),
        P("fsdp"),
        P("fsdp"),
        P("fsdp", None),
        P("fsdp"),
        P("fsdp", None),
        P("fsdp"),
        P("fsdp"),
        P("fsdp"),
        P("fsdp", None),
        P("fsdp"),
        P("fsdp"),
        P(),
        P(),
        P("fsdp", None),
        P("fsdp"),
        P("fsdp"),
        P("fsdp"),
        P("fsdp", None),
        P("fsdp"),
        P("fsdp", None),
        P("fsdp"),
        P("fsdp", None),
        P("fsdp"),
        P("fsdp"),
        P("fsdp"),
        P("fsdp", None),
        P("fsdp"),
        P("fsdp", None),
        P("fsdp"),
    )
    return jax.shard_map(local, mesh=mesh, in_specs=in_specs, out_specs=out_specs, check_vma=False)
```

```python
import functools
import math

import jax
import jax.numpy as jnp
from jax import lax
from jax.experimental import pallas as pl
from jax.experimental.pallas import tpu as pltpu
from jax.sharding import PartitionSpec as P


def layer_norm(inputs, gain_vector, shift_vector):
    centred = inputs - jnp.mean(inputs, -1, keepdims=True)
    variance = jnp.mean(centred * centred, -1, keepdims=True)
    return centred * lax.rsqrt(variance + 1e-06) * gain_vector + shift_vector


def rotary_tables(positions, head_dim):
    quarter = head_dim // 4
    exponent = jnp.arange(quarter, dtype=jnp.float32) * (2.0 / (head_dim // 2))
    inverse = jnp.power(jnp.float32(10000.0), -exponent)
    places = positions.astype(jnp.float32)
    angle_rows = places[:, 0:1] * inverse
    angle_cols = places[:, 1:2] * inverse
    return (jnp.cos(angle_rows), jnp.sin(angle_rows), jnp.cos(angle_cols), jnp.sin(angle_cols))


def rotate(inputs, tables):
    cos_rows, sin_rows, cos_cols, sin_cols = tuple((one_table[:, None, :] for one_table in tables))
    quarter = inputs.shape[-1] // 4
    first_a = inputs[..., :quarter]
    first_b = inputs[..., quarter : 2 * quarter]
    second_a = inputs[..., 2 * quarter : 3 * quarter]
    second_b = inputs[..., 3 * quarter :]
    return jnp.concatenate(
        [
            first_a * cos_rows - first_b * sin_rows,
            first_a * sin_rows + first_b * cos_rows,
            second_a * cos_cols - second_b * sin_cols,
            second_a * sin_cols + second_b * cos_cols,
        ],
        -1,
    )


def head_norm(inputs, gain_vector, shift_vector, head_dim):
    row_count = inputs.shape[0]
    shaped = inputs.reshape(row_count, -1, head_dim)
    return layer_norm(shaped, gain_vector, shift_vector).reshape(row_count, -1)


def head_rotary(inputs, gain_vector, shift_vector, tables, head_dim):
    row_count = inputs.shape[0]
    shaped = inputs.reshape(row_count, -1, head_dim)
    return rotate(layer_norm(shaped, gain_vector, shift_vector), tables).reshape(row_count, -1)


def matmul(left_side, right_side):
    return jnp.dot(left_side, right_side, preferred_element_type=jnp.float32)


def contract_rows(left_side, right_side):
    return lax.dot_general(
        left_side, right_side, (((0,), (0,)), ((), ())), preferred_element_type=jnp.float32
    )


def contract_cols(left_side, right_side):
    return lax.dot_general(
        left_side, right_side, (((1,), (1,)), ((), ())), preferred_element_type=jnp.float32
    )


def column_sums(grads_low):
    return jnp.sum(grads_low.astype(jnp.float32), 0)


def to_float(vectors):
    return tuple((one_vector.astype(jnp.float32) for one_vector in vectors))


def forward_kernel(query_ref, keys_ref, values_ref, mixed_ref, totals_ref, *, scale, valid):
    for head in range(query_ref.shape[0]):
        scores = contract_cols(query_ref[head], keys_ref[head]) * scale
        if valid < scores.shape[1]:
            column = lax.broadcasted_iota(jnp.int32, scores.shape, 1)
            scores = jnp.where(column < valid, scores, -1e30)
        row_top = jnp.max(scores, -1, keepdims=True)
        weights = jnp.exp(scores - row_top)
        totals = jnp.sum(weights, -1, keepdims=True)
        probs = (weights * (1.0 / totals)).astype(jnp.bfloat16)
        mixed_ref[head] = matmul(probs, values_ref[head]).astype(mixed_ref.dtype)
        totals_ref[head] = row_top + jnp.log(totals)


def attend(queries, keys_in, values_in, valid, step_heads=1):
    heads, row_count, head_dim = queries.shape
    key_count = keys_in.shape[1]
    block_rows = min(512, row_count)
    rows_spec = pl.BlockSpec((step_heads, block_rows, head_dim), lambda h, i: (h, i, 0))
    keys_spec = pl.BlockSpec((step_heads, key_count, head_dim), lambda h, i: (h, 0, 0))
    return pl.pallas_call(
        functools.partial(forward_kernel, scale=1.0 / math.sqrt(head_dim), valid=valid),
        grid=(heads // step_heads, row_count // block_rows),
        in_specs=[rows_spec, keys_spec, keys_spec],
        out_specs=[rows_spec, pl.BlockSpec((step_heads, block_rows, 1), lambda h, i: (h, i, 0))],
        out_shape=[
            jax.ShapeDtypeStruct(queries.shape, jnp.bfloat16),
            jax.ShapeDtypeStruct((heads, row_count, 1), jnp.float32),
        ],
        compiler_params=pltpu.CompilerParams(vmem_limit_bytes=40 * 1024 * 1024),
        cost_estimate=pl.CostEstimate(
            flops=4 * heads * row_count * key_count * head_dim,
            bytes_accessed=4 * heads * (row_count + key_count) * head_dim,
            transcendentals=heads * row_count * key_count,
        ),
        name="attend",
    )(queries, keys_in, values_in)


def backward_kernel(
    query_ref,
    keys_ref,
    values_ref,
    totals_ref,
    grad_ref,
    query_grad_ref,
    keys_grad_ref,
    values_grad_ref,
    *,
    scale,
    valid,
):
    first = pl.program_id(1) == 0
    for head in range(query_ref.shape[0]):
        query_block = query_ref[head]
        grad_block = grad_ref[head]
        keys_now = keys_ref[head]
        probs = jnp.exp(contract_cols(query_block, keys_now) * scale - totals_ref[head])
        if valid < probs.shape[1]:
            column = lax.broadcasted_iota(jnp.int32, probs.shape, 1)
            probs = jnp.where(column < valid, probs, 0.0)
        weighted = probs * contract_cols(grad_block, values_ref[head])
        scores_grad = weighted - probs * jnp.sum(weighted, -1, keepdims=True)
        scores_low = (scores_grad * scale).astype(jnp.bfloat16)
        query_grad_ref[head] = matmul(scores_low, keys_now).astype(query_grad_ref.dtype)
        keys_part = contract_rows(scores_low, query_block)
        values_part = contract_rows(probs.astype(jnp.bfloat16), grad_block)

        @pl.when(first)
        def _():
            keys_grad_ref[head] = keys_part
            values_grad_ref[head] = values_part

        @pl.when(jnp.logical_not(first))
        def _():
            keys_grad_ref[head] += keys_part
            values_grad_ref[head] += values_part


def attend_back(queries, keys_in, values_in, totals, grad_out, valid, step_heads=1):
    heads, row_count, head_dim = queries.shape
    key_count = keys_in.shape[1]
    block_rows = min(512, row_count)
    rows_spec = pl.BlockSpec((step_heads, block_rows, head_dim), lambda h, i: (h, i, 0))
    keys_spec = pl.BlockSpec((step_heads, key_count, head_dim), lambda h, i: (h, 0, 0))
    totals_spec = pl.BlockSpec((step_heads, block_rows, 1), lambda h, i: (h, i, 0))
    return pl.pallas_call(
        functools.partial(backward_kernel, scale=1.0 / math.sqrt(head_dim), valid=valid),
        grid=(heads // step_heads, row_count // block_rows),
        in_specs=[rows_spec, keys_spec, keys_spec, totals_spec, rows_spec],
        out_specs=[rows_spec, keys_spec, keys_spec],
        out_shape=[
            jax.ShapeDtypeStruct(queries.shape, jnp.bfloat16),
            jax.ShapeDtypeStruct(keys_in.shape, jnp.float32),
            jax.ShapeDtypeStruct(keys_in.shape, jnp.float32),
        ],
        compiler_params=pltpu.CompilerParams(vmem_limit_bytes=40 * 1024 * 1024),
        cost_estimate=pl.CostEstimate(
            flops=10 * heads * row_count * key_count * head_dim,
            bytes_accessed=8 * heads * (row_count + key_count) * head_dim,
            transcendentals=heads * row_count * key_count,
        ),
        name="attend_back",
    )(queries, keys_in, values_in, totals, grad_out)


def row_grads_kernel(left_ref, right_ref, out_ref):
    product = contract_rows(left_ref[0], right_ref[0])
    rows = out_ref.shape[1]
    for owner in range(out_ref.shape[0]):
        out_ref[owner] = product[owner * rows : (owner + 1) * rows].astype(out_ref.dtype)


def row_grads(lefts, rights, owners):
    count, tokens, width = lefts.shape
    rows = width // owners
    pair_spec = pl.BlockSpec((1, tokens, width), lambda i: (i, 0, 0))
    return pl.pallas_call(
        row_grads_kernel,
        grid=(count,),
        in_specs=[pair_spec, pair_spec],
        out_specs=pl.BlockSpec((owners, rows, width), lambda i: (0, 0, i)),
        out_shape=jax.ShapeDtypeStruct((owners, rows, count * width), jnp.bfloat16),
        compiler_params=pltpu.CompilerParams(vmem_limit_bytes=48 * 1024 * 1024),
        cost_estimate=pl.CostEstimate(
            flops=2 * count * tokens * width * width,
            bytes_accessed=2 * count * (width * width + 2 * tokens * width),
            transcendentals=0,
        ),
        name="row_grads",
    )(lefts, rights)


def side_by_side(pieces):
    return jnp.concatenate([piece.astype(jnp.float32) for piece in pieces], 1)


def pack_kernel(first_ref, second_ref, cols_ref, packed_ref, text_ref, small_ref, out_ref):
    owners, rows = text_ref.shape[:2]
    cols = cols_ref[...]
    products = [contract_rows(half_ref[...], cols) for half_ref in (first_ref, second_ref)]
    for owner in range(owners):
        product = products[owner // (owners // 2)]
        start = (owner % (owners // 2)) * 2 * rows
        line = side_by_side(
            [
                product[start : start + rows],
                product[start + rows : start + 2 * rows],
                packed_ref[owner * rows : (owner + 1) * rows],
                text_ref[owner],
                small_ref[owner],
            ]
        )
        out_ref[owner % 2, owner // 2] = line.astype(out_ref.dtype)


def pack_tail(first, second, cols, packed, text, small):
    owners, rows = text.shape[:2]
    lanes = 2 * cols.shape[1] + packed.shape[1] + text.shape[2] + small.shape[2]
    return pl.pallas_call(
        pack_kernel,
        out_shape=jax.ShapeDtypeStruct((2, owners // 2, rows, lanes), jnp.bfloat16),
        compiler_params=pltpu.CompilerParams(vmem_limit_bytes=48 * 1024 * 1024),
        cost_estimate=pl.CostEstimate(
            flops=4 * first.size * cols.shape[1],
            bytes_accessed=4 * first.size + 4 * owners * rows * lanes,
            transcendentals=0,
        ),
        name="pack_tail",
    )(first, second, cols, packed, text, small)


def tail_kernel(all_ref, skip_ref, packed_ref, text_ref, whole_ref, small_ref):
    ways, rows = all_ref.shape[:2]
    model_width = skip_ref.shape[1]
    width = model_width // ways

    def joined(start, count, size):
        return side_by_side(
            [all_ref[way, :, start : start + size][:count] for way in range(ways)]
        )

    skip_ref[:rows] = joined(0, rows, width)
    skip_ref[rows:] = joined(width, rows, width)
    for third in range(3):
        packed_ref[:, third * model_width : (third + 1) * model_width] = joined(
            (2 + third) * width, rows, width
        )
    for side in range(2):
        text_ref[:, side * model_width : (side + 1) * model_width] = joined(
            (5 + side) * width, text_ref.shape[0], width
        )
    whole_ref[...] = joined(7 * width, rows, 3 * width)
    total = all_ref[0, :, 10 * width :].astype(jnp.float32)
    for way in range(1, ways):
        total += all_ref[way, :, 10 * width :].astype(jnp.float32)
    small_ref[...] = total


def lay_tail(blocks, text_rows):
    ways, rows, lanes = blocks.shape
    width = 2 * rows
    model_width = ways * width
    return pl.pallas_call(
        tail_kernel,
        out_shape=[
            jax.ShapeDtypeStruct((2 * rows, model_width), jnp.float32),
            jax.ShapeDtypeStruct((rows, 3 * model_width), jnp.float32),
            jax.ShapeDtypeStruct((text_rows, 2 * model_width), jnp.float32),
            jax.ShapeDtypeStruct((rows, 3 * model_width), jnp.float32),
            jax.ShapeDtypeStruct((rows, lanes - 10 * width), jnp.float32),
        ],
        compiler_params=pltpu.CompilerParams(vmem_limit_bytes=40 * 1024 * 1024),
        name="lay_tail",
    )(blocks)


def skip_back_kernel(grad_ref, first_ref, second_ref, out_ref):
    grad = grad_ref[...]
    halves = [contract_cols(grad, half_ref[...]) for half_ref in (first_ref, second_ref)]
    rows = grad.shape[1] // 16
    out_ref[...] = side_by_side(
        [half[:, i * rows : (i + 1) * rows] for i in range(16) for half in halves]
    )


def skip_back(grad_low, first_rows):
    tokens, model_width = grad_low.shape
    return pl.pallas_call(
        skip_back_kernel,
        grid=(1,),
        in_specs=[
            pl.BlockSpec((tokens, model_width), lambda i: (0, 0)),
            pl.BlockSpec((model_width, model_width), lambda i: (0, 0)),
            pl.BlockSpec((model_width, model_width), lambda i: (0, 1)),
        ],
        out_specs=pl.BlockSpec((tokens, 2 * model_width), lambda i: (0, 0)),
        out_shape=jax.ShapeDtypeStruct((tokens, 2 * model_width), jnp.float32),
        compiler_params=pltpu.CompilerParams(vmem_limit_bytes=48 * 1024 * 1024),
        cost_estimate=pl.CostEstimate(
            flops=4 * tokens * model_width * model_width,
            bytes_accessed=4 * model_width * (model_width + 2 * tokens),
            transcendentals=0,
        ),
        name="skip_back",
    )(grad_low, first_rows, first_rows)


def units_kernel(all_ref, up_ref, down_ref):
    ways = all_ref.shape[0]
    rows, hidden = up_ref.shape
    units = hidden // ways
    owners = 16
    own = units // owners
    for owner in range(owners):
        start = owner * ways * own
        up_ref[:, start : start + ways * own] = side_by_side(
            [all_ref[way, :rows, owner * own : (owner + 1) * own] for way in range(ways)]
        )
    model_width = down_ref.shape[1]
    split = min(units, model_width)
    for way in range(ways):
        place = slice(way * own, (way + 1) * own)
        down_ref[place, :split] = all_ref[way, :own, units : units + split].astype(jnp.float32)
        if split < model_width:
            down_ref[place, split:] = all_ref[
                way, own : 2 * own, units : units + model_width - split
            ].astype(jnp.float32)


def lay_units(blocks, rows, model_width):
    ways, lines, lanes = blocks.shape
    units = lanes // 2
    return pl.pallas_call(
        units_kernel,
        out_shape=[
            jax.ShapeDtypeStruct((rows, ways * units), jnp.float32),
            jax.ShapeDtypeStruct((ways * units // 16, model_width), jnp.float32),
        ],
        compiler_params=pltpu.CompilerParams(vmem_limit_bytes=40 * 1024 * 1024),
        name="lay_units",
    )(blocks)


def fold_down(part, units, lines):
    first = part[..., :units]
    rest = part[..., units:]
    pad = [(0, 0)] * (part.ndim - 1) + [(0, units - rest.shape[-1])]
    both = jnp.concatenate([first, jnp.pad(rest, pad)], -2)
    return fit_rows(both, lines)


def fit_rows(part, lines):
    pad = [(0, 0)] * part.ndim
    pad[-2] = (0, lines - part.shape[-2])
    return jnp.pad(part, pad)


def swap(blocks, axis_name):
    return lax.all_to_all(blocks, axis_name, split_axis=0, concat_axis=0, tiled=True)


def spread(part, axis_name):
    size = lax.axis_size(axis_name)
    return swap(jnp.broadcast_to(part[None], (size,) + part.shape), axis_name)


def grid_place():
    index = lax.axis_index("seq")
    return index // 4, index % 4


def grid_send(value, pair, step):
    links = [(i, ((i // 4) ^ pair) * 4 + (i + step) % 4) for i in range(8)]
    return lax.ppermute(value, "seq", links)


def gather_tokens(part):
    pair, ring = grid_place()
    mate = grid_send(part, 1, 0)
    below = grid_send(part, 0, 1)
    above = grid_send(part, 0, -1)
    far = grid_send(part, 0, 2)
    mate_below = grid_send(mate, 0, 1)
    mate_above = grid_send(mate, 0, -1)
    mate_far = grid_send(far, 1, 0)
    here, there = pair * 4, (1 - pair) * 4
    buffer = jnp.zeros((8,) + part.shape, part.dtype)
    for one, spot in (
        (part, here + ring),
        (mate, there + ring),
        (below, here + (ring + 3) % 4),
        (above, here + (ring + 1) % 4),
        (far, here + (ring + 2) % 4),
        (mate_below, there + (ring + 3) % 4),
        (mate_above, there + (ring + 1) % 4),
        (mate_far, there + (ring + 2) % 4),
    ):
        buffer = lax.dynamic_update_index_in_dim(buffer, one, spot, 0)
    return buffer.reshape((-1,) + part.shape[1:])


def gather_behind(part):
    return spread(part, "seq").reshape((-1,) + part.shape[1:])


def sum_tokens(partial):
    low = jnp.bfloat16
    blocks = partial.astype(low).reshape((8, -1) + partial.shape[1:])
    pair, ring = grid_place()

    def meant(mate, step):
        spot = jnp.where(mate, 1 - pair, pair) * 4 + (ring + step) % 4
        return lax.dynamic_index_in_dim(blocks, spot, 0, False)

    def total(*parts):
        return sum(part.astype(jnp.float32) for part in parts)

    far_mate = grid_send(meant(True, 2), 1, 0)
    mate_below = grid_send(meant(True, 1), 0, 1)
    mate_above = grid_send(meant(True, 3), 0, -1)
    below = grid_send(meant(False, 1), 0, 1)
    above = grid_send(meant(False, 3), 0, -1)
    far = grid_send(total(meant(False, 2), far_mate).astype(low), 0, 2)
    mate = grid_send(total(meant(True, 0), mate_below, mate_above).astype(low), 1, 0)
    return total(meant(False, 0), below, above, far, mate)


def sum_behind(partial):
    blocks = partial.astype(jnp.bfloat16).reshape((8, -1) + partial.shape[1:])
    return jnp.sum(swap(blocks, "seq").astype(jnp.float32), 0)


def column_blocks(values):
    size = lax.axis_size("seq")
    rows = values.shape[0]
    return values.reshape(rows, size, -1).transpose(1, 0, 2)


def own_columns(weight, groups, size, place):
    rows = weight.shape[0]
    parts = weight.reshape(rows, groups, size, -1)
    taken = lax.dynamic_slice_in_dim(parts, place, 1, 2)
    return taken.reshape(rows, -1)


def after(values, others):
    return lax.optimization_barrier((values, others))[0]


def sum_owners(by_core):
    owners = 2 * by_core.shape[1]
    core = lax.axis_index("fsdp") % 2
    kept = lax.dynamic_index_in_dim(by_core, core, 0, False)
    sent = lax.dynamic_index_in_dim(by_core, 1 - core, 0, False)
    arrived = lax.ppermute(sent, "fsdp", [(i, i ^ 1) for i in range(owners)])
    chip = (kept.astype(jnp.float32) + arrived.astype(jnp.float32)).astype(jnp.bfloat16)
    groups = [list(range(0, owners, 2)), list(range(1, owners, 2))]
    swapped = lax.all_to_all(
        chip, "fsdp", split_axis=0, concat_axis=0, axis_index_groups=groups, tiled=True
    )
    return jnp.sum(swapped.astype(jnp.float32), 0)


def heads_first(values, head_dim):
    rows = values.shape[0]
    return values.reshape(rows, -1, head_dim).transpose(1, 0, 2)


def heads_last(values):
    return values.transpose(1, 0, 2).reshape(values.shape[1], -1)


def local(
    latent,
    skip_input,
    text_tokens,
    condition,
    positions,
    cotangent,
    skip_gain,
    skip_shift,
    skip_weight,
    skip_bias,
    mod_weight,
    mod_bias,
    norm1_gain,
    norm1_shift,
    qkv_weight,
    qkv_bias,
    head_gains,
    head_shifts,
    attn_weight,
    attn_bias,
    norm3_gain,
    norm3_shift,
    cross_q_weight,
    cross_q_bias,
    cross_kv_weight,
    cross_kv_bias,
    cross_weight,
    cross_bias,
    norm2_gain,
    norm2_shift,
    fc1_weight,
    fc1_bias,
    fc2_weight,
    fc2_bias,
):
    ways = lax.axis_size("seq")
    owners = lax.axis_size("fsdp")
    place = lax.axis_index("seq")
    head_dim = head_gains.shape[1]
    tokens, model_width = latent.shape[1:]
    width = model_width // ways
    low = jnp.bfloat16
    gain_table = head_gains.astype(jnp.float32)
    shift_table = head_shifts.astype(jnp.float32)
    tables = rotary_tables(positions, head_dim)

    own_rows = model_width // owners
    packed_own = own_columns(qkv_weight, 3, ways, place)
    packed_pad = -packed_own.shape[1] % 128
    text_own = own_columns(cross_kv_weight, 2, ways, place)
    first_own = jnp.concatenate(
        [
            skip_weight[:own_rows],
            skip_weight[own_rows:],
            jnp.pad(packed_own, ((0, 0), (0, packed_pad))),
            fit_rows(text_own, own_rows),
        ],
        1,
    )
    first_rows = lax.all_gather(first_own, "fsdp", axis=0, tiled=True)
    second_own = jnp.concatenate([attn_weight, cross_q_weight, cross_weight], 1)
    second_own = after(second_own, first_rows)
    second_rows = lax.all_gather(second_own, "fsdp", axis=0, tiled=True)
    unit_rows = fc2_weight.shape[0] // ways
    down_own = lax.dynamic_slice_in_dim(fc2_weight, place * unit_rows, unit_rows, 0)
    up_own = own_columns(fc1_weight, owners, ways, place)
    units = up_own.shape[1]
    lines = max(own_rows, 2 * unit_rows)
    third_own = jnp.concatenate(
        [fit_rows(up_own, lines), fold_down(down_own, units, lines)], 1
    )
    third_own = after(third_own, second_rows)
    third_rows = lax.all_gather(third_own, "fsdp", axis=0, tiled=False)
    pk_start = 2 * model_width
    kv_start = pk_start + 3 * width + packed_pad
    pk_weight = first_rows[:, pk_start : pk_start + 3 * width]
    kv_weight = first_rows.reshape(owners, own_rows, -1)[:, : text_own.shape[0], kv_start:]
    kv_weight = kv_weight.reshape(-1, 2 * width)
    up_weight = third_rows[:, :own_rows, :units].reshape(model_width, units)
    down_weight = jnp.concatenate(
        [
            third_rows[:, :unit_rows, units : units + min(units, model_width)],
            third_rows[:, unit_rows : 2 * unit_rows, units : units + max(model_width - units, 0)],
        ],
        2,
    ).reshape(units, model_width)
    at_weight = second_rows[:, :model_width]
    cq_weight = second_rows[:, model_width : 2 * model_width]
    cr_weight = second_rows[:, 2 * model_width :]

    lifted_f, silu_pull = jax.vjp(jax.nn.silu, condition.astype(jnp.float32))
    lifted = lifted_f.astype(low)
    vectors = (
        skip_gain,
        skip_shift,
        skip_bias,
        mod_bias,
        norm1_gain,
        norm1_shift,
        qkv_bias,
        attn_bias,
        norm3_gain,
        norm3_shift,
        cross_q_bias,
        cross_kv_bias,
        cross_bias,
        norm2_gain,
        norm2_shift,
        fc1_bias,
        fc2_bias,
    )
    vector_own = jnp.concatenate(vectors)
    vector_all = swap(
        jnp.concatenate(
            [
                jnp.broadcast_to(vector_own[None], (owners, vector_own.shape[0])),
                lifted.reshape(owners, own_rows),
            ],
            1,
        ),
        "fsdp",
    )
    pieces = []
    start = 0
    for one_vector in vectors:
        size = one_vector.shape[0]
        pieces.append(vector_all[:, start : start + size].reshape(-1).astype(jnp.float32))
        start += size
    lifted_own = vector_all[:, start:]
    (
        sk_gain,
        sk_shift,
        sk_bias,
        md_bias,
        one_gain,
        one_shift,
        pk_bias,
        at_bias,
        three_gain,
        three_shift,
        cq_bias,
        kv_bias,
        cr_bias,
        two_gain,
        two_shift,
        up_bias,
        down_bias,
    ) = pieces
    pk_bias_own = own_columns(pk_bias[None], 3, ways, place)[0]
    kv_bias_own = own_columns(kv_bias[None], 2, ways, place)[0]
    up_bias_own = own_columns(up_bias[None], owners, ways, place)[0]
    shift_row = (
        jnp.sum(swap(matmul(lifted_own, mod_weight), "fsdp"), 0, keepdims=True) + md_bias
    )
    places_all = spread(positions.astype(jnp.float32), "seq").reshape(-1, 2)
    tables_all = rotary_tables(places_all, head_dim)

    joined = jnp.concatenate([latent[0], skip_input[0]], 1).astype(jnp.float32)
    normed_f, skip_pull = jax.vjp(layer_norm, joined, sk_gain, sk_shift)
    normed = normed_f.astype(low)
    normed_halves = normed.reshape(tokens, owners, 2, own_rows).transpose(2, 0, 1, 3)
    normed_halves = normed_halves.reshape(2, tokens, model_width)
    normed_first = gather_behind(normed[:, :model_width])
    first_now = after(first_rows, (normed_halves, shift_row, places_all))
    stream_zero = (
        matmul(normed_halves[0], first_now[:, :model_width])
        + matmul(normed_halves[1], first_now[:, model_width : 2 * model_width])
        + sk_bias
    )

    entry_f, one_pull = jax.vjp(layer_norm, stream_zero, one_gain, one_shift)
    entry = (entry_f + shift_row).astype(low)

    entry_all = gather_tokens(after(entry, normed_first))

    text_now = text_tokens[0]
    text_count = text_now.shape[0]
    text_packed = matmul(text_now, kv_weight) + kv_bias_own
    text_keys_f, tk_pull = jax.vjp(
        lambda values_in, gains_in: head_norm(values_in, gains_in[3], 0.0, head_dim),
        text_packed[:, :width],
        gain_table,
    )
    text_own = jnp.concatenate(
        [text_keys_f.astype(low), text_packed[:, width:].astype(low)], 1
    )
    text_rows = text_count + -text_count % 16
    text_own = jnp.pad(text_own, ((0, text_rows - text_count), (0, 0)))
    text_spread = spread(after(text_own, entry_all), "seq")
    text_all = text_spread.reshape(ways, text_rows, 2, -1, head_dim)
    text_all = text_all.transpose(2, 0, 3, 1, 4).reshape(2, -1, text_rows, head_dim)
    text_all = jnp.pad(text_all, ((0, 0), (0, 0), (0, -text_rows % 128), (0, 0)))
    packed = matmul(entry_all, pk_weight) + pk_bias_own

    def prepare(query_pre, key_pre, gains_in, shifts_in):
        return (
            head_rotary(query_pre, gains_in[0], shifts_in[0], tables_all, head_dim),
            head_rotary(key_pre, gains_in[1], shifts_in[1], tables_all, head_dim),
        )

    (query_f, key_f), prep_pull = jax.vjp(
        prepare, packed[:, :width], packed[:, width : 2 * width], gain_table, shift_table
    )
    query_h = heads_first(query_f.astype(low), head_dim)
    key_h = heads_first(key_f.astype(low), head_dim)
    value_h = heads_first(packed[:, 2 * width :].astype(low), head_dim)
    all_tokens = query_h.shape[1]
    mixed_h, self_totals = attend(query_h, key_h, value_h, all_tokens)
    mixed_h = after(mixed_h, text_spread)

    def to_heads(values):
        return swap(column_blocks(values), "seq").reshape(all_tokens, -1)

    def to_tokens(values_h):
        blocks = swap(heads_last(values_h).reshape(ways, tokens, width), "seq")
        return blocks.transpose(1, 0, 2).reshape(tokens, model_width)

    mixed = to_tokens(mixed_h)
    grad_all = gather_behind(after(cotangent[0], mixed))
    stream_one = stream_zero + matmul(mixed, at_weight) + at_bias

    cross_in_f, three_pull = jax.vjp(layer_norm, stream_one, three_gain, three_shift)
    cross_in = cross_in_f.astype(low)
    cross_pre = matmul(cross_in, cq_weight) + cq_bias
    cross_query_f, cq_pull = jax.vjp(
        lambda values_in, gains_in, shifts_in: head_rotary(
            values_in, gains_in[2], shifts_in[2], tables, head_dim
        ),
        cross_pre,
        gain_table,
        shift_table,
    )
    cross_query_h = heads_first(cross_query_f.astype(low), head_dim)
    step_heads = min(4, cross_query_h.shape[0])
    cross_h, cross_totals = attend(
        cross_query_h, text_all[0], text_all[1], text_count, step_heads
    )
    cross_mixed = heads_last(cross_h)
    stream_two = stream_one + matmul(cross_mixed, cr_weight) + cr_bias

    mlp_in_f, two_pull = jax.vjp(layer_norm, stream_two, two_gain, two_shift)
    mlp_all = gather_tokens(mlp_in_f.astype(low))
    normed_second = gather_behind(after(normed[:, model_width:], (mlp_all, grad_all)))
    hidden_pre = matmul(mlp_all, up_weight) + up_bias_own
    hidden_f, gelu_pull = jax.vjp(
        lambda values_in: jax.nn.gelu(values_in, approximate=True), hidden_pre
    )
    hidden = hidden_f.astype(low)
    out_partial = matmul(hidden, down_weight).astype(low)
    grad_three = cotangent[0].astype(jnp.float32)
    down_bias_grad = column_sums(cotangent[0])
    pre_grad = gelu_pull(contract_cols(grad_all, down_weight))[0].astype(low)
    up_bias_grad = column_sums(pre_grad)
    mlp_in_grad = sum_tokens(contract_cols(pre_grad, up_weight))
    down_grad = contract_rows(hidden, grad_all).astype(low)
    up_grad = contract_rows(mlp_all, pre_grad).astype(low)
    mlp_grads = jnp.concatenate(
        [
            fit_rows(up_grad.reshape(owners, own_rows, units), lines),
            fold_down(down_grad.reshape(owners, unit_rows, model_width), units, lines),
        ],
        2,
    )
    mlp_owned = lax.psum_scatter(mlp_grads, "fsdp", scatter_dimension=0, tiled=False)
    mlp_in_grad = after(mlp_in_grad, mlp_grads)
    stream_part, two_gain_grad, two_shift_grad = two_pull(mlp_in_grad)
    stream_grad = grad_three + stream_part

    grad_low = stream_grad.astype(low)
    cr_bias_grad = column_sums(grad_low)
    cross_mixed_grad = contract_cols(grad_low, cr_weight).astype(low)

    stream_three = stream_two + sum_behind(after(out_partial, (mlp_in_grad, normed_second))) + down_bias
    layer_out = stream_three.astype(low)[None]
    cross_query_grad, text_key_part, text_value_part = attend_back(
        cross_query_h,
        text_all[0],
        text_all[1],
        cross_totals,
        heads_first(cross_mixed_grad, head_dim),
        text_count,
        step_heads,
    )
    cross_query_grad = heads_last(cross_query_grad)
    cross_out_low = grad_low
    cross_pre_grad, gains_from_cross, shifts_from_cross = cq_pull(
        cross_query_grad.astype(jnp.float32)
    )
    cross_pre_low = cross_pre_grad.astype(low)
    cq_bias_grad = column_sums(cross_pre_low)
    stream_part, three_gain_grad, three_shift_grad = three_pull(
        contract_cols(cross_pre_low, cq_weight)
    )
    stream_grad = stream_grad + stream_part

    grad_low = stream_grad.astype(low)
    at_bias_grad = column_sums(grad_low)
    mixed_grad = contract_cols(grad_low, at_weight).astype(low)
    mixed_back = to_heads(mixed_grad)
    whole_grads = row_grads(
        jnp.stack([mixed, cross_in, cross_mixed]),
        jnp.stack([grad_low, cross_pre_low, cross_out_low]),
        owners,
    )
    row_owned = lax.psum_scatter(whole_grads, "fsdp", scatter_dimension=0, tiled=False)
    mixed_back = after(mixed_back, whole_grads)
    query_grad, key_grad, value_grad = attend_back(
        query_h, key_h, value_h, self_totals, heads_first(mixed_back, head_dim), all_tokens
    )

    text_parts = jnp.stack([text_key_part, text_value_part])[:, :, :text_rows].astype(low)
    text_parts = text_parts.reshape(2, ways, -1, text_rows, head_dim)
    text_parts = text_parts.transpose(1, 3, 0, 2, 4).reshape(ways, text_rows, 2 * width)
    text_parts = after(text_parts, stream_three)
    text_kv_grad = jnp.sum(
        swap(after(text_parts, mixed_back), "seq").astype(jnp.float32), 0
    )[:text_count]
    key_pre_grad, gains_from_text = tk_pull(text_kv_grad[:, :width])
    text_grad_low = jnp.concatenate(
        [key_pre_grad.astype(low), text_kv_grad[:, width:].astype(low)], 1
    )
    kv_weight_grad = contract_rows(text_now, text_grad_low)
    kv_bias_grad = column_sums(text_grad_low)
    text_part = contract_cols(text_grad_low, kv_weight)
    text_part = jnp.pad(text_part.astype(low), ((0, -text_count % (8 * ways)), (0, 0)))
    text_sum = sum_behind(text_part)
    query_pre_grad, key_pre_grad2, gains_from_self, shifts_from_self = prep_pull(
        (
            heads_last(query_grad).astype(jnp.float32),
            heads_last(key_grad).astype(low).astype(jnp.float32),
        )
    )
    packed_grad = jnp.concatenate(
        [
            query_pre_grad.astype(low),
            key_pre_grad2.astype(low),
            heads_last(value_grad).astype(low),
        ],
        1,
    )
    entry_grad = sum_tokens(after(contract_cols(packed_grad, pk_weight), text_kv_grad))
    pk_weight_grad = contract_rows(entry_all, packed_grad)
    pk_bias_grad = column_sums(packed_grad)
    text_total = gather_behind(after(text_sum.astype(low), entry_grad))[:text_count]
    shift_part = jnp.sum(entry_grad, 0)
    stream_part, one_gain_grad, one_shift_grad = one_pull(entry_grad)
    stream_grad = stream_grad + stream_part

    grad_low = stream_grad.astype(low)
    sk_bias_grad = column_sums(grad_low)
    shift_rows = jnp.broadcast_to(
        shift_part.astype(low).reshape(1, ways, width), (ways, ways, width)
    )
    cols_in = jnp.concatenate([column_blocks(after(grad_low, text_total)), shift_rows], 1)
    cols_out = swap(cols_in, "seq")
    grad_cols = cols_out[:, :tokens].reshape(all_tokens, width)
    shift_total = jnp.sum(cols_out[:, tokens:].astype(jnp.float32), 0).reshape(-1)
    shift_all = spread(shift_total.astype(low), "fsdp").astype(jnp.float32)
    joined_grad, sk_gain_grad, sk_shift_grad = skip_pull(skip_back(grad_low, first_rows))

    def placed(own, groups):
        parts = jnp.zeros((groups, ways, own.shape[0] // groups), jnp.float32)
        parts = lax.dynamic_update_slice_in_dim(parts, own.reshape(groups, 1, -1), place, 1)
        return parts.reshape(-1)

    vector_grads = (
        sk_gain_grad,
        sk_shift_grad,
        sk_bias_grad,
        one_gain_grad,
        one_shift_grad,
        placed(pk_bias_grad, 3),
        at_bias_grad,
        three_gain_grad,
        three_shift_grad,
        cq_bias_grad,
        placed(kv_bias_grad, 2),
        cr_bias_grad,
        two_gain_grad,
        two_shift_grad,
        placed(up_bias_grad, owners),
        down_bias_grad,
    )
    table_grads = jnp.concatenate(
        [
            (gains_from_cross + gains_from_text + gains_from_self).reshape(-1),
            (shifts_from_cross + shifts_from_self).reshape(-1),
        ]
    )
    split_three = [part.reshape(owners, -1) for part in vector_grads]
    pk_at = 5
    pk_thirds = placed(pk_bias_grad, 3).reshape(3, model_width)
    split_three[pk_at : pk_at + 1] = [
        pk_thirds[:2].reshape(owners, -1),
        pk_thirds[2].reshape(owners, -1),
    ]
    split_three.append(jnp.broadcast_to(table_grads[None], (owners, table_grads.shape[0])))
    summed_sizes = [part.shape[1] for part in split_three]
    vector_rows = jnp.concatenate(split_three, 1).astype(low)
    vector_pad = -vector_rows.shape[1] % own_rows
    vector_rows = jnp.pad(vector_rows, ((0, 0), (0, vector_pad)))
    tail_sum = sum_owners(
        pack_tail(
            normed_first,
            normed_second,
            grad_cols,
            pk_weight_grad,
            fit_rows(kv_weight_grad.astype(low).reshape(owners, -1, 2 * width), own_rows),
            vector_rows.reshape(owners, own_rows, -1),
        )
    ).astype(low)

    row_sum = jnp.sum(swap(column_blocks(row_owned), "seq").astype(jnp.float32), 0)
    lead = 7 * width
    tail_all = spread(
        jnp.concatenate([tail_sum[:, :lead], row_sum.astype(low), tail_sum[:, lead:]], 1), "seq"
    )
    sk_total, pk_total, kv_total, row_total, small_total = lay_tail(
        tail_all, cross_kv_weight.shape[0]
    )
    at_total = row_total[:, :model_width]
    cq_total = row_total[:, model_width : 2 * model_width]
    cr_total = row_total[:, 2 * model_width :]
    small_total = small_total.reshape(-1)
    vector_totals = []
    start = 0
    for size in summed_sizes:
        vector_totals.append(small_total[start : start + size])
        start += size
    table_total = vector_totals.pop()
    gains_total = table_total[: gain_table.size].reshape(gain_table.shape)
    shifts_total = table_total[gain_table.size :].reshape(shift_table.shape)
    md_weight_grad = lax.dot_general(
        lifted_own.astype(jnp.float32),
        shift_all,
        (((0,), (0,)), ((), ())),
        precision=lax.Precision.HIGHEST,
        preferred_element_type=jnp.float32,
    )
    md_bias_grad = lax.dynamic_slice_in_dim(
        jnp.sum(shift_all, 0), lax.axis_index("fsdp") * own_rows, own_rows, 0
    )
    lifted_part = lax.dot_general(
        shift_all,
        mod_weight.astype(jnp.float32),
        (((1,), (1,)), ((), ())),
        precision=lax.Precision.HIGHEST,
        preferred_element_type=jnp.float32,
    )
    lifted_grad = swap(after(lifted_part, tail_all), "fsdp").reshape(1, model_width)
    condition_grad = silu_pull(lifted_grad)[0]

    mlp_all_grads = lax.all_gather(mlp_owned, "seq", axis=0, tiled=False)
    up_total, down_total = lay_units(mlp_all_grads, own_rows, model_width)
    (
        sk_gain_total,
        sk_shift_total,
        sk_bias_total,
        one_gain_total,
        one_shift_total,
        pk_bias_total,
        value_bias_total,
        at_bias_total,
        three_gain_total,
        three_shift_total,
        cq_bias_total,
        kv_bias_total,
        cr_bias_total,
        two_gain_total,
        two_shift_total,
        up_bias_total,
        down_bias_total,
    ) = vector_totals
    return (
        layer_out,
        joined_grad[:, :model_width].astype(low)[None],
        joined_grad[:, model_width:].astype(low)[None],
        text_total[None],
        condition_grad,
        sk_gain_total,
        sk_shift_total,
        sk_total,
        sk_bias_total,
        md_weight_grad,
        md_bias_grad,
        one_gain_total,
        one_shift_total,
        pk_total,
        pk_bias_total,
        value_bias_total,
        gains_total,
        shifts_total,
        at_total,
        at_bias_total,
        three_gain_total,
        three_shift_total,
        cq_total,
        cq_bias_total,
        kv_total,
        kv_bias_total,
        cr_total,
        cr_bias_total,
        two_gain_total,
        two_shift_total,
        up_total,
        up_bias_total,
        down_total,
        down_bias_total,
    )


def solution(mesh):
    in_specs = (
        P("fsdp", "seq", None),
        P("fsdp", "seq", None),
        P("fsdp", None, None),
        P("fsdp", None),
        P("seq", None),
        P("fsdp", "seq", None),
        P("fsdp"),
        P("fsdp"),
        P("fsdp", None),
        P("fsdp"),
        P("fsdp", None),
        P("fsdp"),
        P("fsdp"),
        P("fsdp"),
        P("fsdp", None),
        P("fsdp"),
        P(),
        P(),
        P("fsdp", None),
        P("fsdp"),
        P("fsdp"),
        P("fsdp"),
        P("fsdp", None),
        P("fsdp"),
        P("fsdp", None),
        P("fsdp"),
        P("fsdp", None),
        P("fsdp"),
        P("fsdp"),
        P("fsdp"),
        P("fsdp", None),
        P("fsdp"),
        P("fsdp", None),
        P("fsdp"),
    )
    out_specs = (
        P("fsdp", "seq", None),
        P("fsdp", "seq", None),
        P("fsdp", "seq", None),
        P("fsdp", None, None),
        P("fsdp", None),
        P("fsdp"),
        P("fsdp"),
        P("fsdp", None),
        P("fsdp"),
        P("fsdp", None),
        P("fsdp"),
        P("fsdp"),
        P("fsdp"),
        P("fsdp", None),
        P("fsdp"),
        P("fsdp"),
        P(),
        P(),
        P("fsdp", None),
        P("fsdp"),
        P("fsdp"),
        P("fsdp"),
        P("fsdp", None),
        P("fsdp"),
        P("fsdp", None),
        P("fsdp"),
        P("fsdp", None),
        P("fsdp"),
        P("fsdp"),
        P("fsdp"),
        P("fsdp", None),
        P("fsdp"),
        P("fsdp", None),
        P("fsdp"),
    )
    return jax.shard_map(local, mesh=mesh, in_specs=in_specs, out_specs=out_specs, check_vma=False)
```

```python
import functools
import math

import jax
import jax.numpy as jnp
from jax import lax
from jax.experimental import pallas as pl
from jax.experimental.pallas import tpu as pltpu
from jax.sharding import PartitionSpec as P


def layer_norm(inputs, gain_vector, shift_vector):
    centred = inputs - jnp.mean(inputs, -1, keepdims=True)
    variance = jnp.mean(centred * centred, -1, keepdims=True)
    return centred * lax.rsqrt(variance + 1e-06) * gain_vector + shift_vector


def rotary_tables(positions, head_dim):
    quarter = head_dim // 4
    exponent = jnp.arange(quarter, dtype=jnp.float32) * (2.0 / (head_dim // 2))
    inverse = jnp.power(jnp.float32(10000.0), -exponent)
    places = positions.astype(jnp.float32)
    angle_rows = places[:, 0:1] * inverse
    angle_cols = places[:, 1:2] * inverse
    return (jnp.cos(angle_rows), jnp.sin(angle_rows), jnp.cos(angle_cols), jnp.sin(angle_cols))


def rotate(inputs, tables):
    cos_rows, sin_rows, cos_cols, sin_cols = tuple((one_table[:, None, :] for one_table in tables))
    quarter = inputs.shape[-1] // 4
    first_a = inputs[..., :quarter]
    first_b = inputs[..., quarter : 2 * quarter]
    second_a = inputs[..., 2 * quarter : 3 * quarter]
    second_b = inputs[..., 3 * quarter :]
    return jnp.concatenate(
        [
            first_a * cos_rows - first_b * sin_rows,
            first_a * sin_rows + first_b * cos_rows,
            second_a * cos_cols - second_b * sin_cols,
            second_a * sin_cols + second_b * cos_cols,
        ],
        -1,
    )


def head_norm(inputs, gain_vector, shift_vector, head_dim):
    row_count = inputs.shape[0]
    shaped = inputs.reshape(row_count, -1, head_dim)
    return layer_norm(shaped, gain_vector, shift_vector).reshape(row_count, -1)


def head_rotary(inputs, gain_vector, shift_vector, tables, head_dim):
    row_count = inputs.shape[0]
    shaped = inputs.reshape(row_count, -1, head_dim)
    return rotate(layer_norm(shaped, gain_vector, shift_vector), tables).reshape(row_count, -1)


def matmul(left_side, right_side):
    return jnp.dot(left_side, right_side, preferred_element_type=jnp.float32)


def contract_rows(left_side, right_side):
    return lax.dot_general(
        left_side, right_side, (((0,), (0,)), ((), ())), preferred_element_type=jnp.float32
    )


def contract_cols(left_side, right_side):
    return lax.dot_general(
        left_side, right_side, (((1,), (1,)), ((), ())), preferred_element_type=jnp.float32
    )


def column_sums(grads_low):
    return jnp.sum(grads_low.astype(jnp.float32), 0)


def to_float(vectors):
    return tuple((one_vector.astype(jnp.float32) for one_vector in vectors))


def forward_kernel(query_ref, keys_ref, values_ref, mixed_ref, totals_ref, *, scale, valid):
    for head in range(query_ref.shape[0]):
        scores = contract_cols(query_ref[head], keys_ref[head]) * scale
        if valid < scores.shape[1]:
            column = lax.broadcasted_iota(jnp.int32, scores.shape, 1)
            scores = jnp.where(column < valid, scores, -1e30)
        row_top = jnp.max(scores, -1, keepdims=True)
        weights = jnp.exp(scores - row_top)
        totals = jnp.sum(weights, -1, keepdims=True)
        probs = (weights * (1.0 / totals)).astype(jnp.bfloat16)
        mixed_ref[head] = matmul(probs, values_ref[head]).astype(mixed_ref.dtype)
        totals_ref[head] = row_top + jnp.log(totals)


def attend(queries, keys_in, values_in, valid, step_heads=1):
    heads, row_count, head_dim = queries.shape
    key_count = keys_in.shape[1]
    block_rows = min(512, row_count)
    rows_spec = pl.BlockSpec((step_heads, block_rows, head_dim), lambda h, i: (h, i, 0))
    keys_spec = pl.BlockSpec((step_heads, key_count, head_dim), lambda h, i: (h, 0, 0))
    return pl.pallas_call(
        functools.partial(forward_kernel, scale=1.0 / math.sqrt(head_dim), valid=valid),
        grid=(heads // step_heads, row_count // block_rows),
        in_specs=[rows_spec, keys_spec, keys_spec],
        out_specs=[rows_spec, pl.BlockSpec((step_heads, block_rows, 1), lambda h, i: (h, i, 0))],
        out_shape=[
            jax.ShapeDtypeStruct(queries.shape, jnp.bfloat16),
            jax.ShapeDtypeStruct((heads, row_count, 1), jnp.float32),
        ],
        compiler_params=pltpu.CompilerParams(vmem_limit_bytes=40 * 1024 * 1024),
        cost_estimate=pl.CostEstimate(
            flops=4 * heads * row_count * key_count * head_dim,
            bytes_accessed=4 * heads * (row_count + key_count) * head_dim,
            transcendentals=heads * row_count * key_count,
        ),
        name="attend",
    )(queries, keys_in, values_in)


def backward_kernel(
    query_ref,
    keys_ref,
    values_ref,
    totals_ref,
    grad_ref,
    query_grad_ref,
    keys_grad_ref,
    values_grad_ref,
    *,
    scale,
    valid,
):
    first = pl.program_id(1) == 0
    for head in range(query_ref.shape[0]):
        query_block = query_ref[head]
        grad_block = grad_ref[head]
        keys_now = keys_ref[head]
        probs = jnp.exp(contract_cols(query_block, keys_now) * scale - totals_ref[head])
        if valid < probs.shape[1]:
            column = lax.broadcasted_iota(jnp.int32, probs.shape, 1)
            probs = jnp.where(column < valid, probs, 0.0)
        weighted = probs * contract_cols(grad_block, values_ref[head])
        scores_grad = weighted - probs * jnp.sum(weighted, -1, keepdims=True)
        scores_low = (scores_grad * scale).astype(jnp.bfloat16)
        query_grad_ref[head] = matmul(scores_low, keys_now).astype(query_grad_ref.dtype)
        keys_part = contract_rows(scores_low, query_block)
        values_part = contract_rows(probs.astype(jnp.bfloat16), grad_block)

        @pl.when(first)
        def _():
            keys_grad_ref[head] = keys_part
            values_grad_ref[head] = values_part

        @pl.when(jnp.logical_not(first))
        def _():
            keys_grad_ref[head] += keys_part
            values_grad_ref[head] += values_part


def attend_back(queries, keys_in, values_in, totals, grad_out, valid, step_heads=1):
    heads, row_count, head_dim = queries.shape
    key_count = keys_in.shape[1]
    block_rows = min(512, row_count)
    rows_spec = pl.BlockSpec((step_heads, block_rows, head_dim), lambda h, i: (h, i, 0))
    keys_spec = pl.BlockSpec((step_heads, key_count, head_dim), lambda h, i: (h, 0, 0))
    totals_spec = pl.BlockSpec((step_heads, block_rows, 1), lambda h, i: (h, i, 0))
    return pl.pallas_call(
        functools.partial(backward_kernel, scale=1.0 / math.sqrt(head_dim), valid=valid),
        grid=(heads // step_heads, row_count // block_rows),
        in_specs=[rows_spec, keys_spec, keys_spec, totals_spec, rows_spec],
        out_specs=[rows_spec, keys_spec, keys_spec],
        out_shape=[
            jax.ShapeDtypeStruct(queries.shape, jnp.bfloat16),
            jax.ShapeDtypeStruct(keys_in.shape, jnp.float32),
            jax.ShapeDtypeStruct(keys_in.shape, jnp.float32),
        ],
        compiler_params=pltpu.CompilerParams(vmem_limit_bytes=40 * 1024 * 1024),
        cost_estimate=pl.CostEstimate(
            flops=10 * heads * row_count * key_count * head_dim,
            bytes_accessed=8 * heads * (row_count + key_count) * head_dim,
            transcendentals=heads * row_count * key_count,
        ),
        name="attend_back",
    )(queries, keys_in, values_in, totals, grad_out)


def row_grads_kernel(left_ref, far_left_ref, right_ref, far_right_ref, out_ref):
    product = contract_rows(left_ref[0], right_ref[0])
    product += contract_rows(far_left_ref[0], far_right_ref[0])
    rows = out_ref.shape[1]
    for chip in range(out_ref.shape[0]):
        out_ref[chip] = product[chip * rows : (chip + 1) * rows].astype(out_ref.dtype)


def row_grads(lefts, rights, owners):
    count, tokens, width = lefts.shape
    rows = width // owners
    core = lax.axis_index("fsdp") % 2
    by_core = lefts.reshape(count, tokens, owners // 2, 2, rows).transpose(3, 0, 1, 2, 4)
    by_core = by_core.reshape(2, count, tokens, width // 2)
    near = lax.dynamic_index_in_dim(by_core, core, 0, False)
    far = swap_cores(lax.dynamic_index_in_dim(by_core, 1 - core, 0, False))
    left_spec = pl.BlockSpec((1, tokens, width // 2), lambda i: (i, 0, 0))
    right_spec = pl.BlockSpec((1, tokens, width), lambda i: (i, 0, 0))
    return pl.pallas_call(
        row_grads_kernel,
        grid=(count,),
        in_specs=[left_spec, left_spec, right_spec, right_spec],
        out_specs=pl.BlockSpec((owners // 2, rows, width), lambda i: (0, 0, i)),
        out_shape=jax.ShapeDtypeStruct((owners // 2, rows, count * width), jnp.bfloat16),
        compiler_params=pltpu.CompilerParams(vmem_limit_bytes=48 * 1024 * 1024),
        cost_estimate=pl.CostEstimate(
            flops=2 * count * tokens * width * width,
            bytes_accessed=2 * count * (width * width // 2 + 3 * tokens * width),
            transcendentals=0,
        ),
        name="row_grads",
    )(near, far, rights, swap_cores(rights))


def side_by_side(pieces):
    return jnp.concatenate([piece.astype(jnp.float32) for piece in pieces], 1)


def pack_kernel(first_ref, second_ref, cols_ref, packed_ref, text_ref, small_ref, out_ref):
    owners, rows = text_ref.shape[:2]
    cols = cols_ref[...]
    products = [contract_rows(half_ref[...], cols) for half_ref in (first_ref, second_ref)]
    for owner in range(owners):
        product = products[owner // (owners // 2)]
        start = (owner % (owners // 2)) * 2 * rows
        line = side_by_side(
            [
                product[start : start + rows],
                product[start + rows : start + 2 * rows],
                packed_ref[owner * rows : (owner + 1) * rows],
                text_ref[owner],
                small_ref[owner],
            ]
        )
        out_ref[owner % 2, owner // 2] = line.astype(out_ref.dtype)


def pack_tail(first, second, cols, packed, text, small):
    owners, rows = text.shape[:2]
    lanes = 2 * cols.shape[1] + packed.shape[1] + text.shape[2] + small.shape[2]
    return pl.pallas_call(
        pack_kernel,
        out_shape=jax.ShapeDtypeStruct((2, owners // 2, rows, lanes), jnp.bfloat16),
        compiler_params=pltpu.CompilerParams(vmem_limit_bytes=48 * 1024 * 1024),
        cost_estimate=pl.CostEstimate(
            flops=4 * first.size * cols.shape[1],
            bytes_accessed=4 * first.size + 4 * owners * rows * lanes,
            transcendentals=0,
        ),
        name="pack_tail",
    )(first, second, cols, packed, text, small)


def tail_kernel(all_ref, skip_ref, packed_ref, text_ref, whole_ref, small_ref):
    ways, rows = all_ref.shape[:2]
    model_width = skip_ref.shape[1]
    width = model_width // ways

    def joined(start, count, size):
        return side_by_side(
            [all_ref[way, :, start : start + size][:count] for way in range(ways)]
        )

    skip_ref[:rows] = joined(0, rows, width)
    skip_ref[rows:] = joined(width, rows, width)
    for third in range(3):
        packed_ref[:, third * model_width : (third + 1) * model_width] = joined(
            (2 + third) * width, rows, width
        )
    for side in range(2):
        text_ref[:, side * model_width : (side + 1) * model_width] = joined(
            (5 + side) * width, text_ref.shape[0], width
        )
    whole_ref[...] = joined(7 * width, rows, 3 * width)
    total = all_ref[0, :, 10 * width :].astype(jnp.float32)
    for way in range(1, ways):
        total += all_ref[way, :, 10 * width :].astype(jnp.float32)
    small_ref[...] = total


def lay_tail(blocks, text_rows):
    ways, rows, lanes = blocks.shape
    width = 2 * rows
    model_width = ways * width
    return pl.pallas_call(
        tail_kernel,
        out_shape=[
            jax.ShapeDtypeStruct((2 * rows, model_width), jnp.float32),
            jax.ShapeDtypeStruct((rows, 3 * model_width), jnp.float32),
            jax.ShapeDtypeStruct((text_rows, 2 * model_width), jnp.float32),
            jax.ShapeDtypeStruct((rows, 3 * model_width), jnp.float32),
            jax.ShapeDtypeStruct((rows, lanes - 10 * width), jnp.float32),
        ],
        compiler_params=pltpu.CompilerParams(vmem_limit_bytes=40 * 1024 * 1024),
        name="lay_tail",
    )(blocks)


def skip_back_kernel(grad_ref, first_ref, second_ref, out_ref):
    grad = grad_ref[...]
    halves = [contract_cols(grad, half_ref[...]) for half_ref in (first_ref, second_ref)]
    rows = grad.shape[1] // 16
    out_ref[...] = side_by_side(
        [half[:, i * rows : (i + 1) * rows] for i in range(16) for half in halves]
    )


def skip_back(grad_low, first_rows):
    tokens, model_width = grad_low.shape
    return pl.pallas_call(
        skip_back_kernel,
        grid=(1,),
        in_specs=[
            pl.BlockSpec((tokens, model_width), lambda i: (0, 0)),
            pl.BlockSpec((model_width, model_width), lambda i: (0, 0)),
            pl.BlockSpec((model_width, model_width), lambda i: (0, 1)),
        ],
        out_specs=pl.BlockSpec((tokens, 2 * model_width), lambda i: (0, 0)),
        out_shape=jax.ShapeDtypeStruct((tokens, 2 * model_width), jnp.float32),
        compiler_params=pltpu.CompilerParams(vmem_limit_bytes=48 * 1024 * 1024),
        cost_estimate=pl.CostEstimate(
            flops=4 * tokens * model_width * model_width,
            bytes_accessed=4 * model_width * (model_width + 2 * tokens),
            transcendentals=0,
        ),
        name="skip_back",
    )(grad_low, first_rows, first_rows)


def units_kernel(all_ref, up_ref, down_ref):
    ways = all_ref.shape[0]
    rows, hidden = up_ref.shape
    units = hidden // ways
    owners = 16
    own = units // owners
    for owner in range(owners):
        start = owner * ways * own
        up_ref[:, start : start + ways * own] = side_by_side(
            [all_ref[way, :rows, owner * own : (owner + 1) * own] for way in range(ways)]
        )
    model_width = down_ref.shape[1]
    split = min(units, model_width)
    for way in range(ways):
        place = slice(way * own, (way + 1) * own)
        down_ref[place, :split] = all_ref[way, :own, units : units + split].astype(jnp.float32)
        if split < model_width:
            down_ref[place, split:] = all_ref[
                way, own : 2 * own, units : units + model_width - split
            ].astype(jnp.float32)


def lay_units(blocks, rows, model_width):
    ways, lines, lanes = blocks.shape
    units = lanes // 2
    return pl.pallas_call(
        units_kernel,
        out_shape=[
            jax.ShapeDtypeStruct((rows, ways * units), jnp.float32),
            jax.ShapeDtypeStruct((ways * units // 16, model_width), jnp.float32),
        ],
        compiler_params=pltpu.CompilerParams(vmem_limit_bytes=40 * 1024 * 1024),
        name="lay_units",
    )(blocks)


def fold_down(part, units, lines):
    first = part[..., :units]
    rest = part[..., units:]
    pad = [(0, 0)] * (part.ndim - 1) + [(0, units - rest.shape[-1])]
    both = jnp.concatenate([first, jnp.pad(rest, pad)], -2)
    return fit_rows(both, lines)


def fit_rows(part, lines):
    pad = [(0, 0)] * part.ndim
    pad[-2] = (0, lines - part.shape[-2])
    return jnp.pad(part, pad)


def swap(blocks, axis_name):
    return lax.all_to_all(blocks, axis_name, split_axis=0, concat_axis=0, tiled=True)


def spread(part, axis_name):
    size = lax.axis_size(axis_name)
    return swap(jnp.broadcast_to(part[None], (size,) + part.shape), axis_name)


def grid_place():
    index = lax.axis_index("seq")
    return index // 4, index % 4


def grid_send(value, pair, step):
    links = [(i, ((i // 4) ^ pair) * 4 + (i + step) % 4) for i in range(8)]
    return lax.ppermute(value, "seq", links)


def gather_tokens(part):
    pair, ring = grid_place()
    mate = grid_send(part, 1, 0)
    below = grid_send(part, 0, 1)
    above = grid_send(part, 0, -1)
    far = grid_send(part, 0, 2)
    mate_below = grid_send(mate, 0, 1)
    mate_above = grid_send(mate, 0, -1)
    mate_far = grid_send(far, 1, 0)
    here, there = pair * 4, (1 - pair) * 4
    buffer = jnp.zeros((8,) + part.shape, part.dtype)
    for one, spot in (
        (part, here + ring),
        (mate, there + ring),
        (below, here + (ring + 3) % 4),
        (above, here + (ring + 1) % 4),
        (far, here + (ring + 2) % 4),
        (mate_below, there + (ring + 3) % 4),
        (mate_above, there + (ring + 1) % 4),
        (mate_far, there + (ring + 2) % 4),
    ):
        buffer = lax.dynamic_update_index_in_dim(buffer, one, spot, 0)
    return buffer.reshape((-1,) + part.shape[1:])


def gather_behind(part):
    return spread(part, "seq").reshape((-1,) + part.shape[1:])


def sum_tokens(partial):
    low = jnp.bfloat16
    blocks = partial.astype(low).reshape((8, -1) + partial.shape[1:])
    pair, ring = grid_place()

    def meant(mate, step):
        spot = jnp.where(mate, 1 - pair, pair) * 4 + (ring + step) % 4
        return lax.dynamic_index_in_dim(blocks, spot, 0, False)

    def total(*parts):
        return sum(part.astype(jnp.float32) for part in parts)

    far_mate = grid_send(meant(True, 2), 1, 0)
    mate_below = grid_send(meant(True, 1), 0, 1)
    mate_above = grid_send(meant(True, 3), 0, -1)
    below = grid_send(meant(False, 1), 0, 1)
    above = grid_send(meant(False, 3), 0, -1)
    far = grid_send(total(meant(False, 2), far_mate).astype(low), 0, 2)
    mate = grid_send(total(meant(True, 0), mate_below, mate_above).astype(low), 1, 0)
    return total(meant(False, 0), below, above, far, mate)


def sum_behind(partial):
    blocks = partial.astype(jnp.bfloat16).reshape((8, -1) + partial.shape[1:])
    return jnp.sum(swap(blocks, "seq").astype(jnp.float32), 0)


def column_blocks(values):
    size = lax.axis_size("seq")
    rows = values.shape[0]
    return values.reshape(rows, size, -1).transpose(1, 0, 2)


def own_columns(weight, groups, size, place):
    rows = weight.shape[0]
    parts = weight.reshape(rows, groups, size, -1)
    taken = lax.dynamic_slice_in_dim(parts, place, 1, 2)
    return taken.reshape(rows, -1)


def after(values, others):
    return lax.optimization_barrier((values, others))[0]


def core_groups(owners):
    return [list(range(0, owners, 2)), list(range(1, owners, 2))]


def swap_cores(value):
    return lax.ppermute(value, "fsdp", [(i, i ^ 1) for i in range(lax.axis_size("fsdp"))])


def sum_cores(by_core):
    core = lax.axis_index("fsdp") % 2
    kept = lax.dynamic_index_in_dim(by_core, core, 0, False)
    arrived = swap_cores(lax.dynamic_index_in_dim(by_core, 1 - core, 0, False))
    return (kept.astype(jnp.float32) + arrived.astype(jnp.float32)).astype(jnp.bfloat16)


def scatter_chips(by_chip):
    return lax.psum_scatter(
        by_chip,
        "fsdp",
        scatter_dimension=0,
        axis_index_groups=core_groups(2 * by_chip.shape[0]),
        tiled=False,
    )


def sum_owners(by_core):
    chip = sum_cores(by_core)
    swapped = lax.all_to_all(
        chip,
        "fsdp",
        split_axis=0,
        concat_axis=0,
        axis_index_groups=core_groups(2 * chip.shape[0]),
        tiled=True,
    )
    return jnp.sum(swapped.astype(jnp.float32), 0)


def heads_first(values, head_dim):
    rows = values.shape[0]
    return values.reshape(rows, -1, head_dim).transpose(1, 0, 2)


def heads_last(values):
    return values.transpose(1, 0, 2).reshape(values.shape[1], -1)


def local(
    latent,
    skip_input,
    text_tokens,
    condition,
    positions,
    cotangent,
    skip_gain,
    skip_shift,
    skip_weight,
    skip_bias,
    mod_weight,
    mod_bias,
    norm1_gain,
    norm1_shift,
    qkv_weight,
    qkv_bias,
    head_gains,
    head_shifts,
    attn_weight,
    attn_bias,
    norm3_gain,
    norm3_shift,
    cross_q_weight,
    cross_q_bias,
    cross_kv_weight,
    cross_kv_bias,
    cross_weight,
    cross_bias,
    norm2_gain,
    norm2_shift,
    fc1_weight,
    fc1_bias,
    fc2_weight,
    fc2_bias,
):
    ways = lax.axis_size("seq")
    owners = lax.axis_size("fsdp")
    place = lax.axis_index("seq")
    head_dim = head_gains.shape[1]
    tokens, model_width = latent.shape[1:]
    width = model_width // ways
    low = jnp.bfloat16
    gain_table = head_gains.astype(jnp.float32)
    shift_table = head_shifts.astype(jnp.float32)
    tables = rotary_tables(positions, head_dim)

    own_rows = model_width // owners
    packed_own = own_columns(qkv_weight, 3, ways, place)
    packed_pad = -packed_own.shape[1] % 128
    text_own = own_columns(cross_kv_weight, 2, ways, place)
    first_own = jnp.concatenate(
        [
            skip_weight[:own_rows],
            skip_weight[own_rows:],
            jnp.pad(packed_own, ((0, 0), (0, packed_pad))),
            fit_rows(text_own, own_rows),
        ],
        1,
    )
    first_rows = lax.all_gather(first_own, "fsdp", axis=0, tiled=True)
    second_own = jnp.concatenate([attn_weight, cross_q_weight, cross_weight], 1)
    unit_rows = fc2_weight.shape[0] // ways
    down_own = lax.dynamic_slice_in_dim(fc2_weight, place * unit_rows, unit_rows, 0)
    up_own = own_columns(fc1_weight, owners, ways, place)
    units = up_own.shape[1]
    lines = max(own_rows, 2 * unit_rows)
    third_own = jnp.concatenate(
        [fit_rows(up_own, lines), fold_down(down_own, units, lines)], 1
    )
    lifted_f, silu_pull = jax.vjp(jax.nn.silu, condition.astype(jnp.float32))
    lifted = lifted_f.astype(low)
    vectors = (
        skip_gain,
        skip_shift,
        skip_bias,
        mod_bias,
        norm1_gain,
        norm1_shift,
        qkv_bias,
        attn_bias,
        norm3_gain,
        norm3_shift,
        cross_q_bias,
        cross_kv_bias,
        cross_bias,
        norm2_gain,
        norm2_shift,
        fc1_bias,
        fc2_bias,
    )
    vector_own = jnp.concatenate(vectors)
    vector_all = swap(
        jnp.concatenate(
            [
                jnp.broadcast_to(vector_own[None], (owners, vector_own.shape[0])),
                lifted.reshape(owners, own_rows),
            ],
            1,
        ),
        "fsdp",
    )
    pieces = []
    start = 0
    for one_vector in vectors:
        size = one_vector.shape[0]
        pieces.append(vector_all[:, start : start + size].reshape(-1).astype(jnp.float32))
        start += size
    lifted_own = vector_all[:, start:]
    second_rows = lax.all_gather(after(second_own, vector_all), "fsdp", axis=0, tiled=True)

    grad_own = jnp.concatenate(
        [cotangent[0], jnp.pad(positions.astype(low), ((0, 0), (0, 126)))], 1
    )
    grad_places = gather_behind(after(grad_own, vector_all))
    grad_all = grad_places[:, :model_width]
    tables_all = rotary_tables(grad_places[:, model_width : model_width + 2], head_dim)
    third_rows = lax.all_gather(after(third_own, grad_places), "fsdp", axis=0, tiled=False)
    (
        sk_gain,
        sk_shift,
        sk_bias,
        md_bias,
        one_gain,
        one_shift,
        pk_bias,
        at_bias,
        three_gain,
        three_shift,
        cq_bias,
        kv_bias,
        cr_bias,
        two_gain,
        two_shift,
        up_bias,
        down_bias,
    ) = pieces
    pk_bias_own = own_columns(pk_bias[None], 3, ways, place)[0]
    kv_bias_own = own_columns(kv_bias[None], 2, ways, place)[0]
    up_bias_own = own_columns(up_bias[None], owners, ways, place)[0]
    shift_parts = after(matmul(lifted_own, mod_weight), grad_places)
    shift_row = jnp.sum(swap(shift_parts, "fsdp"), 0, keepdims=True) + md_bias

    joined = jnp.concatenate([latent[0], skip_input[0]], 1).astype(jnp.float32)
    normed_f, skip_pull = jax.vjp(layer_norm, joined, sk_gain, sk_shift)
    normed = normed_f.astype(low)
    normed_halves = normed.reshape(tokens, owners, 2, own_rows).transpose(2, 0, 1, 3)
    normed_halves = normed_halves.reshape(2, tokens, model_width)
    normed_first = gather_behind(after(normed[:, :model_width], shift_row))
    first_rows = after(first_rows, (normed_halves, shift_row))
    pk_start = 2 * model_width
    kv_start = pk_start + 3 * width + packed_pad
    pk_weight = first_rows[:, pk_start : pk_start + 3 * width]
    kv_weight = first_rows.reshape(owners, own_rows, -1)[:, : text_own.shape[0], kv_start:]
    kv_weight = kv_weight.reshape(-1, 2 * width)
    up_weight = third_rows[:, :own_rows, :units].reshape(model_width, units)
    down_weight = jnp.concatenate(
        [
            third_rows[:, :unit_rows, units : units + min(units, model_width)],
            third_rows[:, unit_rows : 2 * unit_rows, units : units + max(model_width - units, 0)],
        ],
        2,
    ).reshape(units, model_width)
    at_weight = second_rows[:, :model_width]
    cq_weight = second_rows[:, model_width : 2 * model_width]
    cr_weight = second_rows[:, 2 * model_width :]

    stream_zero = (
        matmul(normed_halves[0], first_rows[:, :model_width])
        + matmul(normed_halves[1], first_rows[:, model_width : 2 * model_width])
        + sk_bias
    )

    entry_f, one_pull = jax.vjp(layer_norm, stream_zero, one_gain, one_shift)
    entry = (entry_f + shift_row).astype(low)

    entry_all = gather_tokens(after(entry, normed_first))

    text_now = text_tokens[0]
    text_count = text_now.shape[0]
    text_packed = matmul(text_now, kv_weight) + kv_bias_own
    text_keys_f, tk_pull = jax.vjp(
        lambda values_in, gains_in: head_norm(values_in, gains_in[3], 0.0, head_dim),
        text_packed[:, :width],
        gain_table,
    )
    text_own = jnp.concatenate(
        [text_keys_f.astype(low), text_packed[:, width:].astype(low)], 1
    )
    text_rows = text_count + -text_count % 16
    text_own = jnp.pad(text_own, ((0, text_rows - text_count), (0, 0)))
    text_spread = spread(after(text_own, entry_all), "seq")
    text_all = text_spread.reshape(ways, text_rows, 2, -1, head_dim)
    text_all = text_all.transpose(2, 0, 3, 1, 4).reshape(2, -1, text_rows, head_dim)
    text_all = jnp.pad(text_all, ((0, 0), (0, 0), (0, -text_rows % 128), (0, 0)))
    packed = matmul(entry_all, pk_weight) + pk_bias_own

    def prepare(query_pre, key_pre, gains_in, shifts_in):
        return (
            head_rotary(query_pre, gains_in[0], shifts_in[0], tables_all, head_dim),
            head_rotary(key_pre, gains_in[1], shifts_in[1], tables_all, head_dim),
        )

    (query_f, key_f), prep_pull = jax.vjp(
        prepare, packed[:, :width], packed[:, width : 2 * width], gain_table, shift_table
    )
    query_h = heads_first(query_f.astype(low), head_dim)
    key_h = heads_first(key_f.astype(low), head_dim)
    value_h = heads_first(packed[:, 2 * width :].astype(low), head_dim)
    all_tokens = query_h.shape[1]
    mixed_h, self_totals = attend(query_h, key_h, value_h, all_tokens)
    mixed_h = after(mixed_h, text_spread)

    def to_heads(values):
        return swap(column_blocks(values), "seq").reshape(all_tokens, -1)

    def to_tokens(values_h):
        blocks = swap(heads_last(values_h).reshape(ways, tokens, width), "seq")
        return blocks.transpose(1, 0, 2).reshape(tokens, model_width)

    mixed = to_tokens(mixed_h)
    normed_second = gather_behind(after(normed[:, model_width:], mixed))
    stream_one = stream_zero + matmul(mixed, at_weight) + at_bias

    cross_in_f, three_pull = jax.vjp(layer_norm, stream_one, three_gain, three_shift)
    cross_in = cross_in_f.astype(low)
    cross_pre = matmul(cross_in, cq_weight) + cq_bias
    cross_query_f, cq_pull = jax.vjp(
        lambda values_in, gains_in, shifts_in: head_rotary(
            values_in, gains_in[2], shifts_in[2], tables, head_dim
        ),
        cross_pre,
        gain_table,
        shift_table,
    )
    cross_query_h = heads_first(cross_query_f.astype(low), head_dim)
    step_heads = min(4, cross_query_h.shape[0])
    cross_h, cross_totals = attend(
        cross_query_h, text_all[0], text_all[1], text_count, step_heads
    )
    cross_mixed = heads_last(cross_h)
    stream_two = stream_one + matmul(cross_mixed, cr_weight) + cr_bias

    mlp_in_f, two_pull = jax.vjp(layer_norm, stream_two, two_gain, two_shift)
    mlp_all = gather_tokens(after(mlp_in_f.astype(low), normed_second))
    hidden_pre = matmul(mlp_all, up_weight) + up_bias_own
    hidden_f, gelu_pull = jax.vjp(
        lambda values_in: jax.nn.gelu(values_in, approximate=True), hidden_pre
    )
    hidden = hidden_f.astype(low)
    out_partial = matmul(hidden, down_weight).astype(low)
    grad_three = cotangent[0].astype(jnp.float32)
    down_bias_grad = column_sums(cotangent[0])
    pre_grad = gelu_pull(contract_cols(grad_all, down_weight))[0].astype(low)
    up_bias_grad = column_sums(pre_grad)
    mlp_in_grad = sum_tokens(contract_cols(pre_grad, up_weight))
    down_grad = contract_rows(hidden, grad_all).astype(low)
    up_grad = contract_rows(mlp_all, pre_grad).astype(low)
    mlp_grads = jnp.concatenate(
        [
            fit_rows(up_grad.reshape(owners, own_rows, units), lines),
            fold_down(down_grad.reshape(owners, unit_rows, model_width), units, lines),
        ],
        2,
    )
    mlp_grads = mlp_grads.reshape(owners // 2, 2, lines, 2 * units).transpose(1, 0, 2, 3)
    mlp_owned = scatter_chips(sum_cores(mlp_grads))
    mlp_in_grad = after(mlp_in_grad, mlp_grads)
    stream_part, two_gain_grad, two_shift_grad = two_pull(mlp_in_grad)
    stream_grad = grad_three + stream_part

    grad_low = stream_grad.astype(low)
    cr_bias_grad = column_sums(grad_low)
    cross_mixed_grad = contract_cols(grad_low, cr_weight).astype(low)

    stream_three = stream_two + sum_behind(after(out_partial, mlp_in_grad)) + down_bias
    layer_out = stream_three.astype(low)[None]
    cross_query_grad, text_key_part, text_value_part = attend_back(
        cross_query_h,
        text_all[0],
        text_all[1],
        cross_totals,
        heads_first(cross_mixed_grad, head_dim),
        text_count,
        step_heads,
    )
    cross_query_grad = heads_last(cross_query_grad)
    cross_out_low = grad_low
    cross_pre_grad, gains_from_cross, shifts_from_cross = cq_pull(
        cross_query_grad.astype(jnp.float32)
    )
    cross_pre_low = cross_pre_grad.astype(low)
    cq_bias_grad = column_sums(cross_pre_low)
    stream_part, three_gain_grad, three_shift_grad = three_pull(
        contract_cols(cross_pre_low, cq_weight)
    )
    stream_grad = stream_grad + stream_part

    grad_low = stream_grad.astype(low)
    at_bias_grad = column_sums(grad_low)
    mixed_grad = contract_cols(grad_low, at_weight).astype(low)
    mixed_back = to_heads(after(mixed_grad, stream_three))
    whole_grads = row_grads(
        jnp.stack([mixed, cross_in, cross_mixed]),
        jnp.stack([grad_low, cross_pre_low, cross_out_low]),
        owners,
    )
    row_owned = scatter_chips(whole_grads)
    mixed_back = after(mixed_back, whole_grads)
    query_grad, key_grad, value_grad = attend_back(
        query_h, key_h, value_h, self_totals, heads_first(mixed_back, head_dim), all_tokens
    )

    text_parts = jnp.stack([text_key_part, text_value_part])[:, :, :text_rows].astype(low)
    text_parts = text_parts.reshape(2, ways, -1, text_rows, head_dim)
    text_parts = text_parts.transpose(1, 3, 0, 2, 4).reshape(ways, text_rows, 2 * width)
    text_parts = after(text_parts, stream_three)
    text_kv_grad = jnp.sum(
        swap(after(text_parts, mixed_back), "seq").astype(jnp.float32), 0
    )[:text_count]
    key_pre_grad, gains_from_text = tk_pull(text_kv_grad[:, :width])
    text_grad_low = jnp.concatenate(
        [key_pre_grad.astype(low), text_kv_grad[:, width:].astype(low)], 1
    )
    kv_weight_grad = contract_rows(text_now, text_grad_low)
    kv_bias_grad = column_sums(text_grad_low)
    text_part = contract_cols(text_grad_low, kv_weight)
    text_part = jnp.pad(text_part.astype(low), ((0, -text_count % (8 * ways)), (0, 0)))
    text_sum = sum_behind(text_part)
    query_pre_grad, key_pre_grad2, gains_from_self, shifts_from_self = prep_pull(
        (
            heads_last(query_grad).astype(jnp.float32),
            heads_last(key_grad).astype(low).astype(jnp.float32),
        )
    )
    packed_grad = jnp.concatenate(
        [
            query_pre_grad.astype(low),
            key_pre_grad2.astype(low),
            heads_last(value_grad).astype(low),
        ],
        1,
    )
    pk_weight_grad = contract_rows(entry_all, packed_grad)
    entry_grad = sum_tokens(after(contract_cols(packed_grad, pk_weight), text_kv_grad))
    pk_bias_grad = column_sums(packed_grad)
    entry_grad = after(entry_grad, (pk_weight_grad, text_sum))
    text_total = gather_behind(after(text_sum.astype(low), entry_grad))[:text_count]
    shift_part = jnp.sum(entry_grad, 0)
    stream_part, one_gain_grad, one_shift_grad = one_pull(entry_grad)
    stream_grad = stream_grad + stream_part

    grad_low = stream_grad.astype(low)
    sk_bias_grad = column_sums(grad_low)
    shift_rows = jnp.broadcast_to(
        shift_part.astype(low).reshape(1, ways, width), (ways, ways, width)
    )
    cols_in = jnp.concatenate([column_blocks(after(grad_low, text_total)), shift_rows], 1)
    cols_out = swap(cols_in, "seq")
    grad_cols = cols_out[:, :tokens].reshape(all_tokens, width)
    shift_total = jnp.sum(cols_out[:, tokens:].astype(jnp.float32), 0).reshape(-1)
    joined_grad, sk_gain_grad, sk_shift_grad = skip_pull(skip_back(grad_low, first_rows))

    def placed(own, groups):
        parts = jnp.zeros((groups, ways, own.shape[0] // groups), jnp.float32)
        parts = lax.dynamic_update_slice_in_dim(parts, own.reshape(groups, 1, -1), place, 1)
        return parts.reshape(-1)

    vector_grads = (
        sk_gain_grad,
        sk_shift_grad,
        sk_bias_grad,
        one_gain_grad,
        one_shift_grad,
        placed(pk_bias_grad, 3),
        at_bias_grad,
        three_gain_grad,
        three_shift_grad,
        cq_bias_grad,
        placed(kv_bias_grad, 2),
        cr_bias_grad,
        two_gain_grad,
        two_shift_grad,
        placed(up_bias_grad, owners),
        down_bias_grad,
    )
    table_grads = jnp.concatenate(
        [
            (gains_from_cross + gains_from_text + gains_from_self).reshape(-1),
            (shifts_from_cross + shifts_from_self).reshape(-1),
        ]
    )
    split_three = [part.reshape(owners, -1) for part in vector_grads]
    pk_at = 5
    pk_thirds = placed(pk_bias_grad, 3).reshape(3, model_width)
    split_three[pk_at : pk_at + 1] = [
        pk_thirds[:2].reshape(owners, -1),
        pk_thirds[2].reshape(owners, -1),
    ]
    split_three.append(jnp.broadcast_to(table_grads[None], (owners, table_grads.shape[0])))
    summed_sizes = [part.shape[1] for part in split_three]
    vector_rows = jnp.concatenate(split_three, 1).astype(low)
    vector_pad = -vector_rows.shape[1] % own_rows
    vector_rows = jnp.pad(vector_rows, ((0, 0), (0, vector_pad)))
    tail_sum = sum_owners(
        pack_tail(
            normed_first,
            normed_second,
            after(grad_cols, vector_rows),
            pk_weight_grad,
            fit_rows(kv_weight_grad.astype(low).reshape(owners, -1, 2 * width), own_rows),
            vector_rows.reshape(owners, own_rows, -1),
        )
    ).astype(low)

    row_sum = jnp.sum(swap(column_blocks(row_owned), "seq").astype(jnp.float32), 0)
    lead = 7 * width
    tail_all = spread(
        jnp.concatenate([tail_sum[:, :lead], row_sum.astype(low), tail_sum[:, lead:]], 1), "seq"
    )
    sk_total, pk_total, kv_total, row_total, small_total = lay_tail(
        tail_all, cross_kv_weight.shape[0]
    )
    at_total = row_total[:, :model_width]
    cq_total = row_total[:, model_width : 2 * model_width]
    cr_total = row_total[:, 2 * model_width :]
    small_total = small_total.reshape(-1)
    vector_totals = []
    start = 0
    for size in summed_sizes:
        vector_totals.append(small_total[start : start + size])
        start += size
    table_total = vector_totals.pop()
    gains_total = table_total[: gain_table.size].reshape(gain_table.shape)
    shifts_total = table_total[gain_table.size :].reshape(shift_table.shape)
    shift_all = spread(after(shift_total.astype(low), tail_sum), "fsdp").astype(jnp.float32)
    md_weight_grad = lax.dot_general(
        lifted_own.astype(jnp.float32),
        shift_all,
        (((0,), (0,)), ((), ())),
        precision=lax.Precision.HIGHEST,
        preferred_element_type=jnp.float32,
    )
    md_bias_grad = lax.dynamic_slice_in_dim(
        jnp.sum(shift_all, 0), lax.axis_index("fsdp") * own_rows, own_rows, 0
    )
    lifted_part = lax.dot_general(
        shift_all,
        mod_weight.astype(jnp.float32),
        (((1,), (1,)), ((), ())),
        precision=lax.Precision.HIGHEST,
        preferred_element_type=jnp.float32,
    )
    lifted_grad = swap(after(lifted_part, tail_all), "fsdp").reshape(1, model_width)
    condition_grad = silu_pull(lifted_grad)[0]

    mlp_all_grads = lax.all_gather(mlp_owned, "seq", axis=0, tiled=False)
    up_total, down_total = lay_units(mlp_all_grads, own_rows, model_width)
    (
        sk_gain_total,
        sk_shift_total,
        sk_bias_total,
        one_gain_total,
        one_shift_total,
        pk_bias_total,
        value_bias_total,
        at_bias_total,
        three_gain_total,
        three_shift_total,
        cq_bias_total,
        kv_bias_total,
        cr_bias_total,
        two_gain_total,
        two_shift_total,
        up_bias_total,
        down_bias_total,
    ) = vector_totals
    return (
        layer_out,
        joined_grad[:, :model_width].astype(low)[None],
        joined_grad[:, model_width:].astype(low)[None],
        text_total[None],
        condition_grad,
        sk_gain_total,
        sk_shift_total,
        sk_total,
        sk_bias_total,
        md_weight_grad,
        md_bias_grad,
        one_gain_total,
        one_shift_total,
        pk_total,
        pk_bias_total,
        value_bias_total,
        gains_total,
        shifts_total,
        at_total,
        at_bias_total,
        three_gain_total,
        three_shift_total,
        cq_total,
        cq_bias_total,
        kv_total,
        kv_bias_total,
        cr_total,
        cr_bias_total,
        two_gain_total,
        two_shift_total,
        up_total,
        up_bias_total,
        down_total,
        down_bias_total,
    )


def solution(mesh):
    in_specs = (
        P("fsdp", "seq", None),
        P("fsdp", "seq", None),
        P("fsdp", None, None),
        P("fsdp", None),
        P("seq", None),
        P("fsdp", "seq", None),
        P("fsdp"),
        P("fsdp"),
        P("fsdp", None),
        P("fsdp"),
        P("fsdp", None),
        P("fsdp"),
        P("fsdp"),
        P("fsdp"),
        P("fsdp", None),
        P("fsdp"),
        P(),
        P(),
        P("fsdp", None),
        P("fsdp"),
        P("fsdp"),
        P("fsdp"),
        P("fsdp", None),
        P("fsdp"),
        P("fsdp", None),
        P("fsdp"),
        P("fsdp", None),
        P("fsdp"),
        P("fsdp"),
        P("fsdp"),
        P("fsdp", None),
        P("fsdp"),
        P("fsdp", None),
        P("fsdp"),
    )
    out_specs = (
        P("fsdp", "seq", None),
        P("fsdp", "seq", None),
        P("fsdp", "seq", None),
        P("fsdp", None, None),
        P("fsdp", None),
        P("fsdp"),
        P("fsdp"),
        P("fsdp", None),
        P("fsdp"),
        P("fsdp", None),
        P("fsdp"),
        P("fsdp"),
        P("fsdp"),
        P("fsdp", None),
        P("fsdp"),
        P("fsdp"),
        P(),
        P(),
        P("fsdp", None),
        P("fsdp"),
        P("fsdp"),
        P("fsdp"),
        P("fsdp", None),
        P("fsdp"),
        P("fsdp", None),
        P("fsdp"),
        P("fsdp", None),
        P("fsdp"),
        P("fsdp"),
        P("fsdp"),
        P("fsdp", None),
        P("fsdp"),
        P("fsdp", None),
        P("fsdp"),
    )
    return jax.shard_map(local, mesh=mesh, in_specs=in_specs, out_specs=out_specs, check_vma=False)
```

```python
import functools
import math

import jax
import jax.numpy as jnp
from jax import lax
from jax.experimental import pallas as pl
from jax.experimental.pallas import tpu as pltpu
from jax.sharding import PartitionSpec as P


def layer_norm(inputs, gain_vector, shift_vector):
    centred = inputs - jnp.mean(inputs, -1, keepdims=True)
    variance = jnp.mean(centred * centred, -1, keepdims=True)
    return centred * lax.rsqrt(variance + 1e-06) * gain_vector + shift_vector


def rotary_tables(positions, head_dim):
    quarter = head_dim // 4
    exponent = jnp.arange(quarter, dtype=jnp.float32) * (2.0 / (head_dim // 2))
    inverse = jnp.power(jnp.float32(10000.0), -exponent)
    places = positions.astype(jnp.float32)
    angle_rows = places[:, 0:1] * inverse
    angle_cols = places[:, 1:2] * inverse
    return (jnp.cos(angle_rows), jnp.sin(angle_rows), jnp.cos(angle_cols), jnp.sin(angle_cols))


def rotate(inputs, tables):
    cos_rows, sin_rows, cos_cols, sin_cols = tuple((one_table[:, None, :] for one_table in tables))
    quarter = inputs.shape[-1] // 4
    first_a = inputs[..., :quarter]
    first_b = inputs[..., quarter : 2 * quarter]
    second_a = inputs[..., 2 * quarter : 3 * quarter]
    second_b = inputs[..., 3 * quarter :]
    return jnp.concatenate(
        [
            first_a * cos_rows - first_b * sin_rows,
            first_a * sin_rows + first_b * cos_rows,
            second_a * cos_cols - second_b * sin_cols,
            second_a * sin_cols + second_b * cos_cols,
        ],
        -1,
    )


def head_norm(inputs, gain_vector, shift_vector, head_dim):
    row_count = inputs.shape[0]
    shaped = inputs.reshape(row_count, -1, head_dim)
    return layer_norm(shaped, gain_vector, shift_vector).reshape(row_count, -1)


def head_rotary(inputs, gain_vector, shift_vector, tables, head_dim):
    row_count = inputs.shape[0]
    shaped = inputs.reshape(row_count, -1, head_dim)
    return rotate(layer_norm(shaped, gain_vector, shift_vector), tables).reshape(row_count, -1)


def matmul(left_side, right_side):
    return jnp.dot(left_side, right_side, preferred_element_type=jnp.float32)


def contract_rows(left_side, right_side):
    return lax.dot_general(
        left_side, right_side, (((0,), (0,)), ((), ())), preferred_element_type=jnp.float32
    )


def contract_cols(left_side, right_side):
    return lax.dot_general(
        left_side, right_side, (((1,), (1,)), ((), ())), preferred_element_type=jnp.float32
    )


def column_sums(grads_low):
    return jnp.sum(grads_low.astype(jnp.float32), 0)


def to_float(vectors):
    return tuple((one_vector.astype(jnp.float32) for one_vector in vectors))


def forward_kernel(query_ref, keys_ref, values_ref, mixed_ref, totals_ref, *, scale, valid):
    for head in range(query_ref.shape[0]):
        scores = contract_cols(query_ref[head], keys_ref[head]) * scale
        if valid < scores.shape[1]:
            column = lax.broadcasted_iota(jnp.int32, scores.shape, 1)
            scores = jnp.where(column < valid, scores, -1e30)
        row_top = jnp.max(scores, -1, keepdims=True)
        weights = jnp.exp(scores - row_top)
        totals = jnp.sum(weights, -1, keepdims=True)
        probs = (weights * (1.0 / totals)).astype(jnp.bfloat16)
        mixed_ref[head] = matmul(probs, values_ref[head]).astype(mixed_ref.dtype)
        totals_ref[head] = row_top + jnp.log(totals)


def attend(queries, keys_in, values_in, valid, step_heads=1):
    heads, row_count, head_dim = queries.shape
    key_count = keys_in.shape[1]
    block_rows = min(512, row_count)
    rows_spec = pl.BlockSpec((step_heads, block_rows, head_dim), lambda h, i: (h, i, 0))
    keys_spec = pl.BlockSpec((step_heads, key_count, head_dim), lambda h, i: (h, 0, 0))
    return pl.pallas_call(
        functools.partial(forward_kernel, scale=1.0 / math.sqrt(head_dim), valid=valid),
        grid=(heads // step_heads, row_count // block_rows),
        in_specs=[rows_spec, keys_spec, keys_spec],
        out_specs=[rows_spec, pl.BlockSpec((step_heads, block_rows, 1), lambda h, i: (h, i, 0))],
        out_shape=[
            jax.ShapeDtypeStruct(queries.shape, jnp.bfloat16),
            jax.ShapeDtypeStruct((heads, row_count, 1), jnp.float32),
        ],
        compiler_params=pltpu.CompilerParams(vmem_limit_bytes=40 * 1024 * 1024),
        cost_estimate=pl.CostEstimate(
            flops=4 * heads * row_count * key_count * head_dim,
            bytes_accessed=4 * heads * (row_count + key_count) * head_dim,
            transcendentals=heads * row_count * key_count,
        ),
        name="attend",
    )(queries, keys_in, values_in)


def backward_kernel(
    query_ref,
    keys_ref,
    values_ref,
    totals_ref,
    grad_ref,
    query_grad_ref,
    keys_grad_ref,
    values_grad_ref,
    *,
    scale,
    valid,
):
    first = pl.program_id(1) == 0
    for head in range(query_ref.shape[0]):
        query_block = query_ref[head]
        grad_block = grad_ref[head]
        keys_now = keys_ref[head]
        probs = jnp.exp(contract_cols(query_block, keys_now) * scale - totals_ref[head])
        if valid < probs.shape[1]:
            column = lax.broadcasted_iota(jnp.int32, probs.shape, 1)
            probs = jnp.where(column < valid, probs, 0.0)
        weighted = probs * contract_cols(grad_block, values_ref[head])
        scores_grad = weighted - probs * jnp.sum(weighted, -1, keepdims=True)
        scores_low = (scores_grad * scale).astype(jnp.bfloat16)
        query_grad_ref[head] = matmul(scores_low, keys_now).astype(query_grad_ref.dtype)
        keys_part = contract_rows(scores_low, query_block)
        values_part = contract_rows(probs.astype(jnp.bfloat16), grad_block)

        @pl.when(first)
        def _():
            keys_grad_ref[head] = keys_part
            values_grad_ref[head] = values_part

        @pl.when(jnp.logical_not(first))
        def _():
            keys_grad_ref[head] += keys_part
            values_grad_ref[head] += values_part


def attend_back(queries, keys_in, values_in, totals, grad_out, valid, step_heads=1):
    heads, row_count, head_dim = queries.shape
    key_count = keys_in.shape[1]
    block_rows = min(512, row_count)
    rows_spec = pl.BlockSpec((step_heads, block_rows, head_dim), lambda h, i: (h, i, 0))
    keys_spec = pl.BlockSpec((step_heads, key_count, head_dim), lambda h, i: (h, 0, 0))
    totals_spec = pl.BlockSpec((step_heads, block_rows, 1), lambda h, i: (h, i, 0))
    return pl.pallas_call(
        functools.partial(backward_kernel, scale=1.0 / math.sqrt(head_dim), valid=valid),
        grid=(heads // step_heads, row_count // block_rows),
        in_specs=[rows_spec, keys_spec, keys_spec, totals_spec, rows_spec],
        out_specs=[rows_spec, keys_spec, keys_spec],
        out_shape=[
            jax.ShapeDtypeStruct(queries.shape, jnp.bfloat16),
            jax.ShapeDtypeStruct(keys_in.shape, jnp.float32),
            jax.ShapeDtypeStruct(keys_in.shape, jnp.float32),
        ],
        compiler_params=pltpu.CompilerParams(vmem_limit_bytes=40 * 1024 * 1024),
        cost_estimate=pl.CostEstimate(
            flops=10 * heads * row_count * key_count * head_dim,
            bytes_accessed=8 * heads * (row_count + key_count) * head_dim,
            transcendentals=heads * row_count * key_count,
        ),
        name="attend_back",
    )(queries, keys_in, values_in, totals, grad_out)


def row_grads_kernel(left_ref, far_left_ref, right_ref, far_right_ref, out_ref):
    product = contract_rows(left_ref[0], right_ref[0])
    product += contract_rows(far_left_ref[0], far_right_ref[0])
    rows = out_ref.shape[1]
    for chip in range(out_ref.shape[0]):
        out_ref[chip] = product[chip * rows : (chip + 1) * rows].astype(out_ref.dtype)


def row_grads(lefts, rights, owners):
    count, tokens, width = lefts.shape
    rows = width // owners
    core = lax.axis_index("fsdp") % 2
    by_core = lefts.reshape(count, tokens, owners // 2, 2, rows).transpose(3, 0, 1, 2, 4)
    by_core = by_core.reshape(2, count, tokens, width // 2)
    near = lax.dynamic_index_in_dim(by_core, core, 0, False)
    far = swap_cores(lax.dynamic_index_in_dim(by_core, 1 - core, 0, False))
    left_spec = pl.BlockSpec((1, tokens, width // 2), lambda i: (i, 0, 0))
    right_spec = pl.BlockSpec((1, tokens, width), lambda i: (i, 0, 0))
    return pl.pallas_call(
        row_grads_kernel,
        grid=(count,),
        in_specs=[left_spec, left_spec, right_spec, right_spec],
        out_specs=pl.BlockSpec((owners // 2, rows, width), lambda i: (0, 0, i)),
        out_shape=jax.ShapeDtypeStruct((owners // 2, rows, count * width), jnp.bfloat16),
        compiler_params=pltpu.CompilerParams(vmem_limit_bytes=48 * 1024 * 1024),
        cost_estimate=pl.CostEstimate(
            flops=2 * count * tokens * width * width,
            bytes_accessed=2 * count * (width * width // 2 + 3 * tokens * width),
            transcendentals=0,
        ),
        name="row_grads",
    )(near, far, rights, swap_cores(rights))


def side_by_side(pieces):
    return jnp.concatenate([piece.astype(jnp.float32) for piece in pieces], 1)


def pack_kernel(normed_ref, cols_ref, packed_ref, text_ref, small_ref, out_ref):
    owners, rows = text_ref.shape[:2]
    cols = cols_ref[...]
    middle = normed_ref.shape[1] // 2
    products = [
        contract_rows(normed_ref[:, :middle], cols),
        contract_rows(normed_ref[:, middle:], cols),
    ]
    for owner in range(owners):
        product = products[owner // (owners // 2)]
        start = (owner % (owners // 2)) * 2 * rows
        line = side_by_side(
            [
                product[start : start + rows],
                product[start + rows : start + 2 * rows],
                packed_ref[owner * rows : (owner + 1) * rows],
                text_ref[owner],
                small_ref[owner],
            ]
        )
        out_ref[owner % 2, owner // 2] = line.astype(out_ref.dtype)


def pack_tail(normed, cols, packed, text, small):
    owners, rows = text.shape[:2]
    lanes = 2 * cols.shape[1] + packed.shape[1] + text.shape[2] + small.shape[2]
    return pl.pallas_call(
        pack_kernel,
        out_shape=jax.ShapeDtypeStruct((2, owners // 2, rows, lanes), jnp.bfloat16),
        compiler_params=pltpu.CompilerParams(vmem_limit_bytes=48 * 1024 * 1024),
        cost_estimate=pl.CostEstimate(
            flops=2 * normed.size * cols.shape[1],
            bytes_accessed=2 * normed.size + 4 * owners * rows * lanes,
            transcendentals=0,
        ),
        name="pack_tail",
    )(normed, cols, packed, text, small)


def tail_kernel(all_ref, skip_ref, packed_ref, text_ref, whole_ref, small_ref):
    ways, rows = all_ref.shape[:2]
    model_width = skip_ref.shape[1]
    width = model_width // ways

    def joined(start, count, size):
        return side_by_side(
            [all_ref[way, :, start : start + size][:count] for way in range(ways)]
        )

    skip_ref[:rows] = joined(0, rows, width)
    skip_ref[rows:] = joined(width, rows, width)
    for third in range(3):
        packed_ref[:, third * model_width : (third + 1) * model_width] = joined(
            (2 + third) * width, rows, width
        )
    for side in range(2):
        text_ref[:, side * model_width : (side + 1) * model_width] = joined(
            (5 + side) * width, text_ref.shape[0], width
        )
    whole_ref[...] = joined(7 * width, rows, 3 * width)
    total = all_ref[0, :, 10 * width :].astype(jnp.float32)
    for way in range(1, ways):
        total += all_ref[way, :, 10 * width :].astype(jnp.float32)
    small_ref[...] = total


def lay_tail(blocks, text_rows):
    ways, rows, lanes = blocks.shape
    width = 2 * rows
    model_width = ways * width
    return pl.pallas_call(
        tail_kernel,
        out_shape=[
            jax.ShapeDtypeStruct((2 * rows, model_width), jnp.float32),
            jax.ShapeDtypeStruct((rows, 3 * model_width), jnp.float32),
            jax.ShapeDtypeStruct((text_rows, 2 * model_width), jnp.float32),
            jax.ShapeDtypeStruct((rows, 3 * model_width), jnp.float32),
            jax.ShapeDtypeStruct((rows, lanes - 10 * width), jnp.float32),
        ],
        compiler_params=pltpu.CompilerParams(vmem_limit_bytes=40 * 1024 * 1024),
        name="lay_tail",
    )(blocks)


def skip_back_kernel(grad_ref, first_ref, second_ref, out_ref):
    grad = grad_ref[...]
    halves = [contract_cols(grad, half_ref[...]) for half_ref in (first_ref, second_ref)]
    rows = grad.shape[1] // 16
    out_ref[...] = side_by_side(
        [half[:, i * rows : (i + 1) * rows] for i in range(16) for half in halves]
    )


def skip_back(grad_low, first_rows):
    tokens, model_width = grad_low.shape
    return pl.pallas_call(
        skip_back_kernel,
        grid=(1,),
        in_specs=[
            pl.BlockSpec((tokens, model_width), lambda i: (0, 0)),
            pl.BlockSpec((model_width, model_width), lambda i: (0, 0)),
            pl.BlockSpec((model_width, model_width), lambda i: (0, 1)),
        ],
        out_specs=pl.BlockSpec((tokens, 2 * model_width), lambda i: (0, 0)),
        out_shape=jax.ShapeDtypeStruct((tokens, 2 * model_width), jnp.float32),
        compiler_params=pltpu.CompilerParams(vmem_limit_bytes=48 * 1024 * 1024),
        cost_estimate=pl.CostEstimate(
            flops=4 * tokens * model_width * model_width,
            bytes_accessed=4 * model_width * (model_width + 2 * tokens),
            transcendentals=0,
        ),
        name="skip_back",
    )(grad_low, first_rows, first_rows)


def units_kernel(all_ref, up_ref, down_ref):
    ways = all_ref.shape[0]
    rows, hidden = up_ref.shape
    units = hidden // ways
    owners = 16
    own = units // owners
    for owner in range(owners):
        start = owner * ways * own
        up_ref[:, start : start + ways * own] = side_by_side(
            [all_ref[way, :rows, owner * own : (owner + 1) * own] for way in range(ways)]
        )
    model_width = down_ref.shape[1]
    split = min(units, model_width)
    for way in range(ways):
        place = slice(way * own, (way + 1) * own)
        down_ref[place, :split] = all_ref[way, :own, units : units + split].astype(jnp.float32)
        if split < model_width:
            down_ref[place, split:] = all_ref[
                way, own : 2 * own, units : units + model_width - split
            ].astype(jnp.float32)


def lay_units(blocks, rows, model_width):
    ways, lines, lanes = blocks.shape
    units = lanes // 2
    return pl.pallas_call(
        units_kernel,
        out_shape=[
            jax.ShapeDtypeStruct((rows, ways * units), jnp.float32),
            jax.ShapeDtypeStruct((ways * units // 16, model_width), jnp.float32),
        ],
        compiler_params=pltpu.CompilerParams(vmem_limit_bytes=40 * 1024 * 1024),
        name="lay_units",
    )(blocks)


def fold_down(part, units, lines):
    first = part[..., :units]
    rest = part[..., units:]
    pad = [(0, 0)] * (part.ndim - 1) + [(0, units - rest.shape[-1])]
    both = jnp.concatenate([first, jnp.pad(rest, pad)], -2)
    return fit_rows(both, lines)


def fit_rows(part, lines):
    pad = [(0, 0)] * part.ndim
    pad[-2] = (0, lines - part.shape[-2])
    return jnp.pad(part, pad)


def swap(blocks, axis_name):
    return lax.all_to_all(blocks, axis_name, split_axis=0, concat_axis=0, tiled=True)


def spread(part, axis_name):
    size = lax.axis_size(axis_name)
    return swap(jnp.broadcast_to(part[None], (size,) + part.shape), axis_name)


def grid_place():
    index = lax.axis_index("seq")
    return index // 4, index % 4


def grid_send(value, pair, step):
    links = [(i, ((i // 4) ^ pair) * 4 + (i + step) % 4) for i in range(8)]
    return lax.ppermute(value, "seq", links)


def gather_tokens(part):
    pair, ring = grid_place()
    mate = grid_send(part, 1, 0)
    below = grid_send(part, 0, 1)
    above = grid_send(part, 0, -1)
    far = grid_send(part, 0, 2)
    mate_below = grid_send(mate, 0, 1)
    mate_above = grid_send(mate, 0, -1)
    mate_far = grid_send(far, 1, 0)
    here, there = pair * 4, (1 - pair) * 4
    buffer = jnp.zeros((8,) + part.shape, part.dtype)
    for one, spot in (
        (part, here + ring),
        (mate, there + ring),
        (below, here + (ring + 3) % 4),
        (above, here + (ring + 1) % 4),
        (far, here + (ring + 2) % 4),
        (mate_below, there + (ring + 3) % 4),
        (mate_above, there + (ring + 1) % 4),
        (mate_far, there + (ring + 2) % 4),
    ):
        buffer = lax.dynamic_update_index_in_dim(buffer, one, spot, 0)
    return buffer.reshape((-1,) + part.shape[1:])


def gather_behind(part):
    return spread(part, "seq").reshape((-1,) + part.shape[1:])


def sum_tokens(partial):
    low = jnp.bfloat16
    blocks = partial.astype(low).reshape((8, -1) + partial.shape[1:])
    pair, ring = grid_place()

    def meant(mate, step):
        spot = jnp.where(mate, 1 - pair, pair) * 4 + (ring + step) % 4
        return lax.dynamic_index_in_dim(blocks, spot, 0, False)

    def total(*parts):
        return sum(part.astype(jnp.float32) for part in parts)

    far_mate = grid_send(meant(True, 2), 1, 0)
    mate_below = grid_send(meant(True, 1), 0, 1)
    mate_above = grid_send(meant(True, 3), 0, -1)
    below = grid_send(meant(False, 1), 0, 1)
    above = grid_send(meant(False, 3), 0, -1)
    far = grid_send(total(meant(False, 2), far_mate).astype(low), 0, 2)
    mate = grid_send(total(meant(True, 0), mate_below, mate_above).astype(low), 1, 0)
    return total(meant(False, 0), below, above, far, mate)


def sum_behind(partial):
    blocks = partial.astype(jnp.bfloat16).reshape((8, -1) + partial.shape[1:])
    return jnp.sum(swap(blocks, "seq").astype(jnp.float32), 0)


def column_blocks(values):
    size = lax.axis_size("seq")
    rows = values.shape[0]
    return values.reshape(rows, size, -1).transpose(1, 0, 2)


def own_columns(weight, groups, size, place):
    rows = weight.shape[0]
    parts = weight.reshape(rows, groups, size, -1)
    taken = lax.dynamic_slice_in_dim(parts, place, 1, 2)
    return taken.reshape(rows, -1)


def after(values, *others):
    waits = [other[(0,) * other.ndim].astype(jnp.float32) * 0.0 for other in others]
    return values + sum(waits).astype(values.dtype)


def core_groups(owners):
    return [list(range(0, owners, 2)), list(range(1, owners, 2))]


def swap_cores(value):
    return lax.ppermute(value, "fsdp", [(i, i ^ 1) for i in range(lax.axis_size("fsdp"))])


def sum_cores(by_core):
    core = lax.axis_index("fsdp") % 2
    kept = lax.dynamic_index_in_dim(by_core, core, 0, False)
    arrived = swap_cores(lax.dynamic_index_in_dim(by_core, 1 - core, 0, False))
    return (kept.astype(jnp.float32) + arrived.astype(jnp.float32)).astype(jnp.bfloat16)


def scatter_chips(by_chip):
    return lax.psum_scatter(
        by_chip,
        "fsdp",
        scatter_dimension=0,
        axis_index_groups=core_groups(2 * by_chip.shape[0]),
        tiled=False,
    )


def sum_owners(by_core):
    chip = sum_cores(by_core)
    swapped = lax.all_to_all(
        chip,
        "fsdp",
        split_axis=0,
        concat_axis=0,
        axis_index_groups=core_groups(2 * chip.shape[0]),
        tiled=True,
    )
    return jnp.sum(swapped.astype(jnp.float32), 0)


def heads_first(values, head_dim):
    rows = values.shape[0]
    return values.reshape(rows, -1, head_dim).transpose(1, 0, 2)


def heads_last(values):
    return values.transpose(1, 0, 2).reshape(values.shape[1], -1)


def local(
    latent,
    skip_input,
    text_tokens,
    condition,
    positions,
    cotangent,
    skip_gain,
    skip_shift,
    skip_weight,
    skip_bias,
    mod_weight,
    mod_bias,
    norm1_gain,
    norm1_shift,
    qkv_weight,
    qkv_bias,
    head_gains,
    head_shifts,
    attn_weight,
    attn_bias,
    norm3_gain,
    norm3_shift,
    cross_q_weight,
    cross_q_bias,
    cross_kv_weight,
    cross_kv_bias,
    cross_weight,
    cross_bias,
    norm2_gain,
    norm2_shift,
    fc1_weight,
    fc1_bias,
    fc2_weight,
    fc2_bias,
):
    ways = lax.axis_size("seq")
    owners = lax.axis_size("fsdp")
    place = lax.axis_index("seq")
    head_dim = head_gains.shape[1]
    tokens, model_width = latent.shape[1:]
    width = model_width // ways
    low = jnp.bfloat16
    gain_table = head_gains.astype(jnp.float32)
    shift_table = head_shifts.astype(jnp.float32)
    tables = rotary_tables(positions, head_dim)

    own_rows = model_width // owners
    packed_own = own_columns(qkv_weight, 3, ways, place)
    first_own = jnp.concatenate(
        [skip_weight[:own_rows], skip_weight[own_rows:], packed_own], 1
    )
    first_rows = lax.all_gather(first_own, "fsdp", axis=0, tiled=True)
    kv_own = own_columns(cross_kv_weight, 2, ways, place)
    second_own = jnp.concatenate([attn_weight, cross_q_weight, cross_weight], 1)
    unit_rows = fc2_weight.shape[0] // ways
    down_own = lax.dynamic_slice_in_dim(fc2_weight, place * unit_rows, unit_rows, 0)
    up_own = own_columns(fc1_weight, owners, ways, place)
    units = up_own.shape[1]
    lines = max(own_rows, 2 * unit_rows)
    third_own = jnp.concatenate(
        [fit_rows(up_own, lines), fold_down(down_own, units, lines)], 1
    )
    lifted_f, silu_pull = jax.vjp(jax.nn.silu, condition.astype(jnp.float32))
    lifted = lifted_f.astype(low)
    vectors = (
        skip_gain,
        skip_shift,
        skip_bias,
        mod_bias,
        norm1_gain,
        norm1_shift,
        qkv_bias,
        attn_bias,
        norm3_gain,
        norm3_shift,
        cross_q_bias,
        cross_kv_bias,
        cross_bias,
        norm2_gain,
        norm2_shift,
        fc1_bias,
        fc2_bias,
    )
    vector_own = jnp.concatenate(vectors)
    vector_all = swap(
        jnp.concatenate(
            [
                jnp.broadcast_to(vector_own[None], (owners, vector_own.shape[0])),
                lifted.reshape(owners, own_rows),
            ],
            1,
        ),
        "fsdp",
    )
    pieces = []
    start = 0
    for one_vector in vectors:
        size = one_vector.shape[0]
        pieces.append(vector_all[:, start : start + size].reshape(-1).astype(jnp.float32))
        start += size
    lifted_own = vector_all[:, start:]
    (
        sk_gain,
        sk_shift,
        sk_bias,
        md_bias,
        one_gain,
        one_shift,
        pk_bias,
        at_bias,
        three_gain,
        three_shift,
        cq_bias,
        kv_bias,
        cr_bias,
        two_gain,
        two_shift,
        up_bias,
        down_bias,
    ) = pieces
    pk_bias_own = own_columns(pk_bias[None], 3, ways, place)[0]
    kv_bias_own = own_columns(kv_bias[None], 2, ways, place)[0]
    up_bias_own = own_columns(up_bias[None], owners, ways, place)[0]
    shift_row = (
        jnp.sum(swap(matmul(lifted_own, mod_weight), "fsdp"), 0, keepdims=True) + md_bias
    )

    kv_weight = spread(after(kv_own, vector_all), "fsdp").reshape(-1, 2 * width)
    text_now = text_tokens[0]
    text_count = text_now.shape[0]
    text_packed = matmul(text_now, kv_weight) + kv_bias_own
    text_keys_f, tk_pull = jax.vjp(
        lambda values_in, gains_in: head_norm(values_in, gains_in[3], 0.0, head_dim),
        text_packed[:, :width],
        gain_table,
    )
    text_own = jnp.concatenate(
        [text_keys_f.astype(low), text_packed[:, width:].astype(low)], 1
    )
    text_rows = text_count + -text_count % 16
    place_rows = max(text_rows, tokens)
    text_own = jnp.concatenate(
        [
            fit_rows(text_own, place_rows),
            fit_rows(positions.astype(low), place_rows),
        ],
        1,
    )
    text_spread = spread(text_own, "seq")
    tables_all = rotary_tables(text_spread[:, :tokens, 2 * width :].reshape(-1, 2), head_dim)
    text_all = text_spread[:, :text_rows, : 2 * width]
    text_all = text_all.reshape(ways, text_rows, 2, -1, head_dim)
    text_all = text_all.transpose(2, 0, 3, 1, 4).reshape(2, -1, text_rows, head_dim)
    text_all = jnp.pad(text_all, ((0, 0), (0, 0), (0, -text_rows % 128), (0, 0)))

    joined = jnp.concatenate([latent[0], skip_input[0]], 1).astype(jnp.float32)
    normed_f, skip_pull = jax.vjp(layer_norm, joined, sk_gain, sk_shift)
    normed = normed_f.astype(low)
    normed_halves = normed.reshape(tokens, owners, 2, own_rows).transpose(2, 0, 1, 3)
    normed_halves = normed_halves.reshape(2, tokens, model_width)
    stream_zero = (
        matmul(normed_halves[0], first_rows[:, :model_width])
        + matmul(normed_halves[1], first_rows[:, model_width : 2 * model_width])
        + sk_bias
    )

    pk_weight = first_rows[:, 2 * model_width :]
    second_rows = lax.all_gather(after(second_own, stream_zero), "fsdp", axis=0, tiled=True)
    at_weight = second_rows[:, :model_width]
    cq_weight = second_rows[:, model_width : 2 * model_width]
    cr_weight = second_rows[:, 2 * model_width :]
    entry_f, one_pull = jax.vjp(layer_norm, stream_zero, one_gain, one_shift)
    entry = (entry_f + shift_row).astype(low)

    entry_all = gather_tokens(entry)

    packed = matmul(entry_all, pk_weight) + pk_bias_own

    def prepare(query_pre, key_pre, gains_in, shifts_in):
        return (
            head_rotary(query_pre, gains_in[0], shifts_in[0], tables_all, head_dim),
            head_rotary(key_pre, gains_in[1], shifts_in[1], tables_all, head_dim),
        )

    (query_f, key_f), prep_pull = jax.vjp(
        prepare, packed[:, :width], packed[:, width : 2 * width], gain_table, shift_table
    )
    query_h = heads_first(query_f.astype(low), head_dim)
    key_h = heads_first(key_f.astype(low), head_dim)
    value_h = heads_first(packed[:, 2 * width :].astype(low), head_dim)
    all_tokens = query_h.shape[1]
    mixed_h, self_totals = attend(query_h, key_h, value_h, all_tokens)

    def to_heads(values):
        return swap(column_blocks(values), "seq").reshape(all_tokens, -1)

    def to_tokens(values_h):
        blocks = swap(heads_last(values_h).reshape(ways, tokens, width), "seq")
        return blocks.transpose(1, 0, 2).reshape(tokens, model_width)

    mixed = to_tokens(mixed_h)
    grad_all = gather_behind(after(cotangent[0], mixed))
    third_rows = lax.all_gather(after(third_own, mixed), "fsdp", axis=0, tiled=False)
    up_weight = third_rows[:, :own_rows, :units].reshape(model_width, units)
    down_weight = jnp.concatenate(
        [
            third_rows[:, :unit_rows, units : units + min(units, model_width)],
            third_rows[:, unit_rows : 2 * unit_rows, units : units + max(model_width - units, 0)],
        ],
        2,
    ).reshape(units, model_width)
    stream_one = stream_zero + matmul(mixed, at_weight) + at_bias

    cross_in_f, three_pull = jax.vjp(layer_norm, stream_one, three_gain, three_shift)
    cross_in = cross_in_f.astype(low)
    cross_pre = matmul(cross_in, cq_weight) + cq_bias
    cross_query_f, cq_pull = jax.vjp(
        lambda values_in, gains_in, shifts_in: head_rotary(
            values_in, gains_in[2], shifts_in[2], tables, head_dim
        ),
        cross_pre,
        gain_table,
        shift_table,
    )
    cross_query_h = heads_first(cross_query_f.astype(low), head_dim)
    step_heads = min(4, cross_query_h.shape[0])
    cross_h, cross_totals = attend(
        cross_query_h, text_all[0], text_all[1], text_count, step_heads
    )
    cross_mixed = heads_last(cross_h)
    stream_two = stream_one + matmul(cross_mixed, cr_weight) + cr_bias

    mlp_in_f, two_pull = jax.vjp(layer_norm, stream_two, two_gain, two_shift)
    mlp_all = gather_tokens(after(mlp_in_f.astype(low), grad_all))
    normed_all = lax.all_gather(after(normed, mlp_all), "seq", axis=0, tiled=True)
    hidden_pre = matmul(mlp_all, up_weight) + up_bias_own
    hidden_f, gelu_pull = jax.vjp(
        lambda values_in: jax.nn.gelu(values_in, approximate=True), hidden_pre
    )
    hidden = hidden_f.astype(low)
    out_partial = matmul(hidden, down_weight).astype(low)
    grad_three = cotangent[0].astype(jnp.float32)
    down_bias_grad = column_sums(cotangent[0])
    pre_grad = gelu_pull(contract_cols(grad_all, down_weight))[0].astype(low)
    up_bias_grad = column_sums(pre_grad)
    mlp_in_grad = sum_tokens(contract_cols(pre_grad, up_weight))
    down_grad = contract_rows(hidden, grad_all).astype(low)
    up_grad = contract_rows(mlp_all, pre_grad).astype(low)
    mlp_grads = jnp.concatenate(
        [
            fit_rows(up_grad.reshape(owners, own_rows, units), lines),
            fold_down(down_grad.reshape(owners, unit_rows, model_width), units, lines),
        ],
        2,
    )
    mlp_grads = after(mlp_grads, normed_all).reshape(owners // 2, 2, lines, 2 * units).transpose(1, 0, 2, 3)
    mlp_owned = scatter_chips(sum_cores(mlp_grads))
    mlp_in_grad = after(mlp_in_grad, mlp_grads)
    stream_part, two_gain_grad, two_shift_grad = two_pull(mlp_in_grad)
    stream_grad = grad_three + stream_part

    grad_low = stream_grad.astype(low)
    cr_bias_grad = column_sums(grad_low)
    cross_mixed_grad = contract_cols(grad_low, cr_weight).astype(low)

    cross_query_grad, text_key_part, text_value_part = attend_back(
        cross_query_h,
        text_all[0],
        text_all[1],
        cross_totals,
        heads_first(cross_mixed_grad, head_dim),
        text_count,
        step_heads,
    )
    text_parts = jnp.stack([text_key_part, text_value_part])[:, :, :text_rows].astype(low)
    text_parts = text_parts.reshape(2, ways, -1, text_rows, head_dim)
    text_parts = text_parts.transpose(1, 3, 0, 2, 4).reshape(ways, text_rows, 2 * width)
    text_kv_grad = jnp.sum(
        swap(text_parts, "seq").astype(jnp.float32), 0
    )[:text_count]
    cross_query_grad = heads_last(cross_query_grad)
    cross_out_low = grad_low
    cross_pre_grad, gains_from_cross, shifts_from_cross = cq_pull(
        cross_query_grad.astype(jnp.float32)
    )
    cross_pre_low = cross_pre_grad.astype(low)
    cq_bias_grad = column_sums(cross_pre_low)
    stream_part, three_gain_grad, three_shift_grad = three_pull(
        contract_cols(cross_pre_low, cq_weight)
    )
    stream_grad = stream_grad + stream_part

    grad_low = stream_grad.astype(low)
    at_bias_grad = column_sums(grad_low)
    mixed_grad = contract_cols(grad_low, at_weight).astype(low)
    mixed_back = to_heads(after(mixed_grad, text_kv_grad))
    whole_grads = row_grads(
        jnp.stack([mixed, cross_in, cross_mixed]),
        jnp.stack([grad_low, cross_pre_low, cross_out_low]),
        owners,
    )
    row_owned = scatter_chips(whole_grads)
    mixed_back = after(mixed_back, whole_grads)
    key_pre_grad, gains_from_text = tk_pull(text_kv_grad[:, :width])
    text_grad_low = jnp.concatenate(
        [key_pre_grad.astype(low), text_kv_grad[:, width:].astype(low)], 1
    )
    kv_weight_grad = contract_rows(text_now, text_grad_low)
    kv_bias_grad = column_sums(text_grad_low)
    text_part = contract_cols(text_grad_low, kv_weight)
    text_part = jnp.pad(text_part.astype(low), ((0, -text_count % (8 * ways)), (0, 0)))
    text_sum = sum_behind(text_part)
    stream_three = stream_two + sum_behind(after(out_partial, mixed_back)) + down_bias
    layer_out = stream_three.astype(low)[None]
    query_grad, key_grad, value_grad = attend_back(
        query_h, key_h, value_h, self_totals, heads_first(mixed_back, head_dim), all_tokens
    )

    query_pre_grad, key_pre_grad2, gains_from_self, shifts_from_self = prep_pull(
        (
            heads_last(query_grad).astype(jnp.float32),
            heads_last(key_grad).astype(low).astype(jnp.float32),
        )
    )
    packed_grad = jnp.concatenate(
        [
            query_pre_grad.astype(low),
            key_pre_grad2.astype(low),
            heads_last(value_grad).astype(low),
        ],
        1,
    )
    pk_weight_grad = contract_rows(entry_all, packed_grad)
    entry_grad = sum_tokens(after(contract_cols(packed_grad, pk_weight), stream_three))
    pk_bias_grad = column_sums(packed_grad)
    entry_grad = after(entry_grad, pk_weight_grad)
    shift_part = jnp.sum(entry_grad, 0)
    stream_part, one_gain_grad, one_shift_grad = one_pull(entry_grad)
    stream_grad = stream_grad + stream_part

    grad_low = stream_grad.astype(low)
    sk_bias_grad = column_sums(grad_low)
    shift_rows = jnp.broadcast_to(
        shift_part.astype(low).reshape(1, ways, width), (ways, ways, width)
    )
    cols_in = jnp.concatenate([column_blocks(after(grad_low, text_sum)), shift_rows], 1)
    cols_out = swap(cols_in, "seq")
    grad_cols = cols_out[:, :tokens].reshape(all_tokens, width)
    shift_total = jnp.sum(cols_out[:, tokens:].astype(jnp.float32), 0).reshape(-1)
    joined_grad, sk_gain_grad, sk_shift_grad = skip_pull(skip_back(grad_low, first_rows))

    def placed(own, groups):
        parts = jnp.zeros((groups, ways, own.shape[0] // groups), jnp.float32)
        parts = lax.dynamic_update_slice_in_dim(parts, own.reshape(groups, 1, -1), place, 1)
        return parts.reshape(-1)

    vector_grads = (
        sk_gain_grad,
        sk_shift_grad,
        sk_bias_grad,
        one_gain_grad,
        one_shift_grad,
        placed(pk_bias_grad, 3),
        at_bias_grad,
        three_gain_grad,
        three_shift_grad,
        cq_bias_grad,
        placed(kv_bias_grad, 2),
        cr_bias_grad,
        two_gain_grad,
        two_shift_grad,
        placed(up_bias_grad, owners),
        down_bias_grad,
    )
    table_grads = jnp.concatenate(
        [
            (gains_from_cross + gains_from_text + gains_from_self).reshape(-1),
            (shifts_from_cross + shifts_from_self).reshape(-1),
        ]
    )
    split_three = [part.reshape(owners, -1) for part in vector_grads]
    pk_at = 5
    pk_thirds = placed(pk_bias_grad, 3).reshape(3, model_width)
    split_three[pk_at : pk_at + 1] = [
        pk_thirds[:2].reshape(owners, -1),
        pk_thirds[2].reshape(owners, -1),
    ]
    split_three.append(jnp.broadcast_to(table_grads[None], (owners, table_grads.shape[0])))
    summed_sizes = [part.shape[1] for part in split_three]
    vector_rows = jnp.concatenate(split_three, 1).astype(low)
    vector_pad = -vector_rows.shape[1] % own_rows
    vector_rows = jnp.pad(vector_rows, ((0, 0), (0, vector_pad)))
    latent_mark = jnp.arange(owners) == lax.axis_index("fsdp")
    shift_mine = jnp.where(latent_mark[:, None], shift_total.astype(low), jnp.zeros((), low))
    shift_mine = jnp.broadcast_to(
        shift_mine.reshape(1, own_rows, -1), (owners, own_rows, owners * owners)
    )
    tail_sum = sum_owners(
        pack_tail(
            normed_all,
            grad_cols,
            pk_weight_grad,
            fit_rows(kv_weight_grad.astype(low).reshape(owners, -1, 2 * width), own_rows),
            jnp.concatenate([vector_rows.reshape(owners, own_rows, -1), shift_mine], 2),
        )
    ).astype(low)
    shift_all = tail_sum[:, -owners * owners :].reshape(owners, model_width)
    shift_all = shift_all.astype(jnp.float32)
    tail_sum = tail_sum[:, : -owners * owners]

    row_sum = jnp.sum(swap(column_blocks(row_owned), "seq").astype(jnp.float32), 0)
    lead = 7 * width
    tail_all = spread(
        jnp.concatenate([tail_sum[:, :lead], row_sum.astype(low), tail_sum[:, lead:]], 1), "seq"
    )
    text_total = gather_behind(after(text_sum.astype(low), tail_all))[:text_count]
    sk_total, pk_total, kv_total, row_total, small_total = lay_tail(
        tail_all, cross_kv_weight.shape[0]
    )
    at_total = row_total[:, :model_width]
    cq_total = row_total[:, model_width : 2 * model_width]
    cr_total = row_total[:, 2 * model_width :]
    small_total = small_total.reshape(-1)
    vector_totals = []
    start = 0
    for size in summed_sizes:
        vector_totals.append(small_total[start : start + size])
        start += size
    table_total = vector_totals.pop()
    gains_total = table_total[: gain_table.size].reshape(gain_table.shape)
    shifts_total = table_total[gain_table.size :].reshape(shift_table.shape)
    md_weight_grad = lax.dot_general(
        lifted_own.astype(jnp.float32),
        shift_all,
        (((0,), (0,)), ((), ())),
        precision=lax.Precision.HIGHEST,
        preferred_element_type=jnp.float32,
    )
    md_bias_grad = lax.dynamic_slice_in_dim(
        jnp.sum(shift_all, 0), lax.axis_index("fsdp") * own_rows, own_rows, 0
    )
    lifted_part = lax.dot_general(
        shift_all,
        mod_weight.astype(jnp.float32),
        (((1,), (1,)), ((), ())),
        precision=lax.Precision.HIGHEST,
        preferred_element_type=jnp.float32,
    )
    lifted_grad = swap(after(lifted_part, tail_all), "fsdp").reshape(1, model_width)
    condition_grad = silu_pull(lifted_grad)[0]

    mlp_all_grads = lax.all_gather(after(mlp_owned, row_owned), "seq", axis=0, tiled=False)
    up_total, down_total = lay_units(mlp_all_grads, own_rows, model_width)
    (
        sk_gain_total,
        sk_shift_total,
        sk_bias_total,
        one_gain_total,
        one_shift_total,
        pk_bias_total,
        value_bias_total,
        at_bias_total,
        three_gain_total,
        three_shift_total,
        cq_bias_total,
        kv_bias_total,
        cr_bias_total,
        two_gain_total,
        two_shift_total,
        up_bias_total,
        down_bias_total,
    ) = vector_totals
    return (
        layer_out,
        joined_grad[:, :model_width].astype(low)[None],
        joined_grad[:, model_width:].astype(low)[None],
        text_total[None],
        condition_grad,
        sk_gain_total,
        sk_shift_total,
        sk_total,
        sk_bias_total,
        md_weight_grad,
        md_bias_grad,
        one_gain_total,
        one_shift_total,
        pk_total,
        pk_bias_total,
        value_bias_total,
        gains_total,
        shifts_total,
        at_total,
        at_bias_total,
        three_gain_total,
        three_shift_total,
        cq_total,
        cq_bias_total,
        kv_total,
        kv_bias_total,
        cr_total,
        cr_bias_total,
        two_gain_total,
        two_shift_total,
        up_total,
        up_bias_total,
        down_total,
        down_bias_total,
    )


def solution(mesh):
    in_specs = (
        P("fsdp", "seq", None),
        P("fsdp", "seq", None),
        P("fsdp", None, None),
        P("fsdp", None),
        P("seq", None),
        P("fsdp", "seq", None),
        P("fsdp"),
        P("fsdp"),
        P("fsdp", None),
        P("fsdp"),
        P("fsdp", None),
        P("fsdp"),
        P("fsdp"),
        P("fsdp"),
        P("fsdp", None),
        P("fsdp"),
        P(),
        P(),
        P("fsdp", None),
        P("fsdp"),
        P("fsdp"),
        P("fsdp"),
        P("fsdp", None),
        P("fsdp"),
        P("fsdp", None),
        P("fsdp"),
        P("fsdp", None),
        P("fsdp"),
        P("fsdp"),
        P("fsdp"),
        P("fsdp", None),
        P("fsdp"),
        P("fsdp", None),
        P("fsdp"),
    )
    out_specs = (
        P("fsdp", "seq", None),
        P("fsdp", "seq", None),
        P("fsdp", "seq", None),
        P("fsdp", None, None),
        P("fsdp", None),
        P("fsdp"),
        P("fsdp"),
        P("fsdp", None),
        P("fsdp"),
        P("fsdp", None),
        P("fsdp"),
        P("fsdp"),
        P("fsdp"),
        P("fsdp", None),
        P("fsdp"),
        P("fsdp"),
        P(),
        P(),
        P("fsdp", None),
        P("fsdp"),
        P("fsdp"),
        P("fsdp"),
        P("fsdp", None),
        P("fsdp"),
        P("fsdp", None),
        P("fsdp"),
        P("fsdp", None),
        P("fsdp"),
        P("fsdp"),
        P("fsdp"),
        P("fsdp", None),
        P("fsdp"),
        P("fsdp", None),
        P("fsdp"),
    )
    return jax.shard_map(local, mesh=mesh, in_specs=in_specs, out_specs=out_specs, check_vma=False)
```

```python
import functools
import math

import jax
import jax.numpy as jnp
from jax import lax
from jax.experimental import pallas as pl
from jax.experimental.pallas import tpu as pltpu
from jax.sharding import PartitionSpec as P


def layer_norm(inputs, gain_vector, shift_vector):
    centred = inputs - jnp.mean(inputs, -1, keepdims=True)
    variance = jnp.mean(centred * centred, -1, keepdims=True)
    return centred * lax.rsqrt(variance + 1e-06) * gain_vector + shift_vector


def rotary_tables(positions, head_dim):
    quarter = head_dim // 4
    exponent = jnp.arange(quarter, dtype=jnp.float32) * (2.0 / (head_dim // 2))
    inverse = jnp.power(jnp.float32(10000.0), -exponent)
    places = positions.astype(jnp.float32)
    angle_rows = places[:, 0:1] * inverse
    angle_cols = places[:, 1:2] * inverse
    return (jnp.cos(angle_rows), jnp.sin(angle_rows), jnp.cos(angle_cols), jnp.sin(angle_cols))


def rotate(inputs, tables):
    cos_rows, sin_rows, cos_cols, sin_cols = tuple((one_table[:, None, :] for one_table in tables))
    quarter = inputs.shape[-1] // 4
    first_a = inputs[..., :quarter]
    first_b = inputs[..., quarter : 2 * quarter]
    second_a = inputs[..., 2 * quarter : 3 * quarter]
    second_b = inputs[..., 3 * quarter :]
    return jnp.concatenate(
        [
            first_a * cos_rows - first_b * sin_rows,
            first_a * sin_rows + first_b * cos_rows,
            second_a * cos_cols - second_b * sin_cols,
            second_a * sin_cols + second_b * cos_cols,
        ],
        -1,
    )


def head_norm(inputs, gain_vector, shift_vector, head_dim):
    row_count = inputs.shape[0]
    shaped = inputs.reshape(row_count, -1, head_dim)
    return layer_norm(shaped, gain_vector, shift_vector).reshape(row_count, -1)


def head_rotary(inputs, gain_vector, shift_vector, tables, head_dim):
    row_count = inputs.shape[0]
    shaped = inputs.reshape(row_count, -1, head_dim)
    return rotate(layer_norm(shaped, gain_vector, shift_vector), tables).reshape(row_count, -1)


def matmul(left_side, right_side):
    return jnp.dot(left_side, right_side, preferred_element_type=jnp.float32)


def contract_rows(left_side, right_side):
    return lax.dot_general(
        left_side, right_side, (((0,), (0,)), ((), ())), preferred_element_type=jnp.float32
    )


def contract_cols(left_side, right_side):
    return lax.dot_general(
        left_side, right_side, (((1,), (1,)), ((), ())), preferred_element_type=jnp.float32
    )


def column_sums(grads_low):
    return jnp.sum(grads_low.astype(jnp.float32), 0)


def to_float(vectors):
    return tuple((one_vector.astype(jnp.float32) for one_vector in vectors))


def forward_kernel(query_ref, keys_ref, values_ref, mixed_ref, totals_ref, *, scale, valid):
    for head in range(query_ref.shape[0]):
        scores = contract_cols(query_ref[head], keys_ref[head]) * scale
        if valid < scores.shape[1]:
            column = lax.broadcasted_iota(jnp.int32, scores.shape, 1)
            scores = jnp.where(column < valid, scores, -1e30)
        row_top = jnp.max(scores, -1, keepdims=True)
        weights = jnp.exp(scores - row_top)
        totals = jnp.sum(weights, -1, keepdims=True)
        probs = (weights * (1.0 / totals)).astype(jnp.bfloat16)
        mixed_ref[head] = matmul(probs, values_ref[head]).astype(mixed_ref.dtype)
        totals_ref[head] = row_top + jnp.log(totals)


def attend(queries, keys_in, values_in, valid, step_heads=1):
    heads, row_count, head_dim = queries.shape
    key_count = keys_in.shape[1]
    block_rows = min(512, row_count)
    rows_spec = pl.BlockSpec((step_heads, block_rows, head_dim), lambda h, i: (h, i, 0))
    keys_spec = pl.BlockSpec((step_heads, key_count, head_dim), lambda h, i: (h, 0, 0))
    return pl.pallas_call(
        functools.partial(forward_kernel, scale=1.0 / math.sqrt(head_dim), valid=valid),
        grid=(heads // step_heads, row_count // block_rows),
        in_specs=[rows_spec, keys_spec, keys_spec],
        out_specs=[rows_spec, pl.BlockSpec((step_heads, block_rows, 1), lambda h, i: (h, i, 0))],
        out_shape=[
            jax.ShapeDtypeStruct(queries.shape, jnp.bfloat16),
            jax.ShapeDtypeStruct((heads, row_count, 1), jnp.float32),
        ],
        compiler_params=pltpu.CompilerParams(vmem_limit_bytes=40 * 1024 * 1024),
        cost_estimate=pl.CostEstimate(
            flops=4 * heads * row_count * key_count * head_dim,
            bytes_accessed=4 * heads * (row_count + key_count) * head_dim,
            transcendentals=heads * row_count * key_count,
        ),
        name="attend",
    )(queries, keys_in, values_in)


def backward_kernel(
    query_ref,
    keys_ref,
    values_ref,
    totals_ref,
    grad_ref,
    query_grad_ref,
    keys_grad_ref,
    values_grad_ref,
    *,
    scale,
    valid,
):
    first = pl.program_id(1) == 0
    for head in range(query_ref.shape[0]):
        query_block = query_ref[head]
        grad_block = grad_ref[head]
        keys_now = keys_ref[head]
        probs = jnp.exp(contract_cols(query_block, keys_now) * scale - totals_ref[head])
        if valid < probs.shape[1]:
            column = lax.broadcasted_iota(jnp.int32, probs.shape, 1)
            probs = jnp.where(column < valid, probs, 0.0)
        weighted = probs * contract_cols(grad_block, values_ref[head])
        scores_grad = weighted - probs * jnp.sum(weighted, -1, keepdims=True)
        scores_low = (scores_grad * scale).astype(jnp.bfloat16)
        query_grad_ref[head] = matmul(scores_low, keys_now).astype(query_grad_ref.dtype)
        keys_part = contract_rows(scores_low, query_block)
        values_part = contract_rows(probs.astype(jnp.bfloat16), grad_block)

        @pl.when(first)
        def _():
            keys_grad_ref[head] = keys_part
            values_grad_ref[head] = values_part

        @pl.when(jnp.logical_not(first))
        def _():
            keys_grad_ref[head] += keys_part
            values_grad_ref[head] += values_part


def attend_back(queries, keys_in, values_in, totals, grad_out, valid, step_heads=1):
    heads, row_count, head_dim = queries.shape
    key_count = keys_in.shape[1]
    block_rows = min(512, row_count)
    rows_spec = pl.BlockSpec((step_heads, block_rows, head_dim), lambda h, i: (h, i, 0))
    keys_spec = pl.BlockSpec((step_heads, key_count, head_dim), lambda h, i: (h, 0, 0))
    totals_spec = pl.BlockSpec((step_heads, block_rows, 1), lambda h, i: (h, i, 0))
    return pl.pallas_call(
        functools.partial(backward_kernel, scale=1.0 / math.sqrt(head_dim), valid=valid),
        grid=(heads // step_heads, row_count // block_rows),
        in_specs=[rows_spec, keys_spec, keys_spec, totals_spec, rows_spec],
        out_specs=[rows_spec, keys_spec, keys_spec],
        out_shape=[
            jax.ShapeDtypeStruct(queries.shape, jnp.bfloat16),
            jax.ShapeDtypeStruct(keys_in.shape, jnp.float32),
            jax.ShapeDtypeStruct(keys_in.shape, jnp.float32),
        ],
        compiler_params=pltpu.CompilerParams(vmem_limit_bytes=40 * 1024 * 1024),
        cost_estimate=pl.CostEstimate(
            flops=10 * heads * row_count * key_count * head_dim,
            bytes_accessed=8 * heads * (row_count + key_count) * head_dim,
            transcendentals=heads * row_count * key_count,
        ),
        name="attend_back",
    )(queries, keys_in, values_in, totals, grad_out)


def normalised(values):
    centred = values - jnp.mean(values, -1, keepdims=True)
    scale = lax.rsqrt(jnp.mean(centred * centred, -1, keepdims=True) + 1e-06)
    return centred * scale, scale


def partners(values):
    quarter = values.shape[1] // 4
    return jnp.concatenate(
        [
            values[:, quarter : 2 * quarter],
            values[:, :quarter],
            values[:, 3 * quarter :],
            values[:, 2 * quarter : 3 * quarter],
        ],
        1,
    )


def norm_turn(values, gain, shift, cos_now, sin_now):
    turned = normalised(values)[0] * gain + shift
    return turned * cos_now + partners(turned) * sin_now


def norm_turn_back(grad, values, gain, cos_now, sin_now):
    grad = grad.astype(jnp.bfloat16).astype(jnp.float32)
    grad = grad * cos_now - partners(grad) * sin_now
    normal, scale = normalised(values)
    scaled = grad * gain
    mean_one = jnp.mean(scaled, -1, keepdims=True)
    mean_two = jnp.mean(scaled * normal, -1, keepdims=True)
    return (
        scale * (scaled - mean_one - normal * mean_two),
        jnp.sum(grad * normal, 0, keepdims=True),
        jnp.sum(grad, 0, keepdims=True),
    )


def self_forward_kernel(
    entry_ref,
    weight_ref,
    bias_ref,
    gains_ref,
    shifts_ref,
    cos_ref,
    sin_ref,
    mixed_ref,
    heads_ref,
    pre_ref,
    totals_ref,
    *,
    scale,
):
    low = jnp.bfloat16
    count, all_tokens, head_dim = heads_ref.shape[1:]
    packed = matmul(entry_ref[...], weight_ref[...]) + bias_ref[...]
    pre_ref[...] = packed[:, : 2 * count * head_dim]
    cos_now, sin_now = cos_ref[...], sin_ref[...]
    for head in range(count):
        for kind in range(3):
            start = (kind * count + head) * head_dim
            part = packed[:, start : start + head_dim]
            if kind < 2:
                part = norm_turn(
                    part,
                    gains_ref[kind : kind + 1],
                    shifts_ref[kind : kind + 1],
                    cos_now,
                    sin_now,
                )
            heads_ref[kind, head] = part.astype(low)
    step = min(512, all_tokens)
    for start in range(0, all_tokens, step):
        mixed = []
        for head in range(count):
            query_block = heads_ref[0, head, start : start + step]
            scores = contract_cols(query_block, heads_ref[1, head]) * scale
            row_top = jnp.max(scores, -1, keepdims=True)
            weights = jnp.exp(scores - row_top)
            totals = jnp.sum(weights, -1, keepdims=True)
            probs = (weights * (1.0 / totals)).astype(low)
            mixed.append(matmul(probs, heads_ref[2, head]))
            totals_ref[head, start : start + step] = row_top + jnp.log(totals)
        mixed_ref[start : start + step] = jnp.concatenate(mixed, 1).astype(low)


def self_forward(entry_all, weight, bias, gains, shifts, cos_now, sin_now):
    all_tokens, head_dim = cos_now.shape
    count = weight.shape[1] // (3 * head_dim)
    return pl.pallas_call(
        functools.partial(self_forward_kernel, scale=1.0 / math.sqrt(head_dim)),
        out_shape=[
            jax.ShapeDtypeStruct((all_tokens, count * head_dim), jnp.bfloat16),
            jax.ShapeDtypeStruct((3, count, all_tokens, head_dim), jnp.bfloat16),
            jax.ShapeDtypeStruct((all_tokens, 2 * count * head_dim), jnp.float32),
            jax.ShapeDtypeStruct((count, all_tokens, 1), jnp.float32),
        ],
        compiler_params=pltpu.CompilerParams(vmem_limit_bytes=50 * 1024 * 1024),
        cost_estimate=pl.CostEstimate(
            flops=2 * all_tokens * weight.size + 4 * count * all_tokens**2 * head_dim,
            bytes_accessed=2 * entry_all.size + 2 * weight.size + 16 * all_tokens * weight.shape[1],
            transcendentals=count * all_tokens**2,
        ),
        name="self_forward",
    )(entry_all, weight, bias, gains, shifts, cos_now, sin_now)


def self_backward_kernel(
    heads_ref, totals_ref, grad_ref, pre_ref, gains_ref, cos_ref, sin_ref, out_ref, sums_ref, *, scale
):
    low = jnp.bfloat16
    count, all_tokens, head_dim = heads_ref.shape[1:]
    cos_now, sin_now = cos_ref[...], sin_ref[...]
    step = min(512, all_tokens)
    lanes = [None] * (3 * count)
    sums = None
    for head in range(count):
        keys_now = heads_ref[1, head]
        values_now = heads_ref[2, head]
        keys_grad, values_grad, query_grads = 0.0, 0.0, []
        for start in range(0, all_tokens, step):
            query_block = heads_ref[0, head, start : start + step]
            grad_block = grad_ref[start : start + step, head * head_dim : (head + 1) * head_dim]
            probs = jnp.exp(
                contract_cols(query_block, keys_now) * scale
                - totals_ref[head, start : start + step]
            )
            weighted = probs * contract_cols(grad_block, values_now)
            scores_grad = weighted - probs * jnp.sum(weighted, -1, keepdims=True)
            scores_low = (scores_grad * scale).astype(low)
            query_grads.append(matmul(scores_low, keys_now))
            keys_grad += contract_rows(scores_low, query_block)
            values_grad += contract_rows(probs.astype(low), grad_block)
        grads = (jnp.concatenate(query_grads, 0), keys_grad)
        parts = []
        for kind in range(2):
            start = (kind * count + head) * head_dim
            back, gain_sum, shift_sum = norm_turn_back(
                grads[kind],
                pre_ref[:, start : start + head_dim],
                gains_ref[kind : kind + 1],
                cos_now,
                sin_now,
            )
            lanes[kind * count + head] = back
            parts += [gain_sum, shift_sum]
        lanes[2 * count + head] = values_grad
        parts = jnp.concatenate(parts, 0)
        sums = parts if sums is None else sums + parts
    out_ref[...] = jnp.concatenate(lanes, 1).astype(low)
    sums_ref[...] = sums


def self_backward(heads, totals, grad_out, pre, gains, cos_now, sin_now):
    count, all_tokens, head_dim = heads.shape[1:]
    return pl.pallas_call(
        functools.partial(self_backward_kernel, scale=1.0 / math.sqrt(head_dim)),
        out_shape=[
            jax.ShapeDtypeStruct((all_tokens, 3 * count * head_dim), jnp.bfloat16),
            jax.ShapeDtypeStruct((4, head_dim), jnp.float32),
        ],
        compiler_params=pltpu.CompilerParams(vmem_limit_bytes=50 * 1024 * 1024),
        cost_estimate=pl.CostEstimate(
            flops=10 * count * all_tokens**2 * head_dim,
            bytes_accessed=24 * count * all_tokens * head_dim,
            transcendentals=count * all_tokens**2,
        ),
        name="self_backward",
    )(heads, totals, grad_out, pre, gains, cos_now, sin_now)


def row_grads_kernel(left_ref, far_left_ref, right_ref, far_right_ref, out_ref):
    product = contract_rows(left_ref[0], right_ref[0])
    product += contract_rows(far_left_ref[0], far_right_ref[0])
    rows = out_ref.shape[1]
    for chip in range(out_ref.shape[0]):
        out_ref[chip] = product[chip * rows : (chip + 1) * rows].astype(out_ref.dtype)


def row_grads(lefts, rights, owners):
    count, tokens, width = lefts.shape
    rows = width // owners
    core = lax.axis_index("fsdp") % 2
    by_core = lefts.reshape(count, tokens, owners // 2, 2, rows).transpose(3, 0, 1, 2, 4)
    by_core = by_core.reshape(2, count, tokens, width // 2)
    near = lax.dynamic_index_in_dim(by_core, core, 0, False)
    far = swap_cores(lax.dynamic_index_in_dim(by_core, 1 - core, 0, False))
    left_spec = pl.BlockSpec((1, tokens, width // 2), lambda i: (i, 0, 0))
    right_spec = pl.BlockSpec((1, tokens, width), lambda i: (i, 0, 0))
    return pl.pallas_call(
        row_grads_kernel,
        grid=(count,),
        in_specs=[left_spec, left_spec, right_spec, right_spec],
        out_specs=pl.BlockSpec((owners // 2, rows, width), lambda i: (0, 0, i)),
        out_shape=jax.ShapeDtypeStruct((owners // 2, rows, count * width), jnp.bfloat16),
        compiler_params=pltpu.CompilerParams(vmem_limit_bytes=48 * 1024 * 1024),
        cost_estimate=pl.CostEstimate(
            flops=2 * count * tokens * width * width,
            bytes_accessed=2 * count * (width * width // 2 + 3 * tokens * width),
            transcendentals=0,
        ),
        name="row_grads",
    )(near, far, rights, swap_cores(rights))


def side_by_side(pieces):
    return jnp.concatenate([piece.astype(jnp.float32) for piece in pieces], 1)


def pack_kernel(normed_ref, cols_ref, packed_ref, text_ref, small_ref, out_ref):
    owners, rows = text_ref.shape[:2]
    cols = cols_ref[...]
    middle = normed_ref.shape[1] // 2
    products = [
        contract_rows(normed_ref[:, :middle], cols),
        contract_rows(normed_ref[:, middle:], cols),
    ]
    for owner in range(owners):
        product = products[owner // (owners // 2)]
        start = (owner % (owners // 2)) * 2 * rows
        line = side_by_side(
            [
                product[start : start + rows],
                product[start + rows : start + 2 * rows],
                packed_ref[owner * rows : (owner + 1) * rows],
                text_ref[owner],
                small_ref[owner],
            ]
        )
        out_ref[owner % 2, owner // 2] = line.astype(out_ref.dtype)


def pack_tail(normed, cols, packed, text, small):
    owners, rows = text.shape[:2]
    lanes = 2 * cols.shape[1] + packed.shape[1] + text.shape[2] + small.shape[2]
    return pl.pallas_call(
        pack_kernel,
        out_shape=jax.ShapeDtypeStruct((2, owners // 2, rows, lanes), jnp.bfloat16),
        compiler_params=pltpu.CompilerParams(vmem_limit_bytes=48 * 1024 * 1024),
        cost_estimate=pl.CostEstimate(
            flops=2 * normed.size * cols.shape[1],
            bytes_accessed=2 * normed.size + 4 * owners * rows * lanes,
            transcendentals=0,
        ),
        name="pack_tail",
    )(normed, cols, packed, text, small)


def tail_kernel(all_ref, skip_ref, packed_ref, text_ref, whole_ref, small_ref):
    ways, rows = all_ref.shape[:2]
    model_width = skip_ref.shape[1]
    width = model_width // ways

    def joined(start, count, size):
        return side_by_side(
            [all_ref[way, :, start : start + size][:count] for way in range(ways)]
        )

    skip_ref[:rows] = joined(0, rows, width)
    skip_ref[rows:] = joined(width, rows, width)
    for third in range(3):
        packed_ref[:, third * model_width : (third + 1) * model_width] = joined(
            (2 + third) * width, rows, width
        )
    for side in range(2):
        text_ref[:, side * model_width : (side + 1) * model_width] = joined(
            (5 + side) * width, text_ref.shape[0], width
        )
    whole_ref[...] = joined(7 * width, rows, 3 * width)
    total = all_ref[0, :, 10 * width :].astype(jnp.float32)
    for way in range(1, ways):
        total += all_ref[way, :, 10 * width :].astype(jnp.float32)
    small_ref[...] = total


def lay_tail(blocks, text_rows):
    ways, rows, lanes = blocks.shape
    width = 2 * rows
    model_width = ways * width
    return pl.pallas_call(
        tail_kernel,
        out_shape=[
            jax.ShapeDtypeStruct((2 * rows, model_width), jnp.float32),
            jax.ShapeDtypeStruct((rows, 3 * model_width), jnp.float32),
            jax.ShapeDtypeStruct((text_rows, 2 * model_width), jnp.float32),
            jax.ShapeDtypeStruct((rows, 3 * model_width), jnp.float32),
            jax.ShapeDtypeStruct((rows, lanes - 10 * width), jnp.float32),
        ],
        compiler_params=pltpu.CompilerParams(vmem_limit_bytes=40 * 1024 * 1024),
        name="lay_tail",
    )(blocks)


def skip_back_kernel(grad_ref, first_ref, second_ref, out_ref):
    grad = grad_ref[...]
    halves = [contract_cols(grad, half_ref[...]) for half_ref in (first_ref, second_ref)]
    rows = grad.shape[1] // 16
    out_ref[...] = side_by_side(
        [half[:, i * rows : (i + 1) * rows] for i in range(16) for half in halves]
    )


def skip_back(grad_low, first_rows):
    tokens, model_width = grad_low.shape
    return pl.pallas_call(
        skip_back_kernel,
        grid=(1,),
        in_specs=[
            pl.BlockSpec((tokens, model_width), lambda i: (0, 0)),
            pl.BlockSpec((model_width, model_width), lambda i: (0, 0)),
            pl.BlockSpec((model_width, model_width), lambda i: (0, 1)),
        ],
        out_specs=pl.BlockSpec((tokens, 2 * model_width), lambda i: (0, 0)),
        out_shape=jax.ShapeDtypeStruct((tokens, 2 * model_width), jnp.float32),
        compiler_params=pltpu.CompilerParams(vmem_limit_bytes=48 * 1024 * 1024),
        cost_estimate=pl.CostEstimate(
            flops=4 * tokens * model_width * model_width,
            bytes_accessed=4 * model_width * (model_width + 2 * tokens),
            transcendentals=0,
        ),
        name="skip_back",
    )(grad_low, first_rows, first_rows)


def units_kernel(all_ref, up_ref, down_ref):
    ways = all_ref.shape[0]
    rows, hidden = up_ref.shape
    units = hidden // ways
    owners = 16
    own = units // owners
    for owner in range(owners):
        start = owner * ways * own
        up_ref[:, start : start + ways * own] = side_by_side(
            [all_ref[way, :rows, owner * own : (owner + 1) * own] for way in range(ways)]
        )
    model_width = down_ref.shape[1]
    split = min(units, model_width)
    for way in range(ways):
        place = slice(way * own, (way + 1) * own)
        down_ref[place, :split] = all_ref[way, :own, units : units + split].astype(jnp.float32)
        if split < model_width:
            down_ref[place, split:] = all_ref[
                way, own : 2 * own, units : units + model_width - split
            ].astype(jnp.float32)


def lay_units(blocks, rows, model_width):
    ways, lines, lanes = blocks.shape
    units = lanes // 2
    return pl.pallas_call(
        units_kernel,
        out_shape=[
            jax.ShapeDtypeStruct((rows, ways * units), jnp.float32),
            jax.ShapeDtypeStruct((ways * units // 16, model_width), jnp.float32),
        ],
        compiler_params=pltpu.CompilerParams(vmem_limit_bytes=40 * 1024 * 1024),
        name="lay_units",
    )(blocks)


def fold_down(part, units, lines):
    first = part[..., :units]
    rest = part[..., units:]
    pad = [(0, 0)] * (part.ndim - 1) + [(0, units - rest.shape[-1])]
    both = jnp.concatenate([first, jnp.pad(rest, pad)], -2)
    return fit_rows(both, lines)


def fit_rows(part, lines):
    pad = [(0, 0)] * part.ndim
    pad[-2] = (0, lines - part.shape[-2])
    return jnp.pad(part, pad)


def swap(blocks, axis_name):
    return lax.all_to_all(blocks, axis_name, split_axis=0, concat_axis=0, tiled=True)


def spread(part, axis_name):
    size = lax.axis_size(axis_name)
    return swap(jnp.broadcast_to(part[None], (size,) + part.shape), axis_name)


def grid_place():
    index = lax.axis_index("seq")
    return index // 4, index % 4


def grid_send(value, pair, step):
    links = [(i, ((i // 4) ^ pair) * 4 + (i + step) % 4) for i in range(8)]
    return lax.ppermute(value, "seq", links)


def gather_tokens(part):
    pair, ring = grid_place()
    mate = grid_send(part, 1, 0)
    below = grid_send(part, 0, 1)
    above = grid_send(part, 0, -1)
    far = grid_send(part, 0, 2)
    mate_below = grid_send(mate, 0, 1)
    mate_above = grid_send(mate, 0, -1)
    mate_far = grid_send(far, 1, 0)
    here, there = pair * 4, (1 - pair) * 4
    buffer = jnp.zeros((8,) + part.shape, part.dtype)
    for one, spot in (
        (part, here + ring),
        (mate, there + ring),
        (below, here + (ring + 3) % 4),
        (above, here + (ring + 1) % 4),
        (far, here + (ring + 2) % 4),
        (mate_below, there + (ring + 3) % 4),
        (mate_above, there + (ring + 1) % 4),
        (mate_far, there + (ring + 2) % 4),
    ):
        buffer = lax.dynamic_update_index_in_dim(buffer, one, spot, 0)
    return buffer.reshape((-1,) + part.shape[1:])


def gather_behind(part):
    return spread(part, "seq").reshape((-1,) + part.shape[1:])


def sum_tokens(partial):
    low = jnp.bfloat16
    blocks = partial.astype(low).reshape((8, -1) + partial.shape[1:])
    pair, ring = grid_place()

    def meant(mate, step):
        spot = jnp.where(mate, 1 - pair, pair) * 4 + (ring + step) % 4
        return lax.dynamic_index_in_dim(blocks, spot, 0, False)

    def total(*parts):
        return sum(part.astype(jnp.float32) for part in parts)

    far_mate = grid_send(meant(True, 2), 1, 0)
    mate_below = grid_send(meant(True, 1), 0, 1)
    mate_above = grid_send(meant(True, 3), 0, -1)
    below = grid_send(meant(False, 1), 0, 1)
    above = grid_send(meant(False, 3), 0, -1)
    far = grid_send(total(meant(False, 2), far_mate).astype(low), 0, 2)
    mate = grid_send(total(meant(True, 0), mate_below, mate_above).astype(low), 1, 0)
    return total(meant(False, 0), below, above, far, mate)


def sum_behind(partial):
    blocks = partial.astype(jnp.bfloat16).reshape((8, -1) + partial.shape[1:])
    return jnp.sum(swap(blocks, "seq").astype(jnp.float32), 0)


def column_blocks(values):
    size = lax.axis_size("seq")
    rows = values.shape[0]
    return values.reshape(rows, size, -1).transpose(1, 0, 2)


def own_columns(weight, groups, size, place):
    rows = weight.shape[0]
    parts = weight.reshape(rows, groups, size, -1)
    taken = lax.dynamic_slice_in_dim(parts, place, 1, 2)
    return taken.reshape(rows, -1)


def after(values, *others):
    waits = [other[(0,) * other.ndim].astype(jnp.float32) * 0.0 for other in others]
    return values + sum(waits).astype(values.dtype)


def core_groups(owners):
    return [list(range(0, owners, 2)), list(range(1, owners, 2))]


def swap_cores(value):
    return lax.ppermute(value, "fsdp", [(i, i ^ 1) for i in range(lax.axis_size("fsdp"))])


def sum_cores(by_core):
    core = lax.axis_index("fsdp") % 2
    kept = lax.dynamic_index_in_dim(by_core, core, 0, False)
    arrived = swap_cores(lax.dynamic_index_in_dim(by_core, 1 - core, 0, False))
    return (kept.astype(jnp.float32) + arrived.astype(jnp.float32)).astype(jnp.bfloat16)


def scatter_chips(by_chip):
    return lax.psum_scatter(
        by_chip,
        "fsdp",
        scatter_dimension=0,
        axis_index_groups=core_groups(2 * by_chip.shape[0]),
        tiled=False,
    )


def sum_owners(by_core):
    chip = sum_cores(by_core)
    swapped = lax.all_to_all(
        chip,
        "fsdp",
        split_axis=0,
        concat_axis=0,
        axis_index_groups=core_groups(2 * chip.shape[0]),
        tiled=True,
    )
    return jnp.sum(swapped.astype(jnp.float32), 0)


def heads_first(values, head_dim):
    rows = values.shape[0]
    return values.reshape(rows, -1, head_dim).transpose(1, 0, 2)


def heads_last(values):
    return values.transpose(1, 0, 2).reshape(values.shape[1], -1)


def local(
    latent,
    skip_input,
    text_tokens,
    condition,
    positions,
    cotangent,
    skip_gain,
    skip_shift,
    skip_weight,
    skip_bias,
    mod_weight,
    mod_bias,
    norm1_gain,
    norm1_shift,
    qkv_weight,
    qkv_bias,
    head_gains,
    head_shifts,
    attn_weight,
    attn_bias,
    norm3_gain,
    norm3_shift,
    cross_q_weight,
    cross_q_bias,
    cross_kv_weight,
    cross_kv_bias,
    cross_weight,
    cross_bias,
    norm2_gain,
    norm2_shift,
    fc1_weight,
    fc1_bias,
    fc2_weight,
    fc2_bias,
):
    ways = lax.axis_size("seq")
    owners = lax.axis_size("fsdp")
    place = lax.axis_index("seq")
    head_dim = head_gains.shape[1]
    tokens, model_width = latent.shape[1:]
    width = model_width // ways
    low = jnp.bfloat16
    gain_table = head_gains.astype(jnp.float32)
    shift_table = head_shifts.astype(jnp.float32)
    tables = rotary_tables(positions, head_dim)

    own_rows = model_width // owners
    packed_own = own_columns(qkv_weight, 3, ways, place)
    first_own = jnp.concatenate(
        [skip_weight[:own_rows], skip_weight[own_rows:], packed_own], 1
    )
    first_rows = lax.all_gather(first_own, "fsdp", axis=0, tiled=True)
    kv_own = own_columns(cross_kv_weight, 2, ways, place)
    second_own = jnp.concatenate([attn_weight, cross_q_weight, cross_weight], 1)
    unit_rows = fc2_weight.shape[0] // ways
    down_own = lax.dynamic_slice_in_dim(fc2_weight, place * unit_rows, unit_rows, 0)
    up_own = own_columns(fc1_weight, owners, ways, place)
    units = up_own.shape[1]
    lines = max(own_rows, 2 * unit_rows)
    third_own = jnp.concatenate(
        [fit_rows(up_own, lines), fold_down(down_own, units, lines)], 1
    )
    lifted_f, silu_pull = jax.vjp(jax.nn.silu, condition.astype(jnp.float32))
    lifted = lifted_f.astype(low)
    vectors = (
        skip_gain,
        skip_shift,
        skip_bias,
        mod_bias,
        norm1_gain,
        norm1_shift,
        qkv_bias,
        attn_bias,
        norm3_gain,
        norm3_shift,
        cross_q_bias,
        cross_kv_bias,
        cross_bias,
        norm2_gain,
        norm2_shift,
        fc1_bias,
        fc2_bias,
    )
    vector_own = jnp.concatenate(vectors)
    vector_all = swap(
        jnp.concatenate(
            [
                jnp.broadcast_to(vector_own[None], (owners, vector_own.shape[0])),
                lifted.reshape(owners, own_rows),
            ],
            1,
        ),
        "fsdp",
    )
    pieces = []
    start = 0
    for one_vector in vectors:
        size = one_vector.shape[0]
        pieces.append(vector_all[:, start : start + size].reshape(-1).astype(jnp.float32))
        start += size
    lifted_own = vector_all[:, start:]
    (
        sk_gain,
        sk_shift,
        sk_bias,
        md_bias,
        one_gain,
        one_shift,
        pk_bias,
        at_bias,
        three_gain,
        three_shift,
        cq_bias,
        kv_bias,
        cr_bias,
        two_gain,
        two_shift,
        up_bias,
        down_bias,
    ) = pieces
    pk_bias_own = own_columns(pk_bias[None], 3, ways, place)[0]
    kv_bias_own = own_columns(kv_bias[None], 2, ways, place)[0]
    up_bias_own = own_columns(up_bias[None], owners, ways, place)[0]
    shift_row = (
        jnp.sum(swap(matmul(lifted_own, mod_weight), "fsdp"), 0, keepdims=True) + md_bias
    )

    kv_weight = spread(after(kv_own, vector_all), "fsdp").reshape(-1, 2 * width)
    text_now = text_tokens[0]
    text_count = text_now.shape[0]
    text_packed = matmul(text_now, kv_weight) + kv_bias_own
    text_keys_f, tk_pull = jax.vjp(
        lambda values_in, gains_in: head_norm(values_in, gains_in[3], 0.0, head_dim),
        text_packed[:, :width],
        gain_table,
    )
    text_own = jnp.concatenate(
        [text_keys_f.astype(low), text_packed[:, width:].astype(low)], 1
    )
    text_rows = text_count + -text_count % 16
    place_rows = max(text_rows, tokens)
    text_own = jnp.concatenate(
        [
            fit_rows(text_own, place_rows),
            fit_rows(positions.astype(low), place_rows),
        ],
        1,
    )
    text_spread = spread(text_own, "seq")
    cos_rows, sin_rows, cos_cols, sin_cols = rotary_tables(
        text_spread[:, :tokens, 2 * width :].reshape(-1, 2), head_dim
    )
    cos_all = jnp.concatenate([cos_rows, cos_rows, cos_cols, cos_cols], 1)
    sin_all = jnp.concatenate([-sin_rows, sin_rows, -sin_cols, sin_cols], 1)
    text_all = text_spread[:, :text_rows, : 2 * width]
    text_all = text_all.reshape(ways, text_rows, 2, -1, head_dim)
    text_all = text_all.transpose(2, 0, 3, 1, 4).reshape(2, -1, text_rows, head_dim)
    text_all = jnp.pad(text_all, ((0, 0), (0, 0), (0, -text_rows % 128), (0, 0)))

    joined = jnp.concatenate([latent[0], skip_input[0]], 1).astype(jnp.float32)
    normed_f, skip_pull = jax.vjp(layer_norm, joined, sk_gain, sk_shift)
    normed = normed_f.astype(low)
    normed_halves = normed.reshape(tokens, owners, 2, own_rows).transpose(2, 0, 1, 3)
    normed_halves = normed_halves.reshape(2, tokens, model_width)
    normed_halves = after(normed_halves, shift_row, text_spread)
    stream_zero = (
        matmul(normed_halves[0], first_rows[:, :model_width])
        + matmul(normed_halves[1], first_rows[:, model_width : 2 * model_width])
        + sk_bias
    )

    pk_weight = first_rows[:, 2 * model_width :]
    second_rows = lax.all_gather(after(second_own, stream_zero), "fsdp", axis=0, tiled=True)
    at_weight = second_rows[:, :model_width]
    cq_weight = second_rows[:, model_width : 2 * model_width]
    cr_weight = second_rows[:, 2 * model_width :]
    entry_f, one_pull = jax.vjp(layer_norm, stream_zero, one_gain, one_shift)
    entry = (entry_f + shift_row).astype(low)

    entry_all = gather_tokens(entry)

    mixed_h, heads_h, packed_pre, self_totals = self_forward(
        entry_all, pk_weight, pk_bias_own[None], gain_table, shift_table, cos_all, sin_all
    )
    all_tokens = entry_all.shape[0]

    def to_heads(values):
        return swap(column_blocks(values), "seq").reshape(all_tokens, -1)

    mixed = swap(mixed_h.reshape(ways, tokens, width), "seq")
    mixed = mixed.transpose(1, 0, 2).reshape(tokens, model_width)
    grad_all = gather_behind(after(cotangent[0], mixed))
    third_rows = lax.all_gather(after(third_own, entry_all), "fsdp", axis=0, tiled=False)
    up_weight = third_rows[:, :own_rows, :units].reshape(model_width, units)
    down_weight = jnp.concatenate(
        [
            third_rows[:, :unit_rows, units : units + min(units, model_width)],
            third_rows[:, unit_rows : 2 * unit_rows, units : units + max(model_width - units, 0)],
        ],
        2,
    ).reshape(units, model_width)
    stream_one = stream_zero + matmul(mixed, at_weight) + at_bias

    cross_in_f, three_pull = jax.vjp(layer_norm, stream_one, three_gain, three_shift)
    cross_in = cross_in_f.astype(low)
    cross_pre = matmul(cross_in, cq_weight) + cq_bias
    cross_query_f, cq_pull = jax.vjp(
        lambda values_in, gains_in, shifts_in: head_rotary(
            values_in, gains_in[2], shifts_in[2], tables, head_dim
        ),
        cross_pre,
        gain_table,
        shift_table,
    )
    cross_query_h = heads_first(cross_query_f.astype(low), head_dim)
    step_heads = min(4, cross_query_h.shape[0])
    cross_h, cross_totals = attend(
        cross_query_h, text_all[0], text_all[1], text_count, step_heads
    )
    cross_mixed = heads_last(cross_h)
    stream_two = stream_one + matmul(cross_mixed, cr_weight) + cr_bias

    mlp_in_f, two_pull = jax.vjp(layer_norm, stream_two, two_gain, two_shift)
    mlp_all = gather_tokens(after(mlp_in_f.astype(low), grad_all))
    normed_all = lax.all_gather(after(normed, mlp_all), "seq", axis=0, tiled=True)
    hidden_pre = matmul(mlp_all, up_weight) + up_bias_own
    hidden_f, gelu_pull = jax.vjp(
        lambda values_in: jax.nn.gelu(values_in, approximate=True), hidden_pre
    )
    hidden = hidden_f.astype(low)
    out_partial = matmul(hidden, down_weight).astype(low)
    grad_three = cotangent[0].astype(jnp.float32)
    down_bias_grad = column_sums(cotangent[0])
    pre_grad = gelu_pull(contract_cols(grad_all, down_weight))[0].astype(low)
    up_bias_grad = column_sums(pre_grad)
    mlp_in_grad = sum_tokens(contract_cols(pre_grad, up_weight))
    down_grad = contract_rows(hidden, grad_all).astype(low)
    up_grad = contract_rows(mlp_all, pre_grad).astype(low)
    mlp_grads = jnp.concatenate(
        [
            fit_rows(up_grad.reshape(owners, own_rows, units), lines),
            fold_down(down_grad.reshape(owners, unit_rows, model_width), units, lines),
        ],
        2,
    )
    mlp_grads = mlp_grads.reshape(owners // 2, 2, lines, 2 * units).transpose(1, 0, 2, 3)
    mlp_owned = scatter_chips(sum_cores(mlp_grads))
    mlp_in_grad = after(mlp_in_grad, mlp_grads)
    stream_part, two_gain_grad, two_shift_grad = two_pull(mlp_in_grad)
    stream_grad = grad_three + stream_part

    grad_low = stream_grad.astype(low)
    cr_bias_grad = column_sums(grad_low)
    cross_mixed_grad = contract_cols(grad_low, cr_weight).astype(low)

    cross_query_grad, text_key_part, text_value_part = attend_back(
        cross_query_h,
        text_all[0],
        text_all[1],
        cross_totals,
        heads_first(cross_mixed_grad, head_dim),
        text_count,
        step_heads,
    )
    text_parts = jnp.stack([text_key_part, text_value_part])[:, :, :text_rows].astype(low)
    text_parts = text_parts.reshape(2, ways, -1, text_rows, head_dim)
    text_parts = text_parts.transpose(1, 3, 0, 2, 4).reshape(ways, text_rows, 2 * width)
    text_kv_grad = jnp.sum(
        swap(text_parts, "seq").astype(jnp.float32), 0
    )[:text_count]
    cross_query_grad = heads_last(cross_query_grad)
    cross_out_low = grad_low
    cross_pre_grad, gains_from_cross, shifts_from_cross = cq_pull(
        cross_query_grad.astype(jnp.float32)
    )
    cross_pre_low = cross_pre_grad.astype(low)
    cq_bias_grad = column_sums(cross_pre_low)
    stream_part, three_gain_grad, three_shift_grad = three_pull(
        contract_cols(cross_pre_low, cq_weight)
    )
    stream_grad = stream_grad + stream_part

    grad_low = stream_grad.astype(low)
    at_bias_grad = column_sums(grad_low)
    mixed_grad = contract_cols(grad_low, at_weight).astype(low)
    mixed_back = to_heads(after(mixed_grad, text_kv_grad, normed_all))
    whole_grads = row_grads(
        jnp.stack([mixed, cross_in, cross_mixed]),
        after(jnp.stack([grad_low, cross_pre_low, cross_out_low]), mlp_owned),
        owners,
    )
    row_owned = scatter_chips(whole_grads)
    mixed_back = after(mixed_back, whole_grads)
    key_pre_grad, gains_from_text = tk_pull(text_kv_grad[:, :width])
    text_grad_low = jnp.concatenate(
        [key_pre_grad.astype(low), text_kv_grad[:, width:].astype(low)], 1
    )
    kv_weight_grad = contract_rows(text_now, text_grad_low)
    kv_bias_grad = column_sums(text_grad_low)
    text_part = contract_cols(text_grad_low, kv_weight)
    text_part = jnp.pad(text_part.astype(low), ((0, -text_count % (8 * ways)), (0, 0)))
    text_sum = sum_behind(text_part)
    stream_three = stream_two + sum_behind(after(out_partial, mixed_back)) + down_bias
    layer_out = stream_three.astype(low)[None]
    packed_grad, self_sums = self_backward(
        heads_h, self_totals, mixed_back, packed_pre, gain_table, cos_all, sin_all
    )
    pk_weight_grad = contract_rows(entry_all, packed_grad)
    entry_grad = sum_tokens(after(contract_cols(packed_grad, pk_weight), stream_three))
    pk_bias_grad = column_sums(packed_grad)
    table_pad = ((0, gain_table.shape[0] - 2), (0, 0))
    gains_from_self = jnp.pad(self_sums[0::2], table_pad)
    shifts_from_self = jnp.pad(self_sums[1::2], table_pad)[: shift_table.shape[0]]
    entry_grad = after(entry_grad, pk_weight_grad)
    shift_part = jnp.sum(entry_grad, 0)
    stream_part, one_gain_grad, one_shift_grad = one_pull(entry_grad)
    stream_grad = stream_grad + stream_part

    grad_low = stream_grad.astype(low)
    sk_bias_grad = column_sums(grad_low)
    shift_rows = jnp.broadcast_to(
        shift_part.astype(low).reshape(1, ways, width), (ways, ways, width)
    )
    cols_in = jnp.concatenate([column_blocks(after(grad_low, text_sum)), shift_rows], 1)
    cols_out = swap(cols_in, "seq")
    grad_cols = cols_out[:, :tokens].reshape(all_tokens, width)
    shift_total = jnp.sum(cols_out[:, tokens:].astype(jnp.float32), 0).reshape(-1)
    joined_grad, sk_gain_grad, sk_shift_grad = skip_pull(skip_back(grad_low, first_rows))

    def placed(own, groups):
        parts = jnp.zeros((groups, ways, own.shape[0] // groups), jnp.float32)
        parts = lax.dynamic_update_slice_in_dim(parts, own.reshape(groups, 1, -1), place, 1)
        return parts.reshape(-1)

    vector_grads = (
        sk_gain_grad,
        sk_shift_grad,
        sk_bias_grad,
        one_gain_grad,
        one_shift_grad,
        placed(pk_bias_grad, 3),
        at_bias_grad,
        three_gain_grad,
        three_shift_grad,
        cq_bias_grad,
        placed(kv_bias_grad, 2),
        cr_bias_grad,
        two_gain_grad,
        two_shift_grad,
        placed(up_bias_grad, owners),
        down_bias_grad,
    )
    table_grads = jnp.concatenate(
        [
            (gains_from_cross + gains_from_text + gains_from_self).reshape(-1),
            (shifts_from_cross + shifts_from_self).reshape(-1),
        ]
    )
    split_three = [part.reshape(owners, -1) for part in vector_grads]
    pk_at = 5
    pk_thirds = placed(pk_bias_grad, 3).reshape(3, model_width)
    split_three[pk_at : pk_at + 1] = [
        pk_thirds[:2].reshape(owners, -1),
        pk_thirds[2].reshape(owners, -1),
    ]
    split_three.append(jnp.broadcast_to(table_grads[None], (owners, table_grads.shape[0])))
    summed_sizes = [part.shape[1] for part in split_three]
    vector_rows = jnp.concatenate(split_three, 1).astype(low)
    vector_pad = -vector_rows.shape[1] % own_rows
    vector_rows = jnp.pad(vector_rows, ((0, 0), (0, vector_pad)))
    latent_mark = jnp.arange(owners) == lax.axis_index("fsdp")
    shift_mine = jnp.where(latent_mark[:, None], shift_total.astype(low), jnp.zeros((), low))
    shift_mine = jnp.broadcast_to(
        shift_mine.reshape(1, own_rows, -1), (owners, own_rows, owners * owners)
    )
    tail_sum = sum_owners(
        pack_tail(
            normed_all,
            grad_cols,
            pk_weight_grad,
            fit_rows(kv_weight_grad.astype(low).reshape(owners, -1, 2 * width), own_rows),
            jnp.concatenate([vector_rows.reshape(owners, own_rows, -1), shift_mine], 2),
        )
    ).astype(low)
    shift_all = tail_sum[:, -owners * owners :].reshape(owners, model_width)
    shift_all = shift_all.astype(jnp.float32)
    tail_sum = tail_sum[:, : -owners * owners]

    row_sum = jnp.sum(swap(column_blocks(row_owned), "seq").astype(jnp.float32), 0)
    mlp_all_grads = lax.all_gather(after(mlp_owned, row_owned), "seq", axis=0, tiled=False)
    lead = 7 * width
    tail_all = spread(
        jnp.concatenate([tail_sum[:, :lead], row_sum.astype(low), tail_sum[:, lead:]], 1), "seq"
    )
    text_total = gather_behind(after(text_sum.astype(low), tail_all))[:text_count]
    sk_total, pk_total, kv_total, row_total, small_total = lay_tail(
        tail_all, cross_kv_weight.shape[0]
    )
    at_total = row_total[:, :model_width]
    cq_total = row_total[:, model_width : 2 * model_width]
    cr_total = row_total[:, 2 * model_width :]
    small_total = small_total.reshape(-1)
    vector_totals = []
    start = 0
    for size in summed_sizes:
        vector_totals.append(small_total[start : start + size])
        start += size
    table_total = vector_totals.pop()
    gains_total = table_total[: gain_table.size].reshape(gain_table.shape)
    shifts_total = table_total[gain_table.size :].reshape(shift_table.shape)
    md_weight_grad = lax.dot_general(
        lifted_own.astype(jnp.float32),
        shift_all,
        (((0,), (0,)), ((), ())),
        precision=lax.Precision.HIGHEST,
        preferred_element_type=jnp.float32,
    )
    md_bias_grad = lax.dynamic_slice_in_dim(
        jnp.sum(shift_all, 0), lax.axis_index("fsdp") * own_rows, own_rows, 0
    )
    lifted_part = lax.dot_general(
        shift_all,
        mod_weight.astype(jnp.float32),
        (((1,), (1,)), ((), ())),
        precision=lax.Precision.HIGHEST,
        preferred_element_type=jnp.float32,
    )
    lifted_grad = swap(after(lifted_part, tail_all, mlp_all_grads), "fsdp").reshape(1, model_width)
    condition_grad = silu_pull(lifted_grad)[0]

    up_total, down_total = lay_units(mlp_all_grads, own_rows, model_width)
    (
        sk_gain_total,
        sk_shift_total,
        sk_bias_total,
        one_gain_total,
        one_shift_total,
        pk_bias_total,
        value_bias_total,
        at_bias_total,
        three_gain_total,
        three_shift_total,
        cq_bias_total,
        kv_bias_total,
        cr_bias_total,
        two_gain_total,
        two_shift_total,
        up_bias_total,
        down_bias_total,
    ) = vector_totals
    return (
        layer_out,
        joined_grad[:, :model_width].astype(low)[None],
        joined_grad[:, model_width:].astype(low)[None],
        text_total[None],
        condition_grad,
        sk_gain_total,
        sk_shift_total,
        sk_total,
        sk_bias_total,
        md_weight_grad,
        md_bias_grad,
        one_gain_total,
        one_shift_total,
        pk_total,
        pk_bias_total,
        value_bias_total,
        gains_total,
        shifts_total,
        at_total,
        at_bias_total,
        three_gain_total,
        three_shift_total,
        cq_total,
        cq_bias_total,
        kv_total,
        kv_bias_total,
        cr_total,
        cr_bias_total,
        two_gain_total,
        two_shift_total,
        up_total,
        up_bias_total,
        down_total,
        down_bias_total,
    )


def solution(mesh):
    in_specs = (
        P("fsdp", "seq", None),
        P("fsdp", "seq", None),
        P("fsdp", None, None),
        P("fsdp", None),
        P("seq", None),
        P("fsdp", "seq", None),
        P("fsdp"),
        P("fsdp"),
        P("fsdp", None),
        P("fsdp"),
        P("fsdp", None),
        P("fsdp"),
        P("fsdp"),
        P("fsdp"),
        P("fsdp", None),
        P("fsdp"),
        P(),
        P(),
        P("fsdp", None),
        P("fsdp"),
        P("fsdp"),
        P("fsdp"),
        P("fsdp", None),
        P("fsdp"),
        P("fsdp", None),
        P("fsdp"),
        P("fsdp", None),
        P("fsdp"),
        P("fsdp"),
        P("fsdp"),
        P("fsdp", None),
        P("fsdp"),
        P("fsdp", None),
        P("fsdp"),
    )
    out_specs = (
        P("fsdp", "seq", None),
        P("fsdp", "seq", None),
        P("fsdp", "seq", None),
        P("fsdp", None, None),
        P("fsdp", None),
        P("fsdp"),
        P("fsdp"),
        P("fsdp", None),
        P("fsdp"),
        P("fsdp", None),
        P("fsdp"),
        P("fsdp"),
        P("fsdp"),
        P("fsdp", None),
        P("fsdp"),
        P("fsdp"),
        P(),
        P(),
        P("fsdp", None),
        P("fsdp"),
        P("fsdp"),
        P("fsdp"),
        P("fsdp", None),
        P("fsdp"),
        P("fsdp", None),
        P("fsdp"),
        P("fsdp", None),
        P("fsdp"),
        P("fsdp"),
        P("fsdp"),
        P("fsdp", None),
        P("fsdp"),
        P("fsdp", None),
        P("fsdp"),
    )
    return jax.shard_map(local, mesh=mesh, in_specs=in_specs, out_specs=out_specs, check_vma=False)
```

```python
import functools
import math

import jax
import jax.numpy as jnp
from jax import lax
from jax.experimental import pallas as pl
from jax.experimental.pallas import tpu as pltpu
from jax.sharding import PartitionSpec as P


def layer_norm(inputs, gain_vector, shift_vector):
    centred = inputs - jnp.mean(inputs, -1, keepdims=True)
    variance = jnp.mean(centred * centred, -1, keepdims=True)
    return centred * lax.rsqrt(variance + 1e-06) * gain_vector + shift_vector


def rotary_tables(positions, head_dim):
    quarter = head_dim // 4
    exponent = jnp.arange(quarter, dtype=jnp.float32) * (2.0 / (head_dim // 2))
    inverse = jnp.power(jnp.float32(10000.0), -exponent)
    places = positions.astype(jnp.float32)
    angle_rows = places[:, 0:1] * inverse
    angle_cols = places[:, 1:2] * inverse
    return (jnp.cos(angle_rows), jnp.sin(angle_rows), jnp.cos(angle_cols), jnp.sin(angle_cols))


def rotate(inputs, tables):
    cos_rows, sin_rows, cos_cols, sin_cols = tuple((one_table[:, None, :] for one_table in tables))
    quarter = inputs.shape[-1] // 4
    first_a = inputs[..., :quarter]
    first_b = inputs[..., quarter : 2 * quarter]
    second_a = inputs[..., 2 * quarter : 3 * quarter]
    second_b = inputs[..., 3 * quarter :]
    return jnp.concatenate(
        [
            first_a * cos_rows - first_b * sin_rows,
            first_a * sin_rows + first_b * cos_rows,
            second_a * cos_cols - second_b * sin_cols,
            second_a * sin_cols + second_b * cos_cols,
        ],
        -1,
    )


def head_norm(inputs, gain_vector, shift_vector, head_dim):
    row_count = inputs.shape[0]
    shaped = inputs.reshape(row_count, -1, head_dim)
    return layer_norm(shaped, gain_vector, shift_vector).reshape(row_count, -1)


def head_rotary(inputs, gain_vector, shift_vector, tables, head_dim):
    row_count = inputs.shape[0]
    shaped = inputs.reshape(row_count, -1, head_dim)
    return rotate(layer_norm(shaped, gain_vector, shift_vector), tables).reshape(row_count, -1)


def matmul(left_side, right_side):
    return jnp.dot(left_side, right_side, preferred_element_type=jnp.float32)


def contract_rows(left_side, right_side):
    return lax.dot_general(
        left_side, right_side, (((0,), (0,)), ((), ())), preferred_element_type=jnp.float32
    )


def contract_cols(left_side, right_side):
    return lax.dot_general(
        left_side, right_side, (((1,), (1,)), ((), ())), preferred_element_type=jnp.float32
    )


def column_sums(grads_low):
    return jnp.sum(grads_low.astype(jnp.float32), 0)


def to_float(vectors):
    return tuple((one_vector.astype(jnp.float32) for one_vector in vectors))


def turn_tables(places, head_dim):
    cos_rows, sin_rows, cos_cols, sin_cols = rotary_tables(places, head_dim)
    return (
        jnp.concatenate([cos_rows, cos_rows, cos_cols, cos_cols], 1),
        jnp.concatenate([-sin_rows, sin_rows, -sin_cols, sin_cols], 1),
    )


def normalised(values):
    centred = values - jnp.mean(values, -1, keepdims=True)
    scale = lax.rsqrt(jnp.mean(centred * centred, -1, keepdims=True) + 1e-06)
    return centred * scale, scale


def partners(values):
    quarter = values.shape[1] // 4
    return jnp.concatenate(
        [
            values[:, quarter : 2 * quarter],
            values[:, :quarter],
            values[:, 3 * quarter :],
            values[:, 2 * quarter : 3 * quarter],
        ],
        1,
    )


def norm_turn(values, gain, shift, cos_now, sin_now):
    turned = normalised(values)[0] * gain + shift
    return turned * cos_now + partners(turned) * sin_now


def norm_turn_back(grad, values, gain, cos_now, sin_now):
    grad = grad.astype(jnp.bfloat16).astype(jnp.float32)
    grad = grad * cos_now - partners(grad) * sin_now
    normal, scale = normalised(values)
    scaled = grad * gain
    mean_one = jnp.mean(scaled, -1, keepdims=True)
    mean_two = jnp.mean(scaled * normal, -1, keepdims=True)
    return (
        scale * (scaled - mean_one - normal * mean_two),
        jnp.sum(grad * normal, 0, keepdims=True),
        jnp.sum(grad, 0, keepdims=True),
    )


def self_forward_kernel(
    entry_ref,
    weight_ref,
    bias_ref,
    gains_ref,
    shifts_ref,
    cos_ref,
    sin_ref,
    mixed_ref,
    heads_ref,
    pre_ref,
    totals_ref,
    *,
    scale,
):
    low = jnp.bfloat16
    count, all_tokens, head_dim = heads_ref.shape[1:]
    packed = matmul(entry_ref[...], weight_ref[...]) + bias_ref[...]
    pre_ref[...] = packed[:, : 2 * count * head_dim]
    cos_now, sin_now = cos_ref[...], sin_ref[...]
    for head in range(count):
        for kind in range(3):
            start = (kind * count + head) * head_dim
            part = packed[:, start : start + head_dim]
            if kind < 2:
                part = norm_turn(
                    part,
                    gains_ref[kind : kind + 1],
                    shifts_ref[kind : kind + 1],
                    cos_now,
                    sin_now,
                )
            heads_ref[kind, head] = part.astype(low)
    step = min(512, all_tokens)
    for start in range(0, all_tokens, step):
        mixed = []
        for head in range(count):
            query_block = heads_ref[0, head, start : start + step]
            scores = contract_cols(query_block, heads_ref[1, head]) * scale
            row_top = jnp.max(scores, -1, keepdims=True)
            weights = jnp.exp(scores - row_top)
            totals = jnp.sum(weights, -1, keepdims=True)
            probs = (weights * (1.0 / totals)).astype(low)
            mixed.append(matmul(probs, heads_ref[2, head]))
            totals_ref[head, start : start + step] = row_top + jnp.log(totals)
        mixed_ref[start : start + step] = jnp.concatenate(mixed, 1).astype(low)


def self_forward(entry_all, weight, bias, gains, shifts, cos_now, sin_now):
    all_tokens, head_dim = cos_now.shape
    count = weight.shape[1] // (3 * head_dim)
    return pl.pallas_call(
        functools.partial(self_forward_kernel, scale=1.0 / math.sqrt(head_dim)),
        out_shape=[
            jax.ShapeDtypeStruct((all_tokens, count * head_dim), jnp.bfloat16),
            jax.ShapeDtypeStruct((3, count, all_tokens, head_dim), jnp.bfloat16),
            jax.ShapeDtypeStruct((all_tokens, 2 * count * head_dim), jnp.float32),
            jax.ShapeDtypeStruct((count, all_tokens, 1), jnp.float32),
        ],
        compiler_params=pltpu.CompilerParams(vmem_limit_bytes=50 * 1024 * 1024),
        cost_estimate=pl.CostEstimate(
            flops=2 * all_tokens * weight.size + 4 * count * all_tokens**2 * head_dim,
            bytes_accessed=2 * entry_all.size + 2 * weight.size + 16 * all_tokens * weight.shape[1],
            transcendentals=count * all_tokens**2,
        ),
        name="self_forward",
    )(entry_all, weight, bias, gains, shifts, cos_now, sin_now)


def self_backward_kernel(
    heads_ref, totals_ref, grad_ref, pre_ref, gains_ref, cos_ref, sin_ref, out_ref, sums_ref, *, scale
):
    low = jnp.bfloat16
    count, all_tokens, head_dim = heads_ref.shape[1:]
    cos_now, sin_now = cos_ref[...], sin_ref[...]
    step = min(512, all_tokens)
    lanes = [None] * (3 * count)
    sums = None
    for head in range(count):
        keys_now = heads_ref[1, head]
        values_now = heads_ref[2, head]
        keys_grad, values_grad, query_grads = 0.0, 0.0, []
        for start in range(0, all_tokens, step):
            query_block = heads_ref[0, head, start : start + step]
            grad_block = grad_ref[start : start + step, head * head_dim : (head + 1) * head_dim]
            probs = jnp.exp(
                contract_cols(query_block, keys_now) * scale
                - totals_ref[head, start : start + step]
            )
            weighted = probs * contract_cols(grad_block, values_now)
            scores_grad = weighted - probs * jnp.sum(weighted, -1, keepdims=True)
            scores_low = (scores_grad * scale).astype(low)
            query_grads.append(matmul(scores_low, keys_now))
            keys_grad += contract_rows(scores_low, query_block)
            values_grad += contract_rows(probs.astype(low), grad_block)
        grads = (jnp.concatenate(query_grads, 0), keys_grad)
        parts = []
        for kind in range(2):
            start = (kind * count + head) * head_dim
            back, gain_sum, shift_sum = norm_turn_back(
                grads[kind],
                pre_ref[:, start : start + head_dim],
                gains_ref[kind : kind + 1],
                cos_now,
                sin_now,
            )
            lanes[kind * count + head] = back
            parts += [gain_sum, shift_sum]
        lanes[2 * count + head] = values_grad
        parts = jnp.concatenate(parts, 0)
        sums = parts if sums is None else sums + parts
    out_ref[...] = jnp.concatenate(lanes, 1).astype(low)
    sums_ref[...] = sums


def self_backward(heads, totals, grad_out, pre, gains, cos_now, sin_now):
    count, all_tokens, head_dim = heads.shape[1:]
    return pl.pallas_call(
        functools.partial(self_backward_kernel, scale=1.0 / math.sqrt(head_dim)),
        out_shape=[
            jax.ShapeDtypeStruct((all_tokens, 3 * count * head_dim), jnp.bfloat16),
            jax.ShapeDtypeStruct((4, head_dim), jnp.float32),
        ],
        compiler_params=pltpu.CompilerParams(vmem_limit_bytes=50 * 1024 * 1024),
        cost_estimate=pl.CostEstimate(
            flops=10 * count * all_tokens**2 * head_dim,
            bytes_accessed=24 * count * all_tokens * head_dim,
            transcendentals=count * all_tokens**2,
        ),
        name="self_backward",
    )(heads, totals, grad_out, pre, gains, cos_now, sin_now)


def cross_forward_kernel(
    pre_ref, text_ref, gain_ref, shift_ref, cos_ref, sin_ref, mixed_ref, query_ref, totals_ref, *, scale, valid
):
    low = jnp.bfloat16
    head_dim = cos_ref.shape[1]
    heads = pre_ref.shape[1] // head_dim
    count = heads // text_ref.shape[0]
    width = count * head_dim
    cos_now, sin_now = cos_ref[...], sin_ref[...]
    mixed, queries = [], []
    for head in range(heads):
        lanes = slice(head * head_dim, (head + 1) * head_dim)
        query = norm_turn(pre_ref[:, lanes], gain_ref[...], shift_ref[...], cos_now, sin_now)
        query = query.astype(low)
        queries.append(query)
        start = (head % count) * head_dim
        text = text_ref[head // count]
        scores = contract_cols(query, text[:, start : start + head_dim]) * scale
        column = lax.broadcasted_iota(jnp.int32, scores.shape, 1)
        scores = jnp.where(column < valid, scores, -1e30)
        row_top = jnp.max(scores, -1, keepdims=True)
        weights = jnp.exp(scores - row_top)
        totals = jnp.sum(weights, -1, keepdims=True)
        probs = (weights * (1.0 / totals)).astype(low)
        mixed.append(matmul(probs, text[:, width + start : width + start + head_dim]))
        totals_ref[head] = row_top + jnp.log(totals)
    mixed_ref[...] = jnp.concatenate(mixed, 1).astype(low)
    query_ref[...] = jnp.concatenate(queries, 1)


def cross_forward(pre, text, gain, shift, cos_now, sin_now, valid):
    tokens, model_width = pre.shape
    head_dim = cos_now.shape[1]
    heads = model_width // head_dim
    return pl.pallas_call(
        functools.partial(cross_forward_kernel, scale=1.0 / math.sqrt(head_dim), valid=valid),
        out_shape=[
            jax.ShapeDtypeStruct((tokens, model_width), jnp.bfloat16),
            jax.ShapeDtypeStruct((tokens, model_width), jnp.bfloat16),
            jax.ShapeDtypeStruct((heads, tokens, 1), jnp.float32),
        ],
        compiler_params=pltpu.CompilerParams(vmem_limit_bytes=40 * 1024 * 1024),
        cost_estimate=pl.CostEstimate(
            flops=4 * tokens * text.shape[1] * model_width,
            bytes_accessed=2 * text.size + 8 * pre.size,
            transcendentals=heads * tokens * text.shape[1],
        ),
        name="cross_forward",
    )(pre, text, gain, shift, cos_now, sin_now)


def cross_backward_kernel(
    query_ref,
    text_ref,
    totals_ref,
    grad_ref,
    pre_ref,
    gain_ref,
    cos_ref,
    sin_ref,
    pre_grad_ref,
    text_grad_ref,
    sums_ref,
    *,
    scale,
    valid,
):
    low = jnp.bfloat16
    head_dim = cos_ref.shape[1]
    ways = text_ref.shape[0]
    count = query_ref.shape[1] // head_dim // ways
    width = count * head_dim
    cos_now, sin_now = cos_ref[...], sin_ref[...]
    backs, sums = [], 0.0
    for way in range(ways):
        text = text_ref[way]
        text_grads = [None] * (2 * count)
        for one in range(count):
            head = way * count + one
            lanes = slice(head * head_dim, (head + 1) * head_dim)
            query = query_ref[:, lanes]
            grad = grad_ref[:, lanes]
            keys_now = text[:, one * head_dim : (one + 1) * head_dim]
            values_now = text[:, width + one * head_dim : width + (one + 1) * head_dim]
            probs = jnp.exp(contract_cols(query, keys_now) * scale - totals_ref[head])
            column = lax.broadcasted_iota(jnp.int32, probs.shape, 1)
            probs = jnp.where(column < valid, probs, 0.0)
            weighted = probs * contract_cols(grad, values_now)
            scores_grad = weighted - probs * jnp.sum(weighted, -1, keepdims=True)
            scores_low = (scores_grad * scale).astype(low)
            back, gain_sum, shift_sum = norm_turn_back(
                matmul(scores_low, keys_now), pre_ref[:, lanes], gain_ref[...], cos_now, sin_now
            )
            backs.append(back)
            sums += jnp.concatenate([gain_sum, shift_sum], 0)
            text_grads[one] = contract_rows(scores_low, query)
            text_grads[count + one] = contract_rows(probs.astype(low), grad)
        text_grad_ref[way] = jnp.concatenate(text_grads, 1).astype(low)
    pre_grad_ref[...] = jnp.concatenate(backs, 1).astype(low)
    sums_ref[...] = sums


def cross_backward(query, text, totals, grad, pre, gain, cos_now, sin_now, valid):
    tokens, model_width = pre.shape
    head_dim = cos_now.shape[1]
    ways, text_rows = text.shape[:2]
    return pl.pallas_call(
        functools.partial(cross_backward_kernel, scale=1.0 / math.sqrt(head_dim), valid=valid),
        out_shape=[
            jax.ShapeDtypeStruct((tokens, model_width), jnp.bfloat16),
            jax.ShapeDtypeStruct((ways, text_rows, 2 * model_width // ways), jnp.bfloat16),
            jax.ShapeDtypeStruct((2, head_dim), jnp.float32),
        ],
        compiler_params=pltpu.CompilerParams(vmem_limit_bytes=40 * 1024 * 1024),
        cost_estimate=pl.CostEstimate(
            flops=10 * tokens * text_rows * model_width,
            bytes_accessed=4 * text.size + 10 * pre.size,
            transcendentals=tokens * text_rows * model_width // head_dim,
        ),
        name="cross_backward",
    )(query, text, totals, grad, pre, gain, cos_now, sin_now)


def row_grads_kernel(left_ref, far_left_ref, right_ref, far_right_ref, out_ref):
    product = contract_rows(left_ref[0], right_ref[0])
    product += contract_rows(far_left_ref[0], far_right_ref[0])
    rows = out_ref.shape[1]
    for chip in range(out_ref.shape[0]):
        out_ref[chip] = product[chip * rows : (chip + 1) * rows].astype(out_ref.dtype)


def row_grads(lefts, rights, owners):
    count, tokens, width = lefts.shape
    rows = width // owners
    core = lax.axis_index("fsdp") % 2
    by_core = lefts.reshape(count, tokens, owners // 2, 2, rows).transpose(3, 0, 1, 2, 4)
    by_core = by_core.reshape(2, count, tokens, width // 2)
    near = lax.dynamic_index_in_dim(by_core, core, 0, False)
    far = swap_cores(lax.dynamic_index_in_dim(by_core, 1 - core, 0, False))
    left_spec = pl.BlockSpec((1, tokens, width // 2), lambda i: (i, 0, 0))
    right_spec = pl.BlockSpec((1, tokens, width), lambda i: (i, 0, 0))
    return pl.pallas_call(
        row_grads_kernel,
        grid=(count,),
        in_specs=[left_spec, left_spec, right_spec, right_spec],
        out_specs=pl.BlockSpec((owners // 2, rows, width), lambda i: (0, 0, i)),
        out_shape=jax.ShapeDtypeStruct((owners // 2, rows, count * width), jnp.bfloat16),
        compiler_params=pltpu.CompilerParams(vmem_limit_bytes=48 * 1024 * 1024),
        cost_estimate=pl.CostEstimate(
            flops=2 * count * tokens * width * width,
            bytes_accessed=2 * count * (width * width // 2 + 3 * tokens * width),
            transcendentals=0,
        ),
        name="row_grads",
    )(near, far, rights, swap_cores(rights))


def side_by_side(pieces):
    return jnp.concatenate([piece.astype(jnp.float32) for piece in pieces], 1)


def pack_kernel(normed_ref, grads_ref, packed_ref, text_ref, small_ref, out_ref):
    owners, rows = text_ref.shape[:2]
    product = contract_rows(normed_ref[...], grads_ref[...])
    count = product.shape[0] // owners
    folds = rows // count
    lanes = product.shape[1] // folds
    for owner in range(owners):
        skip = product[owner * count : (owner + 1) * count]
        skip = jnp.concatenate(
            [skip[:, fold * lanes : (fold + 1) * lanes] for fold in range(folds)], 0
        )
        line = side_by_side(
            [
                skip,
                packed_ref[owner * rows : (owner + 1) * rows],
                text_ref[owner],
                small_ref[owner],
            ]
        )
        out_ref[owner % 2, owner // 2] = line.astype(out_ref.dtype)


def pack_tail(normed, grads, packed, text, small):
    owners, rows = text.shape[:2]
    lanes = 2 * text.shape[2] // 2 + packed.shape[1] + text.shape[2] + small.shape[2]
    return pl.pallas_call(
        pack_kernel,
        out_shape=jax.ShapeDtypeStruct((2, owners // 2, rows, lanes), jnp.bfloat16),
        compiler_params=pltpu.CompilerParams(vmem_limit_bytes=48 * 1024 * 1024),
        cost_estimate=pl.CostEstimate(
            flops=2 * normed.size * grads.shape[1],
            bytes_accessed=2 * normed.size + 4 * owners * rows * lanes,
            transcendentals=0,
        ),
        name="pack_tail",
    )(normed, grads, packed, text, small)


def tail_kernel(all_ref, skip_ref, packed_ref, text_ref, whole_ref, small_ref):
    ways, rows = all_ref.shape[:2]
    model_width = skip_ref.shape[1]
    width = model_width // ways

    def joined(start, count, size):
        return side_by_side(
            [all_ref[way, :, start : start + size][:count] for way in range(ways)]
        )

    count = 2 * rows // ways
    folds = rows // count
    skip = []
    for way in range(ways):
        block = all_ref[way, :, : 2 * width].astype(jnp.float32)
        skip.append(
            jnp.concatenate(
                [block[fold * count : (fold + 1) * count] for fold in range(folds)], 1
            )
        )
    skip_ref[...] = jnp.concatenate(skip, 0)
    for third in range(3):
        packed_ref[:, third * model_width : (third + 1) * model_width] = joined(
            (2 + third) * width, rows, width
        )
    for side in range(2):
        text_ref[:, side * model_width : (side + 1) * model_width] = joined(
            (5 + side) * width, text_ref.shape[0], width
        )
    whole_ref[...] = joined(7 * width, rows, 3 * width)
    total = all_ref[0, :, 10 * width :].astype(jnp.float32)
    for way in range(1, ways):
        total += all_ref[way, :, 10 * width :].astype(jnp.float32)
    small_ref[...] = total


def lay_tail(blocks, text_rows):
    ways, rows, lanes = blocks.shape
    width = 2 * rows
    model_width = ways * width
    return pl.pallas_call(
        tail_kernel,
        out_shape=[
            jax.ShapeDtypeStruct((2 * rows, model_width), jnp.float32),
            jax.ShapeDtypeStruct((rows, 3 * model_width), jnp.float32),
            jax.ShapeDtypeStruct((text_rows, 2 * model_width), jnp.float32),
            jax.ShapeDtypeStruct((rows, 3 * model_width), jnp.float32),
            jax.ShapeDtypeStruct((rows, lanes - 10 * width), jnp.float32),
        ],
        compiler_params=pltpu.CompilerParams(vmem_limit_bytes=40 * 1024 * 1024),
        name="lay_tail",
    )(blocks)


def skip_back_kernel(grad_ref, first_ref, second_ref, out_ref):
    grad = grad_ref[...]
    halves = [contract_cols(grad, half_ref[...]) for half_ref in (first_ref, second_ref)]
    rows = grad.shape[1] // 16
    out_ref[...] = side_by_side(
        [half[:, i * rows : (i + 1) * rows] for i in range(16) for half in halves]
    )


def skip_back(grad_low, first_rows):
    tokens, model_width = grad_low.shape
    return pl.pallas_call(
        skip_back_kernel,
        grid=(1,),
        in_specs=[
            pl.BlockSpec((tokens, model_width), lambda i: (0, 0)),
            pl.BlockSpec((model_width, model_width), lambda i: (0, 0)),
            pl.BlockSpec((model_width, model_width), lambda i: (0, 1)),
        ],
        out_specs=pl.BlockSpec((tokens, 2 * model_width), lambda i: (0, 0)),
        out_shape=jax.ShapeDtypeStruct((tokens, 2 * model_width), jnp.float32),
        compiler_params=pltpu.CompilerParams(vmem_limit_bytes=48 * 1024 * 1024),
        cost_estimate=pl.CostEstimate(
            flops=4 * tokens * model_width * model_width,
            bytes_accessed=4 * model_width * (model_width + 2 * tokens),
            transcendentals=0,
        ),
        name="skip_back",
    )(grad_low, first_rows, first_rows)


def units_kernel(all_ref, up_ref, down_ref):
    ways = all_ref.shape[0]
    rows, hidden = up_ref.shape
    units = hidden // ways
    owners = 16
    own = units // owners
    for owner in range(owners):
        start = owner * ways * own
        up_ref[:, start : start + ways * own] = side_by_side(
            [all_ref[way, :rows, owner * own : (owner + 1) * own] for way in range(ways)]
        )
    model_width = down_ref.shape[1]
    split = min(units, model_width)
    for way in range(ways):
        place = slice(way * own, (way + 1) * own)
        down_ref[place, :split] = all_ref[way, :own, units : units + split].astype(jnp.float32)
        if split < model_width:
            down_ref[place, split:] = all_ref[
                way, own : 2 * own, units : units + model_width - split
            ].astype(jnp.float32)


def lay_units(blocks, rows, model_width):
    ways, lines, lanes = blocks.shape
    units = lanes // 2
    return pl.pallas_call(
        units_kernel,
        out_shape=[
            jax.ShapeDtypeStruct((rows, ways * units), jnp.float32),
            jax.ShapeDtypeStruct((ways * units // 16, model_width), jnp.float32),
        ],
        compiler_params=pltpu.CompilerParams(vmem_limit_bytes=40 * 1024 * 1024),
        name="lay_units",
    )(blocks)


def fold_down(part, units, lines):
    first = part[..., :units]
    rest = part[..., units:]
    pad = [(0, 0)] * (part.ndim - 1) + [(0, units - rest.shape[-1])]
    both = jnp.concatenate([first, jnp.pad(rest, pad)], -2)
    return fit_rows(both, lines)


def fit_rows(part, lines):
    pad = [(0, 0)] * part.ndim
    pad[-2] = (0, lines - part.shape[-2])
    return jnp.pad(part, pad)


def swap(blocks, axis_name):
    return lax.all_to_all(blocks, axis_name, split_axis=0, concat_axis=0, tiled=True)


def spread(part, axis_name):
    size = lax.axis_size(axis_name)
    return swap(jnp.broadcast_to(part[None], (size,) + part.shape), axis_name)


def grid_place():
    index = lax.axis_index("seq")
    return index // 4, index % 4


def grid_send(value, pair, step):
    links = [(i, ((i // 4) ^ pair) * 4 + (i + step) % 4) for i in range(8)]
    return lax.ppermute(value, "seq", links)


def gather_tokens(part):
    pair, ring = grid_place()
    mate = grid_send(part, 1, 0)
    below = grid_send(part, 0, 1)
    above = grid_send(part, 0, -1)
    far = grid_send(part, 0, 2)
    mate_below = grid_send(mate, 0, 1)
    mate_above = grid_send(mate, 0, -1)
    mate_far = grid_send(far, 1, 0)
    here, there = pair * 4, (1 - pair) * 4
    buffer = jnp.zeros((8,) + part.shape, part.dtype)
    for one, spot in (
        (part, here + ring),
        (mate, there + ring),
        (below, here + (ring + 3) % 4),
        (above, here + (ring + 1) % 4),
        (far, here + (ring + 2) % 4),
        (mate_below, there + (ring + 3) % 4),
        (mate_above, there + (ring + 1) % 4),
        (mate_far, there + (ring + 2) % 4),
    ):
        buffer = lax.dynamic_update_index_in_dim(buffer, one, spot, 0)
    return buffer.reshape((-1,) + part.shape[1:])


def gather_behind(part):
    return spread(part, "seq").reshape((-1,) + part.shape[1:])


def sum_tokens(partial):
    low = jnp.bfloat16
    blocks = partial.astype(low).reshape((8, -1) + partial.shape[1:])
    pair, ring = grid_place()

    def meant(mate, step):
        spot = jnp.where(mate, 1 - pair, pair) * 4 + (ring + step) % 4
        return lax.dynamic_index_in_dim(blocks, spot, 0, False)

    def total(*parts):
        return sum(part.astype(jnp.float32) for part in parts)

    far_mate = grid_send(meant(True, 2), 1, 0)
    mate_below = grid_send(meant(True, 1), 0, 1)
    mate_above = grid_send(meant(True, 3), 0, -1)
    below = grid_send(meant(False, 1), 0, 1)
    above = grid_send(meant(False, 3), 0, -1)
    far = grid_send(total(meant(False, 2), far_mate).astype(low), 0, 2)
    mate = grid_send(total(meant(True, 0), mate_below, mate_above).astype(low), 1, 0)
    return total(meant(False, 0), below, above, far, mate)


def sum_behind(partial):
    blocks = partial.astype(jnp.bfloat16).reshape((8, -1) + partial.shape[1:])
    return jnp.sum(swap(blocks, "seq").astype(jnp.float32), 0)


def column_blocks(values):
    size = lax.axis_size("seq")
    rows = values.shape[0]
    return values.reshape(rows, size, -1).transpose(1, 0, 2)


def own_columns(weight, groups, size, place):
    rows = weight.shape[0]
    parts = weight.reshape(rows, groups, size, -1)
    taken = lax.dynamic_slice_in_dim(parts, place, 1, 2)
    return taken.reshape(rows, -1)


def after(values, *others):
    waits = [other[(0,) * other.ndim].astype(jnp.float32) * 0.0 for other in others]
    return values + sum(waits).astype(values.dtype)


def core_groups(owners):
    return [list(range(0, owners, 2)), list(range(1, owners, 2))]


def swap_cores(value):
    return lax.ppermute(value, "fsdp", [(i, i ^ 1) for i in range(lax.axis_size("fsdp"))])


def sum_cores(by_core):
    core = lax.axis_index("fsdp") % 2
    kept = lax.dynamic_index_in_dim(by_core, core, 0, False)
    arrived = swap_cores(lax.dynamic_index_in_dim(by_core, 1 - core, 0, False))
    return (kept.astype(jnp.float32) + arrived.astype(jnp.float32)).astype(jnp.bfloat16)


def scatter_chips(by_chip):
    return lax.psum_scatter(
        by_chip,
        "fsdp",
        scatter_dimension=0,
        axis_index_groups=core_groups(2 * by_chip.shape[0]),
        tiled=False,
    )


def sum_owners(by_core):
    chip = sum_cores(by_core)
    swapped = lax.all_to_all(
        chip,
        "fsdp",
        split_axis=0,
        concat_axis=0,
        axis_index_groups=core_groups(2 * chip.shape[0]),
        tiled=True,
    )
    return jnp.sum(swapped.astype(jnp.float32), 0)


def heads_first(values, head_dim):
    rows = values.shape[0]
    return values.reshape(rows, -1, head_dim).transpose(1, 0, 2)


def heads_last(values):
    return values.transpose(1, 0, 2).reshape(values.shape[1], -1)


def local(
    latent,
    skip_input,
    text_tokens,
    condition,
    positions,
    cotangent,
    skip_gain,
    skip_shift,
    skip_weight,
    skip_bias,
    mod_weight,
    mod_bias,
    norm1_gain,
    norm1_shift,
    qkv_weight,
    qkv_bias,
    head_gains,
    head_shifts,
    attn_weight,
    attn_bias,
    norm3_gain,
    norm3_shift,
    cross_q_weight,
    cross_q_bias,
    cross_kv_weight,
    cross_kv_bias,
    cross_weight,
    cross_bias,
    norm2_gain,
    norm2_shift,
    fc1_weight,
    fc1_bias,
    fc2_weight,
    fc2_bias,
):
    ways = lax.axis_size("seq")
    owners = lax.axis_size("fsdp")
    place = lax.axis_index("seq")
    head_dim = head_gains.shape[1]
    tokens, model_width = latent.shape[1:]
    width = model_width // ways
    low = jnp.bfloat16
    gain_table = head_gains.astype(jnp.float32)
    shift_table = head_shifts.astype(jnp.float32)
    cos_own, sin_own = turn_tables(positions, head_dim)

    own_rows = model_width // owners
    packed_own = own_columns(qkv_weight, 3, ways, place)
    first_own = jnp.concatenate(
        [skip_weight[:own_rows], skip_weight[own_rows:], packed_own], 1
    )
    first_rows = lax.all_gather(first_own, "fsdp", axis=0, tiled=True)
    kv_own = own_columns(cross_kv_weight, 2, ways, place)
    second_own = jnp.concatenate([attn_weight, cross_q_weight, cross_weight], 1)
    unit_rows = fc2_weight.shape[0] // ways
    down_own = lax.dynamic_slice_in_dim(fc2_weight, place * unit_rows, unit_rows, 0)
    up_own = own_columns(fc1_weight, owners, ways, place)
    units = up_own.shape[1]
    lines = max(own_rows, 2 * unit_rows)
    third_own = jnp.concatenate(
        [fit_rows(up_own, lines), fold_down(down_own, units, lines)], 1
    )
    lifted_f, silu_pull = jax.vjp(jax.nn.silu, condition.astype(jnp.float32))
    lifted = lifted_f.astype(low)
    vectors = (
        skip_gain,
        skip_shift,
        skip_bias,
        mod_bias,
        norm1_gain,
        norm1_shift,
        qkv_bias,
        attn_bias,
        norm3_gain,
        norm3_shift,
        cross_q_bias,
        cross_kv_bias,
        cross_bias,
        norm2_gain,
        norm2_shift,
        fc1_bias,
        fc2_bias,
    )
    vector_own = jnp.concatenate(vectors)
    vector_all = swap(
        jnp.concatenate(
            [
                jnp.broadcast_to(vector_own[None], (owners, vector_own.shape[0])),
                lifted.reshape(owners, own_rows),
            ],
            1,
        ),
        "fsdp",
    )
    pieces = []
    start = 0
    for one_vector in vectors:
        size = one_vector.shape[0]
        pieces.append(vector_all[:, start : start + size].reshape(-1).astype(jnp.float32))
        start += size
    lifted_own = vector_all[:, start:]
    (
        sk_gain,
        sk_shift,
        sk_bias,
        md_bias,
        one_gain,
        one_shift,
        pk_bias,
        at_bias,
        three_gain,
        three_shift,
        cq_bias,
        kv_bias,
        cr_bias,
        two_gain,
        two_shift,
        up_bias,
        down_bias,
    ) = pieces
    pk_bias_own = own_columns(pk_bias[None], 3, ways, place)[0]
    kv_bias_own = own_columns(kv_bias[None], 2, ways, place)[0]
    up_bias_own = own_columns(up_bias[None], owners, ways, place)[0]
    shift_row = (
        jnp.sum(swap(matmul(lifted_own, mod_weight), "fsdp"), 0, keepdims=True) + md_bias
    )

    kv_weight = spread(after(kv_own, vector_all), "fsdp").reshape(-1, 2 * width)
    text_now = text_tokens[0]
    text_count = text_now.shape[0]
    text_packed = matmul(text_now, kv_weight) + kv_bias_own
    text_keys_f, tk_pull = jax.vjp(
        lambda values_in, gains_in: head_norm(values_in, gains_in[3], 0.0, head_dim),
        text_packed[:, :width],
        gain_table,
    )
    text_own = jnp.concatenate(
        [text_keys_f.astype(low), text_packed[:, width:].astype(low)], 1
    )
    text_rows = text_count + -text_count % 16
    place_rows = max(text_rows, tokens)
    text_own = jnp.concatenate(
        [
            fit_rows(text_own, place_rows),
            fit_rows(positions.astype(low), place_rows),
        ],
        1,
    )
    text_spread = spread(text_own, "seq")
    cos_all, sin_all = turn_tables(
        text_spread[:, :tokens, 2 * width :].reshape(-1, 2), head_dim
    )
    joined = jnp.concatenate([latent[0], skip_input[0]], 1).astype(jnp.float32)
    normed_f, skip_pull = jax.vjp(layer_norm, joined, sk_gain, sk_shift)
    normed = normed_f.astype(low)
    normed_halves = normed.reshape(tokens, owners, 2, own_rows).transpose(2, 0, 1, 3)
    normed_halves = normed_halves.reshape(2, tokens, model_width)
    normed_rows = normed.reshape(tokens, owners, ways, -1).transpose(2, 0, 1, 3)
    normed_rows = normed_rows.reshape(ways, tokens, -1)
    normed_halves = after(normed_halves, shift_row, text_spread)
    stream_zero = (
        matmul(normed_halves[0], first_rows[:, :model_width])
        + matmul(normed_halves[1], first_rows[:, model_width : 2 * model_width])
        + sk_bias
    )

    pk_weight = first_rows[:, 2 * model_width :]
    second_rows = lax.all_gather(after(second_own, stream_zero), "fsdp", axis=0, tiled=True)
    at_weight = second_rows[:, :model_width]
    cq_weight = second_rows[:, model_width : 2 * model_width]
    cr_weight = second_rows[:, 2 * model_width :]
    entry_f, one_pull = jax.vjp(layer_norm, stream_zero, one_gain, one_shift)
    entry = (entry_f + shift_row).astype(low)

    entry_all = gather_tokens(entry)

    mixed_h, heads_h, packed_pre, self_totals = self_forward(
        entry_all, pk_weight, pk_bias_own[None], gain_table, shift_table, cos_all, sin_all
    )
    all_tokens = entry_all.shape[0]
    normed_own = swap(after(normed_rows, entry), "seq").reshape(all_tokens, -1)
    grad_all = gather_behind(after(cotangent[0], normed_own))
    mixed_h = after(mixed_h, grad_all)

    def to_heads(values):
        return swap(column_blocks(values), "seq").reshape(all_tokens, -1)

    mixed = swap(mixed_h.reshape(ways, tokens, width), "seq")
    mixed = mixed.transpose(1, 0, 2).reshape(tokens, model_width)
    third_rows = lax.all_gather(after(third_own, entry_all), "fsdp", axis=0, tiled=False)
    up_weight = third_rows[:, :own_rows, :units].reshape(model_width, units)
    down_weight = jnp.concatenate(
        [
            third_rows[:, :unit_rows, units : units + min(units, model_width)],
            third_rows[:, unit_rows : 2 * unit_rows, units : units + max(model_width - units, 0)],
        ],
        2,
    ).reshape(units, model_width)
    stream_one = stream_zero + matmul(mixed, at_weight) + at_bias

    cross_in_f, three_pull = jax.vjp(layer_norm, stream_one, three_gain, three_shift)
    cross_in = cross_in_f.astype(low)
    cross_pre = matmul(cross_in, cq_weight) + cq_bias
    cross_mixed, cross_query, cross_totals = cross_forward(
        cross_pre, text_spread, gain_table[2:3], shift_table[2:3], cos_own, sin_own, text_count
    )
    stream_two = stream_one + matmul(cross_mixed, cr_weight) + cr_bias

    mlp_in_f, two_pull = jax.vjp(layer_norm, stream_two, two_gain, two_shift)
    mlp_all = gather_tokens(mlp_in_f.astype(low))
    hidden_pre = matmul(mlp_all, up_weight) + up_bias_own
    hidden_f, gelu_pull = jax.vjp(
        lambda values_in: jax.nn.gelu(values_in, approximate=True), hidden_pre
    )
    hidden = hidden_f.astype(low)
    out_partial = matmul(hidden, down_weight).astype(low)
    grad_three = cotangent[0].astype(jnp.float32)
    down_bias_grad = column_sums(cotangent[0])
    pre_grad = gelu_pull(contract_cols(grad_all, down_weight))[0].astype(low)
    up_bias_grad = column_sums(pre_grad)
    mlp_in_grad = sum_tokens(contract_cols(pre_grad, up_weight))
    down_grad = contract_rows(hidden, grad_all).astype(low)
    up_grad = contract_rows(mlp_all, pre_grad).astype(low)
    mlp_grads = jnp.concatenate(
        [
            fit_rows(up_grad.reshape(owners, own_rows, units), lines),
            fold_down(down_grad.reshape(owners, unit_rows, model_width), units, lines),
        ],
        2,
    )
    mlp_grads = mlp_grads.reshape(owners // 2, 2, lines, 2 * units).transpose(1, 0, 2, 3)
    mlp_owned = scatter_chips(sum_cores(mlp_grads))
    mlp_all_grads = lax.all_gather(mlp_owned, "seq", axis=0, tiled=False)
    mlp_in_grad = after(mlp_in_grad, mlp_grads)
    stream_part, two_gain_grad, two_shift_grad = two_pull(mlp_in_grad)
    stream_grad = grad_three + stream_part

    grad_low = stream_grad.astype(low)
    cr_bias_grad = column_sums(grad_low)
    cross_mixed_grad = contract_cols(grad_low, cr_weight).astype(low)

    cross_pre_low, text_parts, cross_sums = cross_backward(
        cross_query,
        text_spread,
        cross_totals,
        cross_mixed_grad,
        cross_pre,
        gain_table[2:3],
        cos_own,
        sin_own,
        text_count,
    )
    text_kv_grad = jnp.sum(swap(text_parts, "seq").astype(jnp.float32), 0)[:text_count]
    cross_out_low = grad_low
    cq_bias_grad = column_sums(cross_pre_low)
    stream_part, three_gain_grad, three_shift_grad = three_pull(
        contract_cols(cross_pre_low, cq_weight)
    )
    stream_grad = stream_grad + stream_part

    grad_low = stream_grad.astype(low)
    at_bias_grad = column_sums(grad_low)
    mixed_grad = contract_cols(grad_low, at_weight).astype(low)
    mixed_back = to_heads(after(mixed_grad, text_kv_grad))
    whole_grads = row_grads(
        jnp.stack([mixed, cross_in, cross_mixed]),
        after(jnp.stack([grad_low, cross_pre_low, cross_out_low]), mlp_all_grads),
        owners,
    )
    row_owned = scatter_chips(whole_grads)
    mixed_back = after(mixed_back, whole_grads)
    key_pre_grad, gains_from_text = tk_pull(text_kv_grad[:, :width])
    text_grad_low = jnp.concatenate(
        [key_pre_grad.astype(low), text_kv_grad[:, width:].astype(low)], 1
    )
    kv_weight_grad = contract_rows(text_now, text_grad_low)
    kv_bias_grad = column_sums(text_grad_low)
    text_part = contract_cols(text_grad_low, kv_weight)
    text_part = jnp.pad(text_part.astype(low), ((0, -text_count % (8 * ways)), (0, 0)))
    text_sum = sum_behind(text_part)
    stream_three = stream_two + sum_behind(after(out_partial, mixed_back)) + down_bias
    layer_out = stream_three.astype(low)[None]
    packed_grad, self_sums = self_backward(
        heads_h, self_totals, mixed_back, packed_pre, gain_table, cos_all, sin_all
    )
    pk_weight_grad = contract_rows(entry_all, packed_grad)
    entry_grad = sum_tokens(after(contract_cols(packed_grad, pk_weight), stream_three))
    pk_bias_grad = column_sums(packed_grad)
    gains_from_self = jnp.concatenate(
        [self_sums[0::2], cross_sums[:1], jnp.zeros_like(cross_sums[:1])], 0
    )
    shifts_now = jnp.concatenate([self_sums[1::2], cross_sums[1:]], 0)
    entry_grad = after(entry_grad, pk_weight_grad)
    shift_part = jnp.sum(entry_grad, 0)
    stream_part, one_gain_grad, one_shift_grad = one_pull(entry_grad)
    stream_grad = stream_grad + stream_part

    grad_low = stream_grad.astype(low)
    sk_bias_grad = column_sums(grad_low)
    shift_row_own = fit_rows(shift_part.astype(low)[None], 16)
    tail_grads = spread(jnp.concatenate([after(grad_low, text_sum), shift_row_own], 0), "seq")
    grad_rows = tail_grads[:, :tokens].reshape(all_tokens, model_width)
    shift_total = jnp.sum(tail_grads[:, tokens].astype(jnp.float32), 0)
    joined_grad, sk_gain_grad, sk_shift_grad = skip_pull(skip_back(grad_low, first_rows))

    def placed(own, groups):
        parts = jnp.zeros((groups, ways, own.shape[0] // groups), jnp.float32)
        parts = lax.dynamic_update_slice_in_dim(parts, own.reshape(groups, 1, -1), place, 1)
        return parts.reshape(-1)

    vector_grads = (
        sk_gain_grad,
        sk_shift_grad,
        sk_bias_grad,
        one_gain_grad,
        one_shift_grad,
        placed(pk_bias_grad, 3),
        at_bias_grad,
        three_gain_grad,
        three_shift_grad,
        cq_bias_grad,
        placed(kv_bias_grad, 2),
        cr_bias_grad,
        two_gain_grad,
        two_shift_grad,
        placed(up_bias_grad, owners),
        down_bias_grad,
    )
    table_grads = jnp.concatenate(
        [
            (gains_from_text + gains_from_self).reshape(-1),
            shifts_now.reshape(-1),
        ]
    )
    split_three = [part.reshape(owners, -1) for part in vector_grads]
    pk_at = 5
    pk_thirds = placed(pk_bias_grad, 3).reshape(3, model_width)
    split_three[pk_at : pk_at + 1] = [
        pk_thirds[:2].reshape(owners, -1),
        pk_thirds[2].reshape(owners, -1),
    ]
    split_three.append(jnp.broadcast_to(table_grads[None], (owners, table_grads.shape[0])))
    summed_sizes = [part.shape[1] for part in split_three]
    vector_rows = jnp.concatenate(split_three, 1).astype(low)
    vector_pad = -vector_rows.shape[1] % own_rows
    vector_rows = jnp.pad(vector_rows, ((0, 0), (0, vector_pad)))
    latent_mark = jnp.arange(owners) == lax.axis_index("fsdp")
    shift_mine = jnp.where(latent_mark[:, None], shift_total.astype(low), jnp.zeros((), low))
    shift_mine = jnp.broadcast_to(
        shift_mine.reshape(1, own_rows, -1), (owners, own_rows, owners * owners)
    )
    tail_sum = sum_owners(
        pack_tail(
            normed_own,
            grad_rows,
            pk_weight_grad,
            fit_rows(kv_weight_grad.astype(low).reshape(owners, -1, 2 * width), own_rows),
            jnp.concatenate([vector_rows.reshape(owners, own_rows, -1), shift_mine], 2),
        )
    ).astype(low)
    shift_all = tail_sum[:, -owners * owners :].reshape(owners, model_width)
    shift_all = shift_all.astype(jnp.float32)
    tail_sum = tail_sum[:, : -owners * owners]

    row_sum = jnp.sum(swap(column_blocks(row_owned), "seq").astype(jnp.float32), 0)
    lead = 7 * width
    tail_all = spread(
        jnp.concatenate([tail_sum[:, :lead], row_sum.astype(low), tail_sum[:, lead:]], 1), "seq"
    )
    text_total = lax.all_gather(
        after(text_sum.astype(low), row_owned), "seq", axis=0, tiled=True
    )[:text_count]
    sk_total, pk_total, kv_total, row_total, small_total = lay_tail(
        tail_all, cross_kv_weight.shape[0]
    )
    at_total = row_total[:, :model_width]
    cq_total = row_total[:, model_width : 2 * model_width]
    cr_total = row_total[:, 2 * model_width :]
    small_total = small_total.reshape(-1)
    vector_totals = []
    start = 0
    for size in summed_sizes:
        vector_totals.append(small_total[start : start + size])
        start += size
    table_total = vector_totals.pop()
    gains_total = table_total[: gain_table.size].reshape(gain_table.shape)
    shifts_total = table_total[gain_table.size :].reshape(shift_table.shape)
    md_weight_grad = lax.dot_general(
        lifted_own.astype(jnp.float32),
        shift_all,
        (((0,), (0,)), ((), ())),
        precision=lax.Precision.HIGHEST,
        preferred_element_type=jnp.float32,
    )
    md_bias_grad = lax.dynamic_slice_in_dim(
        jnp.sum(shift_all, 0), lax.axis_index("fsdp") * own_rows, own_rows, 0
    )
    lifted_part = lax.dot_general(
        shift_all,
        mod_weight.astype(jnp.float32),
        (((1,), (1,)), ((), ())),
        precision=lax.Precision.HIGHEST,
        preferred_element_type=jnp.float32,
    )
    lifted_grad = swap(after(lifted_part, tail_all, text_total), "fsdp").reshape(1, model_width)
    condition_grad = silu_pull(lifted_grad)[0]

    up_total, down_total = lay_units(mlp_all_grads, own_rows, model_width)
    (
        sk_gain_total,
        sk_shift_total,
        sk_bias_total,
        one_gain_total,
        one_shift_total,
        pk_bias_total,
        value_bias_total,
        at_bias_total,
        three_gain_total,
        three_shift_total,
        cq_bias_total,
        kv_bias_total,
        cr_bias_total,
        two_gain_total,
        two_shift_total,
        up_bias_total,
        down_bias_total,
    ) = vector_totals
    return (
        layer_out,
        joined_grad[:, :model_width].astype(low)[None],
        joined_grad[:, model_width:].astype(low)[None],
        text_total[None],
        condition_grad,
        sk_gain_total,
        sk_shift_total,
        sk_total,
        sk_bias_total,
        md_weight_grad,
        md_bias_grad,
        one_gain_total,
        one_shift_total,
        pk_total,
        pk_bias_total,
        value_bias_total,
        gains_total,
        shifts_total,
        at_total,
        at_bias_total,
        three_gain_total,
        three_shift_total,
        cq_total,
        cq_bias_total,
        kv_total,
        kv_bias_total,
        cr_total,
        cr_bias_total,
        two_gain_total,
        two_shift_total,
        up_total,
        up_bias_total,
        down_total,
        down_bias_total,
    )


def solution(mesh):
    in_specs = (
        P("fsdp", "seq", None),
        P("fsdp", "seq", None),
        P("fsdp", None, None),
        P("fsdp", None),
        P("seq", None),
        P("fsdp", "seq", None),
        P("fsdp"),
        P("fsdp"),
        P("fsdp", None),
        P("fsdp"),
        P("fsdp", None),
        P("fsdp"),
        P("fsdp"),
        P("fsdp"),
        P("fsdp", None),
        P("fsdp"),
        P(),
        P(),
        P("fsdp", None),
        P("fsdp"),
        P("fsdp"),
        P("fsdp"),
        P("fsdp", None),
        P("fsdp"),
        P("fsdp", None),
        P("fsdp"),
        P("fsdp", None),
        P("fsdp"),
        P("fsdp"),
        P("fsdp"),
        P("fsdp", None),
        P("fsdp"),
        P("fsdp", None),
        P("fsdp"),
    )
    out_specs = (
        P("fsdp", "seq", None),
        P("fsdp", "seq", None),
        P("fsdp", "seq", None),
        P("fsdp", None, None),
        P("fsdp", None),
        P("fsdp"),
        P("fsdp"),
        P("fsdp", None),
        P("fsdp"),
        P("fsdp", None),
        P("fsdp"),
        P("fsdp"),
        P("fsdp"),
        P("fsdp", None),
        P("fsdp"),
        P("fsdp"),
        P(),
        P(),
        P("fsdp", None),
        P("fsdp"),
        P("fsdp"),
        P("fsdp"),
        P("fsdp", None),
        P("fsdp"),
        P("fsdp", None),
        P("fsdp"),
        P("fsdp", None),
        P("fsdp"),
        P("fsdp"),
        P("fsdp"),
        P("fsdp", None),
        P("fsdp"),
        P("fsdp", None),
        P("fsdp"),
    )
    return jax.shard_map(local, mesh=mesh, in_specs=in_specs, out_specs=out_specs, check_vma=False)
```

```python
import functools
import math

import jax
import jax.numpy as jnp
from jax import lax
from jax.experimental import pallas as pl
from jax.experimental.pallas import tpu as pltpu
from jax.sharding import PartitionSpec as P


def layer_norm(inputs, gain_vector, shift_vector):
    centred = inputs - jnp.mean(inputs, -1, keepdims=True)
    variance = jnp.mean(centred * centred, -1, keepdims=True)
    return centred * lax.rsqrt(variance + 1e-06) * gain_vector + shift_vector


def rotary_tables(positions, head_dim):
    quarter = head_dim // 4
    exponent = jnp.arange(quarter, dtype=jnp.float32) * (2.0 / (head_dim // 2))
    inverse = jnp.power(jnp.float32(10000.0), -exponent)
    places = positions.astype(jnp.float32)
    angle_rows = places[:, 0:1] * inverse
    angle_cols = places[:, 1:2] * inverse
    return (jnp.cos(angle_rows), jnp.sin(angle_rows), jnp.cos(angle_cols), jnp.sin(angle_cols))


def rotate(inputs, tables):
    cos_rows, sin_rows, cos_cols, sin_cols = tuple((one_table[:, None, :] for one_table in tables))
    quarter = inputs.shape[-1] // 4
    first_a = inputs[..., :quarter]
    first_b = inputs[..., quarter : 2 * quarter]
    second_a = inputs[..., 2 * quarter : 3 * quarter]
    second_b = inputs[..., 3 * quarter :]
    return jnp.concatenate(
        [
            first_a * cos_rows - first_b * sin_rows,
            first_a * sin_rows + first_b * cos_rows,
            second_a * cos_cols - second_b * sin_cols,
            second_a * sin_cols + second_b * cos_cols,
        ],
        -1,
    )


def head_norm(inputs, gain_vector, shift_vector, head_dim):
    row_count = inputs.shape[0]
    shaped = inputs.reshape(row_count, -1, head_dim)
    return layer_norm(shaped, gain_vector, shift_vector).reshape(row_count, -1)


def head_rotary(inputs, gain_vector, shift_vector, tables, head_dim):
    row_count = inputs.shape[0]
    shaped = inputs.reshape(row_count, -1, head_dim)
    return rotate(layer_norm(shaped, gain_vector, shift_vector), tables).reshape(row_count, -1)


def matmul(left_side, right_side):
    return jnp.dot(left_side, right_side, preferred_element_type=jnp.float32)


def contract_rows(left_side, right_side):
    return lax.dot_general(
        left_side, right_side, (((0,), (0,)), ((), ())), preferred_element_type=jnp.float32
    )


def contract_cols(left_side, right_side):
    return lax.dot_general(
        left_side, right_side, (((1,), (1,)), ((), ())), preferred_element_type=jnp.float32
    )


def column_sums(grads_low):
    return jnp.sum(grads_low.astype(jnp.float32), 0)


def to_float(vectors):
    return tuple((one_vector.astype(jnp.float32) for one_vector in vectors))


def turn_tables(places, head_dim):
    cos_rows, sin_rows, cos_cols, sin_cols = rotary_tables(places, head_dim)
    return (
        jnp.concatenate([cos_rows, cos_rows, cos_cols, cos_cols], 1),
        jnp.concatenate([-sin_rows, sin_rows, -sin_cols, sin_cols], 1),
    )


def normalised(values):
    centred = values - jnp.mean(values, -1, keepdims=True)
    scale = lax.rsqrt(jnp.mean(centred * centred, -1, keepdims=True) + 1e-06)
    return centred * scale, scale


def partners(values):
    quarter = values.shape[1] // 4
    return jnp.concatenate(
        [
            values[:, quarter : 2 * quarter],
            values[:, :quarter],
            values[:, 3 * quarter :],
            values[:, 2 * quarter : 3 * quarter],
        ],
        1,
    )


def norm_turn(values, gain, shift, cos_now, sin_now):
    turned = normalised(values)[0] * gain + shift
    return turned * cos_now + partners(turned) * sin_now


def norm_turn_back(grad, values, gain, cos_now, sin_now):
    grad = grad.astype(jnp.bfloat16).astype(jnp.float32)
    grad = grad * cos_now - partners(grad) * sin_now
    normal, scale = normalised(values)
    scaled = grad * gain
    mean_one = jnp.mean(scaled, -1, keepdims=True)
    mean_two = jnp.mean(scaled * normal, -1, keepdims=True)
    return (
        scale * (scaled - mean_one - normal * mean_two),
        jnp.sum(grad * normal, 0, keepdims=True),
        jnp.sum(grad, 0, keepdims=True),
    )


def self_forward_kernel(
    entry_ref,
    weight_ref,
    bias_ref,
    gains_ref,
    shifts_ref,
    cos_ref,
    sin_ref,
    mixed_ref,
    heads_ref,
    pre_ref,
    totals_ref,
    *,
    scale,
):
    low = jnp.bfloat16
    count, all_tokens, head_dim = heads_ref.shape[1:]
    packed = matmul(entry_ref[...], weight_ref[...]) + bias_ref[...]
    pre_ref[...] = packed[:, : 2 * count * head_dim]
    cos_now, sin_now = cos_ref[...], sin_ref[...]
    for head in range(count):
        for kind in range(3):
            start = (kind * count + head) * head_dim
            part = packed[:, start : start + head_dim]
            if kind < 2:
                part = norm_turn(
                    part,
                    gains_ref[kind : kind + 1],
                    shifts_ref[kind : kind + 1],
                    cos_now,
                    sin_now,
                )
            heads_ref[kind, head] = part.astype(low)
    step = min(512, all_tokens)
    for start in range(0, all_tokens, step):
        mixed = []
        for head in range(count):
            query_block = heads_ref[0, head, start : start + step]
            scores = contract_cols(query_block, heads_ref[1, head]) * scale
            row_top = jnp.max(scores, -1, keepdims=True)
            weights = jnp.exp(scores - row_top)
            totals = jnp.sum(weights, -1, keepdims=True)
            probs = (weights * (1.0 / totals)).astype(low)
            mixed.append(matmul(probs, heads_ref[2, head]))
            totals_ref[head, start : start + step] = row_top + jnp.log(totals)
        mixed_ref[start : start + step] = jnp.concatenate(mixed, 1).astype(low)


def self_forward(entry_all, weight, bias, gains, shifts, cos_now, sin_now):
    all_tokens, head_dim = cos_now.shape
    count = weight.shape[1] // (3 * head_dim)
    return pl.pallas_call(
        functools.partial(self_forward_kernel, scale=1.0 / math.sqrt(head_dim)),
        out_shape=[
            jax.ShapeDtypeStruct((all_tokens, count * head_dim), jnp.bfloat16),
            jax.ShapeDtypeStruct((3, count, all_tokens, head_dim), jnp.bfloat16),
            jax.ShapeDtypeStruct((all_tokens, 2 * count * head_dim), jnp.float32),
            jax.ShapeDtypeStruct((count, all_tokens, 1), jnp.float32),
        ],
        compiler_params=pltpu.CompilerParams(vmem_limit_bytes=50 * 1024 * 1024),
        cost_estimate=pl.CostEstimate(
            flops=2 * all_tokens * weight.size + 4 * count * all_tokens**2 * head_dim,
            bytes_accessed=2 * entry_all.size + 2 * weight.size + 16 * all_tokens * weight.shape[1],
            transcendentals=count * all_tokens**2,
        ),
        name="self_forward",
    )(entry_all, weight, bias, gains, shifts, cos_now, sin_now)


def self_backward_kernel(
    heads_ref, totals_ref, grad_ref, pre_ref, gains_ref, cos_ref, sin_ref, out_ref, sums_ref, *, scale
):
    low = jnp.bfloat16
    count, all_tokens, head_dim = heads_ref.shape[1:]
    cos_now, sin_now = cos_ref[...], sin_ref[...]
    step = min(512, all_tokens)
    lanes = [None] * (3 * count)
    sums = None
    for head in range(count):
        keys_now = heads_ref[1, head]
        values_now = heads_ref[2, head]
        keys_grad, values_grad, query_grads = 0.0, 0.0, []
        for start in range(0, all_tokens, step):
            query_block = heads_ref[0, head, start : start + step]
            grad_block = grad_ref[start : start + step, head * head_dim : (head + 1) * head_dim]
            probs = jnp.exp(
                contract_cols(query_block, keys_now) * scale
                - totals_ref[head, start : start + step]
            )
            weighted = probs * contract_cols(grad_block, values_now)
            scores_grad = weighted - probs * jnp.sum(weighted, -1, keepdims=True)
            scores_low = (scores_grad * scale).astype(low)
            query_grads.append(matmul(scores_low, keys_now))
            keys_grad += contract_rows(scores_low, query_block)
            values_grad += contract_rows(probs.astype(low), grad_block)
        grads = (jnp.concatenate(query_grads, 0), keys_grad)
        parts = []
        for kind in range(2):
            start = (kind * count + head) * head_dim
            back, gain_sum, shift_sum = norm_turn_back(
                grads[kind],
                pre_ref[:, start : start + head_dim],
                gains_ref[kind : kind + 1],
                cos_now,
                sin_now,
            )
            lanes[kind * count + head] = back
            parts += [gain_sum, shift_sum]
        lanes[2 * count + head] = values_grad
        parts = jnp.concatenate(parts, 0)
        sums = parts if sums is None else sums + parts
    out_ref[...] = jnp.concatenate(lanes, 1).astype(low)
    sums_ref[...] = sums


def self_backward(heads, totals, grad_out, pre, gains, cos_now, sin_now):
    count, all_tokens, head_dim = heads.shape[1:]
    return pl.pallas_call(
        functools.partial(self_backward_kernel, scale=1.0 / math.sqrt(head_dim)),
        out_shape=[
            jax.ShapeDtypeStruct((all_tokens, 3 * count * head_dim), jnp.bfloat16),
            jax.ShapeDtypeStruct((4, head_dim), jnp.float32),
        ],
        compiler_params=pltpu.CompilerParams(vmem_limit_bytes=50 * 1024 * 1024),
        cost_estimate=pl.CostEstimate(
            flops=10 * count * all_tokens**2 * head_dim,
            bytes_accessed=24 * count * all_tokens * head_dim,
            transcendentals=count * all_tokens**2,
        ),
        name="self_backward",
    )(heads, totals, grad_out, pre, gains, cos_now, sin_now)


def cross_forward_kernel(
    pre_ref, text_ref, gain_ref, shift_ref, cos_ref, sin_ref, mixed_ref, query_ref, totals_ref, *, scale, valid
):
    low = jnp.bfloat16
    head_dim = cos_ref.shape[1]
    heads = pre_ref.shape[1] // head_dim
    count = heads // text_ref.shape[0]
    width = count * head_dim
    cos_now, sin_now = cos_ref[...], sin_ref[...]
    mixed, queries = [], []
    for head in range(heads):
        lanes = slice(head * head_dim, (head + 1) * head_dim)
        query = norm_turn(pre_ref[:, lanes], gain_ref[...], shift_ref[...], cos_now, sin_now)
        query = query.astype(low)
        queries.append(query)
        start = (head % count) * head_dim
        text = text_ref[head // count]
        scores = contract_cols(query, text[:, start : start + head_dim]) * scale
        column = lax.broadcasted_iota(jnp.int32, scores.shape, 1)
        scores = jnp.where(column < valid, scores, -1e30)
        row_top = jnp.max(scores, -1, keepdims=True)
        weights = jnp.exp(scores - row_top)
        totals = jnp.sum(weights, -1, keepdims=True)
        probs = (weights * (1.0 / totals)).astype(low)
        mixed.append(matmul(probs, text[:, width + start : width + start + head_dim]))
        totals_ref[head] = row_top + jnp.log(totals)
    mixed_ref[...] = jnp.concatenate(mixed, 1).astype(low)
    query_ref[...] = jnp.concatenate(queries, 1)


def cross_forward(pre, text, gain, shift, cos_now, sin_now, valid):
    tokens, model_width = pre.shape
    head_dim = cos_now.shape[1]
    heads = model_width // head_dim
    return pl.pallas_call(
        functools.partial(cross_forward_kernel, scale=1.0 / math.sqrt(head_dim), valid=valid),
        out_shape=[
            jax.ShapeDtypeStruct((tokens, model_width), jnp.bfloat16),
            jax.ShapeDtypeStruct((tokens, model_width), jnp.bfloat16),
            jax.ShapeDtypeStruct((heads, tokens, 1), jnp.float32),
        ],
        compiler_params=pltpu.CompilerParams(vmem_limit_bytes=40 * 1024 * 1024),
        cost_estimate=pl.CostEstimate(
            flops=4 * tokens * text.shape[1] * model_width,
            bytes_accessed=2 * text.size + 8 * pre.size,
            transcendentals=heads * tokens * text.shape[1],
        ),
        name="cross_forward",
    )(pre, text, gain, shift, cos_now, sin_now)


def cross_backward_kernel(
    query_ref,
    text_ref,
    totals_ref,
    grad_ref,
    pre_ref,
    gain_ref,
    cos_ref,
    sin_ref,
    pre_grad_ref,
    text_grad_ref,
    sums_ref,
    *,
    scale,
    valid,
):
    low = jnp.bfloat16
    head_dim = cos_ref.shape[1]
    ways = text_ref.shape[0]
    count = query_ref.shape[1] // head_dim // ways
    width = count * head_dim
    cos_now, sin_now = cos_ref[...], sin_ref[...]
    backs, sums = [], 0.0
    for way in range(ways):
        text = text_ref[way]
        text_grads = [None] * (2 * count)
        for one in range(count):
            head = way * count + one
            lanes = slice(head * head_dim, (head + 1) * head_dim)
            query = query_ref[:, lanes]
            grad = grad_ref[:, lanes]
            keys_now = text[:, one * head_dim : (one + 1) * head_dim]
            values_now = text[:, width + one * head_dim : width + (one + 1) * head_dim]
            probs = jnp.exp(contract_cols(query, keys_now) * scale - totals_ref[head])
            column = lax.broadcasted_iota(jnp.int32, probs.shape, 1)
            probs = jnp.where(column < valid, probs, 0.0)
            weighted = probs * contract_cols(grad, values_now)
            scores_grad = weighted - probs * jnp.sum(weighted, -1, keepdims=True)
            scores_low = (scores_grad * scale).astype(low)
            back, gain_sum, shift_sum = norm_turn_back(
                matmul(scores_low, keys_now), pre_ref[:, lanes], gain_ref[...], cos_now, sin_now
            )
            backs.append(back)
            sums += jnp.concatenate([gain_sum, shift_sum], 0)
            text_grads[one] = contract_rows(scores_low, query)
            text_grads[count + one] = contract_rows(probs.astype(low), grad)
        text_grad_ref[way] = jnp.concatenate(text_grads, 1).astype(low)
    pre_grad_ref[...] = jnp.concatenate(backs, 1).astype(low)
    sums_ref[...] = sums


def cross_backward(query, text, totals, grad, pre, gain, cos_now, sin_now, valid):
    tokens, model_width = pre.shape
    head_dim = cos_now.shape[1]
    ways, text_rows = text.shape[:2]
    return pl.pallas_call(
        functools.partial(cross_backward_kernel, scale=1.0 / math.sqrt(head_dim), valid=valid),
        out_shape=[
            jax.ShapeDtypeStruct((tokens, model_width), jnp.bfloat16),
            jax.ShapeDtypeStruct((ways, text_rows, 2 * model_width // ways), jnp.bfloat16),
            jax.ShapeDtypeStruct((2, head_dim), jnp.float32),
        ],
        compiler_params=pltpu.CompilerParams(vmem_limit_bytes=40 * 1024 * 1024),
        cost_estimate=pl.CostEstimate(
            flops=10 * tokens * text_rows * model_width,
            bytes_accessed=4 * text.size + 10 * pre.size,
            transcendentals=tokens * text_rows * model_width // head_dim,
        ),
        name="cross_backward",
    )(query, text, totals, grad, pre, gain, cos_now, sin_now)


def row_grads_kernel(left_ref, far_left_ref, right_ref, far_right_ref, out_ref):
    product = contract_rows(left_ref[0], right_ref[0])
    product += contract_rows(far_left_ref[0], far_right_ref[0])
    rows = out_ref.shape[1]
    for chip in range(out_ref.shape[0]):
        out_ref[chip] = product[chip * rows : (chip + 1) * rows].astype(out_ref.dtype)


def row_grads(lefts, rights, owners):
    count, tokens, width = lefts.shape
    rows = width // owners
    core = lax.axis_index("fsdp") % 2
    by_core = lefts.reshape(count, tokens, owners // 2, 2, rows).transpose(3, 0, 1, 2, 4)
    by_core = by_core.reshape(2, count, tokens, width // 2)
    near = lax.dynamic_index_in_dim(by_core, core, 0, False)
    far = swap_cores(lax.dynamic_index_in_dim(by_core, 1 - core, 0, False))
    left_spec = pl.BlockSpec((1, tokens, width // 2), lambda i: (i, 0, 0))
    right_spec = pl.BlockSpec((1, tokens, width), lambda i: (i, 0, 0))
    return pl.pallas_call(
        row_grads_kernel,
        grid=(count,),
        in_specs=[left_spec, left_spec, right_spec, right_spec],
        out_specs=pl.BlockSpec((owners // 2, rows, width), lambda i: (0, 0, i)),
        out_shape=jax.ShapeDtypeStruct((owners // 2, rows, count * width), jnp.bfloat16),
        compiler_params=pltpu.CompilerParams(vmem_limit_bytes=48 * 1024 * 1024),
        cost_estimate=pl.CostEstimate(
            flops=2 * count * tokens * width * width,
            bytes_accessed=2 * count * (width * width // 2 + 3 * tokens * width),
            transcendentals=0,
        ),
        name="row_grads",
    )(near, far, rights, swap_cores(rights))


def side_by_side(pieces):
    return jnp.concatenate([piece.astype(jnp.float32) for piece in pieces], 1)


def pack_kernel(normed_ref, grads_ref, packed_ref, text_ref, small_ref, out_ref):
    owners, rows = text_ref.shape[:2]
    product = contract_rows(normed_ref[...], grads_ref[...])
    count = product.shape[0] // owners
    folds = rows // count
    lanes = product.shape[1] // folds
    for owner in range(owners):
        skip = product[owner * count : (owner + 1) * count]
        skip = jnp.concatenate(
            [skip[:, fold * lanes : (fold + 1) * lanes] for fold in range(folds)], 0
        )
        line = side_by_side(
            [
                skip,
                packed_ref[owner * rows : (owner + 1) * rows],
                text_ref[owner],
                small_ref[owner],
            ]
        )
        out_ref[owner % 2, owner // 2] = line.astype(out_ref.dtype)


def pack_tail(normed, grads, packed, text, small):
    owners, rows = text.shape[:2]
    lanes = 2 * text.shape[2] // 2 + packed.shape[1] + text.shape[2] + small.shape[2]
    return pl.pallas_call(
        pack_kernel,
        out_shape=jax.ShapeDtypeStruct((2, owners // 2, rows, lanes), jnp.bfloat16),
        compiler_params=pltpu.CompilerParams(vmem_limit_bytes=48 * 1024 * 1024),
        cost_estimate=pl.CostEstimate(
            flops=2 * normed.size * grads.shape[1],
            bytes_accessed=2 * normed.size + 4 * owners * rows * lanes,
            transcendentals=0,
        ),
        name="pack_tail",
    )(normed, grads, packed, text, small)


def tail_kernel(all_ref, skip_ref, packed_ref, text_ref, whole_ref, small_ref):
    ways, rows = all_ref.shape[:2]
    model_width = skip_ref.shape[1]
    width = model_width // ways

    def joined(start, count, size):
        return side_by_side(
            [all_ref[way, :, start : start + size][:count] for way in range(ways)]
        )

    count = 2 * rows // ways
    folds = rows // count
    skip = []
    for way in range(ways):
        block = all_ref[way, :, : 2 * width].astype(jnp.float32)
        skip.append(
            jnp.concatenate(
                [block[fold * count : (fold + 1) * count] for fold in range(folds)], 1
            )
        )
    skip_ref[...] = jnp.concatenate(skip, 0)
    for third in range(3):
        packed_ref[:, third * model_width : (third + 1) * model_width] = joined(
            (2 + third) * width, rows, width
        )
    for side in range(2):
        text_ref[:, side * model_width : (side + 1) * model_width] = joined(
            (5 + side) * width, text_ref.shape[0], width
        )
    whole_ref[...] = joined(7 * width, rows, 3 * width)
    total = all_ref[0, :, 10 * width :].astype(jnp.float32)
    for way in range(1, ways):
        total += all_ref[way, :, 10 * width :].astype(jnp.float32)
    small_ref[...] = total


def lay_tail(blocks, text_rows):
    ways, rows, lanes = blocks.shape
    width = 2 * rows
    model_width = ways * width
    return pl.pallas_call(
        tail_kernel,
        out_shape=[
            jax.ShapeDtypeStruct((2 * rows, model_width), jnp.float32),
            jax.ShapeDtypeStruct((rows, 3 * model_width), jnp.float32),
            jax.ShapeDtypeStruct((text_rows, 2 * model_width), jnp.float32),
            jax.ShapeDtypeStruct((rows, 3 * model_width), jnp.float32),
            jax.ShapeDtypeStruct((rows, lanes - 10 * width), jnp.float32),
        ],
        compiler_params=pltpu.CompilerParams(vmem_limit_bytes=40 * 1024 * 1024),
        name="lay_tail",
    )(blocks)


def skip_back_kernel(grad_ref, first_ref, second_ref, out_ref):
    grad = grad_ref[...]
    halves = [contract_cols(grad, half_ref[...]) for half_ref in (first_ref, second_ref)]
    rows = grad.shape[1] // 16
    out_ref[...] = side_by_side(
        [half[:, i * rows : (i + 1) * rows] for i in range(16) for half in halves]
    )


def skip_back(grad_low, first_rows):
    tokens, model_width = grad_low.shape
    return pl.pallas_call(
        skip_back_kernel,
        grid=(1,),
        in_specs=[
            pl.BlockSpec((tokens, model_width), lambda i: (0, 0)),
            pl.BlockSpec((model_width, model_width), lambda i: (0, 0)),
            pl.BlockSpec((model_width, model_width), lambda i: (0, 1)),
        ],
        out_specs=pl.BlockSpec((tokens, 2 * model_width), lambda i: (0, 0)),
        out_shape=jax.ShapeDtypeStruct((tokens, 2 * model_width), jnp.float32),
        compiler_params=pltpu.CompilerParams(vmem_limit_bytes=48 * 1024 * 1024),
        cost_estimate=pl.CostEstimate(
            flops=4 * tokens * model_width * model_width,
            bytes_accessed=4 * model_width * (model_width + 2 * tokens),
            transcendentals=0,
        ),
        name="skip_back",
    )(grad_low, first_rows, first_rows)


def units_kernel(all_ref, up_ref, down_ref):
    ways = all_ref.shape[0]
    rows, hidden = up_ref.shape
    units = hidden // ways
    owners = 16
    own = units // owners
    for owner in range(owners):
        start = owner * ways * own
        up_ref[:, start : start + ways * own] = side_by_side(
            [all_ref[way, :rows, owner * own : (owner + 1) * own] for way in range(ways)]
        )
    model_width = down_ref.shape[1]
    split = min(units, model_width)
    for way in range(ways):
        place = slice(way * own, (way + 1) * own)
        down_ref[place, :split] = all_ref[way, :own, units : units + split].astype(jnp.float32)
        if split < model_width:
            down_ref[place, split:] = all_ref[
                way, own : 2 * own, units : units + model_width - split
            ].astype(jnp.float32)


def lay_units(blocks, rows, model_width):
    ways, lines, lanes = blocks.shape
    units = lanes // 2
    return pl.pallas_call(
        units_kernel,
        out_shape=[
            jax.ShapeDtypeStruct((rows, ways * units), jnp.float32),
            jax.ShapeDtypeStruct((ways * units // 16, model_width), jnp.float32),
        ],
        compiler_params=pltpu.CompilerParams(vmem_limit_bytes=40 * 1024 * 1024),
        name="lay_units",
    )(blocks)


def fold_down(part, units, lines):
    first = part[..., :units]
    rest = part[..., units:]
    pad = [(0, 0)] * (part.ndim - 1) + [(0, units - rest.shape[-1])]
    both = jnp.concatenate([first, jnp.pad(rest, pad)], -2)
    return fit_rows(both, lines)


def fit_rows(part, lines):
    pad = [(0, 0)] * part.ndim
    pad[-2] = (0, lines - part.shape[-2])
    return jnp.pad(part, pad)


def swap(blocks, axis_name):
    return lax.all_to_all(blocks, axis_name, split_axis=0, concat_axis=0, tiled=True)


def spread(part, axis_name):
    size = lax.axis_size(axis_name)
    return swap(jnp.broadcast_to(part[None], (size,) + part.shape), axis_name)


def grid_place():
    index = lax.axis_index("seq")
    return index // 4, index % 4


def grid_send(value, pair, step):
    links = [(i, ((i // 4) ^ pair) * 4 + (i + step) % 4) for i in range(8)]
    return lax.ppermute(value, "seq", links)


def gather_tokens(part):
    pair, ring = grid_place()
    mate = grid_send(part, 1, 0)
    below = grid_send(part, 0, 1)
    above = grid_send(part, 0, -1)
    far = grid_send(part, 0, 2)
    mate_below = grid_send(mate, 0, 1)
    mate_above = grid_send(mate, 0, -1)
    mate_far = grid_send(far, 1, 0)
    here, there = pair * 4, (1 - pair) * 4
    buffer = jnp.zeros((8,) + part.shape, part.dtype)
    for one, spot in (
        (part, here + ring),
        (mate, there + ring),
        (below, here + (ring + 3) % 4),
        (above, here + (ring + 1) % 4),
        (far, here + (ring + 2) % 4),
        (mate_below, there + (ring + 3) % 4),
        (mate_above, there + (ring + 1) % 4),
        (mate_far, there + (ring + 2) % 4),
    ):
        buffer = lax.dynamic_update_index_in_dim(buffer, one, spot, 0)
    return buffer.reshape((-1,) + part.shape[1:])


def gather_behind(part):
    return spread(part, "seq").reshape((-1,) + part.shape[1:])


def sum_tokens(partial):
    low = jnp.bfloat16
    blocks = partial.astype(low).reshape((8, -1) + partial.shape[1:])
    pair, ring = grid_place()

    def meant(mate, step):
        spot = jnp.where(mate, 1 - pair, pair) * 4 + (ring + step) % 4
        return lax.dynamic_index_in_dim(blocks, spot, 0, False)

    def total(*parts):
        return sum(part.astype(jnp.float32) for part in parts)

    far_mate = grid_send(meant(True, 2), 1, 0)
    mate_below = grid_send(meant(True, 1), 0, 1)
    mate_above = grid_send(meant(True, 3), 0, -1)
    below = grid_send(meant(False, 1), 0, 1)
    above = grid_send(meant(False, 3), 0, -1)
    far = grid_send(total(meant(False, 2), far_mate).astype(low), 0, 2)
    mate = grid_send(total(meant(True, 0), mate_below, mate_above).astype(low), 1, 0)
    return total(meant(False, 0), below, above, far, mate)


def sum_behind(partial):
    blocks = partial.astype(jnp.bfloat16).reshape((8, -1) + partial.shape[1:])
    return jnp.sum(swap(blocks, "seq").astype(jnp.float32), 0)


def column_blocks(values):
    size = lax.axis_size("seq")
    rows = values.shape[0]
    return values.reshape(rows, size, -1).transpose(1, 0, 2)


def own_columns(weight, groups, size, place):
    rows = weight.shape[0]
    parts = weight.reshape(rows, groups, size, -1)
    taken = lax.dynamic_slice_in_dim(parts, place, 1, 2)
    return taken.reshape(rows, -1)


def after(values, *others):
    waits = [other[(0,) * other.ndim].astype(jnp.float32) * 0.0 for other in others]
    return values + sum(waits).astype(values.dtype)


def core_groups(owners):
    return [list(range(0, owners, 2)), list(range(1, owners, 2))]


def swap_cores(value):
    return lax.ppermute(value, "fsdp", [(i, i ^ 1) for i in range(lax.axis_size("fsdp"))])


def sum_cores(by_core):
    core = lax.axis_index("fsdp") % 2
    kept = lax.dynamic_index_in_dim(by_core, core, 0, False)
    arrived = swap_cores(lax.dynamic_index_in_dim(by_core, 1 - core, 0, False))
    return (kept.astype(jnp.float32) + arrived.astype(jnp.float32)).astype(jnp.bfloat16)


def scatter_chips(by_chip):
    return lax.psum_scatter(
        by_chip,
        "fsdp",
        scatter_dimension=0,
        axis_index_groups=core_groups(2 * by_chip.shape[0]),
        tiled=False,
    )


def sum_owners(by_core):
    chip = sum_cores(by_core)
    swapped = lax.all_to_all(
        chip,
        "fsdp",
        split_axis=0,
        concat_axis=0,
        axis_index_groups=core_groups(2 * chip.shape[0]),
        tiled=True,
    )
    return jnp.sum(swapped.astype(jnp.float32), 0)


def heads_first(values, head_dim):
    rows = values.shape[0]
    return values.reshape(rows, -1, head_dim).transpose(1, 0, 2)


def heads_last(values):
    return values.transpose(1, 0, 2).reshape(values.shape[1], -1)


def local(
    latent,
    skip_input,
    text_tokens,
    condition,
    positions,
    cotangent,
    skip_gain,
    skip_shift,
    skip_weight,
    skip_bias,
    mod_weight,
    mod_bias,
    norm1_gain,
    norm1_shift,
    qkv_weight,
    qkv_bias,
    head_gains,
    head_shifts,
    attn_weight,
    attn_bias,
    norm3_gain,
    norm3_shift,
    cross_q_weight,
    cross_q_bias,
    cross_kv_weight,
    cross_kv_bias,
    cross_weight,
    cross_bias,
    norm2_gain,
    norm2_shift,
    fc1_weight,
    fc1_bias,
    fc2_weight,
    fc2_bias,
):
    ways = lax.axis_size("seq")
    owners = lax.axis_size("fsdp")
    place = lax.axis_index("seq")
    head_dim = head_gains.shape[1]
    tokens, model_width = latent.shape[1:]
    width = model_width // ways
    low = jnp.bfloat16
    gain_table = head_gains.astype(jnp.float32)
    shift_table = head_shifts.astype(jnp.float32)
    cos_own, sin_own = turn_tables(positions, head_dim)

    own_rows = model_width // owners
    packed_own = own_columns(qkv_weight, 3, ways, place)
    first_own = jnp.concatenate(
        [skip_weight[:own_rows], skip_weight[own_rows:], packed_own], 1
    )
    first_rows = lax.all_gather(first_own, "fsdp", axis=0, tiled=True)
    kv_own = own_columns(cross_kv_weight, 2, ways, place)
    second_own = jnp.concatenate([attn_weight, cross_q_weight, cross_weight], 1)
    unit_rows = fc2_weight.shape[0] // ways
    down_own = lax.dynamic_slice_in_dim(fc2_weight, place * unit_rows, unit_rows, 0)
    up_own = own_columns(fc1_weight, owners, ways, place)
    units = up_own.shape[1]
    lines = max(own_rows, 2 * unit_rows)
    third_own = jnp.concatenate(
        [fit_rows(up_own, lines), fold_down(down_own, units, lines)], 1
    )
    lifted_f, silu_pull = jax.vjp(jax.nn.silu, condition.astype(jnp.float32))
    lifted = lifted_f.astype(low)
    vectors = (
        skip_gain,
        skip_shift,
        skip_bias,
        mod_bias,
        norm1_gain,
        norm1_shift,
        qkv_bias,
        attn_bias,
        norm3_gain,
        norm3_shift,
        cross_q_bias,
        cross_kv_bias,
        cross_bias,
        norm2_gain,
        norm2_shift,
        fc1_bias,
        fc2_bias,
    )
    vector_own = jnp.concatenate(vectors)
    vector_all = swap(
        jnp.concatenate(
            [
                jnp.broadcast_to(vector_own[None], (owners, vector_own.shape[0])),
                lifted.reshape(owners, own_rows),
            ],
            1,
        ),
        "fsdp",
    )
    pieces = []
    start = 0
    for one_vector in vectors:
        size = one_vector.shape[0]
        pieces.append(vector_all[:, start : start + size].reshape(-1).astype(jnp.float32))
        start += size
    lifted_own = vector_all[:, start:]
    (
        sk_gain,
        sk_shift,
        sk_bias,
        md_bias,
        one_gain,
        one_shift,
        pk_bias,
        at_bias,
        three_gain,
        three_shift,
        cq_bias,
        kv_bias,
        cr_bias,
        two_gain,
        two_shift,
        up_bias,
        down_bias,
    ) = pieces
    pk_bias_own = own_columns(pk_bias[None], 3, ways, place)[0]
    kv_bias_own = own_columns(kv_bias[None], 2, ways, place)[0]
    up_bias_own = own_columns(up_bias[None], owners, ways, place)[0]
    shift_row = (
        jnp.sum(swap(matmul(lifted_own, mod_weight), "fsdp"), 0, keepdims=True) + md_bias
    )

    kv_weight = spread(after(kv_own, vector_all), "fsdp").reshape(-1, 2 * width)
    text_now = text_tokens[0]
    text_count = text_now.shape[0]
    text_packed = matmul(text_now, kv_weight) + kv_bias_own
    text_keys_f, tk_pull = jax.vjp(
        lambda values_in, gains_in: head_norm(values_in, gains_in[3], 0.0, head_dim),
        text_packed[:, :width],
        gain_table,
    )
    text_own = jnp.concatenate(
        [text_keys_f.astype(low), text_packed[:, width:].astype(low)], 1
    )
    text_rows = text_count + -text_count % 16
    place_rows = max(text_rows, tokens)
    text_own = jnp.concatenate(
        [
            fit_rows(text_own, place_rows),
            fit_rows(positions.astype(low), place_rows),
        ],
        1,
    )
    text_spread = spread(text_own, "seq")
    cos_all, sin_all = turn_tables(
        text_spread[:, :tokens, 2 * width :].reshape(-1, 2), head_dim
    )
    joined = jnp.concatenate([latent[0], skip_input[0]], 1).astype(jnp.float32)
    normed_f, skip_pull = jax.vjp(layer_norm, joined, sk_gain, sk_shift)
    normed = normed_f.astype(low)
    normed_halves = normed.reshape(tokens, owners, 2, own_rows).transpose(2, 0, 1, 3)
    normed_halves = normed_halves.reshape(2, tokens, model_width)
    normed_rows = normed.reshape(tokens, owners, ways, -1).transpose(2, 0, 1, 3)
    normed_rows = normed_rows.reshape(ways, tokens, -1)
    normed_halves = after(normed_halves, shift_row, text_spread)
    stream_zero = (
        matmul(normed_halves[0], first_rows[:, :model_width])
        + matmul(normed_halves[1], first_rows[:, model_width : 2 * model_width])
        + sk_bias
    )

    pk_weight = first_rows[:, 2 * model_width :]
    second_rows = lax.all_gather(after(second_own, stream_zero), "fsdp", axis=0, tiled=True)
    at_weight = second_rows[:, :model_width]
    cq_weight = second_rows[:, model_width : 2 * model_width]
    cr_weight = second_rows[:, 2 * model_width :]
    entry_f, one_pull = jax.vjp(layer_norm, stream_zero, one_gain, one_shift)
    entry = (entry_f + shift_row).astype(low)

    entry_all = gather_tokens(entry)

    mixed_h, heads_h, packed_pre, self_totals = self_forward(
        entry_all, pk_weight, pk_bias_own[None], gain_table, shift_table, cos_all, sin_all
    )
    all_tokens = entry_all.shape[0]
    grad_all = gather_behind(after(cotangent[0], text_spread))
    mixed_h = after(mixed_h, grad_all)

    def to_heads(values):
        return swap(column_blocks(values), "seq").reshape(all_tokens, -1)

    mixed = swap(mixed_h.reshape(ways, tokens, width), "seq")
    mixed = mixed.transpose(1, 0, 2).reshape(tokens, model_width)
    third_rows = lax.all_gather(after(third_own, packed_pre), "fsdp", axis=0, tiled=False)
    up_weight = third_rows[:, :own_rows, :units].reshape(model_width, units)
    down_weight = jnp.concatenate(
        [
            third_rows[:, :unit_rows, units : units + min(units, model_width)],
            third_rows[:, unit_rows : 2 * unit_rows, units : units + max(model_width - units, 0)],
        ],
        2,
    ).reshape(units, model_width)
    stream_one = stream_zero + matmul(mixed, at_weight) + at_bias

    cross_in_f, three_pull = jax.vjp(layer_norm, stream_one, three_gain, three_shift)
    cross_in = cross_in_f.astype(low)
    cross_pre = matmul(cross_in, cq_weight) + cq_bias
    cross_mixed, cross_query, cross_totals = cross_forward(
        cross_pre, text_spread, gain_table[2:3], shift_table[2:3], cos_own, sin_own, text_count
    )
    stream_two = stream_one + matmul(cross_mixed, cr_weight) + cr_bias

    mlp_in_f, two_pull = jax.vjp(layer_norm, stream_two, two_gain, two_shift)
    normed_own = swap(after(normed_rows, mixed), "seq").reshape(all_tokens, -1)
    mlp_all = gather_tokens(after(mlp_in_f.astype(low), normed_own))
    hidden_pre = matmul(mlp_all, up_weight) + up_bias_own
    hidden_f, gelu_pull = jax.vjp(
        lambda values_in: jax.nn.gelu(values_in, approximate=True), hidden_pre
    )
    hidden = hidden_f.astype(low)
    out_partial = matmul(hidden, down_weight).astype(low)
    grad_three = cotangent[0].astype(jnp.float32)
    down_bias_grad = column_sums(cotangent[0])
    pre_grad = gelu_pull(contract_cols(grad_all, down_weight))[0].astype(low)
    up_bias_grad = column_sums(pre_grad)
    mlp_in_grad = sum_tokens(contract_cols(pre_grad, up_weight))
    down_grad = contract_rows(hidden, grad_all).astype(low)
    up_grad = contract_rows(mlp_all, pre_grad).astype(low)
    mlp_grads = jnp.concatenate(
        [
            fit_rows(up_grad.reshape(owners, own_rows, units), lines),
            fold_down(down_grad.reshape(owners, unit_rows, model_width), units, lines),
        ],
        2,
    )
    mlp_grads = mlp_grads.reshape(owners // 2, 2, lines, 2 * units).transpose(1, 0, 2, 3)
    mlp_owned = scatter_chips(sum_cores(mlp_grads))
    mlp_in_grad = after(mlp_in_grad, mlp_grads)
    stream_part, two_gain_grad, two_shift_grad = two_pull(mlp_in_grad)
    stream_grad = grad_three + stream_part

    grad_low = stream_grad.astype(low)
    cr_bias_grad = column_sums(grad_low)
    cross_mixed_grad = contract_cols(grad_low, cr_weight).astype(low)

    cross_pre_low, text_parts, cross_sums = cross_backward(
        cross_query,
        text_spread,
        cross_totals,
        cross_mixed_grad,
        cross_pre,
        gain_table[2:3],
        cos_own,
        sin_own,
        text_count,
    )
    text_kv_grad = jnp.sum(swap(text_parts, "seq").astype(jnp.float32), 0)[:text_count]
    cross_out_low = grad_low
    cq_bias_grad = column_sums(cross_pre_low)
    stream_part, three_gain_grad, three_shift_grad = three_pull(
        contract_cols(cross_pre_low, cq_weight)
    )
    stream_grad = stream_grad + stream_part

    grad_low = stream_grad.astype(low)
    at_bias_grad = column_sums(grad_low)
    mixed_grad = contract_cols(grad_low, at_weight).astype(low)
    mlp_all_grads = lax.all_gather(after(mlp_owned, grad_low), "seq", axis=0, tiled=False)
    mixed_back = to_heads(after(mixed_grad, text_kv_grad))
    whole_grads = row_grads(
        jnp.stack([mixed, cross_in, cross_mixed]),
        after(jnp.stack([grad_low, cross_pre_low, cross_out_low]), mlp_all_grads),
        owners,
    )
    row_owned = scatter_chips(whole_grads)
    mixed_back = after(mixed_back, whole_grads)
    key_pre_grad, gains_from_text = tk_pull(text_kv_grad[:, :width])
    text_grad_low = jnp.concatenate(
        [key_pre_grad.astype(low), text_kv_grad[:, width:].astype(low)], 1
    )
    kv_weight_grad = contract_rows(text_now, text_grad_low)
    kv_bias_grad = column_sums(text_grad_low)
    text_part = contract_cols(text_grad_low, kv_weight)
    text_part = jnp.pad(text_part.astype(low), ((0, -text_count % (8 * ways)), (0, 0)))
    text_sum = sum_behind(text_part)
    stream_three = stream_two + sum_behind(after(out_partial, mixed_back)) + down_bias
    layer_out = stream_three.astype(low)[None]
    packed_grad, self_sums = self_backward(
        heads_h, self_totals, mixed_back, packed_pre, gain_table, cos_all, sin_all
    )
    pk_weight_grad = contract_rows(entry_all, packed_grad)
    entry_grad = sum_tokens(after(contract_cols(packed_grad, pk_weight), stream_three))
    pk_bias_grad = column_sums(packed_grad)
    gains_from_self = jnp.concatenate(
        [self_sums[0::2], cross_sums[:1], jnp.zeros_like(cross_sums[:1])], 0
    )
    shifts_now = jnp.concatenate([self_sums[1::2], cross_sums[1:]], 0)
    entry_grad = after(entry_grad, pk_weight_grad)
    shift_part = jnp.sum(entry_grad, 0)
    stream_part, one_gain_grad, one_shift_grad = one_pull(entry_grad)
    stream_grad = stream_grad + stream_part

    grad_low = stream_grad.astype(low)
    sk_bias_grad = column_sums(grad_low)
    shift_row_own = fit_rows(shift_part.astype(low)[None], 16)
    text_total = gather_behind(text_sum.astype(low))[:text_count]
    tail_grads = spread(jnp.concatenate([after(grad_low, text_total), shift_row_own], 0), "seq")
    grad_rows = tail_grads[:, :tokens].reshape(all_tokens, model_width)
    shift_total = jnp.sum(tail_grads[:, tokens].astype(jnp.float32), 0)
    joined_grad, sk_gain_grad, sk_shift_grad = skip_pull(skip_back(grad_low, first_rows))

    def placed(own, groups):
        parts = jnp.zeros((groups, ways, own.shape[0] // groups), jnp.float32)
        parts = lax.dynamic_update_slice_in_dim(parts, own.reshape(groups, 1, -1), place, 1)
        return parts.reshape(-1)

    vector_grads = (
        sk_gain_grad,
        sk_shift_grad,
        sk_bias_grad,
        one_gain_grad,
        one_shift_grad,
        placed(pk_bias_grad, 3),
        at_bias_grad,
        three_gain_grad,
        three_shift_grad,
        cq_bias_grad,
        placed(kv_bias_grad, 2),
        cr_bias_grad,
        two_gain_grad,
        two_shift_grad,
        placed(up_bias_grad, owners),
        down_bias_grad,
    )
    table_grads = jnp.concatenate(
        [
            (gains_from_text + gains_from_self).reshape(-1),
            shifts_now.reshape(-1),
        ]
    )
    split_three = [part.reshape(owners, -1) for part in vector_grads]
    pk_at = 5
    pk_thirds = placed(pk_bias_grad, 3).reshape(3, model_width)
    split_three[pk_at : pk_at + 1] = [
        pk_thirds[:2].reshape(owners, -1),
        pk_thirds[2].reshape(owners, -1),
    ]
    split_three.append(jnp.broadcast_to(table_grads[None], (owners, table_grads.shape[0])))
    summed_sizes = [part.shape[1] for part in split_three]
    row_blocks = after(column_blocks(row_owned), shift_total)
    row_sum = jnp.sum(swap(row_blocks, "seq").astype(jnp.float32), 0)
    vector_rows = after(jnp.concatenate(split_three, 1).astype(low), row_sum)
    vector_pad = -vector_rows.shape[1] % own_rows
    vector_rows = jnp.pad(vector_rows, ((0, 0), (0, vector_pad)))
    latent_mark = jnp.arange(owners) == lax.axis_index("fsdp")
    shift_mine = jnp.where(latent_mark[:, None], shift_total.astype(low), jnp.zeros((), low))
    shift_mine = jnp.broadcast_to(
        shift_mine.reshape(1, own_rows, -1), (owners, own_rows, owners * owners)
    )
    tail_sum = sum_owners(
        pack_tail(
            normed_own,
            grad_rows,
            pk_weight_grad,
            fit_rows(kv_weight_grad.astype(low).reshape(owners, -1, 2 * width), own_rows),
            jnp.concatenate([vector_rows.reshape(owners, own_rows, -1), shift_mine], 2),
        )
    ).astype(low)
    shift_all = tail_sum[:, -owners * owners :].reshape(owners, model_width)
    shift_all = shift_all.astype(jnp.float32)
    tail_sum = tail_sum[:, : -owners * owners]

    lead = 7 * width
    tail_all = spread(
        jnp.concatenate([tail_sum[:, :lead], row_sum.astype(low), tail_sum[:, lead:]], 1), "seq"
    )
    sk_total, pk_total, kv_total, row_total, small_total = lay_tail(
        tail_all, cross_kv_weight.shape[0]
    )
    at_total = row_total[:, :model_width]
    cq_total = row_total[:, model_width : 2 * model_width]
    cr_total = row_total[:, 2 * model_width :]
    small_total = small_total.reshape(-1)
    vector_totals = []
    start = 0
    for size in summed_sizes:
        vector_totals.append(small_total[start : start + size])
        start += size
    table_total = vector_totals.pop()
    gains_total = table_total[: gain_table.size].reshape(gain_table.shape)
    shifts_total = table_total[gain_table.size :].reshape(shift_table.shape)
    md_weight_grad = lax.dot_general(
        lifted_own.astype(jnp.float32),
        shift_all,
        (((0,), (0,)), ((), ())),
        precision=lax.Precision.HIGHEST,
        preferred_element_type=jnp.float32,
    )
    md_bias_grad = lax.dynamic_slice_in_dim(
        jnp.sum(shift_all, 0), lax.axis_index("fsdp") * own_rows, own_rows, 0
    )
    lifted_part = lax.dot_general(
        shift_all,
        mod_weight.astype(jnp.float32),
        (((1,), (1,)), ((), ())),
        precision=lax.Precision.HIGHEST,
        preferred_element_type=jnp.float32,
    )
    lifted_grad = swap(after(lifted_part, tail_all), "fsdp").reshape(1, model_width)
    condition_grad = silu_pull(lifted_grad)[0]

    up_total, down_total = lay_units(mlp_all_grads, own_rows, model_width)
    (
        sk_gain_total,
        sk_shift_total,
        sk_bias_total,
        one_gain_total,
        one_shift_total,
        pk_bias_total,
        value_bias_total,
        at_bias_total,
        three_gain_total,
        three_shift_total,
        cq_bias_total,
        kv_bias_total,
        cr_bias_total,
        two_gain_total,
        two_shift_total,
        up_bias_total,
        down_bias_total,
    ) = vector_totals
    return (
        layer_out,
        joined_grad[:, :model_width].astype(low)[None],
        joined_grad[:, model_width:].astype(low)[None],
        text_total[None],
        condition_grad,
        sk_gain_total,
        sk_shift_total,
        sk_total,
        sk_bias_total,
        md_weight_grad,
        md_bias_grad,
        one_gain_total,
        one_shift_total,
        pk_total,
        pk_bias_total,
        value_bias_total,
        gains_total,
        shifts_total,
        at_total,
        at_bias_total,
        three_gain_total,
        three_shift_total,
        cq_total,
        cq_bias_total,
        kv_total,
        kv_bias_total,
        cr_total,
        cr_bias_total,
        two_gain_total,
        two_shift_total,
        up_total,
        up_bias_total,
        down_total,
        down_bias_total,
    )


def solution(mesh):
    in_specs = (
        P("fsdp", "seq", None),
        P("fsdp", "seq", None),
        P("fsdp", None, None),
        P("fsdp", None),
        P("seq", None),
        P("fsdp", "seq", None),
        P("fsdp"),
        P("fsdp"),
        P("fsdp", None),
        P("fsdp"),
        P("fsdp", None),
        P("fsdp"),
        P("fsdp"),
        P("fsdp"),
        P("fsdp", None),
        P("fsdp"),
        P(),
        P(),
        P("fsdp", None),
        P("fsdp"),
        P("fsdp"),
        P("fsdp"),
        P("fsdp", None),
        P("fsdp"),
        P("fsdp", None),
        P("fsdp"),
        P("fsdp", None),
        P("fsdp"),
        P("fsdp"),
        P("fsdp"),
        P("fsdp", None),
        P("fsdp"),
        P("fsdp", None),
        P("fsdp"),
    )
    out_specs = (
        P("fsdp", "seq", None),
        P("fsdp", "seq", None),
        P("fsdp", "seq", None),
        P("fsdp", None, None),
        P("fsdp", None),
        P("fsdp"),
        P("fsdp"),
        P("fsdp", None),
        P("fsdp"),
        P("fsdp", None),
        P("fsdp"),
        P("fsdp"),
        P("fsdp"),
        P("fsdp", None),
        P("fsdp"),
        P("fsdp"),
        P(),
        P(),
        P("fsdp", None),
        P("fsdp"),
        P("fsdp"),
        P("fsdp"),
        P("fsdp", None),
        P("fsdp"),
        P("fsdp", None),
        P("fsdp"),
        P("fsdp", None),
        P("fsdp"),
        P("fsdp"),
        P("fsdp"),
        P("fsdp", None),
        P("fsdp"),
        P("fsdp", None),
        P("fsdp"),
    )
    return jax.shard_map(local, mesh=mesh, in_specs=in_specs, out_specs=out_specs, check_vma=False)
```

```python
import functools
import math

import jax
import jax.numpy as jnp
from jax import lax
from jax.experimental import pallas as pl
from jax.experimental.pallas import tpu as pltpu
from jax.sharding import PartitionSpec as P


def layer_norm(inputs, gain_vector, shift_vector):
    centred = inputs - jnp.mean(inputs, -1, keepdims=True)
    variance = jnp.mean(centred * centred, -1, keepdims=True)
    return centred * lax.rsqrt(variance + 1e-06) * gain_vector + shift_vector


def rotary_tables(positions, head_dim):
    quarter = head_dim // 4
    exponent = jnp.arange(quarter, dtype=jnp.float32) * (2.0 / (head_dim // 2))
    inverse = jnp.power(jnp.float32(10000.0), -exponent)
    places = positions.astype(jnp.float32)
    angle_rows = places[:, 0:1] * inverse
    angle_cols = places[:, 1:2] * inverse
    return (jnp.cos(angle_rows), jnp.sin(angle_rows), jnp.cos(angle_cols), jnp.sin(angle_cols))


def rotate(inputs, tables):
    cos_rows, sin_rows, cos_cols, sin_cols = tuple((one_table[:, None, :] for one_table in tables))
    quarter = inputs.shape[-1] // 4
    first_a = inputs[..., :quarter]
    first_b = inputs[..., quarter : 2 * quarter]
    second_a = inputs[..., 2 * quarter : 3 * quarter]
    second_b = inputs[..., 3 * quarter :]
    return jnp.concatenate(
        [
            first_a * cos_rows - first_b * sin_rows,
            first_a * sin_rows + first_b * cos_rows,
            second_a * cos_cols - second_b * sin_cols,
            second_a * sin_cols + second_b * cos_cols,
        ],
        -1,
    )


def head_norm(inputs, gain_vector, shift_vector, head_dim):
    row_count = inputs.shape[0]
    shaped = inputs.reshape(row_count, -1, head_dim)
    return layer_norm(shaped, gain_vector, shift_vector).reshape(row_count, -1)


def head_rotary(inputs, gain_vector, shift_vector, tables, head_dim):
    row_count = inputs.shape[0]
    shaped = inputs.reshape(row_count, -1, head_dim)
    return rotate(layer_norm(shaped, gain_vector, shift_vector), tables).reshape(row_count, -1)


def matmul(left_side, right_side):
    return jnp.dot(left_side, right_side, preferred_element_type=jnp.float32)


def contract_rows(left_side, right_side):
    return lax.dot_general(
        left_side, right_side, (((0,), (0,)), ((), ())), preferred_element_type=jnp.float32
    )


def contract_cols(left_side, right_side):
    return lax.dot_general(
        left_side, right_side, (((1,), (1,)), ((), ())), preferred_element_type=jnp.float32
    )


def column_sums(grads_low):
    return jnp.sum(grads_low.astype(jnp.float32), 0)


def to_float(vectors):
    return tuple((one_vector.astype(jnp.float32) for one_vector in vectors))


def turn_tables(places, head_dim):
    cos_rows, sin_rows, cos_cols, sin_cols = rotary_tables(places, head_dim)
    return (
        jnp.concatenate([cos_rows, cos_rows, cos_cols, cos_cols], 1),
        jnp.concatenate([-sin_rows, sin_rows, -sin_cols, sin_cols], 1),
    )


def normalised(values):
    centred = values - jnp.mean(values, -1, keepdims=True)
    scale = lax.rsqrt(jnp.mean(centred * centred, -1, keepdims=True) + 1e-06)
    return centred * scale, scale


def partners(values):
    quarter = values.shape[1] // 4
    return jnp.concatenate(
        [
            values[:, quarter : 2 * quarter],
            values[:, :quarter],
            values[:, 3 * quarter :],
            values[:, 2 * quarter : 3 * quarter],
        ],
        1,
    )


def norm_turn(values, gain, shift, cos_now, sin_now):
    turned = normalised(values)[0] * gain + shift
    return turned * cos_now + partners(turned) * sin_now


def norm_turn_back(grad, values, gain, cos_now, sin_now):
    grad = grad.astype(jnp.bfloat16).astype(jnp.float32)
    grad = grad * cos_now - partners(grad) * sin_now
    normal, scale = normalised(values)
    scaled = grad * gain
    mean_one = jnp.mean(scaled, -1, keepdims=True)
    mean_two = jnp.mean(scaled * normal, -1, keepdims=True)
    return (
        scale * (scaled - mean_one - normal * mean_two),
        jnp.sum(grad * normal, 0, keepdims=True),
        jnp.sum(grad, 0, keepdims=True),
    )


def self_forward_kernel(
    entry_ref,
    weight_ref,
    bias_ref,
    gains_ref,
    shifts_ref,
    cos_ref,
    sin_ref,
    mixed_ref,
    heads_ref,
    pre_ref,
    totals_ref,
    *,
    scale,
):
    low = jnp.bfloat16
    count, all_tokens, head_dim = heads_ref.shape[1:]
    packed = matmul(entry_ref[...], weight_ref[...]) + bias_ref[...]
    pre_ref[...] = packed[:, : 2 * count * head_dim]
    cos_now, sin_now = cos_ref[...], sin_ref[...]
    for head in range(count):
        for kind in range(3):
            start = (kind * count + head) * head_dim
            part = packed[:, start : start + head_dim]
            if kind < 2:
                part = norm_turn(
                    part,
                    gains_ref[kind : kind + 1],
                    shifts_ref[kind : kind + 1],
                    cos_now,
                    sin_now,
                )
            heads_ref[kind, head] = part.astype(low)
    step = min(512, all_tokens)
    for start in range(0, all_tokens, step):
        mixed = []
        for head in range(count):
            query_block = heads_ref[0, head, start : start + step]
            scores = contract_cols(query_block, heads_ref[1, head]) * scale
            row_top = jnp.max(scores, -1, keepdims=True)
            weights = jnp.exp(scores - row_top)
            totals = jnp.sum(weights, -1, keepdims=True)
            probs = (weights * (1.0 / totals)).astype(low)
            mixed.append(matmul(probs, heads_ref[2, head]))
            totals_ref[head, start : start + step] = row_top + jnp.log(totals)
        mixed_ref[start : start + step] = jnp.concatenate(mixed, 1).astype(low)


def self_forward(entry_all, weight, bias, gains, shifts, cos_now, sin_now):
    all_tokens, head_dim = cos_now.shape
    count = weight.shape[1] // (3 * head_dim)
    return pl.pallas_call(
        functools.partial(self_forward_kernel, scale=1.0 / math.sqrt(head_dim)),
        out_shape=[
            jax.ShapeDtypeStruct((all_tokens, count * head_dim), jnp.bfloat16),
            jax.ShapeDtypeStruct((3, count, all_tokens, head_dim), jnp.bfloat16),
            jax.ShapeDtypeStruct((all_tokens, 2 * count * head_dim), jnp.float32),
            jax.ShapeDtypeStruct((count, all_tokens, 1), jnp.float32),
        ],
        compiler_params=pltpu.CompilerParams(vmem_limit_bytes=50 * 1024 * 1024),
        cost_estimate=pl.CostEstimate(
            flops=2 * all_tokens * weight.size + 4 * count * all_tokens**2 * head_dim,
            bytes_accessed=2 * entry_all.size + 2 * weight.size + 16 * all_tokens * weight.shape[1],
            transcendentals=count * all_tokens**2,
        ),
        name="self_forward",
    )(entry_all, weight, bias, gains, shifts, cos_now, sin_now)


def self_backward_kernel(
    heads_ref, totals_ref, grad_ref, pre_ref, gains_ref, cos_ref, sin_ref, out_ref, sums_ref, *, scale
):
    low = jnp.bfloat16
    count, all_tokens, head_dim = heads_ref.shape[1:]
    cos_now, sin_now = cos_ref[...], sin_ref[...]
    step = min(512, all_tokens)
    lanes = [None] * (3 * count)
    sums = None
    for head in range(count):
        keys_now = heads_ref[1, head]
        values_now = heads_ref[2, head]
        keys_grad, values_grad, query_grads = 0.0, 0.0, []
        for start in range(0, all_tokens, step):
            query_block = heads_ref[0, head, start : start + step]
            grad_block = grad_ref[start : start + step, head * head_dim : (head + 1) * head_dim]
            probs = jnp.exp(
                contract_cols(query_block, keys_now) * scale
                - totals_ref[head, start : start + step]
            )
            weighted = probs * contract_cols(grad_block, values_now)
            scores_grad = weighted - probs * jnp.sum(weighted, -1, keepdims=True)
            scores_low = (scores_grad * scale).astype(low)
            query_grads.append(matmul(scores_low, keys_now))
            keys_grad += contract_rows(scores_low, query_block)
            values_grad += contract_rows(probs.astype(low), grad_block)
        grads = (jnp.concatenate(query_grads, 0), keys_grad)
        parts = []
        for kind in range(2):
            start = (kind * count + head) * head_dim
            back, gain_sum, shift_sum = norm_turn_back(
                grads[kind],
                pre_ref[:, start : start + head_dim],
                gains_ref[kind : kind + 1],
                cos_now,
                sin_now,
            )
            lanes[kind * count + head] = back
            parts += [gain_sum, shift_sum]
        lanes[2 * count + head] = values_grad
        parts = jnp.concatenate(parts, 0)
        sums = parts if sums is None else sums + parts
    out_ref[...] = jnp.concatenate(lanes, 1).astype(low)
    sums_ref[...] = sums


def self_backward(heads, totals, grad_out, pre, gains, cos_now, sin_now):
    count, all_tokens, head_dim = heads.shape[1:]
    return pl.pallas_call(
        functools.partial(self_backward_kernel, scale=1.0 / math.sqrt(head_dim)),
        out_shape=[
            jax.ShapeDtypeStruct((all_tokens, 3 * count * head_dim), jnp.bfloat16),
            jax.ShapeDtypeStruct((4, head_dim), jnp.float32),
        ],
        compiler_params=pltpu.CompilerParams(vmem_limit_bytes=50 * 1024 * 1024),
        cost_estimate=pl.CostEstimate(
            flops=10 * count * all_tokens**2 * head_dim,
            bytes_accessed=24 * count * all_tokens * head_dim,
            transcendentals=count * all_tokens**2,
        ),
        name="self_backward",
    )(heads, totals, grad_out, pre, gains, cos_now, sin_now)


def cross_forward_kernel(
    pre_ref, text_ref, gain_ref, shift_ref, cos_ref, sin_ref, mixed_ref, query_ref, totals_ref, *, scale, valid
):
    low = jnp.bfloat16
    head_dim = cos_ref.shape[1]
    heads = pre_ref.shape[1] // head_dim
    count = heads // text_ref.shape[0]
    width = count * head_dim
    cos_now, sin_now = cos_ref[...], sin_ref[...]
    mixed, queries = [], []
    for head in range(heads):
        lanes = slice(head * head_dim, (head + 1) * head_dim)
        query = norm_turn(pre_ref[:, lanes], gain_ref[...], shift_ref[...], cos_now, sin_now)
        query = query.astype(low)
        queries.append(query)
        start = (head % count) * head_dim
        text = text_ref[head // count]
        scores = contract_cols(query, text[:, start : start + head_dim]) * scale
        column = lax.broadcasted_iota(jnp.int32, scores.shape, 1)
        scores = jnp.where(column < valid, scores, -1e30)
        row_top = jnp.max(scores, -1, keepdims=True)
        weights = jnp.exp(scores - row_top)
        totals = jnp.sum(weights, -1, keepdims=True)
        probs = (weights * (1.0 / totals)).astype(low)
        mixed.append(matmul(probs, text[:, width + start : width + start + head_dim]))
        totals_ref[head] = row_top + jnp.log(totals)
    mixed_ref[...] = jnp.concatenate(mixed, 1).astype(low)
    query_ref[...] = jnp.concatenate(queries, 1)


def cross_forward(pre, text, gain, shift, cos_now, sin_now, valid):
    tokens, model_width = pre.shape
    head_dim = cos_now.shape[1]
    heads = model_width // head_dim
    return pl.pallas_call(
        functools.partial(cross_forward_kernel, scale=1.0 / math.sqrt(head_dim), valid=valid),
        out_shape=[
            jax.ShapeDtypeStruct((tokens, model_width), jnp.bfloat16),
            jax.ShapeDtypeStruct((tokens, model_width), jnp.bfloat16),
            jax.ShapeDtypeStruct((heads, tokens, 1), jnp.float32),
        ],
        compiler_params=pltpu.CompilerParams(vmem_limit_bytes=40 * 1024 * 1024),
        cost_estimate=pl.CostEstimate(
            flops=4 * tokens * text.shape[1] * model_width,
            bytes_accessed=2 * text.size + 8 * pre.size,
            transcendentals=heads * tokens * text.shape[1],
        ),
        name="cross_forward",
    )(pre, text, gain, shift, cos_now, sin_now)


def cross_backward_kernel(
    query_ref,
    text_ref,
    totals_ref,
    grad_ref,
    pre_ref,
    gain_ref,
    cos_ref,
    sin_ref,
    pre_grad_ref,
    text_grad_ref,
    sums_ref,
    *,
    scale,
    valid,
):
    low = jnp.bfloat16
    head_dim = cos_ref.shape[1]
    ways = text_ref.shape[0]
    count = query_ref.shape[1] // head_dim // ways
    width = count * head_dim
    cos_now, sin_now = cos_ref[...], sin_ref[...]
    backs, sums = [], 0.0
    for way in range(ways):
        text = text_ref[way]
        text_grads = [None] * (2 * count)
        for one in range(count):
            head = way * count + one
            lanes = slice(head * head_dim, (head + 1) * head_dim)
            query = query_ref[:, lanes]
            grad = grad_ref[:, lanes]
            keys_now = text[:, one * head_dim : (one + 1) * head_dim]
            values_now = text[:, width + one * head_dim : width + (one + 1) * head_dim]
            probs = jnp.exp(contract_cols(query, keys_now) * scale - totals_ref[head])
            column = lax.broadcasted_iota(jnp.int32, probs.shape, 1)
            probs = jnp.where(column < valid, probs, 0.0)
            weighted = probs * contract_cols(grad, values_now)
            scores_grad = weighted - probs * jnp.sum(weighted, -1, keepdims=True)
            scores_low = (scores_grad * scale).astype(low)
            back, gain_sum, shift_sum = norm_turn_back(
                matmul(scores_low, keys_now), pre_ref[:, lanes], gain_ref[...], cos_now, sin_now
            )
            backs.append(back)
            sums += jnp.concatenate([gain_sum, shift_sum], 0)
            text_grads[one] = contract_rows(scores_low, query)
            text_grads[count + one] = contract_rows(probs.astype(low), grad)
        text_grad_ref[way] = jnp.concatenate(text_grads, 1).astype(low)
    pre_grad_ref[...] = jnp.concatenate(backs, 1).astype(low)
    sums_ref[...] = sums


def cross_backward(query, text, totals, grad, pre, gain, cos_now, sin_now, valid):
    tokens, model_width = pre.shape
    head_dim = cos_now.shape[1]
    ways, text_rows = text.shape[:2]
    return pl.pallas_call(
        functools.partial(cross_backward_kernel, scale=1.0 / math.sqrt(head_dim), valid=valid),
        out_shape=[
            jax.ShapeDtypeStruct((tokens, model_width), jnp.bfloat16),
            jax.ShapeDtypeStruct((ways, text_rows, 2 * model_width // ways), jnp.bfloat16),
            jax.ShapeDtypeStruct((2, head_dim), jnp.float32),
        ],
        compiler_params=pltpu.CompilerParams(vmem_limit_bytes=40 * 1024 * 1024),
        cost_estimate=pl.CostEstimate(
            flops=10 * tokens * text_rows * model_width,
            bytes_accessed=4 * text.size + 10 * pre.size,
            transcendentals=tokens * text_rows * model_width // head_dim,
        ),
        name="cross_backward",
    )(query, text, totals, grad, pre, gain, cos_now, sin_now)


def row_grads_kernel(left_ref, far_left_ref, right_ref, far_right_ref, out_ref):
    product = contract_rows(left_ref[0], right_ref[0])
    product += contract_rows(far_left_ref[0], far_right_ref[0])
    rows = out_ref.shape[1]
    for chip in range(out_ref.shape[0]):
        out_ref[chip] = product[chip * rows : (chip + 1) * rows].astype(out_ref.dtype)


def row_grads(lefts, rights, owners):
    count, tokens, width = lefts.shape
    rows = width // owners
    core = lax.axis_index("fsdp") % 2
    by_core = lefts.reshape(count, tokens, owners // 2, 2, rows).transpose(3, 0, 1, 2, 4)
    by_core = by_core.reshape(2, count, tokens, width // 2)
    near = lax.dynamic_index_in_dim(by_core, core, 0, False)
    far = swap_cores(lax.dynamic_index_in_dim(by_core, 1 - core, 0, False))
    left_spec = pl.BlockSpec((1, tokens, width // 2), lambda i: (i, 0, 0))
    right_spec = pl.BlockSpec((1, tokens, width), lambda i: (i, 0, 0))
    return pl.pallas_call(
        row_grads_kernel,
        grid=(count,),
        in_specs=[left_spec, left_spec, right_spec, right_spec],
        out_specs=pl.BlockSpec((owners // 2, rows, width), lambda i: (0, 0, i)),
        out_shape=jax.ShapeDtypeStruct((owners // 2, rows, count * width), jnp.bfloat16),
        compiler_params=pltpu.CompilerParams(vmem_limit_bytes=48 * 1024 * 1024),
        cost_estimate=pl.CostEstimate(
            flops=2 * count * tokens * width * width,
            bytes_accessed=2 * count * (width * width // 2 + 3 * tokens * width),
            transcendentals=0,
        ),
        name="row_grads",
    )(near, far, rights, swap_cores(rights))


def side_by_side(pieces):
    return jnp.concatenate([piece.astype(jnp.float32) for piece in pieces], 1)


def pack_kernel(normed_ref, grads_ref, packed_ref, text_ref, small_ref, out_ref):
    owners, rows = text_ref.shape[:2]
    product = contract_rows(normed_ref[...], grads_ref[...])
    count = product.shape[0] // owners
    folds = rows // count
    lanes = product.shape[1] // folds
    for owner in range(owners):
        skip = product[owner * count : (owner + 1) * count]
        skip = jnp.concatenate(
            [skip[:, fold * lanes : (fold + 1) * lanes] for fold in range(folds)], 0
        )
        line = side_by_side(
            [
                skip,
                packed_ref[owner * rows : (owner + 1) * rows],
                text_ref[owner],
                small_ref[owner],
            ]
        )
        out_ref[owner % 2, owner // 2] = line.astype(out_ref.dtype)


def pack_tail(normed, grads, packed, text, small):
    owners, rows = text.shape[:2]
    lanes = 2 * text.shape[2] // 2 + packed.shape[1] + text.shape[2] + small.shape[2]
    return pl.pallas_call(
        pack_kernel,
        out_shape=jax.ShapeDtypeStruct((2, owners // 2, rows, lanes), jnp.bfloat16),
        compiler_params=pltpu.CompilerParams(vmem_limit_bytes=48 * 1024 * 1024),
        cost_estimate=pl.CostEstimate(
            flops=2 * normed.size * grads.shape[1],
            bytes_accessed=2 * normed.size + 4 * owners * rows * lanes,
            transcendentals=0,
        ),
        name="pack_tail",
    )(normed, grads, packed, text, small)


def tail_kernel(all_ref, skip_ref, packed_ref, text_ref, whole_ref, small_ref):
    ways, rows = all_ref.shape[:2]
    model_width = skip_ref.shape[1]
    width = model_width // ways

    def joined(start, count, size):
        return side_by_side(
            [all_ref[way, :, start : start + size][:count] for way in range(ways)]
        )

    count = 2 * rows // ways
    folds = rows // count
    skip = []
    for way in range(ways):
        block = all_ref[way, :, : 2 * width].astype(jnp.float32)
        skip.append(
            jnp.concatenate(
                [block[fold * count : (fold + 1) * count] for fold in range(folds)], 1
            )
        )
    skip_ref[...] = jnp.concatenate(skip, 0)
    for third in range(3):
        packed_ref[:, third * model_width : (third + 1) * model_width] = joined(
            (2 + third) * width, rows, width
        )
    for side in range(2):
        text_ref[:, side * model_width : (side + 1) * model_width] = joined(
            (5 + side) * width, text_ref.shape[0], width
        )
    whole_ref[...] = joined(7 * width, rows, 3 * width)
    total = all_ref[0, :, 10 * width :].astype(jnp.float32)
    for way in range(1, ways):
        total += all_ref[way, :, 10 * width :].astype(jnp.float32)
    small_ref[...] = total


def lay_tail(blocks, text_rows):
    ways, rows, lanes = blocks.shape
    width = 2 * rows
    model_width = ways * width
    return pl.pallas_call(
        tail_kernel,
        out_shape=[
            jax.ShapeDtypeStruct((2 * rows, model_width), jnp.float32),
            jax.ShapeDtypeStruct((rows, 3 * model_width), jnp.float32),
            jax.ShapeDtypeStruct((text_rows, 2 * model_width), jnp.float32),
            jax.ShapeDtypeStruct((rows, 3 * model_width), jnp.float32),
            jax.ShapeDtypeStruct((rows, lanes - 10 * width), jnp.float32),
        ],
        compiler_params=pltpu.CompilerParams(vmem_limit_bytes=40 * 1024 * 1024),
        name="lay_tail",
    )(blocks)


def skip_back_kernel(grad_ref, first_ref, second_ref, out_ref):
    grad = grad_ref[...]
    halves = [contract_cols(grad, half_ref[...]) for half_ref in (first_ref, second_ref)]
    rows = grad.shape[1] // 16
    out_ref[...] = side_by_side(
        [half[:, i * rows : (i + 1) * rows] for i in range(16) for half in halves]
    )


def skip_back(grad_low, first_rows):
    tokens, model_width = grad_low.shape
    return pl.pallas_call(
        skip_back_kernel,
        grid=(1,),
        in_specs=[
            pl.BlockSpec((tokens, model_width), lambda i: (0, 0)),
            pl.BlockSpec((model_width, model_width), lambda i: (0, 0)),
            pl.BlockSpec((model_width, model_width), lambda i: (0, 1)),
        ],
        out_specs=pl.BlockSpec((tokens, 2 * model_width), lambda i: (0, 0)),
        out_shape=jax.ShapeDtypeStruct((tokens, 2 * model_width), jnp.float32),
        compiler_params=pltpu.CompilerParams(vmem_limit_bytes=48 * 1024 * 1024),
        cost_estimate=pl.CostEstimate(
            flops=4 * tokens * model_width * model_width,
            bytes_accessed=4 * model_width * (model_width + 2 * tokens),
            transcendentals=0,
        ),
        name="skip_back",
    )(grad_low, first_rows, first_rows)


def units_kernel(all_ref, up_ref, down_ref):
    ways = all_ref.shape[0]
    rows, hidden = up_ref.shape
    units = hidden // ways
    owners = 16
    own = units // owners
    for owner in range(owners):
        start = owner * ways * own
        up_ref[:, start : start + ways * own] = side_by_side(
            [all_ref[way, :rows, owner * own : (owner + 1) * own] for way in range(ways)]
        )
    model_width = down_ref.shape[1]
    split = min(units, model_width)
    for way in range(ways):
        place = slice(way * own, (way + 1) * own)
        down_ref[place, :split] = all_ref[way, :own, units : units + split].astype(jnp.float32)
        if split < model_width:
            down_ref[place, split:] = all_ref[
                way, own : 2 * own, units : units + model_width - split
            ].astype(jnp.float32)


def lay_units(blocks, rows, model_width):
    ways, lines, lanes = blocks.shape
    units = lanes // 2
    return pl.pallas_call(
        units_kernel,
        out_shape=[
            jax.ShapeDtypeStruct((rows, ways * units), jnp.float32),
            jax.ShapeDtypeStruct((ways * units // 16, model_width), jnp.float32),
        ],
        compiler_params=pltpu.CompilerParams(vmem_limit_bytes=40 * 1024 * 1024),
        name="lay_units",
    )(blocks)


def fold_down(part, units, lines):
    first = part[..., :units]
    rest = part[..., units:]
    pad = [(0, 0)] * (part.ndim - 1) + [(0, units - rest.shape[-1])]
    both = jnp.concatenate([first, jnp.pad(rest, pad)], -2)
    return fit_rows(both, lines)


def fit_rows(part, lines):
    pad = [(0, 0)] * part.ndim
    pad[-2] = (0, lines - part.shape[-2])
    return jnp.pad(part, pad)


def swap(blocks, axis_name):
    return lax.all_to_all(blocks, axis_name, split_axis=0, concat_axis=0, tiled=True)


def spread(part, axis_name):
    size = lax.axis_size(axis_name)
    return swap(jnp.broadcast_to(part[None], (size,) + part.shape), axis_name)


def grid_place():
    index = lax.axis_index("seq")
    return index // 4, index % 4


def grid_send(value, pair, step):
    links = [(i, ((i // 4) ^ pair) * 4 + (i + step) % 4) for i in range(8)]
    return lax.ppermute(value, "seq", links)


def gather_tokens(part):
    pair, ring = grid_place()
    mate = grid_send(part, 1, 0)
    below = grid_send(part, 0, 1)
    above = grid_send(part, 0, -1)
    far = grid_send(part, 0, 2)
    mate_below = grid_send(mate, 0, 1)
    mate_above = grid_send(mate, 0, -1)
    mate_far = grid_send(far, 1, 0)
    here, there = pair * 4, (1 - pair) * 4
    buffer = jnp.zeros((8,) + part.shape, part.dtype)
    for one, spot in (
        (part, here + ring),
        (mate, there + ring),
        (below, here + (ring + 3) % 4),
        (above, here + (ring + 1) % 4),
        (far, here + (ring + 2) % 4),
        (mate_below, there + (ring + 3) % 4),
        (mate_above, there + (ring + 1) % 4),
        (mate_far, there + (ring + 2) % 4),
    ):
        buffer = lax.dynamic_update_index_in_dim(buffer, one, spot, 0)
    return buffer.reshape((-1,) + part.shape[1:])


def gather_behind(part):
    return spread(part, "seq").reshape((-1,) + part.shape[1:])


def sum_tokens(partial):
    low = jnp.bfloat16
    blocks = partial.astype(low).reshape((8, -1) + partial.shape[1:])
    pair, ring = grid_place()

    def meant(mate, step):
        spot = jnp.where(mate, 1 - pair, pair) * 4 + (ring + step) % 4
        return lax.dynamic_index_in_dim(blocks, spot, 0, False)

    def total(*parts):
        return sum(part.astype(jnp.float32) for part in parts)

    far_mate = grid_send(meant(True, 2), 1, 0)
    mate_below = grid_send(meant(True, 1), 0, 1)
    mate_above = grid_send(meant(True, 3), 0, -1)
    below = grid_send(meant(False, 1), 0, 1)
    above = grid_send(meant(False, 3), 0, -1)
    far = grid_send(total(meant(False, 2), far_mate).astype(low), 0, 2)
    mate = grid_send(total(meant(True, 0), mate_below, mate_above).astype(low), 1, 0)
    return total(meant(False, 0), below, above, far, mate)


def sum_behind(partial):
    blocks = partial.astype(jnp.bfloat16).reshape((8, -1) + partial.shape[1:])
    return jnp.sum(swap(blocks, "seq").astype(jnp.float32), 0)


def column_blocks(values):
    size = lax.axis_size("seq")
    rows = values.shape[0]
    return values.reshape(rows, size, -1).transpose(1, 0, 2)


def own_columns(weight, groups, size, place):
    rows = weight.shape[0]
    parts = weight.reshape(rows, groups, size, -1)
    taken = lax.dynamic_slice_in_dim(parts, place, 1, 2)
    return taken.reshape(rows, -1)


def after(values, *others):
    waits = [other[(0,) * other.ndim].astype(jnp.float32) * 0.0 for other in others]
    return values + sum(waits).astype(values.dtype)


def core_groups(owners):
    return [list(range(0, owners, 2)), list(range(1, owners, 2))]


def swap_cores(value):
    return lax.ppermute(value, "fsdp", [(i, i ^ 1) for i in range(lax.axis_size("fsdp"))])


def sum_cores(by_core):
    core = lax.axis_index("fsdp") % 2
    kept = lax.dynamic_index_in_dim(by_core, core, 0, False)
    arrived = swap_cores(lax.dynamic_index_in_dim(by_core, 1 - core, 0, False))
    return (kept.astype(jnp.float32) + arrived.astype(jnp.float32)).astype(jnp.bfloat16)


def scatter_chips(by_chip):
    return lax.psum_scatter(
        by_chip,
        "fsdp",
        scatter_dimension=0,
        axis_index_groups=core_groups(2 * by_chip.shape[0]),
        tiled=False,
    )


def sum_owners(by_core):
    chip = sum_cores(by_core)
    swapped = lax.all_to_all(
        chip,
        "fsdp",
        split_axis=0,
        concat_axis=0,
        axis_index_groups=core_groups(2 * chip.shape[0]),
        tiled=True,
    )
    return jnp.sum(swapped.astype(jnp.float32), 0)


def heads_first(values, head_dim):
    rows = values.shape[0]
    return values.reshape(rows, -1, head_dim).transpose(1, 0, 2)


def heads_last(values):
    return values.transpose(1, 0, 2).reshape(values.shape[1], -1)


def local(
    latent,
    skip_input,
    text_tokens,
    condition,
    positions,
    cotangent,
    skip_gain,
    skip_shift,
    skip_weight,
    skip_bias,
    mod_weight,
    mod_bias,
    norm1_gain,
    norm1_shift,
    qkv_weight,
    qkv_bias,
    head_gains,
    head_shifts,
    attn_weight,
    attn_bias,
    norm3_gain,
    norm3_shift,
    cross_q_weight,
    cross_q_bias,
    cross_kv_weight,
    cross_kv_bias,
    cross_weight,
    cross_bias,
    norm2_gain,
    norm2_shift,
    fc1_weight,
    fc1_bias,
    fc2_weight,
    fc2_bias,
):
    ways = lax.axis_size("seq")
    owners = lax.axis_size("fsdp")
    place = lax.axis_index("seq")
    head_dim = head_gains.shape[1]
    tokens, model_width = latent.shape[1:]
    width = model_width // ways
    low = jnp.bfloat16
    gain_table = head_gains.astype(jnp.float32)
    shift_table = head_shifts.astype(jnp.float32)
    cos_own, sin_own = turn_tables(positions, head_dim)

    own_rows = model_width // owners
    packed_own = own_columns(qkv_weight, 3, ways, place)
    first_own = jnp.concatenate(
        [skip_weight[:own_rows], skip_weight[own_rows:], packed_own], 1
    )
    first_rows = lax.all_gather(first_own, "fsdp", axis=0, tiled=True)
    kv_own = own_columns(cross_kv_weight, 2, ways, place)
    second_own = jnp.concatenate([attn_weight, cross_q_weight, cross_weight], 1)
    unit_rows = fc2_weight.shape[0] // ways
    down_own = lax.dynamic_slice_in_dim(fc2_weight, place * unit_rows, unit_rows, 0)
    up_own = own_columns(fc1_weight, owners, ways, place)
    units = up_own.shape[1]
    lines = max(own_rows, 2 * unit_rows)
    third_own = jnp.concatenate(
        [fit_rows(up_own, lines), fold_down(down_own, units, lines)], 1
    )
    lifted_f, silu_pull = jax.vjp(jax.nn.silu, condition.astype(jnp.float32))
    lifted = lifted_f.astype(low)
    vectors = (
        skip_gain,
        skip_shift,
        skip_bias,
        mod_bias,
        norm1_gain,
        norm1_shift,
        qkv_bias,
        attn_bias,
        norm3_gain,
        norm3_shift,
        cross_q_bias,
        cross_kv_bias,
        cross_bias,
        norm2_gain,
        norm2_shift,
        fc1_bias,
        fc2_bias,
    )
    vector_own = jnp.concatenate(vectors)
    vector_all = swap(
        jnp.concatenate(
            [
                jnp.broadcast_to(vector_own[None], (owners, vector_own.shape[0])),
                lifted.reshape(owners, own_rows),
            ],
            1,
        ),
        "fsdp",
    )
    pieces = []
    start = 0
    for one_vector in vectors:
        size = one_vector.shape[0]
        pieces.append(vector_all[:, start : start + size].reshape(-1).astype(jnp.float32))
        start += size
    lifted_own = vector_all[:, start:]
    (
        sk_gain,
        sk_shift,
        sk_bias,
        md_bias,
        one_gain,
        one_shift,
        pk_bias,
        at_bias,
        three_gain,
        three_shift,
        cq_bias,
        kv_bias,
        cr_bias,
        two_gain,
        two_shift,
        up_bias,
        down_bias,
    ) = pieces
    pk_bias_own = own_columns(pk_bias[None], 3, ways, place)[0]
    kv_bias_own = own_columns(kv_bias[None], 2, ways, place)[0]
    up_bias_own = own_columns(up_bias[None], owners, ways, place)[0]
    shift_row = (
        jnp.sum(swap(matmul(lifted_own, mod_weight), "fsdp"), 0, keepdims=True) + md_bias
    )

    kv_weight = spread(after(kv_own, vector_all), "fsdp").reshape(-1, 2 * width)
    text_now = text_tokens[0]
    text_count = text_now.shape[0]
    text_packed = matmul(text_now, kv_weight) + kv_bias_own
    text_keys_f, tk_pull = jax.vjp(
        lambda values_in, gains_in: head_norm(values_in, gains_in[3], 0.0, head_dim),
        text_packed[:, :width],
        gain_table,
    )
    text_own = jnp.concatenate(
        [text_keys_f.astype(low), text_packed[:, width:].astype(low)], 1
    )
    text_rows = text_count + -text_count % 16
    place_rows = max(text_rows, tokens)
    text_own = jnp.concatenate(
        [
            fit_rows(text_own, place_rows),
            fit_rows(positions.astype(low), place_rows),
        ],
        1,
    )
    text_spread = spread(text_own, "seq")
    cos_all, sin_all = turn_tables(
        text_spread[:, :tokens, 2 * width :].reshape(-1, 2), head_dim
    )
    joined = jnp.concatenate([latent[0], skip_input[0]], 1).astype(jnp.float32)
    normed_f, skip_pull = jax.vjp(layer_norm, joined, sk_gain, sk_shift)
    normed = normed_f.astype(low)
    normed_halves = normed.reshape(tokens, owners, 2, own_rows).transpose(2, 0, 1, 3)
    normed_halves = normed_halves.reshape(2, tokens, model_width)
    normed_rows = normed.reshape(tokens, owners, ways, -1).transpose(2, 0, 1, 3)
    normed_rows = normed_rows.reshape(ways, tokens, -1)
    normed_halves = after(normed_halves, shift_row, text_spread)
    stream_zero = (
        matmul(normed_halves[0], first_rows[:, :model_width])
        + matmul(normed_halves[1], first_rows[:, model_width : 2 * model_width])
        + sk_bias
    )

    pk_weight = first_rows[:, 2 * model_width :]
    second_rows = lax.all_gather(after(second_own, stream_zero), "fsdp", axis=0, tiled=True)
    at_weight = second_rows[:, :model_width]
    cq_weight = second_rows[:, model_width : 2 * model_width]
    cr_weight = second_rows[:, 2 * model_width :]
    entry_f, one_pull = jax.vjp(layer_norm, stream_zero, one_gain, one_shift)
    entry = (entry_f + shift_row).astype(low)

    entry_all = gather_tokens(entry)

    mixed_h, heads_h, packed_pre, self_totals = self_forward(
        entry_all, pk_weight, pk_bias_own[None], gain_table, shift_table, cos_all, sin_all
    )
    all_tokens = entry_all.shape[0]

    def to_heads(values):
        return swap(column_blocks(values), "seq").reshape(all_tokens, -1)

    mixed_normed = swap(
        jnp.concatenate([mixed_h.reshape(ways, tokens, width), normed_rows], 2), "seq"
    )
    mixed = mixed_normed[:, :, :width].transpose(1, 0, 2).reshape(tokens, model_width)
    normed_own = mixed_normed[:, :, width:].reshape(all_tokens, -1)
    third_rows = lax.all_gather(after(third_own, packed_pre), "fsdp", axis=0, tiled=False)
    up_weight = third_rows[:, :own_rows, :units].reshape(model_width, units)
    down_weight = jnp.concatenate(
        [
            third_rows[:, :unit_rows, units : units + min(units, model_width)],
            third_rows[:, unit_rows : 2 * unit_rows, units : units + max(model_width - units, 0)],
        ],
        2,
    ).reshape(units, model_width)
    stream_one = stream_zero + matmul(mixed, at_weight) + at_bias

    cross_in_f, three_pull = jax.vjp(layer_norm, stream_one, three_gain, three_shift)
    cross_in = cross_in_f.astype(low)
    grad_all = lax.all_gather(after(cotangent[0], cross_in), "seq", axis=0, tiled=True)
    cross_pre = matmul(cross_in, cq_weight) + cq_bias
    cross_mixed, cross_query, cross_totals = cross_forward(
        cross_pre, text_spread, gain_table[2:3], shift_table[2:3], cos_own, sin_own, text_count
    )
    stream_two = stream_one + matmul(cross_mixed, cr_weight) + cr_bias

    mlp_in_f, two_pull = jax.vjp(layer_norm, stream_two, two_gain, two_shift)
    mlp_all = gather_tokens(mlp_in_f.astype(low))
    hidden_pre = matmul(mlp_all, up_weight) + after(up_bias_own, grad_all)
    hidden_f, gelu_pull = jax.vjp(
        lambda values_in: jax.nn.gelu(values_in, approximate=True), hidden_pre
    )
    hidden = hidden_f.astype(low)
    out_partial = matmul(hidden, down_weight).astype(low)
    grad_three = cotangent[0].astype(jnp.float32)
    down_bias_grad = column_sums(cotangent[0])
    pre_grad = gelu_pull(contract_cols(grad_all, down_weight))[0].astype(low)
    up_bias_grad = column_sums(pre_grad)
    mlp_in_grad = sum_tokens(contract_cols(pre_grad, up_weight))
    down_grad = contract_rows(hidden, grad_all).astype(low)
    up_grad = contract_rows(mlp_all, pre_grad).astype(low)
    mlp_grads = jnp.concatenate(
        [
            fit_rows(up_grad.reshape(owners, own_rows, units), lines),
            fold_down(down_grad.reshape(owners, unit_rows, model_width), units, lines),
        ],
        2,
    )
    mlp_grads = mlp_grads.reshape(owners // 2, 2, lines, 2 * units).transpose(1, 0, 2, 3)
    mlp_owned = scatter_chips(sum_cores(mlp_grads))
    mlp_in_grad = after(mlp_in_grad, mlp_grads)
    stream_part, two_gain_grad, two_shift_grad = two_pull(mlp_in_grad)
    stream_grad = grad_three + stream_part

    grad_low = stream_grad.astype(low)
    cr_bias_grad = column_sums(grad_low)
    cross_mixed_grad = contract_cols(grad_low, cr_weight).astype(low)

    cross_pre_low, text_parts, cross_sums = cross_backward(
        cross_query,
        text_spread,
        cross_totals,
        cross_mixed_grad,
        cross_pre,
        gain_table[2:3],
        cos_own,
        sin_own,
        text_count,
    )
    text_kv_grad = jnp.sum(swap(text_parts, "seq").astype(jnp.float32), 0)[:text_count]
    cross_out_low = grad_low
    cq_bias_grad = column_sums(cross_pre_low)
    stream_part, three_gain_grad, three_shift_grad = three_pull(
        contract_cols(cross_pre_low, cq_weight)
    )
    stream_grad = stream_grad + stream_part

    grad_low = stream_grad.astype(low)
    at_bias_grad = column_sums(grad_low)
    mixed_grad = contract_cols(grad_low, at_weight).astype(low)
    mixed_back = to_heads(after(mixed_grad, text_kv_grad))
    whole_grads = row_grads(
        jnp.stack([mixed, cross_in, cross_mixed]),
        after(jnp.stack([grad_low, cross_pre_low, cross_out_low]), mlp_owned),
        owners,
    )
    row_owned = scatter_chips(whole_grads)
    mixed_back = after(mixed_back, whole_grads)
    key_pre_grad, gains_from_text = tk_pull(text_kv_grad[:, :width])
    text_grad_low = jnp.concatenate(
        [key_pre_grad.astype(low), text_kv_grad[:, width:].astype(low)], 1
    )
    kv_weight_grad = contract_rows(text_now, text_grad_low)
    kv_bias_grad = column_sums(text_grad_low)
    text_part = contract_cols(text_grad_low, kv_weight)
    text_part = jnp.pad(text_part.astype(low), ((0, -text_count % (8 * ways)), (0, 0)))
    text_sum = sum_behind(text_part)
    packed_grad, self_sums = self_backward(
        heads_h, self_totals, mixed_back, packed_pre, gain_table, cos_all, sin_all
    )
    pk_weight_grad = contract_rows(entry_all, packed_grad)
    entry_grad = sum_tokens(contract_cols(packed_grad, pk_weight))
    pk_bias_grad = column_sums(packed_grad)
    gains_from_self = jnp.concatenate(
        [self_sums[0::2], cross_sums[:1], jnp.zeros_like(cross_sums[:1])], 0
    )
    shifts_now = jnp.concatenate([self_sums[1::2], cross_sums[1:]], 0)
    entry_grad = after(entry_grad, pk_weight_grad)
    shift_part = jnp.sum(entry_grad, 0)
    stream_three = stream_two + sum_tokens(after(out_partial, entry_grad)) + down_bias
    layer_out = stream_three.astype(low)[None]
    stream_part, one_gain_grad, one_shift_grad = one_pull(entry_grad)
    stream_grad = stream_grad + stream_part

    grad_low = stream_grad.astype(low)
    sk_bias_grad = column_sums(grad_low)
    shift_row_own = fit_rows(shift_part.astype(low)[None], 16)
    text_total = gather_behind(text_sum.astype(low))[:text_count]
    tail_grads = spread(jnp.concatenate([after(grad_low, text_total), shift_row_own], 0), "seq")
    grad_rows = tail_grads[:, :tokens].reshape(all_tokens, model_width)
    shift_total = jnp.sum(tail_grads[:, tokens].astype(jnp.float32), 0)
    joined_grad, sk_gain_grad, sk_shift_grad = skip_pull(skip_back(grad_low, first_rows))

    def placed(own, groups):
        parts = jnp.zeros((groups, ways, own.shape[0] // groups), jnp.float32)
        parts = lax.dynamic_update_slice_in_dim(parts, own.reshape(groups, 1, -1), place, 1)
        return parts.reshape(-1)

    vector_grads = (
        sk_gain_grad,
        sk_shift_grad,
        sk_bias_grad,
        one_gain_grad,
        one_shift_grad,
        placed(pk_bias_grad, 3),
        at_bias_grad,
        three_gain_grad,
        three_shift_grad,
        cq_bias_grad,
        placed(kv_bias_grad, 2),
        cr_bias_grad,
        two_gain_grad,
        two_shift_grad,
        placed(up_bias_grad, owners),
        down_bias_grad,
    )
    table_grads = jnp.concatenate(
        [
            (gains_from_text + gains_from_self).reshape(-1),
            shifts_now.reshape(-1),
        ]
    )
    split_three = [part.reshape(owners, -1) for part in vector_grads]
    pk_at = 5
    pk_thirds = placed(pk_bias_grad, 3).reshape(3, model_width)
    split_three[pk_at : pk_at + 1] = [
        pk_thirds[:2].reshape(owners, -1),
        pk_thirds[2].reshape(owners, -1),
    ]
    split_three.append(jnp.broadcast_to(table_grads[None], (owners, table_grads.shape[0])))
    summed_sizes = [part.shape[1] for part in split_three]
    row_blocks = after(column_blocks(row_owned), shift_total)
    row_sum = jnp.sum(swap(row_blocks, "seq").astype(jnp.float32), 0)
    vector_rows = after(jnp.concatenate(split_three, 1).astype(low), row_sum)
    vector_pad = -vector_rows.shape[1] % own_rows
    vector_rows = jnp.pad(vector_rows, ((0, 0), (0, vector_pad)))
    latent_mark = jnp.arange(owners) == lax.axis_index("fsdp")
    shift_mine = jnp.where(latent_mark[:, None], shift_total.astype(low), jnp.zeros((), low))
    shift_mine = jnp.broadcast_to(
        shift_mine.reshape(1, own_rows, -1), (owners, own_rows, owners * owners)
    )
    tail_sum = sum_owners(
        pack_tail(
            normed_own,
            grad_rows,
            pk_weight_grad,
            fit_rows(kv_weight_grad.astype(low).reshape(owners, -1, 2 * width), own_rows),
            jnp.concatenate([vector_rows.reshape(owners, own_rows, -1), shift_mine], 2),
        )
    ).astype(low)
    shift_all = tail_sum[:, -owners * owners :].reshape(owners, model_width)
    shift_all = shift_all.astype(jnp.float32)
    tail_sum = tail_sum[:, : -owners * owners]

    mlp_all_grads = lax.all_gather(after(mlp_owned, row_owned), "seq", axis=0, tiled=False)
    lead = 7 * width
    tail_all = spread(
        jnp.concatenate([tail_sum[:, :lead], row_sum.astype(low), tail_sum[:, lead:]], 1), "seq"
    )
    sk_total, pk_total, kv_total, row_total, small_total = lay_tail(
        tail_all, cross_kv_weight.shape[0]
    )
    at_total = row_total[:, :model_width]
    cq_total = row_total[:, model_width : 2 * model_width]
    cr_total = row_total[:, 2 * model_width :]
    small_total = small_total.reshape(-1)
    vector_totals = []
    start = 0
    for size in summed_sizes:
        vector_totals.append(small_total[start : start + size])
        start += size
    table_total = vector_totals.pop()
    gains_total = table_total[: gain_table.size].reshape(gain_table.shape)
    shifts_total = table_total[gain_table.size :].reshape(shift_table.shape)
    md_weight_grad = lax.dot_general(
        lifted_own.astype(jnp.float32),
        shift_all,
        (((0,), (0,)), ((), ())),
        precision=lax.Precision.HIGHEST,
        preferred_element_type=jnp.float32,
    )
    md_bias_grad = lax.dynamic_slice_in_dim(
        jnp.sum(shift_all, 0), lax.axis_index("fsdp") * own_rows, own_rows, 0
    )
    lifted_part = lax.dot_general(
        shift_all,
        mod_weight.astype(jnp.float32),
        (((1,), (1,)), ((), ())),
        precision=lax.Precision.HIGHEST,
        preferred_element_type=jnp.float32,
    )
    lifted_grad = swap(after(lifted_part, tail_all, mlp_all_grads), "fsdp").reshape(1, model_width)
    condition_grad = silu_pull(lifted_grad)[0]

    up_total, down_total = lay_units(mlp_all_grads, own_rows, model_width)
    (
        sk_gain_total,
        sk_shift_total,
        sk_bias_total,
        one_gain_total,
        one_shift_total,
        pk_bias_total,
        value_bias_total,
        at_bias_total,
        three_gain_total,
        three_shift_total,
        cq_bias_total,
        kv_bias_total,
        cr_bias_total,
        two_gain_total,
        two_shift_total,
        up_bias_total,
        down_bias_total,
    ) = vector_totals
    return (
        layer_out,
        joined_grad[:, :model_width].astype(low)[None],
        joined_grad[:, model_width:].astype(low)[None],
        text_total[None],
        condition_grad,
        sk_gain_total,
        sk_shift_total,
        sk_total,
        sk_bias_total,
        md_weight_grad,
        md_bias_grad,
        one_gain_total,
        one_shift_total,
        pk_total,
        pk_bias_total,
        value_bias_total,
        gains_total,
        shifts_total,
        at_total,
        at_bias_total,
        three_gain_total,
        three_shift_total,
        cq_total,
        cq_bias_total,
        kv_total,
        kv_bias_total,
        cr_total,
        cr_bias_total,
        two_gain_total,
        two_shift_total,
        up_total,
        up_bias_total,
        down_total,
        down_bias_total,
    )


def solution(mesh):
    in_specs = (
        P("fsdp", "seq", None),
        P("fsdp", "seq", None),
        P("fsdp", None, None),
        P("fsdp", None),
        P("seq", None),
        P("fsdp", "seq", None),
        P("fsdp"),
        P("fsdp"),
        P("fsdp", None),
        P("fsdp"),
        P("fsdp", None),
        P("fsdp"),
        P("fsdp"),
        P("fsdp"),
        P("fsdp", None),
        P("fsdp"),
        P(),
        P(),
        P("fsdp", None),
        P("fsdp"),
        P("fsdp"),
        P("fsdp"),
        P("fsdp", None),
        P("fsdp"),
        P("fsdp", None),
        P("fsdp"),
        P("fsdp", None),
        P("fsdp"),
        P("fsdp"),
        P("fsdp"),
        P("fsdp", None),
        P("fsdp"),
        P("fsdp", None),
        P("fsdp"),
    )
    out_specs = (
        P("fsdp", "seq", None),
        P("fsdp", "seq", None),
        P("fsdp", "seq", None),
        P("fsdp", None, None),
        P("fsdp", None),
        P("fsdp"),
        P("fsdp"),
        P("fsdp", None),
        P("fsdp"),
        P("fsdp", None),
        P("fsdp"),
        P("fsdp"),
        P("fsdp"),
        P("fsdp", None),
        P("fsdp"),
        P("fsdp"),
        P(),
        P(),
        P("fsdp", None),
        P("fsdp"),
        P("fsdp"),
        P("fsdp"),
        P("fsdp", None),
        P("fsdp"),
        P("fsdp", None),
        P("fsdp"),
        P("fsdp", None),
        P("fsdp"),
        P("fsdp"),
        P("fsdp"),
        P("fsdp", None),
        P("fsdp"),
        P("fsdp", None),
        P("fsdp"),
    )
    return jax.shard_map(local, mesh=mesh, in_specs=in_specs, out_specs=out_specs, check_vma=False)
```

```python
import functools
import math

import jax
import jax.numpy as jnp
from jax import lax
from jax.experimental import pallas as pl
from jax.experimental.pallas import tpu as pltpu
from jax.sharding import PartitionSpec as P


def layer_norm(inputs, gain_vector, shift_vector):
    centred = inputs - jnp.mean(inputs, -1, keepdims=True)
    variance = jnp.mean(centred * centred, -1, keepdims=True)
    return centred * lax.rsqrt(variance + 1e-06) * gain_vector + shift_vector


def rotary_tables(positions, head_dim):
    quarter = head_dim // 4
    exponent = jnp.arange(quarter, dtype=jnp.float32) * (2.0 / (head_dim // 2))
    inverse = jnp.power(jnp.float32(10000.0), -exponent)
    places = positions.astype(jnp.float32)
    angle_rows = places[:, 0:1] * inverse
    angle_cols = places[:, 1:2] * inverse
    return (jnp.cos(angle_rows), jnp.sin(angle_rows), jnp.cos(angle_cols), jnp.sin(angle_cols))


def rotate(inputs, tables):
    cos_rows, sin_rows, cos_cols, sin_cols = tuple((one_table[:, None, :] for one_table in tables))
    quarter = inputs.shape[-1] // 4
    first_a = inputs[..., :quarter]
    first_b = inputs[..., quarter : 2 * quarter]
    second_a = inputs[..., 2 * quarter : 3 * quarter]
    second_b = inputs[..., 3 * quarter :]
    return jnp.concatenate(
        [
            first_a * cos_rows - first_b * sin_rows,
            first_a * sin_rows + first_b * cos_rows,
            second_a * cos_cols - second_b * sin_cols,
            second_a * sin_cols + second_b * cos_cols,
        ],
        -1,
    )


def head_norm(inputs, gain_vector, shift_vector, head_dim):
    row_count = inputs.shape[0]
    shaped = inputs.reshape(row_count, -1, head_dim)
    return layer_norm(shaped, gain_vector, shift_vector).reshape(row_count, -1)


def head_rotary(inputs, gain_vector, shift_vector, tables, head_dim):
    row_count = inputs.shape[0]
    shaped = inputs.reshape(row_count, -1, head_dim)
    return rotate(layer_norm(shaped, gain_vector, shift_vector), tables).reshape(row_count, -1)


def matmul(left_side, right_side):
    return jnp.dot(left_side, right_side, preferred_element_type=jnp.float32)


def contract_rows(left_side, right_side):
    return lax.dot_general(
        left_side, right_side, (((0,), (0,)), ((), ())), preferred_element_type=jnp.float32
    )


def contract_cols(left_side, right_side):
    return lax.dot_general(
        left_side, right_side, (((1,), (1,)), ((), ())), preferred_element_type=jnp.float32
    )


def column_sums(grads_low):
    return jnp.sum(grads_low.astype(jnp.float32), 0)


def to_float(vectors):
    return tuple((one_vector.astype(jnp.float32) for one_vector in vectors))


def turn_tables(places, head_dim):
    cos_rows, sin_rows, cos_cols, sin_cols = rotary_tables(places, head_dim)
    return (
        jnp.concatenate([cos_rows, cos_rows, cos_cols, cos_cols], 1),
        jnp.concatenate([-sin_rows, sin_rows, -sin_cols, sin_cols], 1),
    )


def normalised(values):
    centred = values - jnp.mean(values, -1, keepdims=True)
    scale = lax.rsqrt(jnp.mean(centred * centred, -1, keepdims=True) + 1e-06)
    return centred * scale, scale


def partners(values):
    quarter = values.shape[1] // 4
    return jnp.concatenate(
        [
            values[:, quarter : 2 * quarter],
            values[:, :quarter],
            values[:, 3 * quarter :],
            values[:, 2 * quarter : 3 * quarter],
        ],
        1,
    )


def norm_turn(values, gain, shift, cos_now, sin_now):
    turned = normalised(values)[0] * gain + shift
    return turned * cos_now + partners(turned) * sin_now


def norm_turn_back(grad, values, gain, cos_now, sin_now):
    grad = grad.astype(jnp.bfloat16).astype(jnp.float32)
    grad = grad * cos_now - partners(grad) * sin_now
    normal, scale = normalised(values)
    scaled = grad * gain
    mean_one = jnp.mean(scaled, -1, keepdims=True)
    mean_two = jnp.mean(scaled * normal, -1, keepdims=True)
    return (
        scale * (scaled - mean_one - normal * mean_two),
        jnp.sum(grad * normal, 0, keepdims=True),
        jnp.sum(grad, 0, keepdims=True),
    )


def self_forward_kernel(
    entry_ref,
    weight_ref,
    bias_ref,
    gains_ref,
    shifts_ref,
    cos_ref,
    sin_ref,
    mixed_ref,
    heads_ref,
    pre_ref,
    totals_ref,
    *,
    scale,
):
    low = jnp.bfloat16
    count, all_tokens, head_dim = heads_ref.shape[1:]
    packed = matmul(entry_ref[...], weight_ref[...]) + bias_ref[...]
    pre_ref[...] = packed[:, : 2 * count * head_dim]
    cos_now, sin_now = cos_ref[...], sin_ref[...]
    for head in range(count):
        for kind in range(3):
            start = (kind * count + head) * head_dim
            part = packed[:, start : start + head_dim]
            if kind < 2:
                part = norm_turn(
                    part,
                    gains_ref[kind : kind + 1],
                    shifts_ref[kind : kind + 1],
                    cos_now,
                    sin_now,
                )
            heads_ref[kind, head] = part.astype(low)
    step = min(512, all_tokens)
    for start in range(0, all_tokens, step):
        mixed = []
        for head in range(count):
            query_block = heads_ref[0, head, start : start + step]
            scores = contract_cols(query_block, heads_ref[1, head]) * scale
            row_top = jnp.max(scores, -1, keepdims=True)
            weights = jnp.exp(scores - row_top)
            totals = jnp.sum(weights, -1, keepdims=True)
            probs = (weights * (1.0 / totals)).astype(low)
            mixed.append(matmul(probs, heads_ref[2, head]))
            totals_ref[head, start : start + step] = row_top + jnp.log(totals)
        mixed_ref[start : start + step] = jnp.concatenate(mixed, 1).astype(low)


def self_forward(entry_all, weight, bias, gains, shifts, cos_now, sin_now):
    all_tokens, head_dim = cos_now.shape
    count = weight.shape[1] // (3 * head_dim)
    return pl.pallas_call(
        functools.partial(self_forward_kernel, scale=1.0 / math.sqrt(head_dim)),
        out_shape=[
            jax.ShapeDtypeStruct((all_tokens, count * head_dim), jnp.bfloat16),
            jax.ShapeDtypeStruct((3, count, all_tokens, head_dim), jnp.bfloat16),
            jax.ShapeDtypeStruct((all_tokens, 2 * count * head_dim), jnp.float32),
            jax.ShapeDtypeStruct((count, all_tokens, 1), jnp.float32),
        ],
        compiler_params=pltpu.CompilerParams(vmem_limit_bytes=50 * 1024 * 1024),
        cost_estimate=pl.CostEstimate(
            flops=2 * all_tokens * weight.size + 4 * count * all_tokens**2 * head_dim,
            bytes_accessed=2 * entry_all.size + 2 * weight.size + 16 * all_tokens * weight.shape[1],
            transcendentals=count * all_tokens**2,
        ),
        name="self_forward",
    )(entry_all, weight, bias, gains, shifts, cos_now, sin_now)


def self_backward_kernel(
    heads_ref, totals_ref, grad_ref, pre_ref, gains_ref, cos_ref, sin_ref, out_ref, sums_ref, *, scale
):
    low = jnp.bfloat16
    count, all_tokens, head_dim = heads_ref.shape[1:]
    cos_now, sin_now = cos_ref[...], sin_ref[...]
    step = min(512, all_tokens)
    lanes = [None] * (3 * count)
    sums = None
    for head in range(count):
        keys_now = heads_ref[1, head]
        values_now = heads_ref[2, head]
        keys_grad, values_grad, query_grads = 0.0, 0.0, []
        for start in range(0, all_tokens, step):
            query_block = heads_ref[0, head, start : start + step]
            grad_block = grad_ref[start : start + step, head * head_dim : (head + 1) * head_dim]
            probs = jnp.exp(
                contract_cols(query_block, keys_now) * scale
                - totals_ref[head, start : start + step]
            )
            weighted = probs * contract_cols(grad_block, values_now)
            scores_grad = weighted - probs * jnp.sum(weighted, -1, keepdims=True)
            scores_low = (scores_grad * scale).astype(low)
            query_grads.append(matmul(scores_low, keys_now))
            keys_grad += contract_rows(scores_low, query_block)
            values_grad += contract_rows(probs.astype(low), grad_block)
        grads = (jnp.concatenate(query_grads, 0), keys_grad)
        parts = []
        for kind in range(2):
            start = (kind * count + head) * head_dim
            back, gain_sum, shift_sum = norm_turn_back(
                grads[kind],
                pre_ref[:, start : start + head_dim],
                gains_ref[kind : kind + 1],
                cos_now,
                sin_now,
            )
            lanes[kind * count + head] = back
            parts += [gain_sum, shift_sum]
        lanes[2 * count + head] = values_grad
        parts = jnp.concatenate(parts, 0)
        sums = parts if sums is None else sums + parts
    out_ref[...] = jnp.concatenate(lanes, 1).astype(low)
    sums_ref[...] = sums


def self_backward(heads, totals, grad_out, pre, gains, cos_now, sin_now):
    count, all_tokens, head_dim = heads.shape[1:]
    return pl.pallas_call(
        functools.partial(self_backward_kernel, scale=1.0 / math.sqrt(head_dim)),
        out_shape=[
            jax.ShapeDtypeStruct((all_tokens, 3 * count * head_dim), jnp.bfloat16),
            jax.ShapeDtypeStruct((4, head_dim), jnp.float32),
        ],
        compiler_params=pltpu.CompilerParams(vmem_limit_bytes=50 * 1024 * 1024),
        cost_estimate=pl.CostEstimate(
            flops=10 * count * all_tokens**2 * head_dim,
            bytes_accessed=24 * count * all_tokens * head_dim,
            transcendentals=count * all_tokens**2,
        ),
        name="self_backward",
    )(heads, totals, grad_out, pre, gains, cos_now, sin_now)


def cross_forward_kernel(
    pre_ref, text_ref, gain_ref, shift_ref, cos_ref, sin_ref, mixed_ref, query_ref, totals_ref, *, scale, valid
):
    low = jnp.bfloat16
    head_dim = cos_ref.shape[1]
    heads = pre_ref.shape[1] // head_dim
    count = heads // text_ref.shape[0]
    width = count * head_dim
    cos_now, sin_now = cos_ref[...], sin_ref[...]
    mixed, queries = [], []
    for head in range(heads):
        lanes = slice(head * head_dim, (head + 1) * head_dim)
        query = norm_turn(pre_ref[:, lanes], gain_ref[...], shift_ref[...], cos_now, sin_now)
        query = query.astype(low)
        queries.append(query)
        start = (head % count) * head_dim
        text = text_ref[head // count]
        scores = contract_cols(query, text[:, start : start + head_dim]) * scale
        column = lax.broadcasted_iota(jnp.int32, scores.shape, 1)
        scores = jnp.where(column < valid, scores, -1e30)
        row_top = jnp.max(scores, -1, keepdims=True)
        weights = jnp.exp(scores - row_top)
        totals = jnp.sum(weights, -1, keepdims=True)
        probs = (weights * (1.0 / totals)).astype(low)
        mixed.append(matmul(probs, text[:, width + start : width + start + head_dim]))
        totals_ref[head] = row_top + jnp.log(totals)
    mixed_ref[...] = jnp.concatenate(mixed, 1).astype(low)
    query_ref[...] = jnp.concatenate(queries, 1)


def cross_forward(pre, text, gain, shift, cos_now, sin_now, valid):
    tokens, model_width = pre.shape
    head_dim = cos_now.shape[1]
    heads = model_width // head_dim
    return pl.pallas_call(
        functools.partial(cross_forward_kernel, scale=1.0 / math.sqrt(head_dim), valid=valid),
        out_shape=[
            jax.ShapeDtypeStruct((tokens, model_width), jnp.bfloat16),
            jax.ShapeDtypeStruct((tokens, model_width), jnp.bfloat16),
            jax.ShapeDtypeStruct((heads, tokens, 1), jnp.float32),
        ],
        compiler_params=pltpu.CompilerParams(vmem_limit_bytes=40 * 1024 * 1024),
        cost_estimate=pl.CostEstimate(
            flops=4 * tokens * text.shape[1] * model_width,
            bytes_accessed=2 * text.size + 8 * pre.size,
            transcendentals=heads * tokens * text.shape[1],
        ),
        name="cross_forward",
    )(pre, text, gain, shift, cos_now, sin_now)


def cross_backward_kernel(
    query_ref,
    text_ref,
    totals_ref,
    grad_ref,
    pre_ref,
    gain_ref,
    cos_ref,
    sin_ref,
    pre_grad_ref,
    text_grad_ref,
    sums_ref,
    *,
    scale,
    valid,
):
    low = jnp.bfloat16
    head_dim = cos_ref.shape[1]
    ways = text_ref.shape[0]
    count = query_ref.shape[1] // head_dim // ways
    width = count * head_dim
    cos_now, sin_now = cos_ref[...], sin_ref[...]
    backs, sums = [], 0.0
    for way in range(ways):
        text = text_ref[way]
        text_grads = [None] * (2 * count)
        for one in range(count):
            head = way * count + one
            lanes = slice(head * head_dim, (head + 1) * head_dim)
            query = query_ref[:, lanes]
            grad = grad_ref[:, lanes]
            keys_now = text[:, one * head_dim : (one + 1) * head_dim]
            values_now = text[:, width + one * head_dim : width + (one + 1) * head_dim]
            probs = jnp.exp(contract_cols(query, keys_now) * scale - totals_ref[head])
            column = lax.broadcasted_iota(jnp.int32, probs.shape, 1)
            probs = jnp.where(column < valid, probs, 0.0)
            weighted = probs * contract_cols(grad, values_now)
            scores_grad = weighted - probs * jnp.sum(weighted, -1, keepdims=True)
            scores_low = (scores_grad * scale).astype(low)
            back, gain_sum, shift_sum = norm_turn_back(
                matmul(scores_low, keys_now), pre_ref[:, lanes], gain_ref[...], cos_now, sin_now
            )
            backs.append(back)
            sums += jnp.concatenate([gain_sum, shift_sum], 0)
            text_grads[one] = contract_rows(scores_low, query)
            text_grads[count + one] = contract_rows(probs.astype(low), grad)
        text_grad_ref[way] = jnp.concatenate(text_grads, 1).astype(low)
    pre_grad_ref[...] = jnp.concatenate(backs, 1).astype(low)
    sums_ref[...] = sums


def cross_backward(query, text, totals, grad, pre, gain, cos_now, sin_now, valid):
    tokens, model_width = pre.shape
    head_dim = cos_now.shape[1]
    ways, text_rows = text.shape[:2]
    return pl.pallas_call(
        functools.partial(cross_backward_kernel, scale=1.0 / math.sqrt(head_dim), valid=valid),
        out_shape=[
            jax.ShapeDtypeStruct((tokens, model_width), jnp.bfloat16),
            jax.ShapeDtypeStruct((ways, text_rows, 2 * model_width // ways), jnp.bfloat16),
            jax.ShapeDtypeStruct((2, head_dim), jnp.float32),
        ],
        compiler_params=pltpu.CompilerParams(vmem_limit_bytes=40 * 1024 * 1024),
        cost_estimate=pl.CostEstimate(
            flops=10 * tokens * text_rows * model_width,
            bytes_accessed=4 * text.size + 10 * pre.size,
            transcendentals=tokens * text_rows * model_width // head_dim,
        ),
        name="cross_backward",
    )(query, text, totals, grad, pre, gain, cos_now, sin_now)


def row_grads_kernel(left_ref, far_left_ref, right_ref, far_right_ref, out_ref):
    product = contract_rows(left_ref[0], right_ref[0])
    product += contract_rows(far_left_ref[0], far_right_ref[0])
    rows = out_ref.shape[1]
    for chip in range(out_ref.shape[0]):
        out_ref[chip] = product[chip * rows : (chip + 1) * rows].astype(out_ref.dtype)


def row_grads(lefts, rights, owners):
    count, tokens, width = lefts.shape
    rows = width // owners
    core = lax.axis_index("fsdp") % 2
    by_core = lefts.reshape(count, tokens, owners // 2, 2, rows).transpose(3, 0, 1, 2, 4)
    by_core = by_core.reshape(2, count, tokens, width // 2)
    near = lax.dynamic_index_in_dim(by_core, core, 0, False)
    far = swap_cores(lax.dynamic_index_in_dim(by_core, 1 - core, 0, False))
    left_spec = pl.BlockSpec((1, tokens, width // 2), lambda i: (i, 0, 0))
    right_spec = pl.BlockSpec((1, tokens, width), lambda i: (i, 0, 0))
    return pl.pallas_call(
        row_grads_kernel,
        grid=(count,),
        in_specs=[left_spec, left_spec, right_spec, right_spec],
        out_specs=pl.BlockSpec((owners // 2, rows, width), lambda i: (0, 0, i)),
        out_shape=jax.ShapeDtypeStruct((owners // 2, rows, count * width), jnp.bfloat16),
        compiler_params=pltpu.CompilerParams(vmem_limit_bytes=48 * 1024 * 1024),
        cost_estimate=pl.CostEstimate(
            flops=2 * count * tokens * width * width,
            bytes_accessed=2 * count * (width * width // 2 + 3 * tokens * width),
            transcendentals=0,
        ),
        name="row_grads",
    )(near, far, rights, swap_cores(rights))


def side_by_side(pieces):
    return jnp.concatenate([piece.astype(jnp.float32) for piece in pieces], 1)


def pack_kernel(normed_ref, grads_ref, packed_ref, text_ref, small_ref, out_ref):
    owners, rows = text_ref.shape[:2]
    product = contract_rows(normed_ref[...], grads_ref[...])
    count = product.shape[0] // owners
    folds = rows // count
    lanes = product.shape[1] // folds
    for owner in range(owners):
        skip = product[owner * count : (owner + 1) * count]
        skip = jnp.concatenate(
            [skip[:, fold * lanes : (fold + 1) * lanes] for fold in range(folds)], 0
        )
        line = side_by_side(
            [
                skip,
                packed_ref[owner * rows : (owner + 1) * rows],
                text_ref[owner],
                small_ref[owner],
            ]
        )
        out_ref[owner % 2, owner // 2] = line.astype(out_ref.dtype)


def pack_tail(normed, grads, packed, text, small):
    owners, rows = text.shape[:2]
    lanes = 2 * text.shape[2] // 2 + packed.shape[1] + text.shape[2] + small.shape[2]
    return pl.pallas_call(
        pack_kernel,
        out_shape=jax.ShapeDtypeStruct((2, owners // 2, rows, lanes), jnp.bfloat16),
        compiler_params=pltpu.CompilerParams(vmem_limit_bytes=48 * 1024 * 1024),
        cost_estimate=pl.CostEstimate(
            flops=2 * normed.size * grads.shape[1],
            bytes_accessed=2 * normed.size + 4 * owners * rows * lanes,
            transcendentals=0,
        ),
        name="pack_tail",
    )(normed, grads, packed, text, small)


def tail_kernel(all_ref, skip_ref, packed_ref, text_ref, whole_ref, small_ref):
    ways, rows = all_ref.shape[:2]
    model_width = skip_ref.shape[1]
    width = model_width // ways

    def joined(start, count, size):
        return side_by_side(
            [all_ref[way, :, start : start + size][:count] for way in range(ways)]
        )

    count = 2 * rows // ways
    folds = rows // count
    skip = []
    for way in range(ways):
        block = all_ref[way, :, : 2 * width].astype(jnp.float32)
        skip.append(
            jnp.concatenate(
                [block[fold * count : (fold + 1) * count] for fold in range(folds)], 1
            )
        )
    skip_ref[...] = jnp.concatenate(skip, 0)
    for third in range(3):
        packed_ref[:, third * model_width : (third + 1) * model_width] = joined(
            (2 + third) * width, rows, width
        )
    for side in range(2):
        text_ref[:, side * model_width : (side + 1) * model_width] = joined(
            (5 + side) * width, text_ref.shape[0], width
        )
    whole_ref[...] = joined(7 * width, rows, 3 * width)
    total = all_ref[0, :, 10 * width :].astype(jnp.float32)
    for way in range(1, ways):
        total += all_ref[way, :, 10 * width :].astype(jnp.float32)
    small_ref[...] = total


def lay_tail(blocks, text_rows):
    ways, rows, lanes = blocks.shape
    width = 2 * rows
    model_width = ways * width
    return pl.pallas_call(
        tail_kernel,
        out_shape=[
            jax.ShapeDtypeStruct((2 * rows, model_width), jnp.float32),
            jax.ShapeDtypeStruct((rows, 3 * model_width), jnp.float32),
            jax.ShapeDtypeStruct((text_rows, 2 * model_width), jnp.float32),
            jax.ShapeDtypeStruct((rows, 3 * model_width), jnp.float32),
            jax.ShapeDtypeStruct((rows, lanes - 10 * width), jnp.float32),
        ],
        compiler_params=pltpu.CompilerParams(vmem_limit_bytes=40 * 1024 * 1024),
        name="lay_tail",
    )(blocks)


def skip_back_kernel(grad_ref, first_ref, second_ref, out_ref):
    grad = grad_ref[...]
    halves = [contract_cols(grad, half_ref[...]) for half_ref in (first_ref, second_ref)]
    rows = grad.shape[1] // 16
    out_ref[...] = side_by_side(
        [half[:, i * rows : (i + 1) * rows] for i in range(16) for half in halves]
    )


def skip_back(grad_low, first_rows):
    tokens, model_width = grad_low.shape
    return pl.pallas_call(
        skip_back_kernel,
        grid=(1,),
        in_specs=[
            pl.BlockSpec((tokens, model_width), lambda i: (0, 0)),
            pl.BlockSpec((model_width, model_width), lambda i: (0, 0)),
            pl.BlockSpec((model_width, model_width), lambda i: (0, 1)),
        ],
        out_specs=pl.BlockSpec((tokens, 2 * model_width), lambda i: (0, 0)),
        out_shape=jax.ShapeDtypeStruct((tokens, 2 * model_width), jnp.float32),
        compiler_params=pltpu.CompilerParams(vmem_limit_bytes=48 * 1024 * 1024),
        cost_estimate=pl.CostEstimate(
            flops=4 * tokens * model_width * model_width,
            bytes_accessed=4 * model_width * (model_width + 2 * tokens),
            transcendentals=0,
        ),
        name="skip_back",
    )(grad_low, first_rows, first_rows)


def units_kernel(all_ref, up_ref, down_ref):
    ways = all_ref.shape[0]
    rows, hidden = up_ref.shape
    units = hidden // ways
    owners = 16
    own = units // owners
    for owner in range(owners):
        start = owner * ways * own
        up_ref[:, start : start + ways * own] = side_by_side(
            [all_ref[way, :rows, owner * own : (owner + 1) * own] for way in range(ways)]
        )
    model_width = down_ref.shape[1]
    split = min(units, model_width)
    for way in range(ways):
        place = slice(way * own, (way + 1) * own)
        down_ref[place, :split] = all_ref[way, :own, units : units + split].astype(jnp.float32)
        if split < model_width:
            down_ref[place, split:] = all_ref[
                way, own : 2 * own, units : units + model_width - split
            ].astype(jnp.float32)


def lay_units(blocks, rows, model_width):
    ways, lines, lanes = blocks.shape
    units = lanes // 2
    return pl.pallas_call(
        units_kernel,
        out_shape=[
            jax.ShapeDtypeStruct((rows, ways * units), jnp.float32),
            jax.ShapeDtypeStruct((ways * units // 16, model_width), jnp.float32),
        ],
        compiler_params=pltpu.CompilerParams(vmem_limit_bytes=40 * 1024 * 1024),
        name="lay_units",
    )(blocks)


def fold_down(part, units, lines):
    first = part[..., :units]
    rest = part[..., units:]
    pad = [(0, 0)] * (part.ndim - 1) + [(0, units - rest.shape[-1])]
    both = jnp.concatenate([first, jnp.pad(rest, pad)], -2)
    return fit_rows(both, lines)


def fit_rows(part, lines):
    pad = [(0, 0)] * part.ndim
    pad[-2] = (0, lines - part.shape[-2])
    return jnp.pad(part, pad)


def swap(blocks, axis_name):
    return lax.all_to_all(blocks, axis_name, split_axis=0, concat_axis=0, tiled=True)


def spread(part, axis_name):
    size = lax.axis_size(axis_name)
    return swap(jnp.broadcast_to(part[None], (size,) + part.shape), axis_name)


def grid_place():
    index = lax.axis_index("seq")
    return index // 4, index % 4


def grid_send(value, pair, step):
    links = [(i, ((i // 4) ^ pair) * 4 + (i + step) % 4) for i in range(8)]
    return lax.ppermute(value, "seq", links)


def gather_tokens(part):
    pair, ring = grid_place()
    mate = grid_send(part, 1, 0)
    below = grid_send(part, 0, 1)
    above = grid_send(part, 0, -1)
    far = grid_send(part, 0, 2)
    mate_below = grid_send(mate, 0, 1)
    mate_above = grid_send(mate, 0, -1)
    mate_far = grid_send(far, 1, 0)
    here, there = pair * 4, (1 - pair) * 4
    buffer = jnp.zeros((8,) + part.shape, part.dtype)
    for one, spot in (
        (part, here + ring),
        (mate, there + ring),
        (below, here + (ring + 3) % 4),
        (above, here + (ring + 1) % 4),
        (far, here + (ring + 2) % 4),
        (mate_below, there + (ring + 3) % 4),
        (mate_above, there + (ring + 1) % 4),
        (mate_far, there + (ring + 2) % 4),
    ):
        buffer = lax.dynamic_update_index_in_dim(buffer, one, spot, 0)
    return buffer.reshape((-1,) + part.shape[1:])


def gather_behind(part):
    return spread(part, "seq").reshape((-1,) + part.shape[1:])


def sum_tokens(partial):
    low = jnp.bfloat16
    blocks = partial.astype(low).reshape((8, -1) + partial.shape[1:])
    pair, ring = grid_place()

    def meant(mate, step):
        spot = jnp.where(mate, 1 - pair, pair) * 4 + (ring + step) % 4
        return lax.dynamic_index_in_dim(blocks, spot, 0, False)

    def total(*parts):
        return sum(part.astype(jnp.float32) for part in parts)

    far_mate = grid_send(meant(True, 2), 1, 0)
    mate_below = grid_send(meant(True, 1), 0, 1)
    mate_above = grid_send(meant(True, 3), 0, -1)
    below = grid_send(meant(False, 1), 0, 1)
    above = grid_send(meant(False, 3), 0, -1)
    far = grid_send(total(meant(False, 2), far_mate).astype(low), 0, 2)
    mate = grid_send(total(meant(True, 0), mate_below, mate_above).astype(low), 1, 0)
    return total(meant(False, 0), below, above, far, mate)


def sum_behind(partial):
    blocks = partial.astype(jnp.bfloat16).reshape((8, -1) + partial.shape[1:])
    return jnp.sum(swap(blocks, "seq").astype(jnp.float32), 0)


def column_blocks(values):
    size = lax.axis_size("seq")
    rows = values.shape[0]
    return values.reshape(rows, size, -1).transpose(1, 0, 2)


def own_columns(weight, groups, size, place):
    rows = weight.shape[0]
    parts = weight.reshape(rows, groups, size, -1)
    taken = lax.dynamic_slice_in_dim(parts, place, 1, 2)
    return taken.reshape(rows, -1)


def after(values, *others):
    waits = [other[(0,) * other.ndim].astype(jnp.float32) * 0.0 for other in others]
    return values + sum(waits).astype(values.dtype)


def core_groups(owners):
    return [list(range(0, owners, 2)), list(range(1, owners, 2))]


def swap_cores(value):
    return lax.ppermute(value, "fsdp", [(i, i ^ 1) for i in range(lax.axis_size("fsdp"))])


def sum_cores(by_core):
    core = lax.axis_index("fsdp") % 2
    kept = lax.dynamic_index_in_dim(by_core, core, 0, False)
    arrived = swap_cores(lax.dynamic_index_in_dim(by_core, 1 - core, 0, False))
    return (kept.astype(jnp.float32) + arrived.astype(jnp.float32)).astype(jnp.bfloat16)


def scatter_chips(by_chip):
    return lax.psum_scatter(
        by_chip,
        "fsdp",
        scatter_dimension=0,
        axis_index_groups=core_groups(2 * by_chip.shape[0]),
        tiled=False,
    )


def sum_owners(by_core):
    chip = sum_cores(by_core)
    swapped = lax.all_to_all(
        chip,
        "fsdp",
        split_axis=0,
        concat_axis=0,
        axis_index_groups=core_groups(2 * chip.shape[0]),
        tiled=True,
    )
    return jnp.sum(swapped.astype(jnp.float32), 0)


def heads_first(values, head_dim):
    rows = values.shape[0]
    return values.reshape(rows, -1, head_dim).transpose(1, 0, 2)


def heads_last(values):
    return values.transpose(1, 0, 2).reshape(values.shape[1], -1)


def local(
    latent,
    skip_input,
    text_tokens,
    condition,
    positions,
    cotangent,
    skip_gain,
    skip_shift,
    skip_weight,
    skip_bias,
    mod_weight,
    mod_bias,
    norm1_gain,
    norm1_shift,
    qkv_weight,
    qkv_bias,
    head_gains,
    head_shifts,
    attn_weight,
    attn_bias,
    norm3_gain,
    norm3_shift,
    cross_q_weight,
    cross_q_bias,
    cross_kv_weight,
    cross_kv_bias,
    cross_weight,
    cross_bias,
    norm2_gain,
    norm2_shift,
    fc1_weight,
    fc1_bias,
    fc2_weight,
    fc2_bias,
):
    ways = lax.axis_size("seq")
    owners = lax.axis_size("fsdp")
    place = lax.axis_index("seq")
    head_dim = head_gains.shape[1]
    tokens, model_width = latent.shape[1:]
    width = model_width // ways
    low = jnp.bfloat16
    gain_table = head_gains.astype(jnp.float32)
    shift_table = head_shifts.astype(jnp.float32)
    cos_own, sin_own = turn_tables(positions, head_dim)

    own_rows = model_width // owners
    packed_own = own_columns(qkv_weight, 3, ways, place)
    first_own = jnp.concatenate(
        [skip_weight[:own_rows], skip_weight[own_rows:], packed_own], 1
    )
    first_rows = lax.all_gather(first_own, "fsdp", axis=0, tiled=True)
    kv_own = own_columns(cross_kv_weight, 2, ways, place)
    second_own = jnp.concatenate([attn_weight, cross_q_weight, cross_weight], 1)
    unit_rows = fc2_weight.shape[0] // ways
    down_own = lax.dynamic_slice_in_dim(fc2_weight, place * unit_rows, unit_rows, 0)
    up_own = own_columns(fc1_weight, owners, ways, place)
    units = up_own.shape[1]
    lines = max(own_rows, 2 * unit_rows)
    third_own = jnp.concatenate(
        [fit_rows(up_own, lines), fold_down(down_own, units, lines)], 1
    )
    lifted_f, silu_pull = jax.vjp(jax.nn.silu, condition.astype(jnp.float32))
    lifted = lifted_f.astype(low)
    vectors = (
        skip_gain,
        skip_shift,
        skip_bias,
        mod_bias,
        norm1_gain,
        norm1_shift,
        qkv_bias,
        attn_bias,
        norm3_gain,
        norm3_shift,
        cross_q_bias,
        cross_kv_bias,
        cross_bias,
        norm2_gain,
        norm2_shift,
        fc1_bias,
        fc2_bias,
    )
    vector_own = jnp.concatenate(vectors)
    vector_all = swap(
        jnp.concatenate(
            [
                jnp.broadcast_to(vector_own[None], (owners, vector_own.shape[0])),
                lifted.reshape(owners, own_rows),
            ],
            1,
        ),
        "fsdp",
    )
    pieces = []
    start = 0
    for one_vector in vectors:
        size = one_vector.shape[0]
        pieces.append(vector_all[:, start : start + size].reshape(-1).astype(jnp.float32))
        start += size
    lifted_own = vector_all[:, start:]
    (
        sk_gain,
        sk_shift,
        sk_bias,
        md_bias,
        one_gain,
        one_shift,
        pk_bias,
        at_bias,
        three_gain,
        three_shift,
        cq_bias,
        kv_bias,
        cr_bias,
        two_gain,
        two_shift,
        up_bias,
        down_bias,
    ) = pieces
    pk_bias_own = own_columns(pk_bias[None], 3, ways, place)[0]
    kv_bias_own = own_columns(kv_bias[None], 2, ways, place)[0]
    up_bias_own = own_columns(up_bias[None], owners, ways, place)[0]
    shift_row = (
        jnp.sum(swap(matmul(lifted_own, mod_weight), "fsdp"), 0, keepdims=True) + md_bias
    )

    kv_weight = spread(after(kv_own, vector_all), "fsdp").reshape(-1, 2 * width)
    text_now = text_tokens[0]
    text_count = text_now.shape[0]
    text_packed = matmul(text_now, kv_weight) + kv_bias_own
    text_keys_f, tk_pull = jax.vjp(
        lambda values_in, gains_in: head_norm(values_in, gains_in[3], 0.0, head_dim),
        text_packed[:, :width],
        gain_table,
    )
    text_own = jnp.concatenate(
        [text_keys_f.astype(low), text_packed[:, width:].astype(low)], 1
    )
    text_rows = text_count + -text_count % 16
    place_rows = max(text_rows, tokens)
    text_own = jnp.concatenate(
        [
            fit_rows(text_own, place_rows),
            fit_rows(positions.astype(low), place_rows),
        ],
        1,
    )
    text_spread = spread(text_own, "seq")
    cos_all, sin_all = turn_tables(
        text_spread[:, :tokens, 2 * width :].reshape(-1, 2), head_dim
    )
    joined = jnp.concatenate([latent[0], skip_input[0]], 1).astype(jnp.float32)
    normed_f, skip_pull = jax.vjp(layer_norm, joined, sk_gain, sk_shift)
    normed = normed_f.astype(low)
    normed_halves = normed.reshape(tokens, owners, 2, own_rows).transpose(2, 0, 1, 3)
    normed_halves = normed_halves.reshape(2, tokens, model_width)
    normed_rows = normed.reshape(tokens, owners, ways, -1).transpose(2, 0, 1, 3)
    normed_rows = normed_rows.reshape(ways, tokens, -1)
    normed_halves = after(normed_halves, shift_row, text_spread)
    stream_zero = (
        matmul(normed_halves[0], first_rows[:, :model_width])
        + matmul(normed_halves[1], first_rows[:, model_width : 2 * model_width])
        + sk_bias
    )

    pk_weight = first_rows[:, 2 * model_width :]
    second_rows = lax.all_gather(after(second_own, stream_zero), "fsdp", axis=0, tiled=True)
    at_weight = second_rows[:, :model_width]
    cq_weight = second_rows[:, model_width : 2 * model_width]
    cr_weight = second_rows[:, 2 * model_width :]
    entry_f, one_pull = jax.vjp(layer_norm, stream_zero, one_gain, one_shift)
    entry = (entry_f + shift_row).astype(low)

    entry_all = gather_tokens(entry)

    mixed_h, heads_h, packed_pre, self_totals = self_forward(
        entry_all, pk_weight, pk_bias_own[None], gain_table, shift_table, cos_all, sin_all
    )
    all_tokens = entry_all.shape[0]

    def to_heads(values):
        return swap(column_blocks(values), "seq").reshape(all_tokens, -1)

    mixed_normed = swap(
        jnp.concatenate([mixed_h.reshape(ways, tokens, width), normed_rows], 2), "seq"
    )
    mixed = mixed_normed[:, :, :width].transpose(1, 0, 2).reshape(tokens, model_width)
    normed_own = mixed_normed[:, :, width:].reshape(all_tokens, -1)
    third_rows = lax.all_gather(after(third_own, packed_pre), "fsdp", axis=0, tiled=False)
    up_weight = third_rows[:, :own_rows, :units].reshape(model_width, units)
    down_weight = jnp.concatenate(
        [
            third_rows[:, :unit_rows, units : units + min(units, model_width)],
            third_rows[:, unit_rows : 2 * unit_rows, units : units + max(model_width - units, 0)],
        ],
        2,
    ).reshape(units, model_width)
    stream_one = stream_zero + matmul(mixed, at_weight) + at_bias

    cross_in_f, three_pull = jax.vjp(layer_norm, stream_one, three_gain, three_shift)
    cross_in = cross_in_f.astype(low)
    grad_all = lax.all_gather(after(cotangent[0], cross_in), "seq", axis=0, tiled=True)
    cross_pre = matmul(cross_in, cq_weight) + cq_bias
    cross_mixed, cross_query, cross_totals = cross_forward(
        cross_pre, text_spread, gain_table[2:3], shift_table[2:3], cos_own, sin_own, text_count
    )
    stream_two = stream_one + matmul(cross_mixed, cr_weight) + cr_bias

    mlp_in_f, two_pull = jax.vjp(layer_norm, stream_two, two_gain, two_shift)
    mlp_all = gather_tokens(mlp_in_f.astype(low))
    hidden_pre = matmul(mlp_all, up_weight) + after(up_bias_own, grad_all)
    hidden_f, gelu_pull = jax.vjp(
        lambda values_in: jax.nn.gelu(values_in, approximate=True), hidden_pre
    )
    hidden = hidden_f.astype(low)
    out_partial = matmul(hidden, down_weight).astype(low)
    grad_three = cotangent[0].astype(jnp.float32)
    down_bias_grad = column_sums(cotangent[0])
    pre_grad = gelu_pull(contract_cols(grad_all, down_weight))[0].astype(low)
    up_bias_grad = column_sums(pre_grad)
    mlp_in_grad = sum_tokens(contract_cols(pre_grad, up_weight))
    down_grad = contract_rows(hidden, grad_all).astype(low)
    up_grad = contract_rows(mlp_all, pre_grad).astype(low)
    mlp_grads = jnp.concatenate(
        [
            fit_rows(up_grad.reshape(owners, own_rows, units), lines),
            fold_down(down_grad.reshape(owners, unit_rows, model_width), units, lines),
        ],
        2,
    )
    mlp_grads = mlp_grads.reshape(owners // 2, 2, lines, 2 * units).transpose(1, 0, 2, 3)
    mlp_owned = scatter_chips(sum_cores(mlp_grads))
    mlp_in_grad = after(mlp_in_grad, mlp_grads)
    stream_part, two_gain_grad, two_shift_grad = two_pull(mlp_in_grad)
    stream_grad = grad_three + stream_part

    grad_low = stream_grad.astype(low)
    cr_bias_grad = column_sums(grad_low)
    cross_mixed_grad = contract_cols(grad_low, cr_weight).astype(low)

    cross_pre_low, text_parts, cross_sums = cross_backward(
        cross_query,
        text_spread,
        cross_totals,
        cross_mixed_grad,
        cross_pre,
        gain_table[2:3],
        cos_own,
        sin_own,
        text_count,
    )
    text_kv_grad = jnp.sum(swap(text_parts, "seq").astype(jnp.float32), 0)[:text_count]
    cross_out_low = grad_low
    cq_bias_grad = column_sums(cross_pre_low)
    stream_part, three_gain_grad, three_shift_grad = three_pull(
        contract_cols(cross_pre_low, cq_weight)
    )
    stream_grad = stream_grad + stream_part

    grad_low = stream_grad.astype(low)
    at_bias_grad = column_sums(grad_low)
    mixed_grad = contract_cols(grad_low, at_weight).astype(low)
    mixed_back = to_heads(after(mixed_grad, text_kv_grad))
    whole_grads = row_grads(
        jnp.stack([mixed, cross_in, cross_mixed]),
        after(jnp.stack([grad_low, cross_pre_low, cross_out_low]), mlp_owned),
        owners,
    )
    row_owned = scatter_chips(whole_grads)
    mixed_back = after(mixed_back, whole_grads)
    key_pre_grad, gains_from_text = tk_pull(text_kv_grad[:, :width])
    text_grad_low = jnp.concatenate(
        [key_pre_grad.astype(low), text_kv_grad[:, width:].astype(low)], 1
    )
    kv_weight_grad = contract_rows(text_now, text_grad_low)
    kv_bias_grad = column_sums(text_grad_low)
    text_part = contract_cols(text_grad_low, kv_weight)
    text_part = jnp.pad(text_part.astype(low), ((0, -text_count % (8 * ways)), (0, 0)))
    text_sum = sum_behind(text_part)
    packed_grad, self_sums = self_backward(
        heads_h, self_totals, mixed_back, packed_pre, gain_table, cos_all, sin_all
    )
    pk_weight_grad = contract_rows(entry_all, packed_grad)
    entry_grad = sum_tokens(contract_cols(packed_grad, pk_weight))
    pk_bias_grad = column_sums(packed_grad)
    gains_from_self = jnp.concatenate(
        [self_sums[0::2], cross_sums[:1], jnp.zeros_like(cross_sums[:1])], 0
    )
    shifts_now = jnp.concatenate([self_sums[1::2], cross_sums[1:]], 0)
    entry_grad = after(entry_grad, pk_weight_grad)
    shift_part = jnp.sum(entry_grad, 0)
    stream_three = stream_two + sum_tokens(after(out_partial, entry_grad)) + down_bias
    layer_out = stream_three.astype(low)[None]
    stream_part, one_gain_grad, one_shift_grad = one_pull(entry_grad)
    stream_grad = stream_grad + stream_part

    grad_low = stream_grad.astype(low)
    sk_bias_grad = column_sums(grad_low)
    shift_row_own = fit_rows(shift_part.astype(low)[None], 16)
    text_total = gather_behind(text_sum.astype(low))[:text_count]
    tail_grads = spread(jnp.concatenate([after(grad_low, text_total), shift_row_own], 0), "seq")
    grad_rows = tail_grads[:, :tokens].reshape(all_tokens, model_width)
    shift_total = jnp.sum(tail_grads[:, tokens].astype(jnp.float32), 0)
    joined_grad, sk_gain_grad, sk_shift_grad = skip_pull(skip_back(grad_low, first_rows))

    def placed(own, groups):
        parts = jnp.zeros((groups, ways, own.shape[0] // groups), jnp.float32)
        parts = lax.dynamic_update_slice_in_dim(parts, own.reshape(groups, 1, -1), place, 1)
        return parts.reshape(-1)

    vector_grads = (
        sk_gain_grad,
        sk_shift_grad,
        sk_bias_grad,
        one_gain_grad,
        one_shift_grad,
        placed(pk_bias_grad, 3),
        at_bias_grad,
        three_gain_grad,
        three_shift_grad,
        cq_bias_grad,
        placed(kv_bias_grad, 2),
        cr_bias_grad,
        two_gain_grad,
        two_shift_grad,
        placed(up_bias_grad, owners),
        down_bias_grad,
    )
    table_grads = jnp.concatenate(
        [
            (gains_from_text + gains_from_self).reshape(-1),
            shifts_now.reshape(-1),
        ]
    )
    split_three = [part.reshape(owners, -1) for part in vector_grads]
    pk_at = 5
    pk_thirds = placed(pk_bias_grad, 3).reshape(3, model_width)
    split_three[pk_at : pk_at + 1] = [
        pk_thirds[:2].reshape(owners, -1),
        pk_thirds[2].reshape(owners, -1),
    ]
    split_three.append(jnp.broadcast_to(table_grads[None], (owners, table_grads.shape[0])))
    summed_sizes = [part.shape[1] for part in split_three]
    row_blocks = after(column_blocks(row_owned), shift_total)
    row_sum = jnp.sum(swap(row_blocks, "seq").astype(jnp.float32), 0)
    vector_rows = after(jnp.concatenate(split_three, 1).astype(low), row_sum, stream_three)
    vector_pad = -vector_rows.shape[1] % own_rows
    vector_rows = jnp.pad(vector_rows, ((0, 0), (0, vector_pad)))
    latent_mark = jnp.arange(owners) == lax.axis_index("fsdp")
    shift_mine = jnp.where(latent_mark[:, None], shift_total.astype(low), jnp.zeros((), low))
    shift_mine = jnp.broadcast_to(
        shift_mine.reshape(1, own_rows, -1), (owners, own_rows, owners * owners)
    )
    tail_sum = sum_owners(
        pack_tail(
            normed_own,
            grad_rows,
            pk_weight_grad,
            fit_rows(kv_weight_grad.astype(low).reshape(owners, -1, 2 * width), own_rows),
            jnp.concatenate([vector_rows.reshape(owners, own_rows, -1), shift_mine], 2),
        )
    ).astype(low)
    shift_all = tail_sum[:, -owners * owners :].reshape(owners, model_width)
    shift_all = shift_all.astype(jnp.float32)
    tail_sum = tail_sum[:, : -owners * owners]

    mlp_all_grads = lax.all_gather(after(mlp_owned, row_owned), "seq", axis=0, tiled=False)
    lead = 7 * width
    tail_all = spread(
        jnp.concatenate([tail_sum[:, :lead], row_sum.astype(low), tail_sum[:, lead:]], 1), "seq"
    )
    sk_total, pk_total, kv_total, row_total, small_total = lay_tail(
        tail_all, cross_kv_weight.shape[0]
    )
    at_total = row_total[:, :model_width]
    cq_total = row_total[:, model_width : 2 * model_width]
    cr_total = row_total[:, 2 * model_width :]
    small_total = small_total.reshape(-1)
    vector_totals = []
    start = 0
    for size in summed_sizes:
        vector_totals.append(small_total[start : start + size])
        start += size
    table_total = vector_totals.pop()
    gains_total = table_total[: gain_table.size].reshape(gain_table.shape)
    shifts_total = table_total[gain_table.size :].reshape(shift_table.shape)
    md_weight_grad = lax.dot_general(
        lifted_own.astype(jnp.float32),
        shift_all,
        (((0,), (0,)), ((), ())),
        precision=lax.Precision.HIGHEST,
        preferred_element_type=jnp.float32,
    )
    md_bias_grad = lax.dynamic_slice_in_dim(
        jnp.sum(shift_all, 0), lax.axis_index("fsdp") * own_rows, own_rows, 0
    )
    lifted_part = lax.dot_general(
        shift_all,
        mod_weight.astype(jnp.float32),
        (((1,), (1,)), ((), ())),
        precision=lax.Precision.HIGHEST,
        preferred_element_type=jnp.float32,
    )
    lifted_grad = swap(after(lifted_part, tail_all, mlp_all_grads), "fsdp").reshape(1, model_width)
    condition_grad = silu_pull(lifted_grad)[0]

    up_total, down_total = lay_units(mlp_all_grads, own_rows, model_width)
    (
        sk_gain_total,
        sk_shift_total,
        sk_bias_total,
        one_gain_total,
        one_shift_total,
        pk_bias_total,
        value_bias_total,
        at_bias_total,
        three_gain_total,
        three_shift_total,
        cq_bias_total,
        kv_bias_total,
        cr_bias_total,
        two_gain_total,
        two_shift_total,
        up_bias_total,
        down_bias_total,
    ) = vector_totals
    return (
        layer_out,
        joined_grad[:, :model_width].astype(low)[None],
        joined_grad[:, model_width:].astype(low)[None],
        text_total[None],
        condition_grad,
        sk_gain_total,
        sk_shift_total,
        sk_total,
        sk_bias_total,
        md_weight_grad,
        md_bias_grad,
        one_gain_total,
        one_shift_total,
        pk_total,
        pk_bias_total,
        value_bias_total,
        gains_total,
        shifts_total,
        at_total,
        at_bias_total,
        three_gain_total,
        three_shift_total,
        cq_total,
        cq_bias_total,
        kv_total,
        kv_bias_total,
        cr_total,
        cr_bias_total,
        two_gain_total,
        two_shift_total,
        up_total,
        up_bias_total,
        down_total,
        down_bias_total,
    )


def solution(mesh):
    in_specs = (
        P("fsdp", "seq", None),
        P("fsdp", "seq", None),
        P("fsdp", None, None),
        P("fsdp", None),
        P("seq", None),
        P("fsdp", "seq", None),
        P("fsdp"),
        P("fsdp"),
        P("fsdp", None),
        P("fsdp"),
        P("fsdp", None),
        P("fsdp"),
        P("fsdp"),
        P("fsdp"),
        P("fsdp", None),
        P("fsdp"),
        P(),
        P(),
        P("fsdp", None),
        P("fsdp"),
        P("fsdp"),
        P("fsdp"),
        P("fsdp", None),
        P("fsdp"),
        P("fsdp", None),
        P("fsdp"),
        P("fsdp", None),
        P("fsdp"),
        P("fsdp"),
        P("fsdp"),
        P("fsdp", None),
        P("fsdp"),
        P("fsdp", None),
        P("fsdp"),
    )
    out_specs = (
        P("fsdp", "seq", None),
        P("fsdp", "seq", None),
        P("fsdp", "seq", None),
        P("fsdp", None, None),
        P("fsdp", None),
        P("fsdp"),
        P("fsdp"),
        P("fsdp", None),
        P("fsdp"),
        P("fsdp", None),
        P("fsdp"),
        P("fsdp"),
        P("fsdp"),
        P("fsdp", None),
        P("fsdp"),
        P("fsdp"),
        P(),
        P(),
        P("fsdp", None),
        P("fsdp"),
        P("fsdp"),
        P("fsdp"),
        P("fsdp", None),
        P("fsdp"),
        P("fsdp", None),
        P("fsdp"),
        P("fsdp", None),
        P("fsdp"),
        P("fsdp"),
        P("fsdp"),
        P("fsdp", None),
        P("fsdp"),
        P("fsdp", None),
        P("fsdp"),
    )
    return jax.shard_map(local, mesh=mesh, in_specs=in_specs, out_specs=out_specs, check_vma=False)
```
